128 devices in a mesh: fsdp: 4 (over z), ctx: 4 (over x), tp: 8 (over y, core).
Axes of the slice: x: 4, y: 4, z: 4, core: 2. Of those that a mesh axis runs over, the one named last changes fastest.
Arguments:
- inputs: bfloat16 [4, 1024, 2048], P('fsdp', 'ctx'), may hold values from -6 to 6
- cotangent: bfloat16 [4, 1024, 2048], P('fsdp', 'ctx'), may hold values from -6 to 6
- segment_ids: int32 [4, 1024], P('fsdp'), may hold values from 0 to 2, as said below
- w_query: bfloat16 [2, 2048, 1024], P(None, ('fsdp', 'ctx'), 'tp'), may hold values from -0.125 to 0.125
- w_shared: bfloat16 [2, 2048, 1024], P(None, ('fsdp', 'ctx')), may hold values from -0.125 to 0.125
- w_zx: bfloat16 [2, 2048, 2, 3072], P(None, ('fsdp', 'ctx'), None, 'tp'), may hold values from -0.125 to 0.125
- w_dt: bfloat16 [2, 2048, 48], P(None, ('fsdp', 'ctx'), 'tp'), may hold values from -0.125 to 0.125
- w_attn_out: bfloat16 [2, 2048, 1024], P(None, ('fsdp', 'ctx'), 'tp'), may hold values from -0.75 to 0.75
- w_ssm_out: bfloat16 [2, 2048, 3072], P(None, ('fsdp', 'ctx'), 'tp'), may hold values from -0.109375 to 0.109375
- w_gate: bfloat16 [2, 2048, 4096], P(None, ('fsdp', 'ctx'), 'tp'), may hold values from -0.125 to 0.125
- w_up: bfloat16 [2, 2048, 4096], P(None, ('fsdp', 'ctx'), 'tp'), may hold values from -0.125 to 0.125
- w_down: bfloat16 [2, 2048, 4096], P(None, ('fsdp', 'ctx'), 'tp'), may hold values from -0.09375 to 0.09375
- gains: float32 [2, 2, 2048], replicated, may hold values from 0.5 to 1.5
- conv_x: float32 [2, 5, 3072], P(None, None, 'tp'), may hold values from -3 to 3
- conv_bc: float32 [2, 5, 512], replicated, may hold values from -3 to 3
- head_params: float32 [2, 3, 48], P(None, None, 'tp'), may hold values from -7 to 2
Outputs:
- layer_out: bfloat16 [4, 1024, 2048], P('fsdp', 'ctx')
- input_grad: float32 [4, 1024, 2048], P('fsdp', 'ctx')
- grad_w_query: float32 [2, 2048, 1024], P(None, ('fsdp', 'ctx'), 'tp')
- grad_w_shared: float32 [2, 2048, 1024], P(None, ('fsdp', 'ctx'))
- grad_w_zx: float32 [2, 2048, 2, 3072], P(None, ('fsdp', 'ctx'), None, 'tp')
- grad_w_dt: float32 [2, 2048, 48], P(None, ('fsdp', 'ctx'), 'tp')
- grad_w_attn_out: float32 [2, 2048, 1024], P(None, ('fsdp', 'ctx'), 'tp')
- grad_w_ssm_out: float32 [2, 2048, 3072], P(None, ('fsdp', 'ctx'), 'tp')
- grad_w_gate: float32 [2, 2048, 4096], P(None, ('fsdp', 'ctx'), 'tp')
- grad_w_up: float32 [2, 2048, 4096], P(None, ('fsdp', 'ctx'), 'tp')
- grad_w_down: float32 [2, 2048, 4096], P(None, ('fsdp', 'ctx'), 'tp')
- grad_gains: float32 [2, 2048], replicated
- grad_conv_x: float32 [2, 5, 3072], P(None, None, 'tp')
- grad_conv_bc: float32 [2, 5, 512], replicated
- grad_head_params: float32 [2, 2, 48], P(None, None, 'tp')
- grad_ffn_gains: float32 [2, 2048], replicated
- grad_skip: float32 [2, 48], P(None, 'tp')
The draws below stay inside these ranges and needn't reach their ends.
Inputs may be any that keep to these rules, and one draw needn't show every extreme that they name: `segment_ids`: each row never falls; document 1 begins within the first 256 places and ends within the last 256 places.
All inputs are finite; a program needn't handle non-finite values.
Results may differ from the reference program's by a relative error of at most 0.035.
Values may be sent and summed in bfloat16 or wider, within the bound.
No kernel may reach another device: no remote copies, remote signals or barrier semaphores. Data moves between devices by JAX's collectives and lax.ppermute only.
A program may use at most 256 MiB of HBM per device.

```python
import math
import jax
import jax.numpy as jnp
from jax import lax

D = 2048
AH = 8
KVH = 2
HD = 128
HS = 48
HP = 64
NSTATE = 256
FF = 4096
CONV = 4
LAYERS = 2
TOK_DEV = 256
XS = 3072
SHARED = 1024
SEQ_LEN = 1024
SEQS = 4


def draw_segment_ids(key, part):
    key = jax.random.fold_in(key, 11)
    first_key, second_key = jax.random.split(key)
    starts = jax.random.randint(first_key, (SEQS, 1), 1, TOK_DEV)
    ends = jax.random.randint(second_key, (SEQS, 1), SEQ_LEN - TOK_DEV + 1, SEQ_LEN)
    places = jnp.arange(SEQ_LEN, dtype=jnp.int32)[None, :]
    return (places >= starts).astype(jnp.int32) + (places >= ends).astype(jnp.int32)


def draw_head_params(key, part):
    key = jax.random.fold_in(key, 23)
    rate_key, bias_key, skip_key = jax.random.split(key, 3)
    log_rates = jax.random.uniform(rate_key, (LAYERS, HS), jnp.float32, math.log(0.005), math.log(0.5))
    biases = jax.random.uniform(bias_key, (LAYERS, HS), jnp.float32, -4.0, -2.0)
    skips = jax.random.uniform(skip_key, (LAYERS, HS), jnp.float32, 0.5, 1.5)
    return jnp.stack([log_rates, biases, skips], axis=1)


def shard_levels(own_key, shape, shards, smallest, top_value):
    level = 1.0
    for dim, parts in shards:
        draws = jax.random.uniform(jax.random.fold_in(jax.random.fold_in(own_key, 6), dim), (parts,), jnp.float32, smallest / len(shards), top_value / len(shards))
        level = level * jnp.repeat(jnp.exp(draws), shape[dim] // parts).reshape((-1,) + (1,) * (len(shape) - 1 - dim))
    return level


def scatter_about(key, shape, deviation, limit, shards=(), kind=jnp.bfloat16):
    result = jax.random.normal(key, shape, jnp.float32) * deviation
    if len(shards) > 0:
        result = shard_levels(key, shape, shards, -0.22, 0.18) * result
    return jnp.clip(result, min=-limit, max=limit).astype(kind)


def setup_inputs(seed: int = 0) -> dict:
    splits = jax.random.split(jax.random.key(seed), 17)
    return {
        "inputs": scatter_about(splits[0], (SEQS, SEQ_LEN, D), 1.0, 6.0, ((0, 4), (1, 4))),
        "cotangent": scatter_about(splits[1], (SEQS, SEQ_LEN, D), 1.0, 6.0, ((0, 4), (1, 4))),
        "segment_ids": draw_segment_ids(jax.random.fold_in(splits[16], 71), 0),
        "w_query": scatter_about(splits[3], (LAYERS, D, AH * HD), D ** -0.5, 0.125, ((1, 16), (2, 8))),
        "w_shared": scatter_about(splits[4], (LAYERS, D, SHARED), D ** -0.5, 0.125, ((1, 16),)),
        "w_zx": scatter_about(splits[5], (LAYERS, D, 2, XS), D ** -0.5, 0.125, ((1, 16), (3, 8))),
        "w_dt": scatter_about(splits[6], (LAYERS, D, HS), D ** -0.5, 0.125, ((1, 16), (2, 8))),
        "w_attn_out": scatter_about(splits[7], (LAYERS, D, AH * HD), (AH * HD // 16) ** -0.5, 0.75, ((1, 16), (2, 8))),
        "w_ssm_out": scatter_about(splits[8], (LAYERS, D, XS), XS ** -0.5, 0.109375, ((1, 16), (2, 8))),
        "w_gate": scatter_about(splits[9], (LAYERS, D, FF), D ** -0.5, 0.125, ((1, 16), (2, 8))),
        "w_up": scatter_about(splits[10], (LAYERS, D, FF), D ** -0.5, 0.125, ((1, 16), (2, 8))),
        "w_down": scatter_about(splits[11], (LAYERS, D, FF), FF ** -0.5, 0.09375, ((1, 16), (2, 8))),
        "gains": jnp.clip(1.0 + 0.1 * jax.random.normal(splits[12], (LAYERS, 2, D), jnp.float32), 0.5, 1.5),
        "conv_x": scatter_about(splits[13], (LAYERS, CONV + 1, XS), CONV ** -0.5, 3.0, ((2, 8),), jnp.float32),
        "conv_bc": scatter_about(splits[14], (LAYERS, CONV + 1, 2 * NSTATE), CONV ** -0.5, 3.0, (), jnp.float32),
        "head_params": draw_head_params(jax.random.fold_in(splits[16], 71), 0),
    }


@jax.custom_vjp
def low(v):
    return lax.optimization_barrier(v.astype(jnp.bfloat16)).astype(jnp.float32)

@jax.custom_vjp
def low_back(v):
    return v

def low_keep(v):
    return (low(v), None)

def low_pass(kept, grad):
    return (grad,)

def back_keep(v):
    return (v, None)

def back_low(kept, grad):
    return (low(grad),)
low.defvjp(low_keep, low_pass)
low_back.defvjp(back_keep, back_low)
norm_eps = 1e-05
rope_base = 100000000000.0
highest = lax.Precision.HIGHEST

def rms_norm(hidden, gain_row):
    inverse_rms = lax.rsqrt(lax.optimization_barrier(jnp.mean(hidden * hidden, axis=-1, keepdims=True)) + norm_eps)
    return hidden * inverse_rms * gain_row

def rotate(values, places, direction):
    half_width = values.shape[-1] // 2
    frequency = rope_base ** (-jnp.arange(half_width, dtype=jnp.float32) / half_width)
    angles = places.astype(jnp.float32)[:, None] * frequency[None, :]
    cosine = jnp.cos(angles)[:, None, :]
    sine_part = jnp.sin(angles)[:, None, :] * direction
    first_half = values[..., :half_width]
    second_half = values[..., half_width:]
    return jnp.concatenate([first_half * cosine - second_half * sine_part, second_half * cosine + first_half * sine_part], axis=-1)

def conv_apply(segments, extended, weight):
    length = extended.shape[-2] - (CONV - 1)
    summed = weight[CONV]
    for offset in range(CONV):
        same_doc = (segments[..., offset:offset + length] == segments[..., CONV - 1:])[..., None]
        summed = summed + jnp.where(same_doc, extended[..., offset:offset + length, :] * weight[offset], 0.0)
    return jax.nn.silu(summed)

def ssd_rates(dt_raw, params):
    step_size = jax.nn.softplus(dt_raw + params[1])
    log_decay = -jnp.exp(params[0]) * step_size
    return (step_size, log_decay)

def ssd_state(segments, seg_prev, xheads, inject, dt_raw, params):
    step_size, log_decay = ssd_rates(dt_raw, params)
    cumulative = jnp.cumsum(log_decay, axis=0)
    final_log = cumulative[-1]
    in_final = (segments == segments[-1]).astype(jnp.float32)
    weights_in = jnp.exp(final_log[None, :] - cumulative) * step_size * in_final[:, None]
    states = jnp.einsum('rh,rhp,rn->hpn', weights_in, xheads, inject, precision=highest)
    decays = jnp.exp(final_log) * (segments[-1] == seg_prev).astype(jnp.float32)
    return (decays, states)

def ssd_apply(segments, seg_prev, xheads, inject, readout, dt_raw, params, state_in):
    step_size, log_decay = ssd_rates(dt_raw, params)
    cumulative = jnp.cumsum(log_decay, axis=0)
    block_len = segments.shape[0]
    places = jnp.arange(block_len, dtype=jnp.int32)
    allowed = (places[:, None] >= places[None, :]) & (segments[:, None] == segments[None, :])
    log_gap = jnp.where(allowed[:, :, None], cumulative[:, None, :] - cumulative[None, :, :], 0.0)
    kernel = jnp.where(allowed[:, :, None], jnp.exp(log_gap), 0.0)
    intersection = jnp.dot(readout, inject.T, precision=highest)
    mixing = intersection[:, :, None] * kernel * step_size[None, :, :]
    outputs = jnp.einsum('tsh,shp->thp', mixing, xheads, precision=highest)
    carried = jnp.exp(cumulative) * (segments == seg_prev).astype(jnp.float32)[:, None]
    outputs = outputs + carried[:, :, None] * jnp.einsum('tn,hpn->thp', readout, state_in, precision=highest)
    return outputs + params[2][None, :, None] * xheads

def layer_forward(hidden, layer_weights, segments, places):
    query_weight, shared_weight, zx_weight, dt_weight, attn_weight, ssm_weight, gate_weight, up_weight, down_weight, gain_pair, conv_x_weight, conv_bc_weight, params = layer_weights
    seq_count, seq_len = segments.shape
    kv_width = KVH * HD
    normed = low(rms_norm(hidden, gain_pair[0]))
    query_raw = low_back(jnp.dot(normed, query_weight, precision=highest))
    shared = low_back(jnp.dot(normed, shared_weight, precision=highest))
    zx_proj = low_back(jnp.dot(normed, zx_weight.reshape(D, 2 * XS), precision=highest))
    dt_raw = low_back(jnp.dot(normed, dt_weight, precision=highest))
    queries = low(rotate(query_raw.reshape(seq_count, seq_len, AH, HD), places, 1.0))
    keys_rot = low(rotate(shared[..., :kv_width].reshape(seq_count, seq_len, KVH, HD), places, 1.0))
    values_low = low(shared[..., kv_width:2 * kv_width].reshape(seq_count, seq_len, KVH, HD))
    keys_rep = jnp.repeat(keys_rot, AH // KVH, axis=2)
    values_rep = jnp.repeat(values_low, AH // KVH, axis=2)
    block_rows = min(512, seq_len)
    scale_factor = HD ** (-0.5)

    def attend(block_index):
        query_block = lax.dynamic_slice_in_dim(queries, block_index * block_rows, block_rows, 1)
        query_seg = lax.dynamic_slice_in_dim(segments, block_index * block_rows, block_rows, 1)
        query_pos = block_index * block_rows + jnp.arange(block_rows, dtype=jnp.int32)
        scores = low_back(jnp.einsum('sqhd,skhd->shqk', query_block, keys_rep, precision=highest) * scale_factor)
        allowed = (query_pos[:, None] >= places[None, :])[None, None] & (query_seg[:, :, None] == segments[:, None, :])[:, None]
        masked = jnp.where(allowed, scores, -1e+30)
        top_score = lax.optimization_barrier(jnp.max(masked, axis=-1, keepdims=True))
        exponent = jnp.exp(masked - top_score)
        probability = low(exponent / lax.optimization_barrier(jnp.sum(exponent, axis=-1, keepdims=True)))
        return jnp.einsum('shqk,skhd->sqhd', probability, values_rep, precision=highest)
    blocks_out = lax.map(jax.checkpoint(attend), jnp.arange(seq_len // block_rows, dtype=jnp.int32))
    attn_heads = jnp.moveaxis(blocks_out, 0, 1).reshape(seq_count, seq_len, AH * HD)
    attn_low = low(low_back(attn_heads))
    attn_out = jnp.dot(attn_low, attn_weight.T, precision=highest)
    zgate = zx_proj[..., :XS]
    x_pre = zx_proj[..., XS:]
    bc_pre = shared[..., 2 * kv_width:]
    seg_ext = jnp.concatenate([jnp.full((seq_count, CONV - 1), -1, jnp.int32), segments], axis=1)
    x_conv = conv_apply(seg_ext, jnp.concatenate([jnp.zeros((seq_count, CONV - 1, XS), jnp.float32), x_pre], axis=1), conv_x_weight)
    bc_conv = conv_apply(seg_ext, jnp.concatenate([jnp.zeros((seq_count, CONV - 1, 2 * NSTATE), jnp.float32), bc_pre], axis=1), conv_bc_weight)
    xheads = x_conv.reshape(seq_count, seq_len, HS, HP)
    inject = bc_conv[..., :NSTATE]
    readout = bc_conv[..., NSTATE:]
    seg_before = jnp.concatenate([jnp.full((seq_count, 1), -1, jnp.int32), segments[:, :-1]], axis=1)

    def span_step(state_in, block_index):
        first_row = block_index * TOK_DEV

        def block_of(member):
            return lax.dynamic_slice_in_dim(member, first_row, TOK_DEV, 1)
        span_seg = block_of(segments)
        span_prev = block_of(seg_before)[:, 0]
        decays, states = jax.vmap(ssd_state, in_axes=(0, 0, 0, 0, 0, None))(span_seg, span_prev, block_of(xheads), block_of(inject), block_of(dt_raw), params)
        outputs = jax.vmap(ssd_apply, in_axes=(0, 0, 0, 0, 0, 0, None, 0))(span_seg, span_prev, block_of(xheads), block_of(inject), block_of(readout), block_of(dt_raw), params, state_in)
        return (decays[:, :, None, None] * state_in + states, outputs)
    final_state, span_outs = lax.scan(jax.checkpoint(span_step), jnp.zeros((seq_count, HS, HP, NSTATE), jnp.float32), jnp.arange(seq_len // TOK_DEV, dtype=jnp.int32))
    ssm_y = jnp.moveaxis(span_outs, 0, 1).reshape(seq_count, seq_len, XS)
    gated = low(ssm_y * jax.nn.silu(zgate))
    ssm_out = jnp.dot(gated, ssm_weight.T, precision=highest)
    mixed = low_back(attn_out + ssm_out)
    hidden1 = hidden + mixed
    normed2 = low(rms_norm(hidden1, gain_pair[1]))
    gate_val = low_back(jnp.dot(normed2, gate_weight, precision=highest))
    up_val = low_back(jnp.dot(normed2, up_weight, precision=highest))
    activation = low(jax.nn.silu(gate_val) * up_val)
    ffn_out = low_back(jnp.dot(activation, down_weight.T, precision=highest))
    return hidden1 + ffn_out

def reference(inputs, cotangent, segment_ids, w_query, w_shared, w_zx, w_dt, w_attn_out, w_ssm_out, w_gate, w_up, w_down, gains, conv_x, conv_bc, head_params):
    places = jnp.arange(SEQ_LEN, dtype=jnp.int32)
    weights = tuple((member.astype(jnp.float32) for member in (w_query, w_shared, w_zx, w_dt, w_attn_out, w_ssm_out, w_gate, w_up, w_down, gains, conv_x, conv_bc, head_params)))

    def forward(hidden, weight_set):
        for layer_index in range(LAYERS):
            hidden = layer_forward(hidden, tuple((member[layer_index] for member in weight_set)), segment_ids, places)
        return hidden
    output, pullback = jax.vjp(forward, inputs.astype(jnp.float32), weights)
    grad_input, grads = pullback(cotangent.astype(jnp.float32))
    return (output.astype(jnp.bfloat16), grad_input, grads[0], grads[1], grads[2], grads[3], grads[4], grads[5], grads[6], grads[7], grads[8], grads[9][:, 0], grads[10], grads[11], grads[12][:, :2], grads[9][:, 1], grads[12][:, 2])
```

```python
from functools import partial

import jax
import jax.numpy as jnp
from jax import lax
from jax.experimental import pallas as pl
from jax.experimental.pallas import tpu as pltpu
from jax.sharding import PartitionSpec as P

HD = 128
HP = 64
NSTATE = 256
CONV = 4
ROWS = 256
SHARE = 32
XLOC = 384
HLOC = 6
PAIRS = 3
SEQ_BLOCKS = 4
MSG = XLOC + 16
VMEM_LIMIT = 32 * 1024 * 1024

norm_eps = 1e-05
rope_base = 100000000000.0
bf16 = jnp.bfloat16
f32 = jnp.float32
i32 = jnp.int32


def along_y(value, steps):
    pairs = [(i, ((i // 2 + steps) % 4) * 2 + i % 2) for i in range(8)]
    return lax.ppermute(value, "tp", pairs)


def other_core(value):
    return lax.ppermute(value, "tp", [(i, i ^ 1) for i in range(8)])


def along_ctx(value, steps):
    first, last = max(0, -steps), min(4, 4 - steps)
    return lax.ppermute(value, "ctx", [(i, i + steps) for i in range(first, last)])


def from_all(value):
    half = [value] + [along_y(value, -k) for k in (1, 2, 3)]
    return tuple(half + [other_core(part) for part in half])


def dot_nn(a, b):
    return jnp.dot(a, b, preferred_element_type=f32)


def dot_nt(a, b):
    return lax.dot_general(a, b, (((1,), (1,)), ((), ())), preferred_element_type=f32)


def dot_tn(a, b):
    return lax.dot_general(a, b, (((0,), (0,)), ((), ())), preferred_element_type=f32)


def shape_of(shape, dtype=f32):
    return jax.ShapeDtypeStruct(shape, dtype)


class Columns:
    def __init__(self, array, start, width):
        self.array, self.start, self.width = array, start, width


def run_kernel(kernel, outs, flags, *args, scratch=(), flops=50_000_000):
    whole = pl.BlockSpec(memory_space=pltpu.VMEM)
    grid = (1,) if any(isinstance(arg, Columns) for arg in args) else ()
    specs, arrays, moved = [], [], sum(o.size * o.dtype.itemsize for o in outs)
    for arg in args:
        if isinstance(arg, Columns):
            rows, index = arg.array.shape[0], arg.start // arg.width
            specs.append(pl.BlockSpec((rows, arg.width), lambda i, index=index: (0, index)))
            arrays.append(arg.array)
            moved += rows * arg.width * 2
        else:
            specs.append(whole)
            arrays.append(arg)
            moved += arg.size * arg.dtype.itemsize
    if flags is not None:
        specs = [pl.BlockSpec(memory_space=pltpu.SMEM)] + specs
        arrays = [flags] + arrays
    return pl.pallas_call(
        kernel,
        grid=grid,
        out_shape=tuple(outs),
        in_specs=specs,
        out_specs=tuple(whole for _ in outs),
        scratch_shapes=list(scratch),
        compiler_params=pltpu.CompilerParams(vmem_limit_bytes=VMEM_LIMIT),
        cost_estimate=pl.CostEstimate(flops=flops, bytes_accessed=moved, transcendentals=0),
    )(*arrays)


def local_block(flags, natural):
    return pl.multiple_of(flags[8 + natural] * SHARE, SHARE)


def rank_block(flags, rank):
    return pl.multiple_of(flags[16 + rank] * ROWS, ROWS)


def lane_index(shape):
    return lax.broadcasted_iota(i32, shape, len(shape) - 1)


def spread(columns, pair):
    low = lane_index((1, 128)) < HP
    return jnp.where(low, columns[:, 2 * pair : 2 * pair + 1], columns[:, 2 * pair + 1 : 2 * pair + 2])


def lanes_of(pair):
    return slice(128 * pair, 128 * pair + 128)


def sigmoid(v):
    return 1.0 / (1.0 + jnp.exp(-v))


def softplus(v):
    return jnp.maximum(v, 0.0) + jnp.log1p(jnp.exp(-jnp.abs(v)))


def conv_sum(ext, mask, weight):
    total = weight[CONV : CONV + 1, :] + ext[8 : 8 + ROWS, :] * weight[3:4, :]
    for tap in range(CONV - 1):
        total = total + mask[:, tap : tap + 1] * ext[5 + tap : 5 + tap + ROWS, :] * weight[tap : tap + 1, :]
    return total


def conv_back(grad_out, ext, mask, weight, work, grad_ref, edge_ref, gweight_ref):
    total = conv_sum(ext, mask, weight)
    sig = sigmoid(total)
    grad = grad_out * sig * (1.0 + total * (1.0 - sig))
    width = grad.shape[1]
    gweight_ref[...] = jnp.zeros((8, width), f32)
    gweight_ref[CONV : CONV + 1, :] = jnp.sum(grad, axis=0, keepdims=True)
    gweight_ref[3:4, :] = jnp.sum(grad * ext[8 : 8 + ROWS, :], axis=0, keepdims=True)
    work[0:8, :] = jnp.zeros((8, width), f32)
    work[264:272, :] = jnp.zeros((8, width), f32)
    own = grad * weight[3:4, :]
    edge = jnp.zeros((8, width), f32)
    for tap in range(CONV - 1):
        part = grad * mask[:, tap : tap + 1]
        gweight_ref[tap : tap + 1, :] = jnp.sum(
            part * ext[5 + tap : 5 + tap + ROWS, :], axis=0, keepdims=True
        )
        work[8:264, :] = part * weight[tap : tap + 1, :]
        own = own + work[11 - tap : 11 - tap + ROWS, :]
        edge = edge + work[3 - tap : 11 - tap, :]
    grad_ref[...] = own
    edge_ref[...] = edge


def pack_kernel(layer, flags, zx, shared, query, dt, out):
    out[:, 0:XLOC] = zx[layer, :, 0, :]
    out[:, XLOC : 2 * XLOC] = zx[layer, :, 1, :]
    out[:, 768:896] = shared[layer, :, pl.ds(pl.multiple_of(flags[0] * 128, 128), 128)]
    out[:, 896:1024] = query[layer]
    out[:, 1024 : 1024 + HLOC] = dt[layer]


def joined(parts):
    return jnp.concatenate([part[...] for part in parts], axis=0)


def proj_kernel(flags, p0, p1, p2, p3, p4, p5, p6, p7, weight, cos, sin, normed, z, xs, query, dtn, work):
    rows = joined((p0, p1, p2, p3, p4, p5, p6, p7))
    normed[...] = rows
    work[...] = dot_nn(rows, weight[...])
    dtn[...] = jnp.zeros((ROWS, 128), f32)
    for block in range(8):
        own = slice(SHARE * block, SHARE * (block + 1))
        from_rows = pl.ds(local_block(flags, block), SHARE)
        z[own, :] = work[from_rows, 0:XLOC]
        xs[own, :] = work[from_rows, XLOC:896]
        head = work[from_rows, 896:1024]
        query[own, :] = (head * cos[own, :] + pltpu.roll(head, 64, 1) * sin[own, :]).astype(bf16)
        dtn[own, 0:HLOC] = work[from_rows, 1024 : 1024 + HLOC]


def shared_kernel(flags, xs, halo, mask, cos, sin, weight, out, ext):
    own = xs[:, XLOC:512]
    ext[0:8, :] = halo[:, XLOC:512]
    ext[8 : 8 + ROWS, :] = own
    turned = own * cos[...] + pltpu.roll(own, 64, 1) * sin[...]
    total = conv_sum(ext, mask, weight)
    rank = flags[0]
    out[...] = jnp.where(rank < 2, turned, jnp.where(rank < 4, own, total * sigmoid(total))).astype(bf16)


def prep_kernel(xs, dtn, halo, mask, weight, params, ext, xc, step, cum, step_t, cum_t):
    ext[0:8, :] = halo[:, 0:XLOC]
    ext[8 : 8 + ROWS, :] = xs[:, 0:XLOC]
    total = conv_sum(ext, mask, weight)
    xc[...] = total * sigmoid(total)
    rate = softplus(dtn[...] + params[1:2, :])
    logs = -jnp.exp(params[0:1, :]) * rate
    rows = lax.broadcasted_iota(i32, (ROWS, ROWS), 0)
    lower = (rows >= lane_index((ROWS, ROWS))).astype(f32)
    running = jnp.dot(lower, logs, precision=lax.Precision.HIGHEST, preferred_element_type=f32)
    step[...] = rate
    cum[...] = running
    step_t[...] = rate.T[0:8, :]
    cum_t[...] = running.T[0:8, :]


def block_decays(flags, cum_t):
    kept = jnp.where(flags[4] == flags[5], 1.0, 0.0)
    return jnp.exp(cum_t[:, ROWS - 1 : ROWS]) * kept


def decay_rows(flags, cum_t):
    rows = jnp.broadcast_to(block_decays(flags, cum_t), (8, NSTATE))
    return jnp.concatenate([rows, jnp.zeros((8, NSTATE), f32)], axis=0).astype(bf16)


def weights_in(flags, step, cum, seg):
    last = cum[ROWS - 1 : ROWS, :]
    gap = jnp.exp(last - cum[...]) * jnp.where(seg[...] == flags[5], 1.0, 0.0)
    return gap, gap * step[...]


def inject_of(flags, shared):
    return jnp.concatenate(
        [shared[pl.ds(rank_block(flags, 4), ROWS), :], shared[pl.ds(rank_block(flags, 5), ROWS), :]], axis=1
    )


def readout_of(flags, shared):
    return jnp.concatenate(
        [shared[pl.ds(rank_block(flags, 6), ROWS), :], shared[pl.ds(rank_block(flags, 7), ROWS), :]], axis=1
    )


def carry_of(flags, cum, seg):
    return jnp.exp(cum[...]) * jnp.where(seg[...] == flags[4], 1.0, 0.0)


def state_kernel(flags, s0, s1, s2, s3, s4, s5, s6, s7, xc, step, cum, cum_t, seg, out, shared):
    for index, part in enumerate((s0, s1, s2, s3, s4, s5, s6, s7)):
        shared[ROWS * index : ROWS * (index + 1), :] = part[...]
    inject = inject_of(flags, shared)
    _, weight = weights_in(flags, step, cum, seg)
    for pair in range(PAIRS):
        weighted = (xc[:, lanes_of(pair)] * spread(weight, pair)).astype(bf16)
        out[lanes_of(pair), :] = dot_tn(weighted, inject).astype(bf16)
    out[XLOC:MSG, :] = decay_rows(flags, cum_t)


def allowed_pairs(seg, seg_row):
    rows = lax.broadcasted_iota(i32, (ROWS, ROWS), 0)
    return (rows >= lane_index((ROWS, ROWS))) & (seg[...] == seg_row)


def intra_kernel(flags, shared, xc, step_t, cum, cum_t, seg, seg_rows, params, out):
    inject, readout = inject_of(flags, shared), readout_of(flags, shared)
    both = dot_nt(readout, inject)
    allowed = allowed_pairs(seg, seg_rows[0:1, :])
    low = lane_index((1, 128)) < HP
    for pair in range(PAIRS):
        x = xc[:, lanes_of(pair)]
        xb = x.astype(bf16)
        heads = []
        for head in (2 * pair, 2 * pair + 1):
            gap = jnp.where(allowed, cum[:, head : head + 1] - cum_t[head : head + 1, :], 0.0)
            decay = jnp.where(allowed, jnp.exp(gap), 0.0)
            mixing = (both * decay * step_t[head : head + 1, :]).astype(bf16)
            heads.append(dot_nn(mixing, xb))
        out[:, lanes_of(pair)] = jnp.where(low, heads[0], heads[1]) + spread(params[2:3, :], pair) * x


def keys_values(flags, shared, halves, swapped):
    head, first = flags[1] // 2, flags[2] == 0
    pairs = [
        (
            shared[pl.ds(rank_block(flags, head), ROWS), :],
            shared[pl.ds(rank_block(flags, 2 + head), ROWS), :],
        )
    ]
    for half, other in zip(halves, swapped):
        mine, theirs = half[...], other[...]
        pairs.append((jnp.where(first, mine, theirs), jnp.where(first, theirs, mine)))
    return pairs


def masked_scores(query, pairs, seg, seg_rows):
    parts = []
    for block, (keys, _) in enumerate(pairs):
        score = dot_nt(query, keys) * HD ** (-0.5)
        keep = seg[...] == seg_rows[block : block + 1, :]
        if block == 0:
            rows = lax.broadcasted_iota(i32, (ROWS, ROWS), 0)
            keep = keep & (rows >= lane_index((ROWS, ROWS)))
        parts.append(jnp.where(keep, score, -1e30))
    return parts


def attention_kernel(flags, query, shared, h1, h2, h3, o1, o2, o3, seg, seg_rows, out, log_total):
    pairs = keys_values(flags, shared, (h1, h2, h3), (o1, o2, o3))
    parts = masked_scores(query[...], pairs, seg, seg_rows)
    top = parts[0].max(axis=1, keepdims=True)
    for part in parts[1:]:
        top = jnp.maximum(top, part.max(axis=1, keepdims=True))
    parts = [jnp.exp(part - top) for part in parts]
    total = sum(part.sum(axis=1, keepdims=True) for part in parts)
    inverse = 1.0 / total
    result = jnp.zeros((ROWS, HD), f32)
    for part, (_, values) in zip(parts, pairs):
        result = result + dot_nn((part * inverse).astype(bf16), values)
    out[...] = result.astype(bf16)
    log_total[...] = jnp.broadcast_to(top + jnp.log(total), (ROWS, HD))


def chained(first, second, third):
    rows1 = first[XLOC:MSG, :].astype(f32)
    rows2 = second[XLOC:MSG, :].astype(f32)
    parts = []
    for head in range(HLOC):
        own = slice(HP * head, HP * head + HP)
        older = second[own, :].astype(f32) + rows2[head : head + 1, :] * third[own, :].astype(f32)
        parts.append(first[own, :].astype(f32) + rows1[head : head + 1, :] * older)
    return jnp.concatenate(parts, axis=0)


def carry_kernel(flags, msg1, msg2, msg3, shared, cum, seg, intra, z, attn, state, ssm_y, cat):
    entering = chained(msg1, msg2, msg3)
    state[...] = entering
    from_state = dot_nt(readout_of(flags, shared), entering.astype(bf16))
    carry = carry_of(flags, cum, seg)
    for pair in range(PAIRS):
        own = lanes_of(pair)
        y = intra[:, own] + spread(carry, pair) * from_state[:, own]
        ssm_y[:, own] = y
        gate = z[:, own]
        gated = (y * gate * sigmoid(gate)).astype(bf16)
        for block in range(8):
            cat[pl.ds(local_block(flags, block), SHARE), 128 + 128 * pair : 256 + 128 * pair] = gated[
                SHARE * block : SHARE * (block + 1), :
            ]
    for block in range(8):
        cat[pl.ds(local_block(flags, block), SHARE), 0:128] = attn[SHARE * block : SHARE * (block + 1), :]


def gate_back_kernel(
    flags, p0, p1, p2, p3, p4, p5, p6, p7, weight, z, ssm_y, shared, cum, cum_t, seg,
    dmix, dattn, dy, dz, msg, work, local,
):
    rows = joined((p0, p1, p2, p3, p4, p5, p6, p7))
    dmix[...] = rows
    local[...] = dot_nn(rows, weight[...])
    for block in range(8):
        own = slice(SHARE * block, SHARE * (block + 1))
        from_rows = pl.ds(local_block(flags, block), SHARE)
        dattn[own, :] = local[from_rows, 0:128].astype(bf16)
        work[own, :] = local[from_rows, 128:512]
    readout = readout_of(flags, shared)
    carry = carry_of(flags, cum, seg)
    for pair in range(PAIRS):
        own = lanes_of(pair)
        gate, grad = z[:, own], work[:, own]
        sig = sigmoid(gate)
        y_grad = grad * gate * sig
        dy[:, own] = y_grad
        dz[:, own] = (grad * ssm_y[:, own] * sig * (1.0 + gate * (1.0 - sig))).astype(bf16)
        msg[own, :] = dot_tn((y_grad * spread(carry, pair)).astype(bf16), readout).astype(bf16)
    msg[XLOC:MSG, :] = decay_rows(flags, cum_t)


def attention_back_kernel(
    flags, dattn, query, shared, h1, h2, h3, o1, o2, o3, log_total, seg, seg_rows, cos, sin,
    dq, mine, theirs,
):
    pairs = keys_values(flags, shared, (h1, h2, h3), (o1, o2, o3))
    first = flags[2] == 0
    q = query[...]
    grad = dattn[...]
    parts = masked_scores(q, pairs, seg, seg_rows)
    logs = log_total[:, 0:1]
    probs = [jnp.exp(part - logs) for part in parts]
    grads = [dot_nt(grad, values) for _, values in pairs]
    inner = sum((p * g).sum(axis=1, keepdims=True) for p, g in zip(probs, grads))
    total = jnp.zeros((ROWS, HD), f32)
    for block, (p, g, (keys, _)) in enumerate(zip(probs, grads, pairs)):
        own = slice(ROWS * block, ROWS * (block + 1))
        score = (p * (g - inner)).astype(bf16)
        total = total + dot_nn(score, keys)
        dkeys = dot_tn(score, q) * HD ** (-0.5)
        dvalues = dot_tn(p.astype(bf16), grad)
        mine[own, :] = jnp.where(first, dkeys, dvalues)
        theirs[own, :] = jnp.where(first, dvalues, dkeys).astype(bf16)
    total = total * HD ** (-0.5)
    dq[...] = (total * cos[...] - pltpu.roll(total, 64, 1) * sin[...]).astype(bf16)


def intra_back_kernel(
    flags, dy, xc, shared, step, cum, step_t, cum_t, seg, seg_rows, state, params,
    dx, dinject, dreadout, dcum, dstep, dskip, row_sums, pair_sum,
):
    inject, readout = inject_of(flags, shared), readout_of(flags, shared)
    both = dot_nt(readout, inject)
    allowed = allowed_pairs(seg, seg_rows[0:1, :])
    low = lane_index((1, 128)) < HP
    carry = carry_of(flags, cum, seg)
    entering = state[...].astype(bf16)
    from_state = dot_nt(readout, entering)
    dboth = jnp.zeros((ROWS, ROWS), f32)
    row_sums[...] = jnp.zeros((128, ROWS), f32)
    dcum[...] = jnp.zeros((ROWS, 128), f32)
    carried = []
    for pair in range(PAIRS):
        own = lanes_of(pair)
        x = xc[:, own]
        xb = x.astype(bf16)
        grad = dy[:, own]
        dskip[:, own] = jnp.sum(grad * x, axis=0, keepdims=True)
        carried.append((grad * spread(carry, pair)).astype(bf16))
        through = grad * from_state[:, own]
        total = spread(params[2:3, :], pair) * grad
        for head in (2 * pair, 2 * pair + 1):
            mine = low if head % 2 == 0 else jnp.logical_not(low)
            gap = jnp.where(allowed, cum[:, head : head + 1] - cum_t[head : head + 1, :], 0.0)
            decay = jnp.where(allowed, jnp.exp(gap), 0.0)
            steps = step_t[head : head + 1, :]
            head_grad = jnp.where(mine, grad, 0.0).astype(bf16)
            dmix = dot_nt(head_grad, xb)
            kept = dmix * decay
            dboth = dboth + kept * steps
            mixed = both * decay
            total = total + dot_tn((mixed * steps).astype(bf16), head_grad)
            passed = dmix * mixed
            row_sums[head : head + 1, :] = jnp.sum(passed, axis=0, keepdims=True)
            dcum[:, head : head + 1] = jnp.sum(passed * steps, axis=1, keepdims=True) + carry[
                :, head : head + 1
            ] * jnp.sum(jnp.where(mine, through, 0.0), axis=1, keepdims=True)
        dx[:, own] = total
    columns = row_sums[...].T
    dstep[...] = columns
    dcum[...] = dcum[...] - step[...] * columns
    dboth_b = dboth.astype(bf16)
    dreadout[...] = dot_nn(dboth_b, inject) + dot_nn(jnp.concatenate(carried, axis=1), entering)
    dinject[...] = dot_tn(dboth_b, readout)


def state_back_kernel(
    flags, msg1, msg2, msg3, shared, xc, step, cum, cum_t, seg, state, params, dtn,
    dx, dinject, dreadout, dcum, dstep, kv0, kv1, kv2, kv3, ext, mask, weight,
    packed, dxpre, edge, gweight, ddt, small, work, dconv, sums,
):
    later = chained(msg1, msg2, msg3)
    later_b = later.astype(bf16)
    inject = inject_of(flags, shared)
    low = lane_index((1, 128)) < HP
    gap, weights = weights_in(flags, step, cum, seg)
    from_later = dot_nt(inject, later_b)
    products = later * state[...]
    decays = block_decays(flags, cum_t)
    sums[...] = jnp.zeros((ROWS, 128), f32)
    weighted = []
    for pair in range(PAIRS):
        own = lanes_of(pair)
        x = xc[:, own]
        scale = spread(weights, pair)
        weighted.append((x * scale).astype(bf16))
        dconv[:, own] = dx[:, own] + scale * from_later[:, own]
        through = x * from_later[:, own]
        for head in (2 * pair, 2 * pair + 1):
            mine = low if head % 2 == 0 else jnp.logical_not(low)
            sums[:, head : head + 1] = jnp.sum(jnp.where(mine, through, 0.0), axis=1, keepdims=True)
    dweights = sums[...]
    moved = dweights * weights
    last = jnp.sum(moved, axis=0, keepdims=True)
    lanes = lane_index((1, 128))
    for head in range(HLOC):
        total = jnp.sum(
            jnp.sum(products[HP * head : HP * head + HP, :], axis=0, keepdims=True), axis=1, keepdims=True
        )
        last = last + jnp.where(lanes == head, total * decays[head : head + 1, :], 0.0)
    rows = lax.broadcasted_iota(i32, (ROWS, 128), 0)
    dcums = dcum[...] - moved + jnp.where(rows == ROWS - 1, last, 0.0)
    square = lax.broadcasted_iota(i32, (ROWS, ROWS), 0)
    upper = (square <= lane_index((ROWS, ROWS))).astype(f32)
    dlogs = jnp.dot(upper, dcums, precision=lax.Precision.HIGHEST, preferred_element_type=f32)
    rate = -jnp.exp(params[0:1, :])
    dsteps = dstep[...] + dweights * gap + dlogs * rate
    ddts = dsteps * sigmoid(dtn[...] + params[1:2, :])
    ddt[...] = ddts
    small[...] = jnp.zeros((8, 128), f32)
    small[0:1, :] = jnp.sum(dlogs * rate * step[...], axis=0, keepdims=True)
    small[1:2, :] = jnp.sum(ddts, axis=0, keepdims=True)
    dinject_all = (dinject[...] + dot_nn(jnp.concatenate(weighted, axis=1), later_b)).astype(bf16)
    dreadout_all = dreadout[...].astype(bf16)
    packed[...] = jnp.zeros((8 * ROWS, 128), bf16)
    grads = kv0[...] + kv1[...].astype(f32) + kv2[...].astype(f32) + kv3[...].astype(f32)
    owner = 2 * flags[2] + flags[1] // 2
    packed[pl.ds(rank_block(flags, owner), ROWS), :] = grads.astype(bf16)
    packed[pl.ds(rank_block(flags, 4), ROWS), :] = dinject_all[:, 0:128]
    packed[pl.ds(rank_block(flags, 5), ROWS), :] = dinject_all[:, 128:256]
    packed[pl.ds(rank_block(flags, 6), ROWS), :] = dreadout_all[:, 0:128]
    packed[pl.ds(rank_block(flags, 7), ROWS), :] = dreadout_all[:, 128:256]
    conv_back(dconv[...], ext, mask, weight, work, dxpre, edge, gweight)


def shared_back_kernel(flags, part0, part1, part2, part3, ext, mask, weight, cos, sin, out, edge, gweight, work):
    grad = part0[...] + part1[...].astype(f32) + part2[...].astype(f32) + part3[...].astype(f32)
    conv_back(grad, ext, mask, weight, work, out, edge, gweight)
    rank = flags[0]
    of_conv = jnp.where(rank < 4, 0.0, 1.0)
    edge[...] = edge[...] * of_conv
    gweight[...] = gweight[...] * of_conv
    turned = grad * cos[...] - pltpu.roll(grad, 64, 1) * sin[...]
    out[...] = jnp.where(rank < 2, turned, jnp.where(rank < 4, grad, out[...]))


def dproj_kernel(flags, dz, dxpre, edge_x, dsh, edge_sh, dq, ddt, out):
    for block in range(8):
        own = slice(SHARE * block, SHARE * (block + 1))
        to_rows = pl.ds(local_block(flags, block), SHARE)
        x, sh = dxpre[own, :], dsh[own, :]
        if block == 7:
            pad = jnp.zeros((SHARE - 8, 128), f32)
            sh = sh + jnp.concatenate([pad, edge_sh[...]], axis=0)
            x = x + jnp.concatenate([jnp.zeros((SHARE - 8, XLOC), f32), edge_x[...]], axis=0)
        out[to_rows, 0:XLOC] = dz[own, :]
        out[to_rows, XLOC : 2 * XLOC] = x.astype(bf16)
        out[to_rows, 768:896] = sh.astype(bf16)
        out[to_rows, 896:1024] = dq[own, :]
        out[to_rows, 1024 : 1024 + HLOC] = ddt[own, 0:HLOC].astype(bf16)


def half_sum_kernel(own, other, keep, send1, send2, send3):
    rows = own.shape[0] // 4
    keep[...] = own[0:rows, :] + other[0:rows, :].astype(f32)
    for index, send in ((1, send1), (2, send2), (3, send3)):
        part = slice(rows * index, rows * (index + 1))
        send[...] = (own[part, :].astype(f32) + other[part, :].astype(f32)).astype(bf16)


def parts_of_sum(own, other, along, sign):
    got = other_core(other)
    rows, width = own.shape[0] // 4, own.shape[1]
    sent = shape_of((rows, width), bf16)
    keep, *sends = run_kernel(half_sum_kernel, [shape_of((rows, width)), sent, sent, sent], None, own, got)
    return (keep,) + tuple(along(send, sign * k) for k, send in zip((1, 2, 3), sends))


def split_kernel(left, weight, own, other):
    result = dot_nt(left[...], weight[...])
    own[...] = result[: ROWS // 2]
    other[...] = result[ROWS // 2 :].astype(bf16)


def summed_rows(left, weight, start, width):
    model, index = weight.shape[0], start // width
    own, other = pl.pallas_call(
        split_kernel,
        grid=(model // 256,),
        out_shape=(shape_of((ROWS // 2, model)), shape_of((ROWS // 2, model), bf16)),
        in_specs=[
            pl.BlockSpec((ROWS, width), lambda i: (0, 0)),
            pl.BlockSpec((256, width), lambda i: (i, index)),
        ],
        out_specs=(
            pl.BlockSpec((ROWS // 2, 256), lambda i: (0, i)),
            pl.BlockSpec((ROWS // 2, 256), lambda i: (0, i)),
        ),
        compiler_params=pltpu.CompilerParams(vmem_limit_bytes=VMEM_LIMIT),
        cost_estimate=pl.CostEstimate(
            flops=2 * ROWS * model * width, bytes_accessed=2 * model * width, transcendentals=0
        ),
    )(left, weight)
    return parts_of_sum(own, other, along_y, 1)


def gate_up_kernel(p0, p1, p2, p3, p4, p5, p6, p7, weight, normed, gate, up, act):
    rows = joined((p0, p1, p2, p3, p4, p5, p6, p7))
    normed[...] = rows
    result = dot_nn(rows, weight[...])
    g, u = result[:, :512], result[:, 512:]
    gate[...] = g
    up[...] = u
    act[...] = (g * sigmoid(g) * u).astype(bf16)


def gate_up_back_kernel(p0, p1, p2, p3, p4, p5, p6, p7, weight, gate, up, dffn, out):
    rows = joined((p0, p1, p2, p3, p4, p5, p6, p7))
    dffn[...] = rows
    dact = dot_nn(rows, weight[...])
    g = gate[...]
    sig = sigmoid(g)
    out[:, :512] = (dact * up[...] * sig * (1.0 + g * (1.0 - sig))).astype(bf16)
    out[:, 512:] = (dact * g * sig).astype(bf16)


def natural_kernel(flags, p0, p1, p2, p3, p4, p5, p6, p7, out):
    local = joined((p0, p1, p2, p3, p4, p5, p6, p7)).astype(out.dtype)
    for block in range(8):
        out[pl.ds(pl.multiple_of(flags[24 + block] * SHARE, SHARE), SHARE), :] = local[
            SHARE * block : SHARE * (block + 1), :
        ]


def add_norm_kernel(hidden, part0, part1, part2, part3, gain, out, normed, inverse):
    total = hidden[...] + part0[...] + (
        part1[...].astype(f32) + part2[...].astype(f32) + part3[...].astype(f32)
    )
    out[...] = total
    scale = lax.rsqrt(jnp.mean(total * total, axis=1, keepdims=True) + norm_eps)
    inverse[...] = jnp.broadcast_to(scale, inverse.shape)
    normed[...] = (total * scale * gain[...]).astype(bf16)


def add_norm(hidden, parts, gain):
    shape = hidden.shape
    return run_kernel(
        add_norm_kernel,
        [shape_of(shape), shape_of(shape, bf16), shape_of((shape[0], 128))],
        None, hidden, *parts, gain[None],
    )


def norm_back_kernel(grad, part0, part1, part2, part3, hidden, inverse, gain, out, rounded, ggain):
    received = part0[...] + (part1[...].astype(f32) + part2[...].astype(f32) + part3[...].astype(f32))
    scale = inverse[:, 0:1]
    unit = hidden[...] * scale
    scaled = received * gain[...]
    ggain[...] = jnp.sum(received * unit, axis=0, keepdims=True)
    total = grad[...] + scale * (scaled - unit * jnp.mean(scaled * unit, axis=1, keepdims=True))
    out[...] = total
    rounded[...] = total.astype(bf16)


def norm_back(grad, parts, hidden, inverse, gain):
    shape = hidden.shape
    return run_kernel(
        norm_back_kernel,
        [shape_of(shape), shape_of(shape, bf16), shape_of((1, shape[1]))],
        None, grad, *parts, hidden, inverse, gain[None],
    )


def gradient_kernel(pairs, *refs):
    out, at = refs[-1], 0
    for index in range(pairs):
        left, right = refs[2 * index], refs[2 * index + 1]
        width = right.shape[1]
        out[:, at : at + width] = dot_tn(left[...], right[...]).astype(bf16)
        at += width


def weight_gradients(pairs, total, block, index, buffer=None):
    rows, model = pairs[0][0].shape
    width = sum(right.shape[1] for _, right in pairs)
    specs, args = [], []
    for left, right in pairs:
        specs += [
            pl.BlockSpec((rows, 256), lambda i: (0, i)),
            pl.BlockSpec(right.shape, lambda i: (0, 0)),
        ]
        args += [left, right]
    aliases = {}
    kernel = partial(gradient_kernel, len(pairs))
    if buffer is not None:
        aliases = {len(args): 0}
        specs.append(pl.BlockSpec(memory_space=pl.ANY))
        args.append(buffer)

        def kernel(*refs):
            gradient_kernel(len(pairs), *refs[:-2], refs[-1])

    return pl.pallas_call(
        kernel,
        grid=(model // 256,),
        out_shape=shape_of((model, total), bf16),
        in_specs=specs,
        out_specs=pl.BlockSpec((256, block), lambda i: (i, index)),
        input_output_aliases=aliases,
        compiler_params=pltpu.CompilerParams(vmem_limit_bytes=VMEM_LIMIT),
        cost_estimate=pl.CostEstimate(
            flops=2 * rows * model * width, bytes_accessed=model * width * 2, transcendentals=0
        ),
    )(*args)


def body(
    inputs, cotangent, segment_ids, w_query, w_shared, w_zx, w_dt, w_attn_out, w_ssm_out, w_gate, w_up, w_down,
    gains, conv_x, conv_bc, head_params,
):
    layers = w_query.shape[0]
    rank, ctx = lax.axis_index("tp"), lax.axis_index("ctx")
    y, core = rank // 2, rank % 2

    def local_of(block_y, block_core):
        return jnp.where(block_core == core, 0, 4) + (block_y - y) % 4

    seg_all = segment_ids[0]
    first_row = ctx * ROWS
    padded = jnp.concatenate([jnp.full((CONV - 1,), -1, i32), seg_all])
    seg_ext = lax.dynamic_slice_in_dim(padded, first_row, ROWS + CONV - 1)
    seg_own = seg_ext[CONV - 1 :]
    seg = seg_own[:, None]
    blocks = seg_all.reshape(SEQ_BLOCKS, ROWS)
    seg_rows = jnp.stack(
        [
            jnp.where(ctx >= back, lax.dynamic_index_in_dim(blocks, jnp.maximum(ctx - back, 0), 0, False), -1)
            for back in range(SEQ_BLOCKS)
        ]
        + [jnp.full((ROWS,), -1, i32)] * 4
    )
    mask = jnp.stack(
        [(seg_ext[tap : tap + ROWS] == seg_own).astype(f32) for tap in range(CONV)] + [jnp.zeros((ROWS,), f32)] * 4,
        axis=1,
    )
    naturals = jnp.arange(8, dtype=i32)
    flags = jnp.concatenate(
        [
            jnp.stack([rank, y, core, ctx, seg_ext[CONV - 2], seg_own[-1], rank, rank]).astype(i32),
            local_of(naturals % 4, naturals // 4).astype(i32),
            local_of(naturals // 2, naturals % 2).astype(i32),
            (jnp.where(naturals < 4, core, 1 - core) * 4 + (y + naturals) % 4).astype(i32),
        ]
    )

    def to_local(value):
        return tuple(lax.dynamic_slice_in_dim(value, flags[24 + k] * SHARE, SHARE, 0) for k in range(8))

    def to_natural(parts, dtype):
        return run_kernel(natural_kernel, [shape_of((ROWS, parts[0].shape[1]), dtype)], flags, *parts)[0]

    half_width = HD // 2
    frequency = rope_base ** (-jnp.arange(half_width, dtype=f32) / half_width)
    places = (first_row + jnp.arange(ROWS, dtype=i32)).astype(f32)
    angles = places[:, None] * frequency[None, :]
    cosine, sine = jnp.cos(angles), jnp.sin(angles)
    cos = jnp.concatenate([cosine, cosine], axis=1)
    sin = jnp.concatenate([-sine, sine], axis=1)

    def rounded_rows(value):
        return jnp.pad(value, ((0, 8 - value.shape[0]), (0, 0)))

    own_conv = jnp.maximum(rank - 4, 0) * 128
    conv_x_rows = [rounded_rows(conv_x[layer]) for layer in range(layers)]
    conv_bc_rows = [
        rounded_rows(lax.dynamic_slice_in_dim(conv_bc[layer], own_conv, 128, 1)) for layer in range(layers)
    ]
    params = [jnp.pad(head_params[layer], ((0, 5), (0, 128 - HLOC))) for layer in range(layers)]

    gathered = []
    for layer in range(layers):
        (proj_weight,) = run_kernel(
            partial(pack_kernel, layer), [shape_of((w_query.shape[1], 1030), bf16)], flags, w_zx, w_shared, w_query, w_dt
        )
        rest = jnp.concatenate(
            [w_gate[layer], w_up[layer], w_down[layer], w_attn_out[layer], w_ssm_out[layer]], axis=1
        )
        gathered.append(
            tuple(lax.all_gather(part, ("fsdp", "ctx"), axis=0, tiled=True) for part in (proj_weight, rest))
        )

    own_rows = to_local(inputs[0])
    hidden = own_rows[0].astype(f32)
    normed_parts, inverse1 = [], None
    for part in own_rows:
        wide = part.astype(f32)
        inverse = lax.rsqrt(jnp.mean(wide * wide, axis=1, keepdims=True) + norm_eps)
        if inverse1 is None:
            inverse1 = jnp.broadcast_to(inverse, (SHARE, 128))
        normed_parts.append((wide * inverse * gains[0, 0]).astype(bf16))
    model = inputs.shape[2]
    normed_shape = shape_of((ROWS, model), bf16)
    saved = []
    for layer in range(layers):
        proj_weight, rest = gathered[layer]
        normed_b, z, xs, query, dtn = run_kernel(
            proj_kernel,
            [
                normed_shape, shape_of((ROWS, XLOC)), shape_of((ROWS, 512)), shape_of((ROWS, HD), bf16),
                shape_of((ROWS, 128)),
            ],
            flags, *normed_parts, proj_weight, cos, sin,
            scratch=[pltpu.VMEM((ROWS, 1030), f32)],
        )
        halo = along_ctx(xs[ROWS - 8 :], 1)
        shared_own, shared_ext = run_kernel(
            shared_kernel,
            [shape_of((ROWS, 128), bf16), shape_of((264, 128))],
            flags, xs, halo, mask, cos, sin, conv_bc_rows[layer],
        )
        shared_parts = from_all(shared_own)
        x_ext, xc, step, cum, step_t, cum_t = run_kernel(
            prep_kernel,
            [
                shape_of((264, XLOC)), shape_of((ROWS, XLOC)), shape_of((ROWS, 128)), shape_of((ROWS, 128)),
                shape_of((8, ROWS)), shape_of((8, ROWS)),
            ],
            None, xs, dtn, halo, mask, conv_x_rows[layer], params[layer],
        )
        message, shared = run_kernel(
            state_kernel,
            [shape_of((MSG, NSTATE), bf16), shape_of((8 * ROWS, 128), bf16)],
            flags, *shared_parts, xc, step, cum, cum_t, seg,
        )
        kv_half = lax.dynamic_slice_in_dim(shared, flags[16 + 2 * core + y // 2] * ROWS, ROWS, 0)
        earlier = tuple(along_ctx(message, back) for back in (1, 2, 3))
        halves = tuple(along_ctx(kv_half, back) for back in (1, 2, 3))
        kv = halves + tuple(other_core(half) for half in halves)
        (intra,) = run_kernel(
            intra_kernel, [shape_of((ROWS, XLOC))],
            flags, shared, xc, step_t, cum, cum_t, seg, seg_rows, params[layer],
        )
        attn, log_total = run_kernel(
            attention_kernel, [shape_of((ROWS, HD), bf16), shape_of((ROWS, HD))],
            flags, query, shared, *kv, seg, seg_rows,
        )
        state, ssm_y, cat = run_kernel(
            carry_kernel,
            [shape_of((XLOC, NSTATE)), shape_of((ROWS, XLOC)), shape_of((ROWS, 512), bf16)],
            flags, *earlier, shared, cum, seg, intra, z, attn,
        )
        hidden1, normed2, inverse2 = add_norm(hidden, summed_rows(cat, rest, 1536, 512), gains[layer, 1])
        wide = shape_of((ROWS, 512))
        normed2_b, gate, up, act_b = run_kernel(
            gate_up_kernel, [normed_shape, wide, wide, shape_of((ROWS, 512), bf16)],
            None, *from_all(normed2), Columns(rest, 0, 1024),
        )
        next_gain = gains[min(layer + 1, layers - 1), 0]
        hidden2, next_normed, next_inverse = add_norm(hidden1, summed_rows(act_b, rest, 1024, 512), next_gain)
        saved.append(
            (
                hidden, normed_b, inverse1, shared_ext, shared, query, x_ext, xc, z, dtn, step, cum, step_t, cum_t,
                kv, log_total, state, ssm_y, cat, hidden1, inverse2, normed2_b, gate, up, act_b,
            )
        )
        hidden, inverse1 = hidden2, next_inverse
        if layer + 1 < layers:
            normed_parts = from_all(next_normed)
    layer_out = to_natural(from_all(hidden.astype(bf16)), bf16)

    dffn_parts = to_local(cotangent[0])
    grad_hidden = dffn_parts[0].astype(f32)
    weight_sums = [None] * layers
    small_sums = [None] * layers
    for layer in reversed(range(layers)):
        (
            hidden, normed_b, inverse1, shared_ext, shared, query, x_ext, xc, z, dtn, step, cum, step_t, cum_t,
            kv, log_total, state, ssm_y, cat, hidden1, inverse2, normed2_b, gate, up, act_b,
        ) = saved[layer]
        proj_weight, rest = gathered[layer]
        dffn_b, dgate_up = run_kernel(
            gate_up_back_kernel, [normed_shape, shape_of((ROWS, 1024), bf16)],
            None, *dffn_parts, Columns(rest, 1024, 512), gate, up,
        )
        parts = summed_rows(dgate_up, rest, 0, 1024)
        grads = weight_gradients([(normed2_b, dgate_up), (dffn_b, act_b)], 3078, 1536, 0)
        parts, grads = lax.optimization_barrier((parts, grads))
        grad_mid, dmix, ggain2 = norm_back(grad_hidden, parts, hidden1, inverse2, gains[layer, 1])
        dmix_b, dattn, dy, dz, message = run_kernel(
            gate_back_kernel,
            [
                normed_shape, shape_of((ROWS, HD), bf16), shape_of((ROWS, XLOC)), shape_of((ROWS, XLOC), bf16),
                shape_of((MSG, NSTATE), bf16),
            ],
            flags, *from_all(dmix), Columns(rest, 1536, 512), z, ssm_y, shared, cum, cum_t, seg,
            scratch=[pltpu.VMEM((ROWS, XLOC), f32), pltpu.VMEM((ROWS, 512), f32)],
        )
        after = tuple(along_ctx(message, -ahead) for ahead in (1, 2, 3))
        dq, mine, theirs = run_kernel(
            attention_back_kernel,
            [shape_of((ROWS, HD), bf16), shape_of((4 * ROWS, HD)), shape_of((4 * ROWS, HD), bf16)],
            flags, dattn, query, shared, *kv, log_total, seg, seg_rows, cos, sin,
        )
        dkv = parts_of_sum(mine, theirs, along_ctx, -1)
        dx, dinject, dreadout, dcum, dstep, dskip = run_kernel(
            intra_back_kernel,
            [
                shape_of((ROWS, XLOC)), shape_of((ROWS, NSTATE)), shape_of((ROWS, NSTATE)), shape_of((ROWS, 128)),
                shape_of((ROWS, 128)), shape_of((1, XLOC)),
            ],
            flags, dy, xc, shared, step, cum, step_t, cum_t, seg, seg_rows, state, params[layer],
            scratch=[pltpu.VMEM((128, ROWS), f32), pltpu.VMEM((8, 128), f32)],
        )
        grads = weight_gradients([(dmix_b, cat)], 3078, 512, 3, grads)
        after, dkv, grads = lax.optimization_barrier((after, dkv, grads))
        packed, dxpre, edge_x, gconv_x, ddt, gheads = run_kernel(
            state_back_kernel,
            [
                shape_of((8 * ROWS, 128), bf16), shape_of((ROWS, XLOC)), shape_of((8, XLOC)), shape_of((8, XLOC)),
                shape_of((ROWS, 128)), shape_of((8, 128)),
            ],
            flags, *after, shared, xc, step, cum, cum_t, seg, state, params[layer], dtn,
            dx, dinject, dreadout, dcum, dstep, *dkv, x_ext, mask, conv_x_rows[layer],
            scratch=[pltpu.VMEM((272, XLOC), f32), pltpu.VMEM((ROWS, XLOC), f32), pltpu.VMEM((ROWS, 128), f32)],
        )
        edge_x = along_ctx(edge_x, -1)
        dshared_parts = parts_of_sum(packed[: 4 * ROWS], packed[4 * ROWS :], along_y, 1)
        dsh, edge_sh, gconv_sh = run_kernel(
            shared_back_kernel,
            [shape_of((ROWS, 128)), shape_of((8, 128)), shape_of((8, 128))],
            flags, *dshared_parts, shared_ext, mask, conv_bc_rows[layer], cos, sin,
            scratch=[pltpu.VMEM((272, 128), f32)],
        )
        edge_sh = along_ctx(edge_sh, -1)
        (dproj,) = run_kernel(
            dproj_kernel, [shape_of((ROWS, 1030), bf16)], flags, dz, dxpre, edge_x, dsh, edge_sh, dq, ddt
        )
        grads = weight_gradients([(normed_b, dproj)], 3078, 2048, 1, grads)
        parts = summed_rows(dproj, proj_weight, 0, 1030)
        parts, grads = lax.optimization_barrier((parts, grads))
        weight_sums[layer] = lax.psum_scatter(grads, ("fsdp", "ctx"), scatter_dimension=0, tiled=True)
        grad_hidden, rounded, ggain1 = norm_back(grad_mid, parts, hidden, inverse1, gains[layer, 0])
        dffn_parts = from_all(rounded)
        small_sums[layer] = jnp.concatenate(
            [
                ggain1.reshape(-1),
                ggain2.reshape(-1),
                gconv_sh[: CONV + 1].reshape(-1),
                gconv_x[: CONV + 1].reshape(-1),
                gheads[0],
                gheads[1],
                jnp.pad(dskip.reshape(HLOC, HP).sum(axis=1), (0, 128 - HLOC)),
            ]
        )
    input_grad = to_natural(dffn_parts, f32)

    small = jnp.stack(small_sums).astype(bf16)
    peers = 16
    small = lax.all_to_all(
        jnp.broadcast_to(small[None], (peers, *small.shape)), ("fsdp", "ctx"), 0, 0, tiled=True
    )
    small = jnp.sum(small.astype(f32), axis=0)
    at_conv = 2 * model + (CONV + 1) * 128
    over_tp = small[:, :at_conv].astype(bf16)
    over_tp = lax.all_to_all(jnp.broadcast_to(over_tp[None], (8, *over_tp.shape)), "tp", 0, 0, tiled=True)
    over_tp = over_tp.astype(f32)
    ggains = jnp.sum(over_tp[:, :, : 2 * model], axis=0)
    gconv_bc = over_tp[4:, :, 2 * model :].reshape(4, layers, CONV + 1, 128)
    gconv_bc = jnp.moveaxis(gconv_bc, 0, 2).reshape(layers, CONV + 1, 512)
    rest = small[:, at_conv:]
    gconv_x = rest[:, : (CONV + 1) * XLOC].reshape(layers, CONV + 1, XLOC)
    gheads = rest[:, (CONV + 1) * XLOC :].reshape(layers, 3, 128)[:, :, :HLOC]

    def stacked(start, width):
        return jnp.stack([part[:, start : start + width] for part in weight_sums]).astype(f32)

    grad_shared = []
    for part in weight_sums:
        pieces = jnp.stack(from_all(part[:, 2816:2944]))
        grad_shared.append(
            jnp.concatenate([lax.dynamic_index_in_dim(pieces, flags[16 + k], 0, False) for k in range(8)], axis=1)
        )
    grad_zx = jnp.stack([stacked(2048, XLOC), stacked(2048 + XLOC, XLOC)], axis=2)
    return (
        layer_out[None],
        input_grad[None],
        stacked(2944, 128),
        jnp.stack(grad_shared).astype(f32),
        grad_zx,
        stacked(3072, HLOC),
        stacked(1536, 128),
        stacked(1664, 384),
        stacked(0, 512),
        stacked(512, 512),
        stacked(1024, 512),
        ggains[:, :model],
        gconv_x,
        gconv_bc,
        gheads[:, :2],
        ggains[:, model:],
        gheads[:, 2],
    )


def solution(mesh):
    columns = P(None, ("fsdp", "ctx"), "tp")
    rows = P("fsdp", "ctx", None)
    return jax.shard_map(
        body,
        mesh=mesh,
        in_specs=(
            rows, rows, P("fsdp", None), columns, P(None, ("fsdp", "ctx"), None),
            P(None, ("fsdp", "ctx"), None, "tp"), columns, columns, columns, columns, columns, columns,
            P(), P(None, None, "tp"), P(), P(None, None, "tp"),
        ),
        out_specs=(
            rows, rows, columns, P(None, ("fsdp", "ctx"), None), P(None, ("fsdp", "ctx"), None, "tp"),
            columns, columns, columns, columns, columns, columns,
            P(), P(None, None, "tp"), P(), P(None, None, "tp"), P(), P(None, "tp"),
        ),
        check_vma=False,
    )
```

```python
import math
from functools import partial

import jax
import jax.numpy as jnp
from jax import lax
from jax.experimental import pallas as pl
from jax.experimental.pallas import tpu as pltpu
from jax.sharding import PartitionSpec as P

HD = 128
HP = 64
NSTATE = 256
CONV = 4
ROWS = 256
SHARE = 32
XLOC = 384
PROJ = 1152
LATE = 640
HLOC = 6
PAIRS = 3
SEQ_BLOCKS = 4
MSG = XLOC + 16
KV = 128
VMEM_LIMIT = 16 * 1024 * 1024

norm_eps = 1e-05
rope_base = 100000000000.0
bf16 = jnp.bfloat16
f32 = jnp.float32
i32 = jnp.int32


def along_y(value, steps):
    pairs = [(i, ((i // 2 + steps) % 4) * 2 + i % 2) for i in range(8)]
    return lax.ppermute(value, "tp", pairs)


def other_core(value):
    return lax.ppermute(value, "tp", [(i, i ^ 1) for i in range(8)])


def along_ctx(value, steps):
    first, last = max(0, -steps), min(4, 4 - steps)
    return lax.ppermute(value, "ctx", [(i, i + steps) for i in range(first, last)])


def ring(value, axis, steps):
    return lax.ppermute(value, axis, [(i, (i + steps) % 4) for i in range(4)])


def from_all(value):
    half = [value] + [along_y(value, -k) for k in (1, 2, 3)]
    return tuple(half + [other_core(part) for part in half])


def dot_nn(a, b):
    return jnp.dot(a, b, preferred_element_type=f32)


def dot_nt(a, b):
    return lax.dot_general(a, b, (((1,), (1,)), ((), ())), preferred_element_type=f32)


def dot_tn(a, b):
    return lax.dot_general(a, b, (((0,), (0,)), ((), ())), preferred_element_type=f32)


def shape_of(shape, dtype=f32):
    return jax.ShapeDtypeStruct(shape, dtype)


class Columns:
    def __init__(self, array, block=0, width=None, rows=None, keep=False):
        self.array, self.block, self.keep = array, block, keep
        self.shape = (rows or array.shape[0],) + array.shape[1:-1] + (width or array.shape[-1],)

    def spec(self):
        place = (0,) * (len(self.shape) - 1) + (self.block,)
        return pl.BlockSpec(self.shape, lambda i: place, pipeline_mode=pl.Buffered(1))


class Layer:
    def __init__(self, array, layer):
        self.array, self.layer, self.keep = array, layer, True
        self.shape = (1,) + array.shape[1:]

    def spec(self):
        place = (self.layer,) + (0,) * (len(self.shape) - 1)
        return pl.BlockSpec(self.shape, lambda i: place, pipeline_mode=pl.Buffered(1))


def stored(array):
    return Columns(array, keep=True)


def passed(arrays):
    return [Columns(array) for array in arrays]


def kept(shape, dtype=f32):
    return pltpu.HBM(shape, dtype)


def fetch_kernel(places, *refs):
    count = len(places)
    sources, outs, sems = refs[:count], refs[count : 2 * count], refs[-1]
    copies = []
    for (start, pieces), source, out in zip(places, sources, outs):
        rows, width = out.shape[0] // pieces, out.shape[1]
        for index in range(pieces):
            own = pl.ds(rows * index, rows)
            copies.append(
                pltpu.make_async_copy(
                    source.at[own, pl.ds(start, width)], out.at[own, :], sems.at[len(copies)]
                )
            )
    for copy in copies:
        copy.start()
    for copy in copies:
        copy.wait()


def fetched_all(name, sources):
    places = [(start, 4 if array.shape[0] == 2048 and width > 128 else 1) for array, start, width in sources]
    whole = pl.BlockSpec(memory_space=pltpu.VMEM)
    return pl.pallas_call(
        partial(fetch_kernel, places),
        name=name,
        out_shape=tuple(pltpu.VMEM((array.shape[0], width), array.dtype) for array, _, width in sources),
        in_specs=[pl.BlockSpec(memory_space=pltpu.HBM)] * len(sources),
        out_specs=tuple(whole for _ in sources),
        scratch_shapes=[pltpu.SemaphoreType.DMA((sum(pieces for _, pieces in places),))],
        compiler_params=pltpu.CompilerParams(vmem_limit_bytes=VMEM_LIMIT),
        cost_estimate=pl.CostEstimate(
            flops=0, bytes_accessed=sum(2 * array.shape[0] * width for array, _, width in sources), transcendentals=0
        ),
    )(*(pltpu.with_memory_space_constraint(array, pltpu.HBM) for array, _, _ in sources))


def fetched(name, array, start, width):
    return fetched_all(name, [(array, start, width)])[0]


def restored(name, arrays):
    return fetched_all(name, [(array, 0, array.shape[1]) for array in arrays])


def run_kernel(kernel, outs, flags, *args, scratch=(), flops=50_000_000):
    whole = pl.BlockSpec(memory_space=pltpu.VMEM)
    own = [isinstance(arg, (Columns, Layer)) for arg in args]
    specs, arrays, out_specs = [], [], []
    for arg, copied in zip(args, own):
        specs.append(arg.spec() if copied else whole)
        array = arg.array if copied else arg
        arrays.append(pltpu.with_memory_space_constraint(array, pltpu.HBM) if copied and arg.keep else array)
    for out in outs:
        in_vmem = isinstance(out, jax.ShapeDtypeStruct)
        out_specs.append(whole if in_vmem else pl.BlockSpec(out.shape, lambda i, n=len(out.shape): (0,) * n))
        own.append(not in_vmem)
    moved = sum(2 * math.prod(arg.shape) for arg in args) + sum(2 * math.prod(o.shape) for o in outs)
    if flags is not None:
        specs = [pl.BlockSpec(memory_space=pltpu.SMEM)] + specs
        arrays = [flags] + arrays
    return pl.pallas_call(
        kernel,
        grid=(1,) if any(own) else (),
        out_shape=tuple(outs),
        in_specs=specs,
        out_specs=tuple(out_specs),
        scratch_shapes=list(scratch),
        compiler_params=pltpu.CompilerParams(vmem_limit_bytes=VMEM_LIMIT),
        cost_estimate=pl.CostEstimate(flops=flops, bytes_accessed=moved, transcendentals=0),
    )(*arrays)


def local_block(flags, natural):
    return pl.multiple_of(flags[8 + natural] * SHARE, SHARE)


def rank_block(flags, rank):
    return pl.multiple_of(flags[16 + rank] * ROWS, ROWS)


def lane_index(shape):
    return lax.broadcasted_iota(i32, shape, len(shape) - 1)


def spread(columns, pair):
    low = lane_index((1, 128)) < HP
    return jnp.where(low, columns[:, 2 * pair : 2 * pair + 1], columns[:, 2 * pair + 1 : 2 * pair + 2])


def lanes_of(pair):
    return slice(128 * pair, 128 * pair + 128)


def turned(value, table, sign):
    return value * table[:, 0:128] + sign * (pltpu.roll(value, 64, 1) * table[:, 128:256])


def segments(table):
    return table[:, 259:260]


def sigmoid(v):
    return 1.0 / (1.0 + jnp.exp(-v))


def softplus(v):
    return jnp.maximum(v, 0.0) + jnp.log1p(jnp.exp(-jnp.abs(v)))


def conv_sum(ext, table, weight):
    total = weight[CONV : CONV + 1, :] + ext[8 : 8 + ROWS, :] * weight[3:4, :]
    for tap in range(CONV - 1):
        total = total + table[:, 256 + tap : 257 + tap] * ext[5 + tap : 5 + tap + ROWS, :] * weight[tap : tap + 1, :]
    return total


def conv_back(grad_out, ext, table, weight, work, grad_ref, edge_ref, gweight_ref):
    total = conv_sum(ext, table, weight)
    sig = sigmoid(total)
    grad = grad_out * sig * (1.0 + total * (1.0 - sig))
    width = grad.shape[1]
    gweight_ref[...] = jnp.zeros((8, width), f32)
    gweight_ref[CONV : CONV + 1, :] = jnp.sum(grad, axis=0, keepdims=True)
    gweight_ref[3:4, :] = jnp.sum(grad * ext[8 : 8 + ROWS, :], axis=0, keepdims=True)
    work[0:8, :] = jnp.zeros((8, width), f32)
    work[264:272, :] = jnp.zeros((8, width), f32)
    own = grad * weight[3:4, :]
    edge = jnp.zeros((8, width), f32)
    for tap in range(CONV - 1):
        part = grad * table[:, 256 + tap : 257 + tap]
        gweight_ref[tap : tap + 1, :] = jnp.sum(
            part * ext[5 + tap : 5 + tap + ROWS, :], axis=0, keepdims=True
        )
        work[8:264, :] = part * weight[tap : tap + 1, :]
        own = own + work[11 - tap : 11 - tap + ROWS, :]
        edge = edge + work[3 - tap : 11 - tap, :]
    grad_ref[...] = own
    edge_ref[...] = edge


def pack_kernel(place, *refs):
    out, at, index = refs[-1], 0, 0
    while index < len(refs) - 1:
        ref = refs[index]
        if len(ref.shape) == 4:
            out[:, at : at + XLOC] = ref[0, :, 0, :]
            out[:, at + XLOC : at + 512] = refs[index + 1][0]
            out[:, at + 512 : at + 896] = ref[0, :, 1, :]
            at, index = at + 896, index + 2
            continue
        width = min(ref.shape[2], 512)
        if width == HLOC:
            out[:, at : at + 128] = jnp.zeros((out.shape[0], 128), bf16)
            out[:, at : at + HLOC] = ref[0]
            width = 128
        elif ref.shape[2] == 1024:
            width = 128
            out[:, at : at + width] = ref[0, :, pl.ds(pl.multiple_of(place[0] * 128, 128), 128)]
        else:
            out[:, at : at + width] = ref[0]
        at, index = at + width, index + 1


def first_kernel(flags, rows, cotangent, gain, normed, inverse, hidden, hidden_kept, grads, grad):
    for block in range(8):
        own = slice(SHARE * block, SHARE * (block + 1))
        from_rows = pl.ds(pl.multiple_of(flags[24 + block] * SHARE, SHARE), SHARE)
        wide = rows[0, from_rows, :].astype(f32)
        scale = lax.rsqrt(jnp.mean(wide * wide, axis=1, keepdims=True) + norm_eps)
        normed[own, :] = (wide * scale * gain[0:1, :]).astype(bf16)
        grads[own, :] = cotangent[0, from_rows, :]
        if block == 0:
            hidden[...] = wide
            hidden_kept[...] = wide
            inverse[...] = jnp.broadcast_to(scale, inverse.shape)
            grad[...] = cotangent[0, from_rows, :].astype(f32)


def joined(parts):
    return parts[0][...] if len(parts) == 1 else jnp.concatenate([part[...] for part in parts], axis=0)


def proj_kernel(flags, *refs):
    parts, (weight, table, normed, z, z_kept, xs, query, query_kept, dtn, dtn_kept, work) = refs[:-11], refs[-11:]
    rows = joined(parts)
    normed[...] = rows
    work[...] = dot_nn(rows, weight[...])
    for block in range(8):
        own = slice(SHARE * block, SHARE * (block + 1))
        from_rows = pl.ds(local_block(flags, block), SHARE)
        for out in (z, z_kept):
            out[own, :] = work[from_rows, 0:XLOC]
        xs[own, :] = work[from_rows, 512:1024]
        head = turned(work[from_rows, XLOC:512], table[own, :], 1.0).astype(bf16)
        for out in (query, query_kept):
            out[own, :] = head
        for out in (dtn, dtn_kept):
            out[own, :] = work[from_rows, 1024:PROJ]


def shared_kernel(flags, xs, halo, table, small, out, ext):
    own = xs[:, XLOC:512]
    ext[0:8, :] = halo[:, XLOC:512]
    ext[8 : 8 + ROWS, :] = own
    total = conv_sum(ext, table, small[:, XLOC:512])
    rank = flags[0]
    out[...] = jnp.where(
        rank < 2, turned(own, table, 1.0), jnp.where(rank < 4, own, total * sigmoid(total))
    ).astype(bf16)


def prep_kernel(xs, dtn, halo, table, small, ext, xc, xc_kept, rates, rates_kept, rates_t, rates_t_kept):
    ext[0:8, :] = halo[:, 0:XLOC]
    ext[8 : 8 + ROWS, :] = xs[:, 0:XLOC]
    total = conv_sum(ext, table, small[:, 0:XLOC])
    for out in (xc, xc_kept):
        out[...] = total * sigmoid(total)
    params = small[:, 512:640]
    rate = softplus(dtn[...] + params[1:2, :])
    logs = -jnp.exp(params[0:1, :]) * rate
    rows = lax.broadcasted_iota(i32, (ROWS, ROWS), 0)
    lower = (rows >= lane_index((ROWS, ROWS))).astype(f32)
    running = jnp.dot(lower, logs, precision=lax.Precision.HIGHEST, preferred_element_type=f32)
    for out in (rates, rates_kept):
        out[:, 0:128] = rate
        out[:, 128:256] = running
    rate_t, running_t = rate.T[0:8, :], running.T[0:8, :]
    for out in (rates_t, rates_t_kept):
        out[0:8, :] = rate_t
        out[8:16, :] = running_t


def block_decays(flags, rates_t):
    kept = jnp.where(flags[4] == flags[5], 1.0, 0.0)
    return jnp.exp(rates_t[8:16, ROWS - 1 : ROWS]) * kept


def decay_rows(flags, rates_t):
    rows = jnp.broadcast_to(block_decays(flags, rates_t), (8, NSTATE))
    return jnp.concatenate([rows, jnp.zeros((8, NSTATE), f32)], axis=0).astype(bf16)


def weights_in(rates, table):
    last = rates[ROWS - 1 : ROWS, 128:256]
    gap = jnp.exp(last - rates[:, 128:256]) * table[:, 261:262]
    return gap, gap * rates[:, 0:128]


def rank_columns(flags, shared, first):
    return jnp.concatenate(
        [shared[pl.ds(rank_block(flags, rank), ROWS), :] for rank in (first, first + 1)], axis=1
    )


def inject_of(flags, shared):
    return rank_columns(flags, shared, 4)


def readout_of(flags, shared):
    return rank_columns(flags, shared, 6)


def carry_of(rates, table):
    return jnp.exp(rates[:, 128:256]) * table[:, 260:261]


def state_kernel(flags, s0, s1, s2, s3, s4, s5, s6, s7, xc, rates, rates_t, table, out, shared, shared_kept):
    for index, part in enumerate((s0, s1, s2, s3, s4, s5, s6, s7)):
        shared[ROWS * index : ROWS * (index + 1), :] = part[...]
        shared_kept[ROWS * index : ROWS * (index + 1), :] = part[...]
    inject = inject_of(flags, shared)
    _, weight = weights_in(rates, table)
    for pair in range(PAIRS):
        weighted = (xc[:, lanes_of(pair)] * spread(weight, pair)).astype(bf16)
        out[KV + 128 * pair : KV + 128 * (pair + 1), :] = dot_tn(weighted, inject).astype(bf16)
    out[KV + XLOC : KV + MSG, :] = decay_rows(flags, rates_t)
    half = shared[pl.ds(rank_block(flags, 2 * flags[2] + flags[1] // 2), ROWS), :]
    out[0:KV, :] = jnp.concatenate([half[0:128], half[128:256]], axis=1)


def halves_kernel(msg1, msg2, msg3, out):
    for index, msg in enumerate((msg1, msg2, msg3)):
        out[KV * index : KV * (index + 1), :] = msg[...]


def allowed_pairs(table, seg_rows):
    rows = lax.broadcasted_iota(i32, (ROWS, ROWS), 0)
    return (rows >= lane_index((ROWS, ROWS))) & (segments(table) == seg_rows[0:1, :])


def head_decay(allowed, rates, rates_t, head):
    gap = rates[:, 128 + head : 129 + head] - rates_t[8 + head : 9 + head, :]
    return jnp.where(allowed, jnp.exp(jnp.where(allowed, gap, 0.0)), 0.0)


def intra_kernel(flags, shared, xc, rates, rates_t, table, seg_rows, small, out):
    inject, readout = inject_of(flags, shared), readout_of(flags, shared)
    both = dot_nt(readout, inject)
    allowed = allowed_pairs(table, seg_rows)
    low = lane_index((1, 128)) < HP
    for pair in range(PAIRS):
        x = xc[:, lanes_of(pair)]
        xb = x.astype(bf16)
        heads = []
        for head in (2 * pair, 2 * pair + 1):
            decay = head_decay(allowed, rates, rates_t, head)
            heads.append(dot_nn((both * decay * rates_t[head : head + 1, :]).astype(bf16), xb))
        out[:, lanes_of(pair)] = jnp.where(low, heads[0], heads[1]) + spread(small[2:3, 512:640], pair) * x


def keys_values(flags, shared, halves, swapped):
    head, first = flags[1] // 2, flags[2] == 0
    pairs = [
        (
            shared[pl.ds(rank_block(flags, head), ROWS), :],
            shared[pl.ds(rank_block(flags, 2 + head), ROWS), :],
        )
    ]
    for index, half in enumerate(halves):
        packed = half[...], swapped[KV * index : KV * (index + 1), :]
        mine, theirs = (jnp.concatenate([part[:, 0:128], part[:, 128:256]], axis=0) for part in packed)
        pairs.append((jnp.where(first, mine, theirs), jnp.where(first, theirs, mine)))
    return pairs


def masked_scores(query, pairs, table, seg_rows):
    parts = []
    for block, (keys, _) in enumerate(pairs):
        score = dot_nt(query, keys) * HD ** (-0.5)
        keep = segments(table) == seg_rows[block : block + 1, :]
        if block == 0:
            rows = lax.broadcasted_iota(i32, (ROWS, ROWS), 0)
            keep = keep & (rows >= lane_index((ROWS, ROWS)))
        parts.append(jnp.where(keep, score, -1e30))
    return parts


def attention_kernel(flags, query, shared, h1, h2, h3, swapped, table, seg_rows, out, log_total, kept):
    pairs = keys_values(flags, shared, (h1, h2, h3), swapped)
    for block, (keys, values) in enumerate(pairs):
        kept[ROWS * block : ROWS * (block + 1), 0:HD] = keys
        kept[ROWS * block : ROWS * (block + 1), HD : 2 * HD] = values
    parts = masked_scores(query[...], pairs, table, seg_rows)
    top = parts[0].max(axis=1, keepdims=True)
    for part in parts[1:]:
        top = jnp.maximum(top, part.max(axis=1, keepdims=True))
    parts = [jnp.exp(part - top) for part in parts]
    total = sum(part.sum(axis=1, keepdims=True) for part in parts)
    inverse = 1.0 / total
    result = jnp.zeros((ROWS, HD), f32)
    for part, (_, values) in zip(parts, pairs):
        result = result + dot_nn((part * inverse).astype(bf16), values)
    out[...] = result.astype(bf16)
    log_total[...] = jnp.broadcast_to(top + jnp.log(total), (ROWS, HD))


def chained(first, second, third, base):
    rows1 = first[base + XLOC : base + MSG, :].astype(f32)
    rows2 = second[base + XLOC : base + MSG, :].astype(f32)
    parts = []
    for head in range(HLOC):
        own = slice(base + HP * head, base + HP * head + HP)
        older = second[own, :].astype(f32) + rows2[head : head + 1, :] * third[own, :].astype(f32)
        parts.append(first[own, :].astype(f32) + rows1[head : head + 1, :] * older)
    return jnp.concatenate(parts, axis=0)


def carry_kernel(flags, msg1, msg2, msg3, shared, rates, table, intra, z, attn, state, ssm_y, cat, cat_kept):
    entering = chained(msg1, msg2, msg3, KV)
    state[...] = entering
    from_state = dot_nt(readout_of(flags, shared), entering.astype(bf16))
    carry = carry_of(rates, table)
    for pair in range(PAIRS):
        own = lanes_of(pair)
        y = intra[:, own] + spread(carry, pair) * from_state[:, own]
        ssm_y[:, own] = y
        gate = z[:, own]
        gated = (y * gate * sigmoid(gate)).astype(bf16)
        for block in range(8):
            for out in (cat, cat_kept):
                out[pl.ds(local_block(flags, block), SHARE), 128 + 128 * pair : 256 + 128 * pair] = gated[
                    SHARE * block : SHARE * (block + 1), :
                ]
    for block in range(8):
        for out in (cat, cat_kept):
            out[pl.ds(local_block(flags, block), SHARE), 0:128] = attn[SHARE * block : SHARE * (block + 1), :]


def gate_back_kernel(
    flags, p0, p1, p2, p3, p4, p5, p6, p7, weight, z, ssm_y, shared, rates, rates_t, table,
    dmix, dattn, dy, dz, msg, work, local,
):
    rows = joined((p0, p1, p2, p3, p4, p5, p6, p7))
    dmix[...] = rows
    local[...] = dot_nn(rows, weight[...])
    for block in range(8):
        own = slice(SHARE * block, SHARE * (block + 1))
        from_rows = pl.ds(local_block(flags, block), SHARE)
        dattn[own, :] = local[from_rows, 0:128].astype(bf16)
        work[own, :] = local[from_rows, 128:512]
    readout = readout_of(flags, shared)
    carry = carry_of(rates, table)
    for pair in range(PAIRS):
        own = lanes_of(pair)
        gate, grad = z[:, own], work[:, own]
        sig = sigmoid(gate)
        y_grad = grad * gate * sig
        dy[:, own] = y_grad
        dz[:, own] = (grad * ssm_y[:, own] * sig * (1.0 + gate * (1.0 - sig))).astype(bf16)
        msg[own, :] = dot_tn((y_grad * spread(carry, pair)).astype(bf16), readout).astype(bf16)
    msg[XLOC:MSG, :] = decay_rows(flags, rates_t)


def attention_back_kernel(
    flags, dattn, dz, query, kept, log_total, table, seg_rows,
    early, mine, theirs,
):
    pairs = []
    for block in range(SEQ_BLOCKS):
        own = slice(ROWS * block, ROWS * (block + 1))
        pairs.append((kept[own, 0:HD], kept[own, HD : 2 * HD]))
    first = flags[2] == 0
    q = query[...]
    grad = dattn[...]
    parts = masked_scores(q, pairs, table, seg_rows)
    logs = log_total[:, 0:1]
    probs = [jnp.exp(part - logs) for part in parts]
    grads = [dot_nt(grad, values) for _, values in pairs]
    inner = sum((p * g).sum(axis=1, keepdims=True) for p, g in zip(probs, grads))
    total = jnp.zeros((ROWS, HD), f32)
    for block, (p, g, (keys, _)) in enumerate(zip(probs, grads, pairs)):
        own = slice(ROWS * block, ROWS * (block + 1))
        score = (p * (g - inner)).astype(bf16)
        total = total + dot_nn(score, keys)
        dkeys = dot_tn(score, q) * HD ** (-0.5)
        dvalues = dot_tn(p.astype(bf16), grad)
        mine[own, :] = jnp.where(first, dkeys, dvalues)
        theirs[own, :] = jnp.where(first, dvalues, dkeys).astype(bf16)
    total = total * HD ** (-0.5)
    dq = turned(total, table, -1.0).astype(bf16)
    for block in range(8):
        own = slice(SHARE * block, SHARE * (block + 1))
        to_rows = pl.ds(local_block(flags, block), SHARE)
        early[to_rows, 0:XLOC] = dz[own, :]
        early[to_rows, XLOC:512] = dq[own, :]


def intra_back_kernel(
    flags, dy, xc, shared, rates, rates_t, table, seg_rows, state, small,
    dx, dshared, drates, dskip, row_sums, dcum,
):
    inject, readout = inject_of(flags, shared), readout_of(flags, shared)
    both = dot_nt(readout, inject)
    allowed = allowed_pairs(table, seg_rows)
    low = lane_index((1, 128)) < HP
    carry = carry_of(rates, table)
    entering = state[...].astype(bf16)
    from_state = dot_nt(readout, entering)
    dboth = jnp.zeros((ROWS, ROWS), f32)
    row_sums[...] = jnp.zeros((128, ROWS), f32)
    dcum[...] = jnp.zeros((ROWS, 128), f32)
    carried = []
    for pair in range(PAIRS):
        own = lanes_of(pair)
        x = xc[:, own]
        xb = x.astype(bf16)
        grad = dy[:, own]
        dskip[:, own] = jnp.sum(grad * x, axis=0, keepdims=True)
        carried.append((grad * spread(carry, pair)).astype(bf16))
        through = grad * from_state[:, own]
        total = spread(small[2:3, 512:640], pair) * grad
        for head in (2 * pair, 2 * pair + 1):
            mine = low if head % 2 == 0 else jnp.logical_not(low)
            decay = head_decay(allowed, rates, rates_t, head)
            steps = rates_t[head : head + 1, :]
            head_grad = jnp.where(mine, grad, 0.0).astype(bf16)
            dmix = dot_nt(head_grad, xb)
            kept = dmix * decay
            dboth = dboth + kept * steps
            mixed = both * decay
            total = total + dot_tn((mixed * steps).astype(bf16), head_grad)
            passed = dmix * mixed
            row_sums[head : head + 1, :] = jnp.sum(passed, axis=0, keepdims=True)
            dcum[:, head : head + 1] = jnp.sum(passed * steps, axis=1, keepdims=True) + carry[
                :, head : head + 1
            ] * jnp.sum(jnp.where(mine, through, 0.0), axis=1, keepdims=True)
        dx[:, own] = total
    columns = row_sums[...].T
    drates[:, 0:128] = columns
    drates[:, 128:256] = dcum[...] - rates[:, 0:128] * columns
    dboth_b = dboth.astype(bf16)
    dshared[:, NSTATE:] = dot_nn(dboth_b, inject) + dot_nn(jnp.concatenate(carried, axis=1), entering)
    dshared[:, 0:NSTATE] = dot_tn(dboth_b, readout)


def state_back_kernel(
    flags, msg1, msg2, msg3, shared, xc, rates, rates_t, table, state, small, dtn,
    dx, dshared, drates, kv0, kv1, kv2, kv3, ext,
    packed, dxpre, edge, gweight, ddt, heads, work, dconv, sums,
):
    later = chained(msg1, msg2, msg3, 0)
    later_b = later.astype(bf16)
    inject = inject_of(flags, shared)
    low = lane_index((1, 128)) < HP
    params = small[:, 512:640]
    gap, weights = weights_in(rates, table)
    from_later = dot_nt(inject, later_b)
    products = later * state[...]
    decays = block_decays(flags, rates_t)
    sums[...] = jnp.zeros((ROWS, 128), f32)
    weighted = []
    for pair in range(PAIRS):
        own = lanes_of(pair)
        x = xc[:, own]
        scale = spread(weights, pair)
        weighted.append((x * scale).astype(bf16))
        dconv[:, own] = dx[:, own] + scale * from_later[:, own]
        through = x * from_later[:, own]
        for head in (2 * pair, 2 * pair + 1):
            mine = low if head % 2 == 0 else jnp.logical_not(low)
            sums[:, head : head + 1] = jnp.sum(jnp.where(mine, through, 0.0), axis=1, keepdims=True)
    dweights = sums[...]
    moved = dweights * weights
    last = jnp.sum(moved, axis=0, keepdims=True)
    lanes = lane_index((1, 128))
    for head in range(HLOC):
        total = jnp.sum(
            jnp.sum(products[HP * head : HP * head + HP, :], axis=0, keepdims=True), axis=1, keepdims=True
        )
        last = last + jnp.where(lanes == head, total * decays[head : head + 1, :], 0.0)
    rows = lax.broadcasted_iota(i32, (ROWS, 128), 0)
    dcums = drates[:, 128:256] - moved + jnp.where(rows == ROWS - 1, last, 0.0)
    square = lax.broadcasted_iota(i32, (ROWS, ROWS), 0)
    upper = (square <= lane_index((ROWS, ROWS))).astype(f32)
    dlogs = jnp.dot(upper, dcums, precision=lax.Precision.HIGHEST, preferred_element_type=f32)
    rate = -jnp.exp(params[0:1, :])
    dsteps = drates[:, 0:128] + dweights * gap + dlogs * rate
    ddts = dsteps * sigmoid(dtn[...] + params[1:2, :])
    ddt[...] = ddts
    heads[...] = jnp.zeros((8, 128), f32)
    heads[0:1, :] = jnp.sum(dlogs * rate * rates[:, 0:128], axis=0, keepdims=True)
    heads[1:2, :] = jnp.sum(ddts, axis=0, keepdims=True)
    dinject_all = (dshared[:, 0:NSTATE] + dot_nn(jnp.concatenate(weighted, axis=1), later_b)).astype(bf16)
    dreadout_all = dshared[:, NSTATE:].astype(bf16)
    packed[...] = jnp.zeros((8 * ROWS, 128), bf16)
    grads = kv0[...] + kv1[...].astype(f32) + kv2[...].astype(f32) + kv3[...].astype(f32)
    owner = 2 * flags[2] + flags[1] // 2
    packed[pl.ds(rank_block(flags, owner), ROWS), :] = grads.astype(bf16)
    packed[pl.ds(rank_block(flags, 4), ROWS), :] = dinject_all[:, 0:128]
    packed[pl.ds(rank_block(flags, 5), ROWS), :] = dinject_all[:, 128:256]
    packed[pl.ds(rank_block(flags, 6), ROWS), :] = dreadout_all[:, 0:128]
    packed[pl.ds(rank_block(flags, 7), ROWS), :] = dreadout_all[:, 128:256]
    conv_back(dconv[...], ext, table, small[:, 0:XLOC], work, dxpre, edge, gweight)


def shared_back_kernel(flags, part0, part1, part2, part3, ext, table, small, out, edge, gweight, work):
    grad = part0[...] + part1[...].astype(f32) + part2[...].astype(f32) + part3[...].astype(f32)
    conv_back(grad, ext, table, small[:, XLOC:512], work, out, edge, gweight)
    rank = flags[0]
    of_conv = jnp.where(rank < 4, 0.0, 1.0)
    edge[...] = edge[...] * of_conv
    gweight[...] = gweight[...] * of_conv
    out[...] = jnp.where(rank < 2, turned(grad, table, -1.0), jnp.where(rank < 4, grad, out[...]))


def late_kernel(flags, dxpre, edge_x, dsh, edge_sh, ddt, out):
    for block in range(8):
        own = slice(SHARE * block, SHARE * (block + 1))
        to_rows = pl.ds(local_block(flags, block), SHARE)
        x, sh = dxpre[own, :], dsh[own, :]
        if block == 7:
            pad = jnp.zeros((SHARE - 8, 128), f32)
            sh = sh + jnp.concatenate([pad, edge_sh[...]], axis=0)
            x = x + jnp.concatenate([jnp.zeros((SHARE - 8, XLOC), f32), edge_x[...]], axis=0)
        out[to_rows, 0:XLOC] = x.astype(bf16)
        out[to_rows, XLOC:512] = sh.astype(bf16)
        out[to_rows, 512:LATE] = jnp.where(lane_index((1, 128)) < HLOC, ddt[own, :], 0.0).astype(bf16)


def half_sum_kernel(own, other, keep, send1, send2, send3):
    rows = own.shape[0] // 4
    keep[...] = own[0:rows, :] + other[0:rows, :].astype(f32)
    for index, send in ((1, send1), (2, send2), (3, send3)):
        part = slice(rows * index, rows * (index + 1))
        send[...] = (own[part, :].astype(f32) + other[part, :].astype(f32)).astype(bf16)


def parts_of_sum(own, other, along, sign):
    return parts_from(own, other_core(other), along, sign)


def parts_from(own, got, along, sign):
    rows, width = own.shape[0] // 4, own.shape[1]
    sent = shape_of((rows, width), bf16)
    keep, *sends = run_kernel(half_sum_kernel, [kept((rows, width)), sent, sent, sent], None, own, Columns(got))
    return (keep,) + tuple(along(send, sign * k) for k, send in zip((1, 2, 3), sends))


def split_kernel(*refs):
    lefts, weight, own, other = refs[:-3], refs[-3], refs[-2], refs[-1]
    left = lefts[0][...] if len(lefts) == 1 else jnp.concatenate([ref[...] for ref in lefts], axis=1)
    result = dot_nt(left, weight[...])
    own[...] = result[: ROWS // 2]
    other[...] = result[ROWS // 2 :].astype(bf16)


def summed_rows(lefts, weight):
    model, width = weight.shape
    own, other = pl.pallas_call(
        split_kernel,
        grid=(model // 512,),
        out_shape=(shape_of((ROWS // 2, model)), shape_of((ROWS // 2, model), bf16)),
        in_specs=[pl.BlockSpec(left.shape, lambda i: (0, 0)) for left in lefts]
        + [pl.BlockSpec((512, width), lambda i: (i, 0))],
        out_specs=(
            pl.BlockSpec((ROWS // 2, 512), lambda i: (0, i)),
            pl.BlockSpec((ROWS // 2, 512), lambda i: (0, i)),
        ),
        compiler_params=pltpu.CompilerParams(vmem_limit_bytes=VMEM_LIMIT),
        cost_estimate=pl.CostEstimate(
            flops=2 * ROWS * model * width, bytes_accessed=2 * model * width, transcendentals=0
        ),
    )(*lefts, weight)
    return parts_of_sum(own, other, along_y, 1)


def gate_up_kernel(p0, p1, p2, p3, p4, p5, p6, p7, weight, normed, gate, up, act, act_kept):
    rows = joined((p0, p1, p2, p3, p4, p5, p6, p7))
    normed[...] = rows
    result = dot_nn(rows, weight[...])
    g, u = result[:, :512], result[:, 512:]
    gate[...] = g
    up[...] = u
    for out in (act, act_kept):
        out[...] = (g * sigmoid(g) * u).astype(bf16)


def gate_up_back_kernel(*refs):
    parts, (weight, gate, up, dffn, out) = refs[:-5], refs[-5:]
    rows = joined(parts)
    dffn[...] = rows
    dact = dot_nn(rows, weight[...])
    g = gate[...]
    sig = sigmoid(g)
    out[:, :512] = (dact * up[...] * sig * (1.0 + g * (1.0 - sig))).astype(bf16)
    out[:, 512:] = (dact * g * sig).astype(bf16)


def natural_kernel(flags, p0, p1, p2, p3, p4, p5, p6, p7, out):
    local = joined((p0, p1, p2, p3, p4, p5, p6, p7)).astype(out.dtype)
    for block in range(8):
        out[pl.ds(pl.multiple_of(flags[24 + block] * SHARE, SHARE), SHARE), :] = local[
            SHARE * block : SHARE * (block + 1), :
        ]


def add_norm_kernel(hidden, part0, part1, part2, part3, gain, out, out_kept, normed, inverse):
    total = hidden[...] + part0[...] + (
        part1[...].astype(f32) + part2[...].astype(f32) + part3[...].astype(f32)
    )
    out[...] = total
    out_kept[...] = total
    scale = lax.rsqrt(jnp.mean(total * total, axis=1, keepdims=True) + norm_eps)
    inverse[...] = jnp.broadcast_to(scale, inverse.shape)
    normed[...] = (total * scale * gain[...]).astype(bf16)


def add_norm(hidden, parts, gain):
    shape = hidden.shape
    return run_kernel(
        add_norm_kernel,
        [shape_of(shape), kept(shape), shape_of(shape, bf16), kept((shape[0], 128))],
        None, hidden, *passed(parts), gain[None],
    )


def output_kernel(hidden, part0, part1, part2, part3, out):
    total = hidden[...] + part0[...] + (
        part1[...].astype(f32) + part2[...].astype(f32) + part3[...].astype(f32)
    )
    out[...] = total.astype(bf16)


def norm_back_kernel(grad, part0, part1, part2, part3, hidden, inverse, gain, out, rounded, ggain):
    received = part0[...] + (part1[...].astype(f32) + part2[...].astype(f32) + part3[...].astype(f32))
    scale = inverse[:, 0:1]
    unit = hidden[...] * scale
    scaled = received * gain[...]
    ggain[...] = jnp.sum(received * unit, axis=0, keepdims=True)
    total = grad[...] + scale * (scaled - unit * jnp.mean(scaled * unit, axis=1, keepdims=True))
    out[...] = total
    rounded[...] = total.astype(bf16)


def norm_back(grad, parts, hidden, inverse, gain):
    shape = hidden.shape
    return run_kernel(
        norm_back_kernel,
        [kept(shape), shape_of(shape, bf16), kept((1, shape[1]))],
        None, grad, *passed(parts), stored(hidden), stored(inverse), gain[None],
    )


def gradient_kernel(pairs, *refs):
    out, at = refs[-1], 0
    for index in range(pairs):
        left, right = refs[2 * index], refs[2 * index + 1]
        width = right.shape[1]
        out[:, at : at + width] = dot_tn(left[...], right[...]).astype(bf16)
        at += width


def weight_gradients(pairs, total, block, index, buffer=None):
    rows, model = pairs[0][0].shape
    width = sum(right.shape[1] for _, right in pairs)
    specs, args = [], []
    for left, right in pairs:
        specs += [
            pl.BlockSpec((rows, 512), lambda i: (0, i)),
            pl.BlockSpec(right.shape, lambda i: (0, 0)),
        ]
        args += [left, right]
    aliases = {}
    kernel = partial(gradient_kernel, len(pairs))
    if buffer is not None:
        aliases = {len(args): 0}
        specs.append(pl.BlockSpec(memory_space=pltpu.HBM))
        args.append(buffer)

        def kernel(*refs):
            gradient_kernel(len(pairs), *refs[:-2], refs[-1])

    return pl.pallas_call(
        kernel,
        grid=(model // 512,),
        out_shape=pltpu.HBM((model, total), bf16),
        in_specs=specs,
        out_specs=pl.BlockSpec((512, block), lambda i: (i, index)),
        input_output_aliases=aliases,
        compiler_params=pltpu.CompilerParams(vmem_limit_bytes=VMEM_LIMIT),
        cost_estimate=pl.CostEstimate(
            flops=2 * rows * model * width, bytes_accessed=model * width * 2, transcendentals=0
        ),
    )(*args)


def owned_kernel(left, right, small, out):
    result = dot_tn(left[...], right[...]).astype(bf16)
    for index in range(2):
        out[index, :, 0:LATE] = result[128 * index : 128 * (index + 1)]
        out[index, :, LATE : LATE + 128] = small[...]


def owned_gradients(left, right, small):
    rows, model = left.shape
    width = right.shape[1]
    return pl.pallas_call(
        owned_kernel,
        grid=(model // 256,),
        out_shape=shape_of((16, model // 16, width + 128), bf16),
        in_specs=[
            pl.BlockSpec((rows, 256), lambda i: (0, i)),
            pl.BlockSpec(right.shape, lambda i: (0, 0)),
            pl.BlockSpec(small.shape, lambda i: (0, 0)),
        ],
        out_specs=pl.BlockSpec((2, model // 16, width + 128), lambda i: (i, 0, 0)),
        compiler_params=pltpu.CompilerParams(vmem_limit_bytes=VMEM_LIMIT),
        cost_estimate=pl.CostEstimate(
            flops=2 * rows * model * width, bytes_accessed=model * width * 2, transcendentals=0
        ),
    )(left, right, small)


def small_kernel(gain1, gain2, conv_sh, conv_x, heads, skip, out):
    out[...] = jnp.zeros(out.shape, bf16)
    for row in range(16):
        own = slice(128 * row, 128 * row + 128)
        out[row : row + 1, :] = gain1[:, own].astype(bf16)
        out[16 + row : 17 + row, :] = gain2[:, own].astype(bf16)
    out[32:37, :] = conv_sh[0:5, :].astype(bf16)
    for tap in range(CONV + 1):
        for pair in range(PAIRS):
            row = 37 + PAIRS * tap + pair
            out[row : row + 1, :] = conv_x[tap : tap + 1, lanes_of(pair)].astype(bf16)
    out[52:54, :] = heads[0:2, :].astype(bf16)
    lanes = lane_index((1, 128))
    sums = jnp.zeros((1, 128), f32)
    for pair in range(PAIRS):
        part = skip[:, lanes_of(pair)]
        for half in range(2):
            mine = (lanes < HP) if half == 0 else (lanes >= HP)
            total = jnp.sum(jnp.where(mine, part, 0.0), axis=1, keepdims=True)
            sums = sums + jnp.where(lanes == 2 * pair + half, total, 0.0)
    out[54:55, :] = sums.astype(bf16)


def block_sum_kernel(values, shared, late, over_tp, conv_x, heads):
    whole = values[0].astype(f32)
    for index in range(1, 16):
        whole = whole + values[index].astype(f32)
    shared[...] = whole[:, XLOC:512].astype(bf16)
    late[...] = whole[:, 0:LATE]
    total = whole[:, LATE : LATE + 128]
    over_tp[...] = jnp.zeros(over_tp.shape, bf16)
    for layer in range(2):
        first = 64 * layer
        over_tp[48 * layer : 48 * layer + 37, :] = total[first : first + 37, :].astype(bf16)
        for tap in range(CONV + 1):
            for pair in range(PAIRS):
                row = first + 37 + PAIRS * tap + pair
                conv_x[5 * layer + tap : 5 * layer + tap + 1, lanes_of(pair)] = total[row : row + 1, :]
        heads[3 * layer : 3 * layer + 3, :] = total[first + 52 : first + 55, :]


def small_last_kernel(flags, p0, p1, p2, p3, p4, p5, p6, p7, gains1, gains2, conv_bc, every):
    total = jnp.zeros((96, 128), f32)
    for index, part in enumerate((p0, p1, p2, p3, p4, p5, p6, p7)):
        every[index] = part[...].astype(f32)
        total = total + every[index]
    for layer in range(2):
        for row in range(16):
            own = slice(128 * row, 128 * row + 128)
            at = 48 * layer + row
            gains1[layer : layer + 1, own] = total[at : at + 1, :]
            gains2[layer : layer + 1, own] = total[at + 16 : at + 17, :]
        for rank in range(4):
            part = every[flags[20 + rank]]
            conv_bc[5 * layer : 5 * layer + 5, 128 * rank : 128 * rank + 128] = part[
                48 * layer + 32 : 48 * layer + 37, :
            ]


def shared_last_kernel(flags, *refs):
    parts, out = refs[:-1], refs[-1]
    rows = jnp.stack([part[...] for part in parts[:8]]), jnp.stack([part[...] for part in parts[8:]])
    for layer in range(2):
        for index in range(8):
            for rank in range(8):

                @pl.when(flags[16 + rank] == index)
                def _():
                    out[layer, :, 128 * rank : 128 * rank + 128] = rows[layer][index].astype(f32)


def outputs_kernel(lower, upper, late, query, dt, attn, ssm, gate, up, down, z, x):
    for layer, ref in ((0, lower), (1, upper)):
        for index, out in enumerate((gate, up, down)):
            out[layer] = ref[:, 512 * index : 512 * (index + 1)].astype(f32)
        attn[layer] = ref[:, 1536:1664].astype(f32)
        ssm[layer] = ref[:, 1664:2048].astype(f32)
        z[layer] = ref[:, 2048:2432].astype(f32)
        query[layer] = ref[:, 2432:2560].astype(f32)
    x[0] = late[:, 0:XLOC]
    dt[0] = late[:, 512 : 512 + HLOC]
    x[1] = lower[:, 2560:2944].astype(f32)
    dt[1] = lower[:, 3072 : 3072 + HLOC].astype(f32)


def body(
    inputs, cotangent, segment_ids, w_query, w_shared, w_zx, w_dt, w_attn_out, w_ssm_out, w_gate, w_up, w_down,
    gains, conv_x, conv_bc, head_params,
):
    layers = w_query.shape[0]
    rank, ctx = lax.axis_index("tp"), lax.axis_index("ctx")
    y, core = rank // 2, rank % 2
    model = inputs.shape[2]

    def local_of(block_y, block_core):
        return jnp.where(block_core == core, 0, 4) + (block_y - y) % 4

    seg_all = segment_ids[0]
    first_row = ctx * ROWS
    padded = jnp.concatenate([jnp.full((CONV - 1,), -1, i32), seg_all])
    seg_ext = lax.dynamic_slice_in_dim(padded, first_row, ROWS + CONV - 1)
    seg_own = seg_ext[CONV - 1 :]
    blocks = seg_all.reshape(SEQ_BLOCKS, ROWS)
    seg_rows = jnp.stack(
        [
            jnp.where(ctx >= back, lax.dynamic_index_in_dim(blocks, jnp.maximum(ctx - back, 0), 0, False), -1)
            for back in range(SEQ_BLOCKS)
        ]
        + [jnp.full((ROWS,), -1, i32)] * 4
    ).astype(f32)
    naturals = jnp.arange(8, dtype=i32)
    flags = jnp.concatenate(
        [
            jnp.stack([rank, y, core, ctx, seg_ext[CONV - 2], seg_own[-1], rank, rank]).astype(i32),
            local_of(naturals % 4, naturals // 4).astype(i32),
            local_of(naturals // 2, naturals % 2).astype(i32),
            (jnp.where(naturals < 4, core, 1 - core) * 4 + (y + naturals) % 4).astype(i32),
        ]
    )

    half_width = HD // 2
    frequency = rope_base ** (-jnp.arange(half_width, dtype=f32) / half_width)
    places = (first_row + jnp.arange(ROWS, dtype=i32)).astype(f32)
    angles = places[:, None] * frequency[None, :]
    cosine, sine = jnp.cos(angles), jnp.sin(angles)
    marks = [seg_ext[tap : tap + ROWS] == seg_own for tap in range(CONV - 1)]
    marks += [seg_own, seg_own == seg_ext[CONV - 2], seg_own == seg_own[-1]]
    marks = jnp.pad(jnp.stack([mark.astype(f32) for mark in marks], axis=1), ((0, 0), (0, 122)))
    table = jnp.concatenate([cosine, cosine, -sine, sine, marks], axis=1)

    own_conv = jnp.maximum(rank - 4, 0) * 128
    small = []
    for layer in range(layers):
        rows = [conv_x[layer], lax.dynamic_slice_in_dim(conv_bc[layer], own_conv, 128, 1)]
        rows.append(jnp.pad(head_params[layer], ((0, 2), (0, 128 - HLOC))))
        small.append(jnp.pad(jnp.concatenate(rows, axis=1), ((0, 3), (0, 0))))

    def packed(*members):
        width = sum(
            {4: 2 * XLOC}.get(member.ndim, 128 if member.shape[2] in (1024, HLOC) else member.shape[2])
            for member, _ in members
        )
        (columns,) = run_kernel(
            pack_kernel,
            [shape_of((w_query.shape[1], width), bf16)],
            rank.astype(i32).reshape(1),
            *(Layer(member, layer) for member, layer in members),
        )
        return lax.all_gather(columns, ("fsdp", "ctx"), axis=0, tiled=True)

    def proj_members(layer):
        return [(member, layer) for member in (w_zx, w_query, w_shared, w_dt)]

    weight_a = packed(*proj_members(0), (w_attn_out, 0), (w_ssm_out, 0))
    weight_b = packed(*proj_members(1), (w_gate, 0), (w_up, 0), (w_down, 0))
    weight_c = packed((w_gate, 1), (w_up, 1), (w_down, 1), (w_attn_out, 1), (w_ssm_out, 1))
    proj_place = [(weight_a, 0, PROJ), (weight_b, 0, PROJ)]
    out_place = [(weight_a, PROJ, 512), (weight_c, 1536, 512)]
    gate_up_place = [(weight_b, PROJ, 1024), (weight_c, 0, 1024)]
    down_place = [(weight_b, PROJ + 1024, 512), (weight_c, 1024, 512)]

    def together(*values):
        return lax.optimization_barrier(values)

    weight_a, table, seg_rows, small = together(weight_a, table, seg_rows, small)
    normed_shape = shape_of((ROWS, model), bf16)
    normed_kept = kept((ROWS, model), bf16)
    share = shape_of((SHARE, model))
    normed_b, inverse1, hidden, hidden_kept, dffn_b, grad_hidden = run_kernel(
        first_kernel,
        [normed_shape, kept((SHARE, 128)), share, kept((SHARE, model)), normed_kept, kept((SHARE, model))],
        flags, inputs, cotangent, gains[0],
    )
    weight_a, normed_b = together(weight_a, normed_b)
    proj_place[0] = (weight_a, 0, PROJ)
    out_place[0] = (weight_a, PROJ, 512)
    normed_parts, dffn_parts = (normed_b,), (dffn_b,)
    saved = []
    wide = shape_of((ROWS, 512))
    proj_weight = fetched("proj_0", *proj_place[0])
    for layer in range(layers):
        normed_b, z, z_kept, xs, query, query_kept, dtn, dtn_kept = run_kernel(
            proj_kernel,
            [
                normed_kept, shape_of((ROWS, XLOC)), kept((ROWS, XLOC)), wide, shape_of((ROWS, HD), bf16),
                kept((ROWS, HD), bf16), shape_of((ROWS, 128)), kept((ROWS, 128)),
            ],
            flags, *(passed(normed_parts) if layer > 0 else normed_parts), proj_weight, table,
            scratch=[pltpu.VMEM((ROWS, PROJ), f32)],
        )
        halo = along_ctx(xs[ROWS - 8 :], 1)
        shared_own, shared_ext = run_kernel(
            shared_kernel,
            [shape_of((ROWS, 128), bf16), kept((264, 128))],
            flags, xs, Columns(halo), table, small[layer],
        )
        shared_parts = from_all(shared_own)
        x_ext, xc, xc_kept, rates, rates_kept, rates_t, rates_t_kept = run_kernel(
            prep_kernel,
            [
                kept((264, XLOC)), shape_of((ROWS, XLOC)), kept((ROWS, XLOC)), shape_of((ROWS, 256)),
                kept((ROWS, 256)), shape_of((16, ROWS)), kept((16, ROWS)),
            ],
            None, xs, dtn, Columns(halo), table, small[layer],
        )
        message, shared, shared_kept = run_kernel(
            state_kernel,
            [shape_of((KV + MSG, NSTATE), bf16), shape_of((8 * ROWS, 128), bf16), kept((8 * ROWS, 128), bf16)],
            flags, *passed(shared_parts), xc, rates, rates_t, table,
        )
        earlier = tuple(along_ctx(message, back) for back in (1, 2, 3))
        (intra,) = run_kernel(
            intra_kernel, [shape_of((ROWS, XLOC))],
            flags, shared, xc, rates, rates_t, table, seg_rows, small[layer],
        )
        earlier, out_weight, intra = together(earlier, fetched(f"out_{layer}", *out_place[layer]), intra)
        halves = [Columns(part, 0, NSTATE, rows=KV) for part in earlier]
        (swapped,) = run_kernel(halves_kernel, [shape_of((3 * KV, NSTATE), bf16)], None, *halves)
        attn, log_total, pairs = run_kernel(
            attention_kernel,
            [shape_of((ROWS, HD), bf16), kept((ROWS, HD)), kept((SEQ_BLOCKS * ROWS, 2 * HD), bf16)],
            flags, query, shared, *halves, Columns(other_core(swapped)), table, seg_rows,
        )
        state, ssm_y, cat, cat_kept = run_kernel(
            carry_kernel,
            [kept((XLOC, NSTATE)), kept((ROWS, XLOC)), shape_of((ROWS, 512), bf16), kept((ROWS, 512), bf16)],
            flags, *passed(earlier), shared, rates, table, intra, z, attn,
        )
        parts = summed_rows([cat], out_weight)
        if layer > 0:
            parts, gate_up_weight = together(parts, fetched(f"gate_up_{layer}", *gate_up_place[layer]))
        hidden1, hidden1_kept, normed2, inverse2 = add_norm(hidden, parts, gains[layer, 1])
        normed_parts = from_all(normed2)
        if layer > 0:
            normed_parts, down_weight = together(normed_parts, fetched(f"down_{layer}", *down_place[layer]))
        else:
            gate_up_weight, down_weight = fetched_all("ffn_0", [gate_up_place[layer], down_place[layer]])
        wide_kept = kept((ROWS, 512))
        normed2_b, gate, up, act_b, act_kept = run_kernel(
            gate_up_kernel, [normed_kept, wide_kept, wide_kept, shape_of((ROWS, 512), bf16), kept((ROWS, 512), bf16)],
            None, *passed(normed_parts), gate_up_weight,
        )
        saved.append(
            (
                hidden_kept, normed_b, inverse1, shared_ext, shared_kept, query_kept, x_ext, xc_kept, z_kept, dtn_kept,
                rates_kept, rates_t_kept, pairs, log_total, state, ssm_y, cat_kept, hidden1_kept, inverse2, normed2_b,
                gate, up, act_kept,
            )
        )
        if layer + 1 < layers:
            hidden, hidden_kept, next_normed, inverse1 = add_norm(
                hidden1, summed_rows([act_b], down_weight), gains[layer + 1, 0]
            )
            normed_parts, proj_weight = together(from_all(next_normed), fetched("proj_1", *proj_place[layer + 1]))

    weight_sums = [None] * layers
    small_parts = [None] * layers
    inner = None
    for layer in reversed(range(layers)):
        (
            hidden, normed_b, inverse1, shared_ext, shared, query, x_ext, xc, z, dtn, rates, rates_t,
            pairs, log_total, state, ssm_y, cat, hidden1, inverse2, normed2_b, gate, up, act_b,
        ) = saved[layer]
        last = layer == 0
        dffn_b, dgate_up = run_kernel(
            gate_up_back_kernel, [normed_kept, shape_of((ROWS, 1024), bf16)],
            None, *passed(dffn_parts), down_weight, stored(gate), stored(up),
        )
        parts = summed_rows([dgate_up], gate_up_weight)
        outer = weight_gradients([(normed2_b, dgate_up), (dffn_b, act_b)], 3200 if last else 2560, 1536, 0, inner)
        parts, outer = lax.optimization_barrier((parts, outer))
        grad_mid, dmix, ggain2 = norm_back(grad_hidden, parts, hidden1, inverse2, gains[layer, 1])
        dmix_parts = from_all(dmix)
        fetch = fetched_all(
            f"mixer_{layer}",
            [out_place[layer]]
            + [(array, 0, array.shape[1]) for array in (z, ssm_y, shared, rates, rates_t, xc, query, pairs, state)],
        )
        dmix_parts, fetch = together(dmix_parts, fetch)
        out_weight, z, ssm_y, shared, rates, rates_t, xc, query, pairs, state = fetch
        dmix_b, dattn, dy, dz, message = run_kernel(
            gate_back_kernel,
            [
                normed_kept, shape_of((ROWS, HD), bf16), shape_of((ROWS, XLOC)), shape_of((ROWS, XLOC), bf16),
                shape_of((MSG, NSTATE), bf16),
            ],
            flags, *passed(dmix_parts), out_weight, z, ssm_y, shared, rates, rates_t, table,
            scratch=[pltpu.VMEM((ROWS, XLOC), f32), pltpu.VMEM((ROWS, 512), f32)],
        )
        after = tuple(along_ctx(message, -ahead) for ahead in (1, 2, 3))
        early, mine, theirs = run_kernel(
            attention_back_kernel,
            [kept((ROWS, 512), bf16), shape_of((4 * ROWS, HD)), shape_of((4 * ROWS, HD), bf16)],
            flags, dattn, dz, query, pairs, stored(log_total), table, seg_rows,
        )
        got = other_core(theirs)
        dx, dshared, drates, dskip = run_kernel(
            intra_back_kernel,
            [kept((ROWS, XLOC)), kept((ROWS, 2 * NSTATE)), kept((ROWS, 256)), kept((1, XLOC))],
            flags, dy, xc, shared, rates, rates_t, table, seg_rows, state, small[layer],
            scratch=[pltpu.VMEM((128, ROWS), f32), pltpu.VMEM((ROWS, 128), f32)],
        )
        got, dx = lax.optimization_barrier((got, dx))
        dkv = parts_from(mine, got, along_ctx, -1)
        outer = weight_gradients([(dmix_b, cat)], outer.shape[1], 512, 3, outer)
        outer = weight_gradients([(normed_b, early)], outer.shape[1], 512, 4, outer)
        after, dkv, outer, proj_weight = together(after, dkv, outer, fetched(f"proj_again_{layer}", *proj_place[layer]))
        packed_grads, dxpre, edge_x, gconv_x, ddt, gheads = run_kernel(
            state_back_kernel,
            [
                shape_of((8 * ROWS, 128), bf16), kept((ROWS, XLOC)), shape_of((8, XLOC)), kept((8, XLOC)),
                kept((ROWS, 128)), kept((8, 128)),
            ],
            flags, *passed(after), shared, xc, rates, rates_t, table, state, small[layer], stored(dtn), stored(dx), stored(dshared), stored(drates), *passed(dkv), stored(x_ext),
            scratch=[pltpu.VMEM((272, XLOC), f32), pltpu.VMEM((ROWS, XLOC), f32), pltpu.VMEM((ROWS, 128), f32)],
        )
        if last:
            outer, weight_sums[1] = together(outer, weight_sums[1])
        weight_sums[layer] = lax.psum_scatter(outer, ("fsdp", "ctx"), scatter_dimension=0, tiled=True)
        edge_x = along_ctx(edge_x, -1)
        dshared_parts = parts_of_sum(packed_grads[: 4 * ROWS], packed_grads[4 * ROWS :], along_y, 1)
        dsh, edge_sh, gconv_sh = run_kernel(
            shared_back_kernel,
            [shape_of((ROWS, 128)), shape_of((8, 128)), kept((8, 128))],
            flags, *passed(dshared_parts), stored(shared_ext), table, small[layer],
            scratch=[pltpu.VMEM((272, 128), f32)],
        )
        edge_sh = along_ctx(edge_sh, -1)
        (late,) = run_kernel(
            late_kernel, [shape_of((ROWS, LATE), bf16)], flags, stored(dxpre), Columns(edge_x), dsh,
            Columns(edge_sh), stored(ddt),
        )
        parts = summed_rows([early, late], proj_weight)
        if not last:
            inner = weight_gradients([(normed_b, late)], 3200, LATE, 4)
            parts, inner = together(parts, inner)
        grad_hidden, rounded, ggain1 = norm_back(grad_mid, parts, hidden, inverse1, gains[layer, 0])
        dffn_parts = from_all(rounded)
        if not last:
            down_weight, gate_up_weight = fetched_all("ffn_again", [down_place[layer - 1], gate_up_place[layer - 1]])
            dffn_parts, down_weight, gate_up_weight = together(dffn_parts, down_weight, gate_up_weight)
            last_hidden1, last_act = hidden1, act_b
        (small_parts[layer],) = run_kernel(
            small_kernel, [shape_of((64, 128), bf16)],
            None, *map(stored, (ggain1, ggain2, gconv_sh, gconv_x, gheads, dskip)),
        )
    small_all = jnp.concatenate(small_parts, axis=0)
    owned = lax.all_to_all(owned_gradients(normed_b, late, small_all), ("fsdp", "ctx"), 0, 0, tiled=True)
    (input_grad,) = run_kernel(natural_kernel, [kept((ROWS, model))], flags, *passed(dffn_parts))
    last_act, down_weight, _ = together(last_act, fetched("down_last", *down_place[1]), small_parts[0])
    (layer_out,) = run_kernel(
        output_kernel, [shape_of((SHARE, model), bf16)], None,
        stored(last_hidden1), *passed(summed_rows([last_act], down_weight)),
    )
    (layer_out,) = run_kernel(natural_kernel, [normed_kept], flags, *passed(from_all(layer_out)))
    owned, layer_out, input_grad = together(owned, layer_out, input_grad)
    late_shared, late_sum, over_tp, gconv_x, gheads = run_kernel(
        block_sum_kernel,
        [
            shape_of((model // 16, 128), bf16), shape_of((model // 16, LATE)), shape_of((96, 128), bf16),
            shape_of((layers * (CONV + 1), XLOC)), shape_of((8, 128)),
        ],
        None, Columns(owned),
    )
    ggains1, ggains2, gconv_bc = run_kernel(
        small_last_kernel,
        [shape_of((layers, model)), shape_of((layers, model)), shape_of((layers * (CONV + 1), 512))],
        flags, *passed(from_all(over_tp)),
        scratch=[pltpu.VMEM((8, 96, 128), f32)],
    )
    gconv_x = gconv_x.reshape(layers, CONV + 1, XLOC)
    gconv_bc = gconv_bc.reshape(layers, CONV + 1, 512)
    gheads = gheads[: 3 * layers].reshape(layers, 3, 128)[:, :, :HLOC]

    lower, upper = weight_sums
    (grad_shared,) = run_kernel(
        shared_last_kernel,
        [shape_of((layers, model // 16, 1024))],
        flags, *passed(from_all(late_shared)), *passed(from_all(lower[:, 2944:3072])),
    )

    def pair_of(width):
        return shape_of((layers, model // 16, width))

    grad_query, grad_dt, grad_attn, grad_ssm, grad_gate, grad_up, grad_down, grad_z, grad_x = run_kernel(
        outputs_kernel, [pair_of(width) for width in (128, HLOC, 128, 384, 512, 512, 512, XLOC, XLOC)],
        None, Columns(lower), Columns(upper), late_sum,
    )
    return (
        layer_out[None],
        input_grad[None],
        grad_query,
        grad_shared,
        jnp.stack([grad_z, grad_x], axis=2),
        grad_dt,
        grad_attn,
        grad_ssm,
        grad_gate,
        grad_up,
        grad_down,
        ggains1,
        gconv_x,
        gconv_bc,
        gheads[:, :2],
        ggains2,
        gheads[:, 2],
    )


def solution(mesh):
    columns = P(None, ("fsdp", "ctx"), "tp")
    rows = P("fsdp", "ctx", None)
    return jax.shard_map(
        body,
        mesh=mesh,
        in_specs=(
            rows, rows, P("fsdp", None), columns, P(None, ("fsdp", "ctx"), None),
            P(None, ("fsdp", "ctx"), None, "tp"), columns, columns, columns, columns, columns, columns,
            P(), P(None, None, "tp"), P(), P(None, None, "tp"),
        ),
        out_specs=(
            rows, rows, columns, P(None, ("fsdp", "ctx"), None), P(None, ("fsdp", "ctx"), None, "tp"),
            columns, columns, columns, columns, columns, columns,
            P(), P(None, None, "tp"), P(), P(None, None, "tp"), P(), P(None, "tp"),
        ),
        check_vma=False,
    )
```

```python
import math
from functools import partial

import jax
import jax.numpy as jnp
from jax import lax
from jax.experimental import pallas as pl
from jax.experimental.pallas import tpu as pltpu
from jax.sharding import PartitionSpec as P

HD = 128
HP = 64
NSTATE = 256
CONV = 4
ROWS = 256
SHARE = 32
XLOC = 384
PROJ = 1152
LATE = 640
HLOC = 6
PAIRS = 3
SEQ_BLOCKS = 4
MSG = XLOC + 16
KV = 128
VMEM_LIMIT = 16 * 1024 * 1024

norm_eps = 1e-05
rope_base = 100000000000.0
bf16 = jnp.bfloat16
f32 = jnp.float32
i32 = jnp.int32


def along_y(value, steps):
    pairs = [(i, ((i // 2 + steps) % 4) * 2 + i % 2) for i in range(8)]
    return lax.ppermute(value, "tp", pairs)


def other_core(value):
    return lax.ppermute(value, "tp", [(i, i ^ 1) for i in range(8)])


def along_ctx(value, steps):
    first, last = max(0, -steps), min(4, 4 - steps)
    return lax.ppermute(value, "ctx", [(i, i + steps) for i in range(first, last)])


def ring(value, axis, steps):
    return lax.ppermute(value, axis, [(i, (i + steps) % 4) for i in range(4)])


def from_all(value, beside=None):
    half = [value] + [along_y(value, -k) for k in (1, 2, 3)]
    if beside is not None:
        half, beside = lax.optimization_barrier((half, beside))
    parts = tuple(half + [other_core(part) for part in half])
    return parts if beside is None else (parts, beside)


def dot_nn(a, b):
    return jnp.dot(a, b, preferred_element_type=f32)


def dot_nt(a, b):
    return lax.dot_general(a, b, (((1,), (1,)), ((), ())), preferred_element_type=f32)


def dot_tn(a, b):
    return lax.dot_general(a, b, (((0,), (0,)), ((), ())), preferred_element_type=f32)


def shape_of(shape, dtype=f32):
    return jax.ShapeDtypeStruct(shape, dtype)


class Columns:
    def __init__(self, array, block=0, width=None, rows=None, keep=False):
        self.array, self.block, self.keep = array, block, keep
        self.shape = (rows or array.shape[0],) + array.shape[1:-1] + (width or array.shape[-1],)

    def spec(self):
        place = (0,) * (len(self.shape) - 1) + (self.block,)
        return pl.BlockSpec(self.shape, lambda i: place, pipeline_mode=pl.Buffered(1))


class Layer:
    def __init__(self, array, layer):
        self.array, self.layer, self.keep = array, layer, True
        self.shape = (1,) + array.shape[1:]

    def spec(self):
        place = (self.layer,) + (0,) * (len(self.shape) - 1)
        return pl.BlockSpec(self.shape, lambda i: place, pipeline_mode=pl.Buffered(1))


def stored(array):
    return Columns(array, keep=True)


def summands(parts):
    return [stored(parts[0])] + passed(parts[1:])


def passed(arrays):
    return [Columns(array) for array in arrays]


def kept(shape, dtype=f32):
    return pltpu.HBM(shape, dtype)


def fetch_kernel(places, *refs):
    count = len(places)
    sources, outs, sems = refs[:count], refs[count : 2 * count], refs[-1]
    copies = []
    for (start, pieces), source, out in zip(places, sources, outs):
        rows, width = out.shape[0] // pieces, out.shape[1]
        for index in range(pieces):
            own = pl.ds(rows * index, rows)
            copies.append(
                pltpu.make_async_copy(
                    source.at[own, pl.ds(start, width)], out.at[own, :], sems.at[len(copies)]
                )
            )
    for copy in copies:
        copy.start()
    for copy in copies:
        copy.wait()


def fetched_all(name, sources):
    places = [(start, 4 if array.shape[0] == 2048 and width > 128 else 1) for array, start, width in sources]
    whole = pl.BlockSpec(memory_space=pltpu.VMEM)
    return pl.pallas_call(
        partial(fetch_kernel, places),
        name=name,
        out_shape=tuple(pltpu.VMEM((array.shape[0], width), array.dtype) for array, _, width in sources),
        in_specs=[pl.BlockSpec(memory_space=pltpu.HBM)] * len(sources),
        out_specs=tuple(whole for _ in sources),
        scratch_shapes=[pltpu.SemaphoreType.DMA((sum(pieces for _, pieces in places),))],
        compiler_params=pltpu.CompilerParams(vmem_limit_bytes=VMEM_LIMIT),
        cost_estimate=pl.CostEstimate(
            flops=0, bytes_accessed=sum(2 * array.shape[0] * width for array, _, width in sources), transcendentals=0
        ),
    )(*(pltpu.with_memory_space_constraint(array, pltpu.HBM) for array, _, _ in sources))


def fetched(name, array, start, width):
    return fetched_all(name, [(array, start, width)])[0]


def restored(name, arrays):
    return fetched_all(name, [(array, 0, array.shape[1]) for array in arrays])


def run_kernel(kernel, outs, flags, *args, scratch=(), flops=50_000_000):
    whole = pl.BlockSpec(memory_space=pltpu.VMEM)
    own = [isinstance(arg, (Columns, Layer)) for arg in args]
    specs, arrays, out_specs = [], [], []
    for arg, copied in zip(args, own):
        specs.append(arg.spec() if copied else whole)
        array = arg.array if copied else arg
        arrays.append(pltpu.with_memory_space_constraint(array, pltpu.HBM) if copied and arg.keep else array)
    for out in outs:
        in_vmem = isinstance(out, jax.ShapeDtypeStruct)
        out_specs.append(whole if in_vmem else pl.BlockSpec(out.shape, lambda i, n=len(out.shape): (0,) * n))
        own.append(not in_vmem)
    moved = sum(2 * math.prod(arg.shape) for arg in args) + sum(2 * math.prod(o.shape) for o in outs)
    if flags is not None:
        specs = [pl.BlockSpec(memory_space=pltpu.SMEM)] + specs
        arrays = [flags] + arrays
    return pl.pallas_call(
        kernel,
        grid=(1,) if any(own) else (),
        out_shape=tuple(outs),
        in_specs=specs,
        out_specs=tuple(out_specs),
        scratch_shapes=list(scratch),
        compiler_params=pltpu.CompilerParams(vmem_limit_bytes=VMEM_LIMIT),
        cost_estimate=pl.CostEstimate(flops=flops, bytes_accessed=moved, transcendentals=0),
    )(*arrays)


def local_block(flags, natural):
    return pl.multiple_of(flags[8 + natural] * SHARE, SHARE)


def rank_block(flags, rank):
    return pl.multiple_of(flags[16 + rank] * ROWS, ROWS)


def lane_index(shape):
    return lax.broadcasted_iota(i32, shape, len(shape) - 1)


def spread(columns, pair):
    low = lane_index((1, 128)) < HP
    return jnp.where(low, columns[:, 2 * pair : 2 * pair + 1], columns[:, 2 * pair + 1 : 2 * pair + 2])


def lanes_of(pair):
    return slice(128 * pair, 128 * pair + 128)


def turned(value, table, sign):
    return value * table[:, 0:128] + sign * (pltpu.roll(value, 64, 1) * table[:, 128:256])


def segments(table):
    return table[:, 259:260]


def sigmoid(v):
    return 1.0 / (1.0 + jnp.exp(-v))


def softplus(v):
    return jnp.maximum(v, 0.0) + jnp.log1p(jnp.exp(-jnp.abs(v)))


def conv_sum(ext, table, weight):
    total = weight[CONV : CONV + 1, :] + ext[8 : 8 + ROWS, :] * weight[3:4, :]
    for tap in range(CONV - 1):
        total = total + table[:, 256 + tap : 257 + tap] * ext[5 + tap : 5 + tap + ROWS, :] * weight[tap : tap + 1, :]
    return total


def conv_back(grad_out, ext, table, weight, work, grad_ref, edge_ref, gweight_ref):
    total = conv_sum(ext, table, weight)
    sig = sigmoid(total)
    grad = grad_out * sig * (1.0 + total * (1.0 - sig))
    width = grad.shape[1]
    gweight_ref[...] = jnp.zeros((8, width), f32)
    gweight_ref[CONV : CONV + 1, :] = jnp.sum(grad, axis=0, keepdims=True)
    gweight_ref[3:4, :] = jnp.sum(grad * ext[8 : 8 + ROWS, :], axis=0, keepdims=True)
    work[0:8, :] = jnp.zeros((8, width), f32)
    work[264:272, :] = jnp.zeros((8, width), f32)
    own = grad * weight[3:4, :]
    edge = jnp.zeros((8, width), f32)
    for tap in range(CONV - 1):
        part = grad * table[:, 256 + tap : 257 + tap]
        gweight_ref[tap : tap + 1, :] = jnp.sum(
            part * ext[5 + tap : 5 + tap + ROWS, :], axis=0, keepdims=True
        )
        work[8:264, :] = part * weight[tap : tap + 1, :]
        own = own + work[11 - tap : 11 - tap + ROWS, :]
        edge = edge + work[3 - tap : 11 - tap, :]
    grad_ref[...] = own
    edge_ref[...] = edge


def pack_kernel(place, *refs):
    out, at, index = refs[-1], 0, 0
    while index < len(refs) - 1:
        ref = refs[index]
        if len(ref.shape) == 4:
            out[:, at : at + XLOC] = ref[0, :, 0, :]
            out[:, at + XLOC : at + 512] = refs[index + 1][0]
            out[:, at + 512 : at + 896] = ref[0, :, 1, :]
            at, index = at + 896, index + 2
            continue
        width = min(ref.shape[2], 512)
        if width == HLOC:
            out[:, at : at + 128] = jnp.zeros((out.shape[0], 128), bf16)
            out[:, at : at + HLOC] = ref[0]
            width = 128
        elif ref.shape[2] == 1024:
            width = 128
            out[:, at : at + width] = ref[0, :, pl.ds(pl.multiple_of(place[0] * 128, 128), 128)]
        else:
            out[:, at : at + width] = ref[0]
        at, index = at + width, index + 1


def first_kernel(flags, rows, cotangent, gain, normed, inverse, hidden_kept, grads, grad):
    for block in range(8):
        own = slice(SHARE * block, SHARE * (block + 1))
        from_rows = pl.ds(pl.multiple_of(flags[24 + block] * SHARE, SHARE), SHARE)
        wide = rows[0, from_rows, :].astype(f32)
        scale = lax.rsqrt(jnp.mean(wide * wide, axis=1, keepdims=True) + norm_eps)
        normed[own, :] = (wide * scale * gain[0:1, :]).astype(bf16)
        grads[own, :] = cotangent[0, from_rows, :]
        if block == 0:
            hidden_kept[...] = wide
            inverse[...] = jnp.broadcast_to(scale, inverse.shape)
            grad[...] = cotangent[0, from_rows, :].astype(f32)


def joined(parts):
    return parts[0][...] if len(parts) == 1 else jnp.concatenate([part[...] for part in parts], axis=0)


def proj_kernel(flags, *refs):
    parts, (weight, table, normed, z, z_kept, xs, query, query_kept, dtn, dtn_kept, work) = refs[:-11], refs[-11:]
    rows = joined(parts)
    normed[...] = rows
    work[...] = dot_nn(rows, weight[...])
    for block in range(8):
        own = slice(SHARE * block, SHARE * (block + 1))
        from_rows = pl.ds(local_block(flags, block), SHARE)
        for out in (z, z_kept):
            out[own, :] = work[from_rows, 0:XLOC]
        xs[own, :] = work[from_rows, 512:1024]
        head = turned(work[from_rows, XLOC:512], table[own, :], 1.0).astype(bf16)
        for out in (query, query_kept):
            out[own, :] = head
        for out in (dtn, dtn_kept):
            out[own, :] = work[from_rows, 1024:PROJ]


def shared_kernel(flags, xs, halo, table, small, out, ext):
    own = xs[:, XLOC:512]
    ext[0:8, :] = halo[:, XLOC:512]
    ext[8 : 8 + ROWS, :] = own
    total = conv_sum(ext, table, small[:, XLOC:512])
    rank = flags[0]
    out[...] = jnp.where(
        rank < 2, turned(own, table, 1.0), jnp.where(rank < 4, own, total * sigmoid(total))
    ).astype(bf16)


def prep_kernel(xs, dtn, halo, table, small, ext, xc, xc_kept, rates, rates_kept, rates_t, rates_t_kept):
    ext[0:8, :] = halo[:, 0:XLOC]
    ext[8 : 8 + ROWS, :] = xs[:, 0:XLOC]
    total = conv_sum(ext, table, small[:, 0:XLOC])
    for out in (xc, xc_kept):
        out[...] = total * sigmoid(total)
    params = small[:, 512:640]
    rate = softplus(dtn[...] + params[1:2, :])
    logs = -jnp.exp(params[0:1, :]) * rate
    rows = lax.broadcasted_iota(i32, (ROWS, ROWS), 0)
    lower = (rows >= lane_index((ROWS, ROWS))).astype(f32)
    running = jnp.dot(lower, logs, precision=lax.Precision.HIGHEST, preferred_element_type=f32)
    for out in (rates, rates_kept):
        out[:, 0:128] = rate
        out[:, 128:256] = running
    rate_t, running_t = rate.T[0:8, :], running.T[0:8, :]
    for out in (rates_t, rates_t_kept):
        out[0:8, :] = rate_t
        out[8:16, :] = running_t


def block_decays(flags, rates_t):
    kept = jnp.where(flags[4] == flags[5], 1.0, 0.0)
    return jnp.exp(rates_t[8:16, ROWS - 1 : ROWS]) * kept


def decay_rows(flags, rates_t):
    rows = jnp.broadcast_to(block_decays(flags, rates_t), (8, NSTATE))
    return jnp.concatenate([rows, jnp.zeros((8, NSTATE), f32)], axis=0).astype(bf16)


def weights_in(rates, table):
    last = rates[ROWS - 1 : ROWS, 128:256]
    gap = jnp.exp(last - rates[:, 128:256]) * table[:, 261:262]
    return gap, gap * rates[:, 0:128]


def rank_columns(flags, shared, first):
    return jnp.concatenate(
        [shared[pl.ds(rank_block(flags, rank), ROWS), :] for rank in (first, first + 1)], axis=1
    )


def inject_of(flags, shared):
    return rank_columns(flags, shared, 4)


def readout_of(flags, shared):
    return rank_columns(flags, shared, 6)


def carry_of(rates, table):
    return jnp.exp(rates[:, 128:256]) * table[:, 260:261]


def state_kernel(flags, s0, s1, s2, s3, s4, s5, s6, s7, xc, rates, rates_t, table, out, shared, shared_kept):
    for index, part in enumerate((s0, s1, s2, s3, s4, s5, s6, s7)):
        shared[ROWS * index : ROWS * (index + 1), :] = part[...]
        shared_kept[ROWS * index : ROWS * (index + 1), :] = part[...]
    inject = inject_of(flags, shared)
    _, weight = weights_in(rates, table)
    for pair in range(PAIRS):
        weighted = (xc[:, lanes_of(pair)] * spread(weight, pair)).astype(bf16)
        out[KV + 128 * pair : KV + 128 * (pair + 1), :] = dot_tn(weighted, inject).astype(bf16)
    out[KV + XLOC : KV + MSG, :] = decay_rows(flags, rates_t)
    half = shared[pl.ds(rank_block(flags, 2 * flags[2] + flags[1] // 2), ROWS), :]
    out[0:KV, :] = jnp.concatenate([half[0:128], half[128:256]], axis=1)


def halves_kernel(msg1, msg2, msg3, out):
    for index, msg in enumerate((msg1, msg2, msg3)):
        out[KV * index : KV * (index + 1), :] = msg[...]


def allowed_pairs(table, seg_rows):
    rows = lax.broadcasted_iota(i32, (ROWS, ROWS), 0)
    return (rows >= lane_index((ROWS, ROWS))) & (segments(table) == seg_rows[0:1, :])


def head_decay(allowed, rates, rates_t, head):
    gap = rates[:, 128 + head : 129 + head] - rates_t[8 + head : 9 + head, :]
    return jnp.where(allowed, jnp.exp(jnp.where(allowed, gap, 0.0)), 0.0)


def intra_kernel(flags, shared, xc, rates, rates_t, table, seg_rows, small, out):
    inject, readout = inject_of(flags, shared), readout_of(flags, shared)
    both = dot_nt(readout, inject)
    allowed = allowed_pairs(table, seg_rows)
    low = lane_index((1, 128)) < HP
    for pair in range(PAIRS):
        x = xc[:, lanes_of(pair)]
        xb = x.astype(bf16)
        heads = []
        for head in (2 * pair, 2 * pair + 1):
            decay = head_decay(allowed, rates, rates_t, head)
            heads.append(dot_nn((both * decay * rates_t[head : head + 1, :]).astype(bf16), xb))
        out[:, lanes_of(pair)] = jnp.where(low, heads[0], heads[1]) + spread(small[2:3, 512:640], pair) * x


def keys_values(flags, shared, halves, swapped):
    head, first = flags[1] // 2, flags[2] == 0
    pairs = [
        (
            shared[pl.ds(rank_block(flags, head), ROWS), :],
            shared[pl.ds(rank_block(flags, 2 + head), ROWS), :],
        )
    ]
    for index, half in enumerate(halves):
        packed = half[...], swapped[KV * index : KV * (index + 1), :]
        mine, theirs = (jnp.concatenate([part[:, 0:128], part[:, 128:256]], axis=0) for part in packed)
        pairs.append((jnp.where(first, mine, theirs), jnp.where(first, theirs, mine)))
    return pairs


def masked_scores(query, pairs, table, seg_rows):
    parts = []
    for block, (keys, _) in enumerate(pairs):
        score = dot_nt(query, keys) * HD ** (-0.5)
        keep = segments(table) == seg_rows[block : block + 1, :]
        if block == 0:
            rows = lax.broadcasted_iota(i32, (ROWS, ROWS), 0)
            keep = keep & (rows >= lane_index((ROWS, ROWS)))
        parts.append(jnp.where(keep, score, -1e30))
    return parts


def attention_kernel(flags, query, shared, h1, h2, h3, swapped, table, seg_rows, out, log_total, kept):
    pairs = keys_values(flags, shared, (h1, h2, h3), swapped)
    for block, (keys, values) in enumerate(pairs):
        kept[ROWS * block : ROWS * (block + 1), 0:HD] = keys
        kept[ROWS * block : ROWS * (block + 1), HD : 2 * HD] = values
    parts = masked_scores(query[...], pairs, table, seg_rows)
    top = parts[0].max(axis=1, keepdims=True)
    for part in parts[1:]:
        top = jnp.maximum(top, part.max(axis=1, keepdims=True))
    parts = [jnp.exp(part - top) for part in parts]
    total = sum(part.sum(axis=1, keepdims=True) for part in parts)
    inverse = 1.0 / total
    result = jnp.zeros((ROWS, HD), f32)
    for part, (_, values) in zip(parts, pairs):
        result = result + dot_nn((part * inverse).astype(bf16), values)
    out[...] = result.astype(bf16)
    log_total[...] = jnp.broadcast_to(top + jnp.log(total), (ROWS, HD))


def chained(first, second, third, base):
    rows1 = first[base + XLOC : base + MSG, :].astype(f32)
    rows2 = second[base + XLOC : base + MSG, :].astype(f32)
    parts = []
    for head in range(HLOC):
        own = slice(base + HP * head, base + HP * head + HP)
        older = second[own, :].astype(f32) + rows2[head : head + 1, :] * third[own, :].astype(f32)
        parts.append(first[own, :].astype(f32) + rows1[head : head + 1, :] * older)
    return jnp.concatenate(parts, axis=0)


def carry_kernel(flags, msg1, msg2, msg3, shared, rates, table, intra, z, attn, state, ssm_y, cat, cat_kept):
    entering = chained(msg1, msg2, msg3, KV)
    state[...] = entering
    from_state = dot_nt(readout_of(flags, shared), entering.astype(bf16))
    carry = carry_of(rates, table)
    for pair in range(PAIRS):
        own = lanes_of(pair)
        y = intra[:, own] + spread(carry, pair) * from_state[:, own]
        ssm_y[:, own] = y
        gate = z[:, own]
        gated = (y * gate * sigmoid(gate)).astype(bf16)
        for block in range(8):
            for out in (cat, cat_kept):
                out[pl.ds(local_block(flags, block), SHARE), 128 + 128 * pair : 256 + 128 * pair] = gated[
                    SHARE * block : SHARE * (block + 1), :
                ]
    for block in range(8):
        for out in (cat, cat_kept):
            out[pl.ds(local_block(flags, block), SHARE), 0:128] = attn[SHARE * block : SHARE * (block + 1), :]


def gate_back_kernel(
    flags, p0, p1, p2, p3, p4, p5, p6, p7, weight, z, ssm_y, shared, rates, rates_t, table,
    dmix, dattn, dy, dz, msg, work, local,
):
    rows = joined((p0, p1, p2, p3, p4, p5, p6, p7))
    dmix[...] = rows
    local[...] = dot_nn(rows, weight[...])
    for block in range(8):
        own = slice(SHARE * block, SHARE * (block + 1))
        from_rows = pl.ds(local_block(flags, block), SHARE)
        dattn[own, :] = local[from_rows, 0:128].astype(bf16)
        work[own, :] = local[from_rows, 128:512]
    readout = readout_of(flags, shared)
    carry = carry_of(rates, table)
    for pair in range(PAIRS):
        own = lanes_of(pair)
        gate, grad = z[:, own], work[:, own]
        sig = sigmoid(gate)
        y_grad = grad * gate * sig
        dy[:, own] = y_grad
        dz[:, own] = (grad * ssm_y[:, own] * sig * (1.0 + gate * (1.0 - sig))).astype(bf16)
        msg[own, :] = dot_tn((y_grad * spread(carry, pair)).astype(bf16), readout).astype(bf16)
    msg[XLOC:MSG, :] = decay_rows(flags, rates_t)


def attention_back_kernel(
    flags, dattn, dz, query, kept, log_total, table, seg_rows,
    early, mine, theirs,
):
    pairs = []
    for block in range(SEQ_BLOCKS):
        own = slice(ROWS * block, ROWS * (block + 1))
        pairs.append((kept[own, 0:HD], kept[own, HD : 2 * HD]))
    first = flags[2] == 0
    q = query[...]
    grad = dattn[...]
    parts = masked_scores(q, pairs, table, seg_rows)
    logs = log_total[:, 0:1]
    probs = [jnp.exp(part - logs) for part in parts]
    grads = [dot_nt(grad, values) for _, values in pairs]
    inner = sum((p * g).sum(axis=1, keepdims=True) for p, g in zip(probs, grads))
    total = jnp.zeros((ROWS, HD), f32)
    for block, (p, g, (keys, _)) in enumerate(zip(probs, grads, pairs)):
        own = slice(ROWS * block, ROWS * (block + 1))
        score = (p * (g - inner)).astype(bf16)
        total = total + dot_nn(score, keys)
        dkeys = dot_tn(score, q) * HD ** (-0.5)
        dvalues = dot_tn(p.astype(bf16), grad)
        mine[own, :] = jnp.where(first, dkeys, dvalues)
        theirs[own, :] = jnp.where(first, dvalues, dkeys).astype(bf16)
    total = total * HD ** (-0.5)
    dq = turned(total, table, -1.0).astype(bf16)
    for block in range(8):
        own = slice(SHARE * block, SHARE * (block + 1))
        to_rows = pl.ds(local_block(flags, block), SHARE)
        early[to_rows, 0:XLOC] = dz[own, :]
        early[to_rows, XLOC:512] = dq[own, :]


def intra_back_kernel(
    flags, dy, xc, shared, rates, rates_t, table, seg_rows, state, small,
    dx, dshared, drates, dskip, row_sums, dcum,
):
    inject, readout = inject_of(flags, shared), readout_of(flags, shared)
    both = dot_nt(readout, inject)
    allowed = allowed_pairs(table, seg_rows)
    low = lane_index((1, 128)) < HP
    carry = carry_of(rates, table)
    entering = state[...].astype(bf16)
    from_state = dot_nt(readout, entering)
    dboth = jnp.zeros((ROWS, ROWS), f32)
    row_sums[...] = jnp.zeros((128, ROWS), f32)
    dcum[...] = jnp.zeros((ROWS, 128), f32)
    carried = []
    for pair in range(PAIRS):
        own = lanes_of(pair)
        x = xc[:, own]
        xb = x.astype(bf16)
        grad = dy[:, own]
        dskip[:, own] = jnp.sum(grad * x, axis=0, keepdims=True)
        carried.append((grad * spread(carry, pair)).astype(bf16))
        through = grad * from_state[:, own]
        total = spread(small[2:3, 512:640], pair) * grad
        for head in (2 * pair, 2 * pair + 1):
            mine = low if head % 2 == 0 else jnp.logical_not(low)
            decay = head_decay(allowed, rates, rates_t, head)
            steps = rates_t[head : head + 1, :]
            head_grad = jnp.where(mine, grad, 0.0).astype(bf16)
            dmix = dot_nt(head_grad, xb)
            kept = dmix * decay
            dboth = dboth + kept * steps
            mixed = both * decay
            total = total + dot_tn((mixed * steps).astype(bf16), head_grad)
            passed = dmix * mixed
            row_sums[head : head + 1, :] = jnp.sum(passed, axis=0, keepdims=True)
            dcum[:, head : head + 1] = jnp.sum(passed * steps, axis=1, keepdims=True) + carry[
                :, head : head + 1
            ] * jnp.sum(jnp.where(mine, through, 0.0), axis=1, keepdims=True)
        dx[:, own] = total
    columns = row_sums[...].T
    drates[:, 0:128] = columns
    drates[:, 128:256] = dcum[...] - rates[:, 0:128] * columns
    dboth_b = dboth.astype(bf16)
    dshared[:, NSTATE:] = dot_nn(dboth_b, inject) + dot_nn(jnp.concatenate(carried, axis=1), entering)
    dshared[:, 0:NSTATE] = dot_tn(dboth_b, readout)


def state_back_kernel(
    flags, msg1, msg2, msg3, shared, xc, rates, rates_t, table, state, small, dtn,
    dx, dshared, drates, kv0, kv1, kv2, kv3, ext,
    packed, dxpre, edge, gweight, ddt, heads, work, dconv, sums,
):
    later = chained(msg1, msg2, msg3, 0)
    later_b = later.astype(bf16)
    inject = inject_of(flags, shared)
    low = lane_index((1, 128)) < HP
    params = small[:, 512:640]
    gap, weights = weights_in(rates, table)
    from_later = dot_nt(inject, later_b)
    products = later * state[...]
    decays = block_decays(flags, rates_t)
    sums[...] = jnp.zeros((ROWS, 128), f32)
    weighted = []
    for pair in range(PAIRS):
        own = lanes_of(pair)
        x = xc[:, own]
        scale = spread(weights, pair)
        weighted.append((x * scale).astype(bf16))
        dconv[:, own] = dx[:, own] + scale * from_later[:, own]
        through = x * from_later[:, own]
        for head in (2 * pair, 2 * pair + 1):
            mine = low if head % 2 == 0 else jnp.logical_not(low)
            sums[:, head : head + 1] = jnp.sum(jnp.where(mine, through, 0.0), axis=1, keepdims=True)
    dweights = sums[...]
    moved = dweights * weights
    last = jnp.sum(moved, axis=0, keepdims=True)
    lanes = lane_index((1, 128))
    for head in range(HLOC):
        total = jnp.sum(
            jnp.sum(products[HP * head : HP * head + HP, :], axis=0, keepdims=True), axis=1, keepdims=True
        )
        last = last + jnp.where(lanes == head, total * decays[head : head + 1, :], 0.0)
    rows = lax.broadcasted_iota(i32, (ROWS, 128), 0)
    dcums = drates[:, 128:256] - moved + jnp.where(rows == ROWS - 1, last, 0.0)
    square = lax.broadcasted_iota(i32, (ROWS, ROWS), 0)
    upper = (square <= lane_index((ROWS, ROWS))).astype(f32)
    dlogs = jnp.dot(upper, dcums, precision=lax.Precision.HIGHEST, preferred_element_type=f32)
    rate = -jnp.exp(params[0:1, :])
    dsteps = drates[:, 0:128] + dweights * gap + dlogs * rate
    ddts = dsteps * sigmoid(dtn[...] + params[1:2, :])
    ddt[...] = ddts
    heads[...] = jnp.zeros((8, 128), f32)
    heads[0:1, :] = jnp.sum(dlogs * rate * rates[:, 0:128], axis=0, keepdims=True)
    heads[1:2, :] = jnp.sum(ddts, axis=0, keepdims=True)
    dinject_all = (dshared[:, 0:NSTATE] + dot_nn(jnp.concatenate(weighted, axis=1), later_b)).astype(bf16)
    dreadout_all = dshared[:, NSTATE:].astype(bf16)
    packed[...] = jnp.zeros((8 * ROWS, 128), bf16)
    grads = kv0[...] + kv1[...].astype(f32) + kv2[...].astype(f32) + kv3[...].astype(f32)
    owner = 2 * flags[2] + flags[1] // 2
    packed[pl.ds(rank_block(flags, owner), ROWS), :] = grads.astype(bf16)
    packed[pl.ds(rank_block(flags, 4), ROWS), :] = dinject_all[:, 0:128]
    packed[pl.ds(rank_block(flags, 5), ROWS), :] = dinject_all[:, 128:256]
    packed[pl.ds(rank_block(flags, 6), ROWS), :] = dreadout_all[:, 0:128]
    packed[pl.ds(rank_block(flags, 7), ROWS), :] = dreadout_all[:, 128:256]
    conv_back(dconv[...], ext, table, small[:, 0:XLOC], work, dxpre, edge, gweight)


def shared_back_kernel(flags, part0, part1, part2, part3, ext, table, small, out, edge, gweight, work):
    grad = part0[...] + part1[...].astype(f32) + part2[...].astype(f32) + part3[...].astype(f32)
    conv_back(grad, ext, table, small[:, XLOC:512], work, out, edge, gweight)
    rank = flags[0]
    of_conv = jnp.where(rank < 4, 0.0, 1.0)
    edge[...] = edge[...] * of_conv
    gweight[...] = gweight[...] * of_conv
    out[...] = jnp.where(rank < 2, turned(grad, table, -1.0), jnp.where(rank < 4, grad, out[...]))


def late_kernel(flags, dxpre, edge_x, dsh, edge_sh, ddt, out):
    for block in range(8):
        own = slice(SHARE * block, SHARE * (block + 1))
        to_rows = pl.ds(local_block(flags, block), SHARE)
        x, sh = dxpre[own, :], dsh[own, :]
        if block == 7:
            pad = jnp.zeros((SHARE - 8, 128), f32)
            sh = sh + jnp.concatenate([pad, edge_sh[...]], axis=0)
            x = x + jnp.concatenate([jnp.zeros((SHARE - 8, XLOC), f32), edge_x[...]], axis=0)
        out[to_rows, 0:XLOC] = x.astype(bf16)
        out[to_rows, XLOC:512] = sh.astype(bf16)
        out[to_rows, 512:LATE] = jnp.where(lane_index((1, 128)) < HLOC, ddt[own, :], 0.0).astype(bf16)


def half_sum_kernel(own, other, keep, send1, send2, send3):
    rows = own.shape[0] // 4
    keep[...] = own[0:rows, :] + other[0:rows, :].astype(f32)
    for index, send in ((1, send1), (2, send2), (3, send3)):
        part = slice(rows * index, rows * (index + 1))
        send[...] = (own[part, :].astype(f32) + other[part, :].astype(f32)).astype(bf16)


def parts_of_sum(own, other, along, sign):
    return parts_from(own, other_core(other), along, sign)


def parts_from(own, got, along, sign):
    rows, width = own.shape[0] // 4, own.shape[1]
    sent = shape_of((rows, width), bf16)
    keep, *sends = run_kernel(half_sum_kernel, [kept((rows, width)), sent, sent, sent], None, own, Columns(got))
    return (keep,) + tuple(along(send, sign * k) for k, send in zip((1, 2, 3), sends))


def split_kernel(*refs):
    lefts, weight, own, other = refs[:-3], refs[-3], refs[-2], refs[-1]
    left = lefts[0][...] if len(lefts) == 1 else jnp.concatenate([ref[...] for ref in lefts], axis=1)
    result = dot_nt(left, weight[...])
    own[...] = result[: ROWS // 2]
    other[...] = result[ROWS // 2 :].astype(bf16)


def summed_rows(lefts, weight):
    model, width = weight.shape
    own, other = pl.pallas_call(
        split_kernel,
        grid=(model // 512,),
        out_shape=(shape_of((ROWS // 2, model)), shape_of((ROWS // 2, model), bf16)),
        in_specs=[pl.BlockSpec(left.shape, lambda i: (0, 0)) for left in lefts]
        + [pl.BlockSpec((512, width), lambda i: (i, 0))],
        out_specs=(
            pl.BlockSpec((ROWS // 2, 512), lambda i: (0, i)),
            pl.BlockSpec((ROWS // 2, 512), lambda i: (0, i)),
        ),
        compiler_params=pltpu.CompilerParams(vmem_limit_bytes=VMEM_LIMIT),
        cost_estimate=pl.CostEstimate(
            flops=2 * ROWS * model * width, bytes_accessed=2 * model * width, transcendentals=0
        ),
    )(*lefts, weight)
    return parts_of_sum(own, other, along_y, 1)


def gate_up_kernel(p0, p1, p2, p3, p4, p5, p6, p7, weight, normed, gate, up, act, act_kept):
    rows = joined((p0, p1, p2, p3, p4, p5, p6, p7))
    normed[...] = rows
    result = dot_nn(rows, weight[...])
    g, u = result[:, :512], result[:, 512:]
    gate[...] = g
    up[...] = u
    for out in (act, act_kept):
        out[...] = (g * sigmoid(g) * u).astype(bf16)


def gate_up_back_kernel(*refs):
    parts, (weight, gate, up, dffn, out) = refs[:-5], refs[-5:]
    rows = joined(parts)
    dffn[...] = rows
    dact = dot_nn(rows, weight[...])
    g = gate[...]
    sig = sigmoid(g)
    out[:, :512] = (dact * up[...] * sig * (1.0 + g * (1.0 - sig))).astype(bf16)
    out[:, 512:] = (dact * g * sig).astype(bf16)


def natural_kernel(flags, p0, p1, p2, p3, p4, p5, p6, p7, out):
    local = joined((p0, p1, p2, p3, p4, p5, p6, p7)).astype(out.dtype)
    for block in range(8):
        out[pl.ds(pl.multiple_of(flags[24 + block] * SHARE, SHARE), SHARE), :] = local[
            SHARE * block : SHARE * (block + 1), :
        ]


def add_norm_kernel(hidden, part0, part1, part2, part3, gain, out_kept, normed, inverse):
    total = hidden[...] + part0[...] + (
        part1[...].astype(f32) + part2[...].astype(f32) + part3[...].astype(f32)
    )
    out_kept[...] = total
    scale = lax.rsqrt(jnp.mean(total * total, axis=1, keepdims=True) + norm_eps)
    inverse[...] = jnp.broadcast_to(scale, inverse.shape)
    normed[...] = (total * scale * gain[...]).astype(bf16)


def add_norm(hidden, parts, gain):
    shape = hidden.shape
    return run_kernel(
        add_norm_kernel,
        [kept(shape), shape_of(shape, bf16), kept((shape[0], 128))],
        None, stored(hidden), *summands(parts), gain[None],
    )


def output_kernel(hidden, part0, part1, part2, part3, out):
    total = hidden[...] + part0[...] + (
        part1[...].astype(f32) + part2[...].astype(f32) + part3[...].astype(f32)
    )
    out[...] = total.astype(bf16)


def norm_back_kernel(grad, part0, part1, part2, part3, hidden, inverse, gain, out, rounded, ggain):
    received = part0[...] + (part1[...].astype(f32) + part2[...].astype(f32) + part3[...].astype(f32))
    scale = inverse[:, 0:1]
    unit = hidden[...] * scale
    scaled = received * gain[...]
    ggain[...] = jnp.sum(received * unit, axis=0, keepdims=True)
    total = grad[...] + scale * (scaled - unit * jnp.mean(scaled * unit, axis=1, keepdims=True))
    out[...] = total
    rounded[...] = total.astype(bf16)


def norm_back(grad, parts, hidden, inverse, gain):
    shape = hidden.shape
    return run_kernel(
        norm_back_kernel,
        [kept(shape), shape_of(shape, bf16), kept((1, shape[1]))],
        None, stored(grad), *summands(parts), stored(hidden), stored(inverse), gain[None],
    )


def gradient_kernel(pairs, *refs):
    out, at = refs[-1], 0
    for index in range(pairs):
        left, right = refs[2 * index], refs[2 * index + 1]
        width = right.shape[1]
        out[:, at : at + width] = dot_tn(left[...], right[...]).astype(bf16)
        at += width
    if at < out.shape[1]:
        out[:, at:] = jnp.zeros((out.shape[0], out.shape[1] - at), bf16)


def weight_gradients(pairs, total, block, index, buffer=None):
    rows, model = pairs[0][0].shape
    width = sum(right.shape[1] for _, right in pairs)
    specs, args = [], []
    for left, right in pairs:
        specs += [
            pl.BlockSpec((rows, 512), lambda i: (0, i)),
            pl.BlockSpec(right.shape, lambda i: (0, 0)),
        ]
        args += [left, right]
    aliases = {}
    kernel = partial(gradient_kernel, len(pairs))
    if buffer is not None:
        aliases = {len(args): 0}
        specs.append(pl.BlockSpec(memory_space=pltpu.HBM))
        args.append(buffer)

        def kernel(*refs):
            gradient_kernel(len(pairs), *refs[:-2], refs[-1])

    return pl.pallas_call(
        kernel,
        grid=(model // 512,),
        out_shape=pltpu.HBM((model, total), bf16),
        in_specs=specs,
        out_specs=pl.BlockSpec((512, block), lambda i: (i, index)),
        input_output_aliases=aliases,
        compiler_params=pltpu.CompilerParams(vmem_limit_bytes=VMEM_LIMIT),
        cost_estimate=pl.CostEstimate(
            flops=2 * rows * model * width, bytes_accessed=model * width * 2, transcendentals=0
        ),
    )(*args)


def owned_kernel(pairs, *refs):
    out, at = refs[-1], 0
    for pair in range(pairs):
        left, right = refs[2 * pair], refs[2 * pair + 1]
        result = dot_tn(left[...], right[...]).astype(bf16)
        width = right.shape[1]
        for index in range(2):
            out[index, :, at : at + width] = result[128 * index : 128 * (index + 1)]
        at += width
    if at < out.shape[2]:
        for index in range(2):
            out[index, :, at:] = refs[2 * pairs][...]


def owned_gradients(pairs, small=None):
    rows, model = pairs[0][0].shape
    width = sum(right.shape[1] for _, right in pairs)
    specs, args = [], []
    for left, right in pairs:
        specs += [pl.BlockSpec((rows, 256), lambda i: (0, i)), pl.BlockSpec(right.shape, lambda i: (0, 0))]
        args += [left, right]
    if small is not None:
        specs.append(pl.BlockSpec(small.shape, lambda i: (0, 0)))
        args.append(small)
        width += small.shape[1]
    return pl.pallas_call(
        partial(owned_kernel, len(pairs)),
        grid=(model // 256,),
        out_shape=pltpu.HBM((16, model // 16, width), bf16),
        in_specs=specs,
        out_specs=pl.BlockSpec((2, model // 16, width), lambda i: (i, 0, 0)),
        compiler_params=pltpu.CompilerParams(vmem_limit_bytes=VMEM_LIMIT),
        cost_estimate=pl.CostEstimate(
            flops=2 * rows * model * width, bytes_accessed=model * width * 2, transcendentals=0
        ),
    )(*args)


def small_kernel(gain1, gain2, conv_sh, conv_x, heads, skip, out):
    out[...] = jnp.zeros(out.shape, bf16)
    for row in range(16):
        own = slice(128 * row, 128 * row + 128)
        out[row : row + 1, :] = gain1[:, own].astype(bf16)
        out[16 + row : 17 + row, :] = gain2[:, own].astype(bf16)
    out[32:37, :] = conv_sh[0:5, :].astype(bf16)
    for tap in range(CONV + 1):
        for pair in range(PAIRS):
            row = 37 + PAIRS * tap + pair
            out[row : row + 1, :] = conv_x[tap : tap + 1, lanes_of(pair)].astype(bf16)
    out[52:54, :] = heads[0:2, :].astype(bf16)
    lanes = lane_index((1, 128))
    sums = jnp.zeros((1, 128), f32)
    for pair in range(PAIRS):
        part = skip[:, lanes_of(pair)]
        for half in range(2):
            mine = (lanes < HP) if half == 0 else (lanes >= HP)
            total = jnp.sum(jnp.where(mine, part, 0.0), axis=1, keepdims=True)
            sums = sums + jnp.where(lanes == 2 * pair + half, total, 0.0)
    out[54:55, :] = sums.astype(bf16)


def owner_sum(values):
    total = values[0].astype(f32)
    for index in range(1, 16):
        total = total + values[index].astype(f32)
    return total


def block_sum_kernel(values, over_tp, late, conv_x, heads):
    whole = owner_sum(values)
    late[...] = whole[:, 0:LATE]
    total = whole[:, LATE : LATE + 128]
    over_tp[0:128, :] = whole[:, XLOC:512].astype(bf16)
    over_tp[128:224, :] = jnp.zeros((96, 128), bf16)
    for layer in range(2):
        first = 64 * layer
        over_tp[128 + 48 * layer : 165 + 48 * layer, :] = total[first : first + 37, :].astype(bf16)
        for tap in range(CONV + 1):
            for pair in range(PAIRS):
                row = first + 37 + PAIRS * tap + pair
                conv_x[5 * layer + tap : 5 * layer + tap + 1, lanes_of(pair)] = total[row : row + 1, :]
        heads[3 * layer : 3 * layer + 3, :] = total[first + 52 : first + 55, :]


def early_outputs_kernel(upper, lower, mixed, attn, ssm, gate, up, down, query, z):
    sums = owner_sum(mixed)
    attn[0] = sums[:, 0:128]
    ssm[0] = sums[:, 128:512]
    z[0] = sums[:, 512:896]
    query[0] = sums[:, 896:1024]
    attn[1] = upper[:, 1536:1664].astype(f32)
    ssm[1] = upper[:, 1664:2048].astype(f32)
    z[1] = upper[:, 2048:2432].astype(f32)
    query[1] = upper[:, 2432:2560].astype(f32)
    for layer, ref in ((0, lower), (1, upper)):
        for index, out in enumerate((gate, up, down)):
            out[layer] = ref[:, 512 * index : 512 * (index + 1)].astype(f32)


def last_outputs_kernel(flags, *refs):
    parts, other, (late, upper_late, z) = refs[:8], refs[8:16], refs[16:19]
    zx, dt, shared, gains1, gains2, conv_bc, every = refs[19:]
    zx[0, :, 0, :] = z[0]
    zx[1, :, 0, :] = z[1]
    zx[0, :, 1, :] = late[:, 0:XLOC]
    zx[1, :, 1, :] = upper_late[:, 0:XLOC].astype(f32)
    dt[0] = late[:, 512 : 512 + HLOC]
    dt[1] = upper_late[:, 512 : 512 + HLOC].astype(f32)
    total = jnp.zeros((96, 128), f32)
    for index, part in enumerate(parts):
        every[index] = part[...].astype(f32)
        total = total + part[128:224, :].astype(f32)
    for index, part in enumerate(other):
        every[8 + index, 0:128, :] = part[...].astype(f32)
    for rank in range(8):
        own = slice(128 * rank, 128 * rank + 128)
        shared[0, :, own] = every[flags[16 + rank], 0:128, :]
        shared[1, :, own] = every[8 + flags[16 + rank], 0:128, :]
    for layer in range(2):
        for row in range(16):
            own = slice(128 * row, 128 * row + 128)
            at = 48 * layer + row
            gains1[layer : layer + 1, own] = total[at : at + 1, :]
            gains2[layer : layer + 1, own] = total[at + 16 : at + 17, :]
        for rank in range(4):
            part = every[flags[20 + rank], 160 + 48 * layer : 168 + 48 * layer, :]
            conv_bc[5 * layer : 5 * layer + 5, 128 * rank : 128 * rank + 128] = part[0:5, :]


def body(
    inputs, cotangent, segment_ids, w_query, w_shared, w_zx, w_dt, w_attn_out, w_ssm_out, w_gate, w_up, w_down,
    gains, conv_x, conv_bc, head_params,
):
    layers = w_query.shape[0]
    rank, ctx = lax.axis_index("tp"), lax.axis_index("ctx")
    y, core = rank // 2, rank % 2
    model = inputs.shape[2]

    def local_of(block_y, block_core):
        return jnp.where(block_core == core, 0, 4) + (block_y - y) % 4

    seg_all = segment_ids[0]
    first_row = ctx * ROWS
    padded = jnp.concatenate([jnp.full((CONV - 1,), -1, i32), seg_all])
    seg_ext = lax.dynamic_slice_in_dim(padded, first_row, ROWS + CONV - 1)
    seg_own = seg_ext[CONV - 1 :]
    blocks = seg_all.reshape(SEQ_BLOCKS, ROWS)
    seg_rows = jnp.stack(
        [
            jnp.where(ctx >= back, lax.dynamic_index_in_dim(blocks, jnp.maximum(ctx - back, 0), 0, False), -1)
            for back in range(SEQ_BLOCKS)
        ]
        + [jnp.full((ROWS,), -1, i32)] * 4
    ).astype(f32)
    naturals = jnp.arange(8, dtype=i32)
    flags = jnp.concatenate(
        [
            jnp.stack([rank, y, core, ctx, seg_ext[CONV - 2], seg_own[-1], rank, rank]).astype(i32),
            local_of(naturals % 4, naturals // 4).astype(i32),
            local_of(naturals // 2, naturals % 2).astype(i32),
            (jnp.where(naturals < 4, core, 1 - core) * 4 + (y + naturals) % 4).astype(i32),
        ]
    )

    half_width = HD // 2
    frequency = rope_base ** (-jnp.arange(half_width, dtype=f32) / half_width)
    places = (first_row + jnp.arange(ROWS, dtype=i32)).astype(f32)
    angles = places[:, None] * frequency[None, :]
    cosine, sine = jnp.cos(angles), jnp.sin(angles)
    marks = [seg_ext[tap : tap + ROWS] == seg_own for tap in range(CONV - 1)]
    marks += [seg_own, seg_own == seg_ext[CONV - 2], seg_own == seg_own[-1]]
    marks = jnp.pad(jnp.stack([mark.astype(f32) for mark in marks], axis=1), ((0, 0), (0, 122)))
    table = jnp.concatenate([cosine, cosine, -sine, sine, marks], axis=1)

    own_conv = jnp.maximum(rank - 4, 0) * 128
    small = []
    for layer in range(layers):
        rows = [conv_x[layer], lax.dynamic_slice_in_dim(conv_bc[layer], own_conv, 128, 1)]
        rows.append(jnp.pad(head_params[layer], ((0, 2), (0, 128 - HLOC))))
        small.append(jnp.pad(jnp.concatenate(rows, axis=1), ((0, 3), (0, 0))))

    def packed(*members):
        width = sum(
            {4: 2 * XLOC}.get(member.ndim, 128 if member.shape[2] in (1024, HLOC) else member.shape[2])
            for member, _ in members
        )
        (columns,) = run_kernel(
            pack_kernel,
            [shape_of((w_query.shape[1], width), bf16)],
            rank.astype(i32).reshape(1),
            *(Layer(member, layer) for member, layer in members),
        )
        return lax.all_gather(columns, ("fsdp", "ctx"), axis=0, tiled=True)

    def proj_members(layer):
        return [(member, layer) for member in (w_zx, w_query, w_shared, w_dt)]

    weight_a = packed(*proj_members(0), (w_attn_out, 0), (w_ssm_out, 0))
    weight_b = packed(*proj_members(1), (w_gate, 0), (w_up, 0), (w_down, 0))
    weight_c = packed((w_gate, 1), (w_up, 1), (w_down, 1), (w_attn_out, 1), (w_ssm_out, 1))
    proj_place = [(weight_a, 0, PROJ), (weight_b, 0, PROJ)]
    out_place = [(weight_a, PROJ, 512), (weight_c, 1536, 512)]
    gate_up_place = [(weight_b, PROJ, 1024), (weight_c, 0, 1024)]
    down_place = [(weight_b, PROJ + 1024, 512), (weight_c, 1024, 512)]

    def together(*values):
        return lax.optimization_barrier(values)

    weight_a, table, seg_rows, small = together(weight_a, table, seg_rows, small)
    normed_shape = shape_of((ROWS, model), bf16)
    normed_kept = kept((ROWS, model), bf16)
    normed_b, inverse1, hidden, dffn_b, grad_hidden = run_kernel(
        first_kernel,
        [normed_shape, kept((SHARE, 128)), kept((SHARE, model)), normed_kept, kept((SHARE, model))],
        flags, inputs, cotangent, gains[0],
    )
    weight_a, normed_b = together(weight_a, normed_b)
    proj_place[0] = (weight_a, 0, PROJ)
    out_place[0] = (weight_a, PROJ, 512)
    normed_parts, dffn_parts = (normed_b,), (dffn_b,)
    saved = []
    wide = shape_of((ROWS, 512))
    proj_weight = fetched("proj_0", *proj_place[0])
    for layer in range(layers):
        normed_b, z, z_kept, xs, query, query_kept, dtn, dtn_kept = run_kernel(
            proj_kernel,
            [
                normed_kept, shape_of((ROWS, XLOC)), kept((ROWS, XLOC)), wide, shape_of((ROWS, HD), bf16),
                kept((ROWS, HD), bf16), shape_of((ROWS, 128)), kept((ROWS, 128)),
            ],
            flags, *(passed(normed_parts) if layer > 0 else normed_parts), proj_weight, table,
            scratch=[pltpu.VMEM((ROWS, PROJ), f32)],
        )
        halo = along_ctx(xs[ROWS - 8 :], 1)
        shared_own, shared_ext = run_kernel(
            shared_kernel,
            [shape_of((ROWS, 128), bf16), kept((264, 128))],
            flags, xs, Columns(halo), table, small[layer],
        )
        shared_parts = from_all(shared_own)
        x_ext, xc, xc_kept, rates, rates_kept, rates_t, rates_t_kept = run_kernel(
            prep_kernel,
            [
                kept((264, XLOC)), shape_of((ROWS, XLOC)), kept((ROWS, XLOC)), shape_of((ROWS, 256)),
                kept((ROWS, 256)), shape_of((16, ROWS)), kept((16, ROWS)),
            ],
            None, xs, dtn, Columns(halo), table, small[layer],
        )
        message, shared, shared_kept = run_kernel(
            state_kernel,
            [shape_of((KV + MSG, NSTATE), bf16), shape_of((8 * ROWS, 128), bf16), kept((8 * ROWS, 128), bf16)],
            flags, *passed(shared_parts), xc, rates, rates_t, table,
        )
        earlier = tuple(along_ctx(message, back) for back in (1, 2, 3))
        (intra,) = run_kernel(
            intra_kernel, [shape_of((ROWS, XLOC))],
            flags, shared, xc, rates, rates_t, table, seg_rows, small[layer],
        )
        earlier, out_weight, intra = together(earlier, fetched(f"out_{layer}", *out_place[layer]), intra)
        halves = [Columns(part, 0, NSTATE, rows=KV) for part in earlier]
        (swapped,) = run_kernel(halves_kernel, [shape_of((3 * KV, NSTATE), bf16)], None, *halves)
        attn, log_total, pairs = run_kernel(
            attention_kernel,
            [shape_of((ROWS, HD), bf16), kept((ROWS, HD)), kept((SEQ_BLOCKS * ROWS, 2 * HD), bf16)],
            flags, query, shared, *halves, Columns(other_core(swapped)), table, seg_rows,
        )
        state, ssm_y, cat, cat_kept = run_kernel(
            carry_kernel,
            [kept((XLOC, NSTATE)), kept((ROWS, XLOC)), shape_of((ROWS, 512), bf16), kept((ROWS, 512), bf16)],
            flags, *passed(earlier), shared, rates, table, intra, z, attn,
        )
        parts = summed_rows([cat], out_weight)
        if layer > 0:
            parts, gate_up_weight = together(parts, fetched(f"gate_up_{layer}", *gate_up_place[layer]))
        hidden1, normed2, inverse2 = add_norm(hidden, parts, gains[layer, 1])
        if layer > 0:
            normed_parts, down_weight = from_all(normed2, fetched("down_1", *down_place[layer]))
        else:
            normed_parts = from_all(normed2)
            gate_up_weight, down_weight = fetched_all("ffn_0", [gate_up_place[layer], down_place[layer]])
        wide_kept = kept((ROWS, 512))
        normed2_b, gate, up, act_b, act_kept = run_kernel(
            gate_up_kernel, [normed_kept, wide_kept, wide_kept, shape_of((ROWS, 512), bf16), kept((ROWS, 512), bf16)],
            None, *passed(normed_parts), gate_up_weight,
        )
        saved.append(
            (
                hidden, normed_b, inverse1, shared_ext, shared_kept, query_kept, x_ext, xc_kept, z_kept, dtn_kept,
                rates_kept, rates_t_kept, pairs, log_total, state, ssm_y, cat_kept, hidden1, inverse2, normed2_b,
                gate, up, act_kept,
            )
        )
        if layer + 1 < layers:
            hidden, next_normed, inverse1 = add_norm(
                hidden1, summed_rows([act_b], down_weight), gains[layer + 1, 0]
            )
            normed_parts, proj_weight = from_all(next_normed, fetched("proj_1", *proj_place[layer + 1]))

    weight_sums = [None] * layers
    small_parts = [None] * layers
    inner = None
    for layer in reversed(range(layers)):
        (
            hidden, normed_b, inverse1, shared_ext, shared, query, x_ext, xc, z, dtn, rates, rates_t,
            pairs, log_total, state, ssm_y, cat, hidden1, inverse2, normed2_b, gate, up, act_b,
        ) = saved[layer]
        last = layer == 0
        dffn_b, dgate_up = run_kernel(
            gate_up_back_kernel, [normed_kept, shape_of((ROWS, 1024), bf16)],
            None, *passed(dffn_parts), down_weight, stored(gate), stored(up),
        )
        parts = summed_rows([dgate_up], gate_up_weight)
        outer = weight_gradients([(normed2_b, dgate_up), (dffn_b, act_b)], 2304 if last else 2560, 1536, 0, inner)
        parts, outer = lax.optimization_barrier((parts, outer))
        if last:
            outer, weight_sums[1] = together(outer, weight_sums[1])
            weight_sums[0] = lax.psum_scatter(outer, ("fsdp", "ctx"), scatter_dimension=0, tiled=True)
        grad_mid, dmix, ggain2 = norm_back(grad_hidden, parts, hidden1, inverse2, gains[layer, 1])
        dmix_parts = from_all(dmix)
        dmix_parts, fetch = from_all(
            dmix,
            fetched_all(
                f"mixer_{layer}",
                [out_place[layer]]
                + [(array, 0, array.shape[1]) for array in (z, ssm_y, shared, rates, rates_t, xc, query, pairs, state)],
            ),
        )
        out_weight, z, ssm_y, shared, rates, rates_t, xc, query, pairs, state = fetch
        dmix_b, dattn, dy, dz, message = run_kernel(
            gate_back_kernel,
            [
                normed_kept, shape_of((ROWS, HD), bf16), shape_of((ROWS, XLOC)), shape_of((ROWS, XLOC), bf16),
                shape_of((MSG, NSTATE), bf16),
            ],
            flags, *passed(dmix_parts), out_weight, z, ssm_y, shared, rates, rates_t, table,
            scratch=[pltpu.VMEM((ROWS, XLOC), f32), pltpu.VMEM((ROWS, 512), f32)],
        )
        after = tuple(along_ctx(message, -ahead) for ahead in (1, 2, 3))
        early, mine, theirs = run_kernel(
            attention_back_kernel,
            [kept((ROWS, 512), bf16), shape_of((4 * ROWS, HD)), shape_of((4 * ROWS, HD), bf16)],
            flags, dattn, dz, query, pairs, stored(log_total), table, seg_rows,
        )
        got = other_core(theirs)
        dx, dshared, drates, dskip = run_kernel(
            intra_back_kernel,
            [kept((ROWS, XLOC)), kept((ROWS, 2 * NSTATE)), kept((ROWS, 256)), kept((1, XLOC))],
            flags, dy, xc, shared, rates, rates_t, table, seg_rows, state, small[layer],
            scratch=[pltpu.VMEM((128, ROWS), f32), pltpu.VMEM((ROWS, 128), f32)],
        )
        got, dx = lax.optimization_barrier((got, dx))
        dkv = parts_from(mine, got, along_ctx, -1)
        if last:
            mixed_grads = owned_gradients([(dmix_b, cat), (normed_b, early)])
            after, dkv, mixed_grads = together(after, dkv, mixed_grads)
            mixed_grads = lax.all_to_all(mixed_grads, ("fsdp", "ctx"), 0, 0, tiled=True)
        else:
            outer = weight_gradients([(dmix_b, cat)], outer.shape[1], 512, 3, outer)
            outer = weight_gradients([(normed_b, early)], outer.shape[1], 512, 4, outer)
            after, dkv, outer = together(after, dkv, outer)
            weight_sums[1] = lax.psum_scatter(outer, ("fsdp", "ctx"), scatter_dimension=0, tiled=True)
        packed_grads, dxpre, edge_x, gconv_x, ddt, gheads = run_kernel(
            state_back_kernel,
            [
                shape_of((8 * ROWS, 128), bf16), kept((ROWS, XLOC)), shape_of((8, XLOC)), kept((8, XLOC)),
                kept((ROWS, 128)), kept((8, 128)),
            ],
            flags, *passed(after), shared, xc, rates, rates_t, table, state, small[layer], stored(dtn), stored(dx), stored(dshared), stored(drates), *summands(dkv), stored(x_ext),
            scratch=[pltpu.VMEM((272, XLOC), f32), pltpu.VMEM((ROWS, XLOC), f32), pltpu.VMEM((ROWS, 128), f32)],
        )
        edge_x = along_ctx(edge_x, -1)
        dshared_parts = parts_of_sum(packed_grads[: 4 * ROWS], packed_grads[4 * ROWS :], along_y, 1)
        dsh, edge_sh, gconv_sh = run_kernel(
            shared_back_kernel,
            [shape_of((ROWS, 128)), shape_of((8, 128)), kept((8, 128))],
            flags, *summands(dshared_parts), stored(shared_ext), table, small[layer],
            scratch=[pltpu.VMEM((272, 128), f32)],
        )
        edge_sh, proj_weight = together(
            along_ctx(edge_sh, -1), fetched(f"proj_again_{layer}", *proj_place[layer])
        )
        (late,) = run_kernel(
            late_kernel, [shape_of((ROWS, LATE), bf16)], flags, stored(dxpre), Columns(edge_x), dsh,
            Columns(edge_sh), stored(ddt),
        )
        parts = summed_rows([early, late], proj_weight)
        if not last:
            inner = weight_gradients([(normed_b, late)], 2304, 768, 2)
            parts, inner = together(parts, inner)
        grad_hidden, rounded, ggain1 = norm_back(grad_mid, parts, hidden, inverse1, gains[layer, 0])
        if last:
            dffn_parts = from_all(rounded)
        else:
            dffn_parts, (down_weight, gate_up_weight) = from_all(
                rounded, fetched_all("ffn_again", [down_place[layer - 1], gate_up_place[layer - 1]])
            )
            last_hidden1, last_act = hidden1, act_b
        (small_parts[layer],) = run_kernel(
            small_kernel, [shape_of((64, 128), bf16)],
            None, *map(stored, (ggain1, ggain2, gconv_sh, gconv_x, gheads, dskip)),
        )
    small_all = jnp.concatenate(small_parts, axis=0)
    owned = owned_gradients([(normed_b, late)], small_all)
    owned = lax.all_to_all(owned, ("fsdp", "ctx"), 0, 0, tiled=True)
    (input_grad,) = run_kernel(natural_kernel, [kept((ROWS, model))], flags, *passed(dffn_parts))
    last_act, down_weight, _ = together(last_act, fetched("down_last", *down_place[1]), small_parts[0])
    (layer_out,) = run_kernel(
        output_kernel, [shape_of((SHARE, model), bf16)], None,
        stored(last_hidden1), *summands(summed_rows([last_act], down_weight)),
    )
    (layer_out,) = run_kernel(natural_kernel, [normed_kept], flags, *passed(from_all(layer_out)))
    lower, upper = weight_sums

    def pair_of(width):
        return shape_of((layers, model // 16, width))

    grad_attn, grad_ssm, grad_gate, grad_up, grad_down, grad_query, grad_z = run_kernel(
        early_outputs_kernel,
        [
            *(kept((layers, model // 16, width)) for width in (128, 384, 512, 512, 512, 128)),
            pair_of(XLOC),
        ],
        None, Columns(upper), Columns(lower), Columns(mixed_grads),
    )
    upper_late = lower[:, 1536 : 1536 + LATE]
    upper_shared = from_all(upper_late[:, XLOC:512])
    owned, layer_out, input_grad, upper_shared, grad_z = together(
        owned, layer_out, input_grad, upper_shared, grad_z
    )
    over_tp, late_sum, gconv_x, gheads = run_kernel(
        block_sum_kernel,
        [
            shape_of((224, 128), bf16), shape_of((model // 16, LATE)), shape_of((layers * (CONV + 1), XLOC)),
            shape_of((8, 128)),
        ],
        None, Columns(owned),
    )
    grad_zx, grad_dt, grad_shared, ggains1, ggains2, gconv_bc = run_kernel(
        last_outputs_kernel,
        [
            shape_of((layers, model // 16, 2, XLOC)), pair_of(HLOC), pair_of(1024), shape_of((layers, model)),
            shape_of((layers, model)), shape_of((layers * (CONV + 1), 512)),
        ],
        flags, *passed(from_all(over_tp)), *passed(upper_shared), late_sum, Columns(upper_late), grad_z,
        scratch=[pltpu.VMEM((16, 224, 128), f32)],
    )
    gconv_x = gconv_x.reshape(layers, CONV + 1, XLOC)
    gconv_bc = gconv_bc.reshape(layers, CONV + 1, 512)
    gheads = gheads[: 3 * layers].reshape(layers, 3, 128)[:, :, :HLOC]
    return (
        layer_out[None],
        input_grad[None],
        grad_query,
        grad_shared,
        grad_zx,
        grad_dt,
        grad_attn,
        grad_ssm,
        grad_gate,
        grad_up,
        grad_down,
        ggains1,
        gconv_x,
        gconv_bc,
        gheads[:, :2],
        ggains2,
        gheads[:, 2],
    )


def solution(mesh):
    columns = P(None, ("fsdp", "ctx"), "tp")
    rows = P("fsdp", "ctx", None)
    return jax.shard_map(
        body,
        mesh=mesh,
        in_specs=(
            rows, rows, P("fsdp", None), columns, P(None, ("fsdp", "ctx"), None),
            P(None, ("fsdp", "ctx"), None, "tp"), columns, columns, columns, columns, columns, columns,
            P(), P(None, None, "tp"), P(), P(None, None, "tp"),
        ),
        out_specs=(
            rows, rows, columns, P(None, ("fsdp", "ctx"), None), P(None, ("fsdp", "ctx"), None, "tp"),
            columns, columns, columns, columns, columns, columns,
            P(), P(None, None, "tp"), P(), P(None, None, "tp"), P(), P(None, "tp"),
        ),
        check_vma=False,
    )
```

```python
import math
from functools import partial

import jax
import jax.numpy as jnp
from jax import lax
from jax.experimental import pallas as pl
from jax.experimental.pallas import tpu as pltpu
from jax.sharding import PartitionSpec as P

HD = 128
HP = 64
NSTATE = 256
CONV = 4
ROWS = 256
SHARE = 32
XLOC = 384
PROJ = 1152
LATE = 640
HLOC = 6
PAIRS = 3
SEQ_BLOCKS = 4
MSG = XLOC + 16
KV = 128
VMEM_LIMIT = 16 * 1024 * 1024

norm_eps = 1e-05
rope_base = 100000000000.0
bf16 = jnp.bfloat16
f32 = jnp.float32
i32 = jnp.int32


def along_y(value, steps):
    pairs = [(i, ((i // 2 + steps) % 4) * 2 + i % 2) for i in range(8)]
    return lax.ppermute(value, "tp", pairs)


def other_core(value):
    return lax.ppermute(value, "tp", [(i, i ^ 1) for i in range(8)])


def along_ctx(value, steps):
    first, last = max(0, -steps), min(4, 4 - steps)
    return lax.ppermute(value, "ctx", [(i, i + steps) for i in range(first, last)])


def ring(value, axis, steps):
    return lax.ppermute(value, axis, [(i, (i + steps) % 4) for i in range(4)])


def from_all(value, beside=None):
    half = [value] + [along_y(value, -k) for k in (1, 2, 3)]
    if beside is not None:
        half[1], beside = lax.optimization_barrier((half[1], beside))
    parts = tuple(half + [other_core(part) for part in half])
    return parts if beside is None else (parts, beside)


def dot_nn(a, b):
    return jnp.dot(a, b, preferred_element_type=f32)


def dot_nt(a, b):
    return lax.dot_general(a, b, (((1,), (1,)), ((), ())), preferred_element_type=f32)


def dot_tn(a, b):
    return lax.dot_general(a, b, (((0,), (0,)), ((), ())), preferred_element_type=f32)


def shape_of(shape, dtype=f32):
    return jax.ShapeDtypeStruct(shape, dtype)


class Columns:
    def __init__(self, array, block=0, width=None, rows=None, keep=False):
        self.array, self.block, self.keep = array, block, keep
        self.shape = (rows or array.shape[0],) + array.shape[1:-1] + (width or array.shape[-1],)

    def spec(self):
        place = (0,) * (len(self.shape) - 1) + (self.block,)
        return pl.BlockSpec(self.shape, lambda i: place, pipeline_mode=pl.Buffered(1))


class Layer:
    def __init__(self, array, layer):
        self.array, self.layer, self.keep = array, layer, True
        self.shape = (1,) + array.shape[1:]

    def spec(self):
        place = (self.layer,) + (0,) * (len(self.shape) - 1)
        return pl.BlockSpec(self.shape, lambda i: place, pipeline_mode=pl.Buffered(1))


def stored(array):
    return Columns(array, keep=True)


def summands(parts):
    return [stored(parts[0])] + passed(parts[1:])


def passed(arrays):
    return [Columns(array) for array in arrays]


def kept(shape, dtype=f32):
    return pltpu.HBM(shape, dtype)


def fetch_kernel(places, *refs):
    count = len(places)
    sources, outs, sems = refs[:count], refs[count : 2 * count], refs[-1]
    copies = []
    for (start, pieces), source, out in zip(places, sources, outs):
        rows, width = out.shape[0] // pieces, out.shape[1]
        for index in range(pieces):
            own = pl.ds(rows * index, rows)
            copies.append(
                pltpu.make_async_copy(
                    source.at[own, pl.ds(start, width)], out.at[own, :], sems.at[len(copies)]
                )
            )
    for copy in copies:
        copy.start()
    for copy in copies:
        copy.wait()


def fetched_all(name, sources):
    places = [(start, 4 if array.shape[0] == 2048 and width > 128 else 1) for array, start, width in sources]
    whole = pl.BlockSpec(memory_space=pltpu.VMEM)
    return pl.pallas_call(
        partial(fetch_kernel, places),
        name=name,
        out_shape=tuple(pltpu.VMEM((array.shape[0], width), array.dtype) for array, _, width in sources),
        in_specs=[pl.BlockSpec(memory_space=pltpu.HBM)] * len(sources),
        out_specs=tuple(whole for _ in sources),
        scratch_shapes=[pltpu.SemaphoreType.DMA((sum(pieces for _, pieces in places),))],
        compiler_params=pltpu.CompilerParams(vmem_limit_bytes=VMEM_LIMIT),
        cost_estimate=pl.CostEstimate(
            flops=0, bytes_accessed=sum(2 * array.shape[0] * width for array, _, width in sources), transcendentals=0
        ),
    )(*(pltpu.with_memory_space_constraint(array, pltpu.HBM) for array, _, _ in sources))


def fetched(name, array, start, width):
    return fetched_all(name, [(array, start, width)])[0]


def restored(name, arrays):
    return fetched_all(name, [(array, 0, array.shape[1]) for array in arrays])


def run_kernel(kernel, outs, flags, *args, scratch=(), flops=50_000_000):
    whole = pl.BlockSpec(memory_space=pltpu.VMEM)
    own = [isinstance(arg, (Columns, Layer)) for arg in args]
    specs, arrays, out_specs = [], [], []
    for arg, copied in zip(args, own):
        specs.append(arg.spec() if copied else whole)
        array = arg.array if copied else arg
        arrays.append(pltpu.with_memory_space_constraint(array, pltpu.HBM) if copied and arg.keep else array)
    for out in outs:
        in_vmem = isinstance(out, jax.ShapeDtypeStruct)
        out_specs.append(whole if in_vmem else pl.BlockSpec(out.shape, lambda i, n=len(out.shape): (0,) * n))
        own.append(not in_vmem)
    moved = sum(2 * math.prod(arg.shape) for arg in args) + sum(2 * math.prod(o.shape) for o in outs)
    if flags is not None:
        specs = [pl.BlockSpec(memory_space=pltpu.SMEM)] + specs
        arrays = [flags] + arrays
    return pl.pallas_call(
        kernel,
        grid=(1,) if any(own) else (),
        out_shape=tuple(outs),
        in_specs=specs,
        out_specs=tuple(out_specs),
        scratch_shapes=list(scratch),
        compiler_params=pltpu.CompilerParams(vmem_limit_bytes=VMEM_LIMIT),
        cost_estimate=pl.CostEstimate(flops=flops, bytes_accessed=moved, transcendentals=0),
    )(*arrays)


def local_block(flags, natural):
    return pl.multiple_of(flags[8 + natural] * SHARE, SHARE)


def rank_block(flags, rank):
    return pl.multiple_of(flags[16 + rank] * ROWS, ROWS)


def lane_index(shape):
    return lax.broadcasted_iota(i32, shape, len(shape) - 1)


def spread(columns, pair):
    low = lane_index((1, 128)) < HP
    return jnp.where(low, columns[:, 2 * pair : 2 * pair + 1], columns[:, 2 * pair + 1 : 2 * pair + 2])


def lanes_of(pair):
    return slice(128 * pair, 128 * pair + 128)


def turned(value, table, sign):
    return value * table[:, 0:128] + sign * (pltpu.roll(value, 64, 1) * table[:, 128:256])


def segments(table):
    return table[:, 259:260]


def sigmoid(v):
    return 1.0 / (1.0 + jnp.exp(-v))


def softplus(v):
    return jnp.maximum(v, 0.0) + jnp.log1p(jnp.exp(-jnp.abs(v)))


def conv_sum(ext, table, weight):
    total = weight[CONV : CONV + 1, :] + ext[8 : 8 + ROWS, :] * weight[3:4, :]
    for tap in range(CONV - 1):
        total = total + table[:, 256 + tap : 257 + tap] * ext[5 + tap : 5 + tap + ROWS, :] * weight[tap : tap + 1, :]
    return total


def conv_back(grad_out, ext, table, weight, work, grad_ref, edge_ref, gweight_ref):
    total = conv_sum(ext, table, weight)
    sig = sigmoid(total)
    grad = grad_out * sig * (1.0 + total * (1.0 - sig))
    width = grad.shape[1]
    gweight_ref[...] = jnp.zeros((8, width), f32)
    gweight_ref[CONV : CONV + 1, :] = jnp.sum(grad, axis=0, keepdims=True)
    gweight_ref[3:4, :] = jnp.sum(grad * ext[8 : 8 + ROWS, :], axis=0, keepdims=True)
    work[0:8, :] = jnp.zeros((8, width), f32)
    work[264:272, :] = jnp.zeros((8, width), f32)
    own = grad * weight[3:4, :]
    edge = jnp.zeros((8, width), f32)
    for tap in range(CONV - 1):
        part = grad * table[:, 256 + tap : 257 + tap]
        gweight_ref[tap : tap + 1, :] = jnp.sum(
            part * ext[5 + tap : 5 + tap + ROWS, :], axis=0, keepdims=True
        )
        work[8:264, :] = part * weight[tap : tap + 1, :]
        own = own + work[11 - tap : 11 - tap + ROWS, :]
        edge = edge + work[3 - tap : 11 - tap, :]
    grad_ref[...] = own
    edge_ref[...] = edge


def pack_kernel(place, *refs):
    out, at, index = refs[-1], 0, 0
    while index < len(refs) - 1:
        ref = refs[index]
        if len(ref.shape) == 4:
            out[:, at : at + XLOC] = ref[0, :, 0, :]
            out[:, at + XLOC : at + 512] = refs[index + 1][0]
            out[:, at + 512 : at + 896] = ref[0, :, 1, :]
            at, index = at + 896, index + 2
            continue
        width = min(ref.shape[2], 512)
        if width == HLOC:
            out[:, at : at + 128] = jnp.zeros((out.shape[0], 128), bf16)
            out[:, at : at + HLOC] = ref[0]
            width = 128
        elif ref.shape[2] == 1024:
            width = 128
            out[:, at : at + width] = ref[0, :, pl.ds(pl.multiple_of(place[0] * 128, 128), 128)]
        else:
            out[:, at : at + width] = ref[0]
        at, index = at + width, index + 1


def first_kernel(flags, rows, cotangent, gain, normed, inverse, hidden_kept, grads, grad):
    for block in range(8):
        own = slice(SHARE * block, SHARE * (block + 1))
        from_rows = pl.ds(pl.multiple_of(flags[24 + block] * SHARE, SHARE), SHARE)
        wide = rows[0, from_rows, :].astype(f32)
        scale = lax.rsqrt(jnp.mean(wide * wide, axis=1, keepdims=True) + norm_eps)
        normed[own, :] = (wide * scale * gain[0:1, :]).astype(bf16)
        grads[own, :] = cotangent[0, from_rows, :]
        if block == 0:
            hidden_kept[...] = wide
            inverse[...] = jnp.broadcast_to(scale, inverse.shape)
            grad[...] = cotangent[0, from_rows, :].astype(f32)


def joined(parts):
    return parts[0][...] if len(parts) == 1 else jnp.concatenate([part[...] for part in parts], axis=0)


def proj_kernel(flags, *refs):
    parts, (weight, table, normed, z, z_kept, xs, query, query_kept, dtn, dtn_kept, work) = refs[:-11], refs[-11:]
    rows = joined(parts)
    normed[...] = rows
    work[...] = dot_nn(rows, weight[...])
    for block in range(8):
        own = slice(SHARE * block, SHARE * (block + 1))
        from_rows = pl.ds(local_block(flags, block), SHARE)
        for out in (z, z_kept):
            out[own, :] = work[from_rows, 0:XLOC]
        xs[own, :] = work[from_rows, 512:1024]
        head = turned(work[from_rows, XLOC:512], table[own, :], 1.0).astype(bf16)
        for out in (query, query_kept):
            out[own, :] = head
        for out in (dtn, dtn_kept):
            out[own, :] = work[from_rows, 1024:PROJ]


def shared_kernel(flags, xs, halo, table, small, out, ext):
    own = xs[:, XLOC:512]
    ext[0:8, :] = halo[:, XLOC:512]
    ext[8 : 8 + ROWS, :] = own
    total = conv_sum(ext, table, small[:, XLOC:512])
    rank = flags[0]
    out[...] = jnp.where(
        rank < 2, turned(own, table, 1.0), jnp.where(rank < 4, own, total * sigmoid(total))
    ).astype(bf16)


def prep_kernel(xs, dtn, halo, table, small, ext, xc, xc_kept, rates, rates_kept, rates_t, rates_t_kept):
    ext[0:8, :] = halo[:, 0:XLOC]
    ext[8 : 8 + ROWS, :] = xs[:, 0:XLOC]
    total = conv_sum(ext, table, small[:, 0:XLOC])
    for out in (xc, xc_kept):
        out[...] = total * sigmoid(total)
    params = small[:, 512:640]
    rate = softplus(dtn[...] + params[1:2, :])
    logs = -jnp.exp(params[0:1, :]) * rate
    rows = lax.broadcasted_iota(i32, (ROWS, ROWS), 0)
    lower = (rows >= lane_index((ROWS, ROWS))).astype(f32)
    running = jnp.dot(lower, logs, precision=lax.Precision.HIGHEST, preferred_element_type=f32)
    for out in (rates, rates_kept):
        out[:, 0:128] = rate
        out[:, 128:256] = running
    rate_t, running_t = rate.T[0:8, :], running.T[0:8, :]
    for out in (rates_t, rates_t_kept):
        out[0:8, :] = rate_t
        out[8:16, :] = running_t


def block_decays(flags, rates_t):
    kept = jnp.where(flags[4] == flags[5], 1.0, 0.0)
    return jnp.exp(rates_t[8:16, ROWS - 1 : ROWS]) * kept


def decay_rows(flags, rates_t):
    rows = jnp.broadcast_to(block_decays(flags, rates_t), (8, NSTATE))
    return jnp.concatenate([rows, jnp.zeros((8, NSTATE), f32)], axis=0).astype(bf16)


def weights_in(rates, table):
    last = rates[ROWS - 1 : ROWS, 128:256]
    gap = jnp.exp(last - rates[:, 128:256]) * table[:, 261:262]
    return gap, gap * rates[:, 0:128]


def rank_columns(flags, shared, first):
    return jnp.concatenate(
        [shared[pl.ds(rank_block(flags, rank), ROWS), :] for rank in (first, first + 1)], axis=1
    )


def inject_of(flags, shared):
    return rank_columns(flags, shared, 4)


def readout_of(flags, shared):
    return rank_columns(flags, shared, 6)


def carry_of(rates, table):
    return jnp.exp(rates[:, 128:256]) * table[:, 260:261]


def state_kernel(flags, s0, s1, s2, s3, s4, s5, s6, s7, xc, rates, rates_t, table, out, shared, shared_kept):
    for index, part in enumerate((s0, s1, s2, s3, s4, s5, s6, s7)):
        shared[ROWS * index : ROWS * (index + 1), :] = part[...]
        shared_kept[ROWS * index : ROWS * (index + 1), :] = part[...]
    inject = inject_of(flags, shared)
    _, weight = weights_in(rates, table)
    for pair in range(PAIRS):
        weighted = (xc[:, lanes_of(pair)] * spread(weight, pair)).astype(bf16)
        out[KV + 128 * pair : KV + 128 * (pair + 1), :] = dot_tn(weighted, inject).astype(bf16)
    out[KV + XLOC : KV + MSG, :] = decay_rows(flags, rates_t)
    half = shared[pl.ds(rank_block(flags, 2 * flags[2] + flags[1] // 2), ROWS), :]
    out[0:KV, :] = jnp.concatenate([half[0:128], half[128:256]], axis=1)


def halves_kernel(msg1, msg2, msg3, out):
    for index, msg in enumerate((msg1, msg2, msg3)):
        out[KV * index : KV * (index + 1), :] = msg[...]


def allowed_pairs(table, seg_rows):
    rows = lax.broadcasted_iota(i32, (ROWS, ROWS), 0)
    return (rows >= lane_index((ROWS, ROWS))) & (segments(table) == seg_rows[0:1, :])


def head_decay(allowed, rates, rates_t, head):
    gap = rates[:, 128 + head : 129 + head] - rates_t[8 + head : 9 + head, :]
    return jnp.where(allowed, jnp.exp(jnp.where(allowed, gap, 0.0)), 0.0)


def intra_kernel(flags, shared, xc, rates, rates_t, table, seg_rows, small, out):
    inject, readout = inject_of(flags, shared), readout_of(flags, shared)
    both = dot_nt(readout, inject)
    allowed = allowed_pairs(table, seg_rows)
    low = lane_index((1, 128)) < HP
    for pair in range(PAIRS):
        x = xc[:, lanes_of(pair)]
        xb = x.astype(bf16)
        heads = []
        for head in (2 * pair, 2 * pair + 1):
            decay = head_decay(allowed, rates, rates_t, head)
            heads.append(dot_nn((both * decay * rates_t[head : head + 1, :]).astype(bf16), xb))
        out[:, lanes_of(pair)] = jnp.where(low, heads[0], heads[1]) + spread(small[2:3, 512:640], pair) * x


def keys_values(flags, shared, halves, swapped):
    head, first = flags[1] // 2, flags[2] == 0
    pairs = [
        (
            shared[pl.ds(rank_block(flags, head), ROWS), :],
            shared[pl.ds(rank_block(flags, 2 + head), ROWS), :],
        )
    ]
    for index, half in enumerate(halves):
        packed = half[...], swapped[KV * index : KV * (index + 1), :]
        mine, theirs = (jnp.concatenate([part[:, 0:128], part[:, 128:256]], axis=0) for part in packed)
        pairs.append((jnp.where(first, mine, theirs), jnp.where(first, theirs, mine)))
    return pairs


def masked_scores(query, pairs, table, seg_rows):
    parts = []
    for block, (keys, _) in enumerate(pairs):
        score = dot_nt(query, keys) * HD ** (-0.5)
        keep = segments(table) == seg_rows[block : block + 1, :]
        if block == 0:
            rows = lax.broadcasted_iota(i32, (ROWS, ROWS), 0)
            keep = keep & (rows >= lane_index((ROWS, ROWS)))
        parts.append(jnp.where(keep, score, -1e30))
    return parts


def attention_kernel(flags, query, shared, h1, h2, h3, swapped, table, seg_rows, out, log_total, kept):
    pairs = keys_values(flags, shared, (h1, h2, h3), swapped)
    for block, (keys, values) in enumerate(pairs):
        kept[ROWS * block : ROWS * (block + 1), 0:HD] = keys
        kept[ROWS * block : ROWS * (block + 1), HD : 2 * HD] = values
    parts = masked_scores(query[...], pairs, table, seg_rows)
    top = parts[0].max(axis=1, keepdims=True)
    for part in parts[1:]:
        top = jnp.maximum(top, part.max(axis=1, keepdims=True))
    parts = [jnp.exp(part - top) for part in parts]
    total = sum(part.sum(axis=1, keepdims=True) for part in parts)
    inverse = 1.0 / total
    result = jnp.zeros((ROWS, HD), f32)
    for part, (_, values) in zip(parts, pairs):
        result = result + dot_nn((part * inverse).astype(bf16), values)
    out[...] = result.astype(bf16)
    log_total[...] = jnp.broadcast_to(top + jnp.log(total), (ROWS, HD))


def chained(first, second, third, base):
    rows1 = first[base + XLOC : base + MSG, :].astype(f32)
    rows2 = second[base + XLOC : base + MSG, :].astype(f32)
    parts = []
    for head in range(HLOC):
        own = slice(base + HP * head, base + HP * head + HP)
        older = second[own, :].astype(f32) + rows2[head : head + 1, :] * third[own, :].astype(f32)
        parts.append(first[own, :].astype(f32) + rows1[head : head + 1, :] * older)
    return jnp.concatenate(parts, axis=0)


def carry_kernel(flags, msg1, msg2, msg3, shared, rates, table, intra, z, attn, state, ssm_y, cat, cat_kept):
    entering = chained(msg1, msg2, msg3, KV)
    state[...] = entering
    from_state = dot_nt(readout_of(flags, shared), entering.astype(bf16))
    carry = carry_of(rates, table)
    for pair in range(PAIRS):
        own = lanes_of(pair)
        y = intra[:, own] + spread(carry, pair) * from_state[:, own]
        ssm_y[:, own] = y
        gate = z[:, own]
        gated = (y * gate * sigmoid(gate)).astype(bf16)
        for block in range(8):
            for out in (cat, cat_kept):
                out[pl.ds(local_block(flags, block), SHARE), 128 + 128 * pair : 256 + 128 * pair] = gated[
                    SHARE * block : SHARE * (block + 1), :
                ]
    for block in range(8):
        for out in (cat, cat_kept):
            out[pl.ds(local_block(flags, block), SHARE), 0:128] = attn[SHARE * block : SHARE * (block + 1), :]


def gate_back_kernel(
    flags, p0, p1, p2, p3, p4, p5, p6, p7, weight, z, ssm_y, shared, rates, rates_t, table,
    dmix, dattn, dy, dz, msg, work, local,
):
    rows = joined((p0, p1, p2, p3, p4, p5, p6, p7))
    dmix[...] = rows
    local[...] = dot_nn(rows, weight[...])
    for block in range(8):
        own = slice(SHARE * block, SHARE * (block + 1))
        from_rows = pl.ds(local_block(flags, block), SHARE)
        dattn[own, :] = local[from_rows, 0:128].astype(bf16)
        work[own, :] = local[from_rows, 128:512]
    readout = readout_of(flags, shared)
    carry = carry_of(rates, table)
    for pair in range(PAIRS):
        own = lanes_of(pair)
        gate, grad = z[:, own], work[:, own]
        sig = sigmoid(gate)
        y_grad = grad * gate * sig
        dy[:, own] = y_grad
        dz[:, own] = (grad * ssm_y[:, own] * sig * (1.0 + gate * (1.0 - sig))).astype(bf16)
        msg[own, :] = dot_tn((y_grad * spread(carry, pair)).astype(bf16), readout).astype(bf16)
    msg[XLOC:MSG, :] = decay_rows(flags, rates_t)


def attention_back_kernel(
    flags, dattn, dz, query, kept, log_total, table, seg_rows,
    early, mine, theirs,
):
    pairs = []
    for block in range(SEQ_BLOCKS):
        own = slice(ROWS * block, ROWS * (block + 1))
        pairs.append((kept[own, 0:HD], kept[own, HD : 2 * HD]))
    first = flags[2] == 0
    q = query[...]
    grad = dattn[...]
    parts = masked_scores(q, pairs, table, seg_rows)
    logs = log_total[:, 0:1]
    probs = [jnp.exp(part - logs) for part in parts]
    grads = [dot_nt(grad, values) for _, values in pairs]
    inner = sum((p * g).sum(axis=1, keepdims=True) for p, g in zip(probs, grads))
    total = jnp.zeros((ROWS, HD), f32)
    for block, (p, g, (keys, _)) in enumerate(zip(probs, grads, pairs)):
        own = slice(ROWS * block, ROWS * (block + 1))
        score = (p * (g - inner)).astype(bf16)
        total = total + dot_nn(score, keys)
        dkeys = dot_tn(score, q) * HD ** (-0.5)
        dvalues = dot_tn(p.astype(bf16), grad)
        mine[own, :] = jnp.where(first, dkeys, dvalues)
        theirs[own, :] = jnp.where(first, dvalues, dkeys).astype(bf16)
    total = total * HD ** (-0.5)
    dq = turned(total, table, -1.0).astype(bf16)
    for block in range(8):
        own = slice(SHARE * block, SHARE * (block + 1))
        to_rows = pl.ds(local_block(flags, block), SHARE)
        early[to_rows, 0:XLOC] = dz[own, :]
        early[to_rows, XLOC:512] = dq[own, :]


def intra_back_kernel(
    flags, dy, xc, shared, rates, rates_t, table, seg_rows, state, small,
    dx, dshared, drates, dskip, row_sums, dcum,
):
    inject, readout = inject_of(flags, shared), readout_of(flags, shared)
    both = dot_nt(readout, inject)
    allowed = allowed_pairs(table, seg_rows)
    low = lane_index((1, 128)) < HP
    carry = carry_of(rates, table)
    entering = state[...].astype(bf16)
    from_state = dot_nt(readout, entering)
    dboth = jnp.zeros((ROWS, ROWS), f32)
    row_sums[...] = jnp.zeros((128, ROWS), f32)
    dcum[...] = jnp.zeros((ROWS, 128), f32)
    carried = []
    for pair in range(PAIRS):
        own = lanes_of(pair)
        x = xc[:, own]
        xb = x.astype(bf16)
        grad = dy[:, own]
        dskip[:, own] = jnp.sum(grad * x, axis=0, keepdims=True)
        carried.append((grad * spread(carry, pair)).astype(bf16))
        through = grad * from_state[:, own]
        total = spread(small[2:3, 512:640], pair) * grad
        for head in (2 * pair, 2 * pair + 1):
            mine = low if head % 2 == 0 else jnp.logical_not(low)
            decay = head_decay(allowed, rates, rates_t, head)
            steps = rates_t[head : head + 1, :]
            head_grad = jnp.where(mine, grad, 0.0).astype(bf16)
            dmix = dot_nt(head_grad, xb)
            kept = dmix * decay
            dboth = dboth + kept * steps
            mixed = both * decay
            total = total + dot_tn((mixed * steps).astype(bf16), head_grad)
            passed = dmix * mixed
            row_sums[head : head + 1, :] = jnp.sum(passed, axis=0, keepdims=True)
            dcum[:, head : head + 1] = jnp.sum(passed * steps, axis=1, keepdims=True) + carry[
                :, head : head + 1
            ] * jnp.sum(jnp.where(mine, through, 0.0), axis=1, keepdims=True)
        dx[:, own] = total
    columns = row_sums[...].T
    drates[:, 0:128] = columns
    drates[:, 128:256] = dcum[...] - rates[:, 0:128] * columns
    dboth_b = dboth.astype(bf16)
    dshared[:, NSTATE:] = dot_nn(dboth_b, inject) + dot_nn(jnp.concatenate(carried, axis=1), entering)
    dshared[:, 0:NSTATE] = dot_tn(dboth_b, readout)


def state_back_kernel(
    flags, msg1, msg2, msg3, shared, xc, rates, rates_t, table, state, small, dtn,
    dx, dshared, drates, kv0, kv1, kv2, kv3, ext,
    packed, dxpre, edge, gweight, ddt, heads, work, dconv, sums,
):
    later = chained(msg1, msg2, msg3, 0)
    later_b = later.astype(bf16)
    inject = inject_of(flags, shared)
    low = lane_index((1, 128)) < HP
    params = small[:, 512:640]
    gap, weights = weights_in(rates, table)
    from_later = dot_nt(inject, later_b)
    products = later * state[...]
    decays = block_decays(flags, rates_t)
    sums[...] = jnp.zeros((ROWS, 128), f32)
    weighted = []
    for pair in range(PAIRS):
        own = lanes_of(pair)
        x = xc[:, own]
        scale = spread(weights, pair)
        weighted.append((x * scale).astype(bf16))
        dconv[:, own] = dx[:, own] + scale * from_later[:, own]
        through = x * from_later[:, own]
        for head in (2 * pair, 2 * pair + 1):
            mine = low if head % 2 == 0 else jnp.logical_not(low)
            sums[:, head : head + 1] = jnp.sum(jnp.where(mine, through, 0.0), axis=1, keepdims=True)
    dweights = sums[...]
    moved = dweights * weights
    last = jnp.sum(moved, axis=0, keepdims=True)
    lanes = lane_index((1, 128))
    for head in range(HLOC):
        total = jnp.sum(
            jnp.sum(products[HP * head : HP * head + HP, :], axis=0, keepdims=True), axis=1, keepdims=True
        )
        last = last + jnp.where(lanes == head, total * decays[head : head + 1, :], 0.0)
    rows = lax.broadcasted_iota(i32, (ROWS, 128), 0)
    dcums = drates[:, 128:256] - moved + jnp.where(rows == ROWS - 1, last, 0.0)
    square = lax.broadcasted_iota(i32, (ROWS, ROWS), 0)
    upper = (square <= lane_index((ROWS, ROWS))).astype(f32)
    dlogs = jnp.dot(upper, dcums, precision=lax.Precision.HIGHEST, preferred_element_type=f32)
    rate = -jnp.exp(params[0:1, :])
    dsteps = drates[:, 0:128] + dweights * gap + dlogs * rate
    ddts = dsteps * sigmoid(dtn[...] + params[1:2, :])
    ddt[...] = ddts
    heads[...] = jnp.zeros((8, 128), f32)
    heads[0:1, :] = jnp.sum(dlogs * rate * rates[:, 0:128], axis=0, keepdims=True)
    heads[1:2, :] = jnp.sum(ddts, axis=0, keepdims=True)
    dinject_all = (dshared[:, 0:NSTATE] + dot_nn(jnp.concatenate(weighted, axis=1), later_b)).astype(bf16)
    dreadout_all = dshared[:, NSTATE:].astype(bf16)
    packed[...] = jnp.zeros((8 * ROWS, 128), bf16)
    grads = kv0[...] + kv1[...].astype(f32) + kv2[...].astype(f32) + kv3[...].astype(f32)
    owner = 2 * flags[2] + flags[1] // 2
    packed[pl.ds(rank_block(flags, owner), ROWS), :] = grads.astype(bf16)
    packed[pl.ds(rank_block(flags, 4), ROWS), :] = dinject_all[:, 0:128]
    packed[pl.ds(rank_block(flags, 5), ROWS), :] = dinject_all[:, 128:256]
    packed[pl.ds(rank_block(flags, 6), ROWS), :] = dreadout_all[:, 0:128]
    packed[pl.ds(rank_block(flags, 7), ROWS), :] = dreadout_all[:, 128:256]
    conv_back(dconv[...], ext, table, small[:, 0:XLOC], work, dxpre, edge, gweight)


def shared_back_kernel(flags, part0, part1, part2, part3, ext, table, small, out, edge, gweight, work):
    grad = part0[...] + part1[...].astype(f32) + part2[...].astype(f32) + part3[...].astype(f32)
    conv_back(grad, ext, table, small[:, XLOC:512], work, out, edge, gweight)
    rank = flags[0]
    of_conv = jnp.where(rank < 4, 0.0, 1.0)
    edge[...] = edge[...] * of_conv
    gweight[...] = gweight[...] * of_conv
    out[...] = jnp.where(rank < 2, turned(grad, table, -1.0), jnp.where(rank < 4, grad, out[...]))


def late_kernel(flags, dxpre, edge_x, dsh, edge_sh, ddt, out):
    for block in range(8):
        own = slice(SHARE * block, SHARE * (block + 1))
        to_rows = pl.ds(local_block(flags, block), SHARE)
        x, sh = dxpre[own, :], dsh[own, :]
        if block == 7:
            pad = jnp.zeros((SHARE - 8, 128), f32)
            sh = sh + jnp.concatenate([pad, edge_sh[...]], axis=0)
            x = x + jnp.concatenate([jnp.zeros((SHARE - 8, XLOC), f32), edge_x[...]], axis=0)
        out[to_rows, 0:XLOC] = x.astype(bf16)
        out[to_rows, XLOC:512] = sh.astype(bf16)
        out[to_rows, 512:LATE] = jnp.where(lane_index((1, 128)) < HLOC, ddt[own, :], 0.0).astype(bf16)


def half_sum_kernel(own, other, keep, send1, send2, send3):
    rows = own.shape[0] // 4
    keep[...] = own[0:rows, :] + other[0:rows, :].astype(f32)
    for index, send in ((1, send1), (2, send2), (3, send3)):
        part = slice(rows * index, rows * (index + 1))
        send[...] = (own[part, :].astype(f32) + other[part, :].astype(f32)).astype(bf16)


def parts_of_sum(own, other, along, sign):
    return parts_from(own, other_core(other), along, sign)


def parts_from(own, got, along, sign):
    rows, width = own.shape[0] // 4, own.shape[1]
    sent = shape_of((rows, width), bf16)
    keep, *sends = run_kernel(half_sum_kernel, [kept((rows, width)), sent, sent, sent], None, own, Columns(got))
    return (keep,) + tuple(along(send, sign * k) for k, send in zip((1, 2, 3), sends))


def split_kernel(*refs):
    lefts, weight, own, other = refs[:-3], refs[-3], refs[-2], refs[-1]
    left = lefts[0][...] if len(lefts) == 1 else jnp.concatenate([ref[...] for ref in lefts], axis=1)
    result = dot_nt(left, weight[...])
    own[...] = result[: ROWS // 2]
    other[...] = result[ROWS // 2 :].astype(bf16)


def summed_rows(lefts, weight):
    model, width = weight.shape
    own, other = pl.pallas_call(
        split_kernel,
        grid=(model // 512,),
        out_shape=(shape_of((ROWS // 2, model)), shape_of((ROWS // 2, model), bf16)),
        in_specs=[pl.BlockSpec(left.shape, lambda i: (0, 0)) for left in lefts]
        + [pl.BlockSpec((512, width), lambda i: (i, 0))],
        out_specs=(
            pl.BlockSpec((ROWS // 2, 512), lambda i: (0, i)),
            pl.BlockSpec((ROWS // 2, 512), lambda i: (0, i)),
        ),
        compiler_params=pltpu.CompilerParams(vmem_limit_bytes=VMEM_LIMIT),
        cost_estimate=pl.CostEstimate(
            flops=2 * ROWS * model * width, bytes_accessed=2 * model * width, transcendentals=0
        ),
    )(*lefts, weight)
    return parts_of_sum(own, other, along_y, 1)


def gate_up_kernel(p0, p1, p2, p3, p4, p5, p6, p7, weight, normed, gate, up, act, act_kept):
    rows = joined((p0, p1, p2, p3, p4, p5, p6, p7))
    normed[...] = rows
    result = dot_nn(rows, weight[...])
    g, u = result[:, :512], result[:, 512:]
    gate[...] = g
    up[...] = u
    for out in (act, act_kept):
        out[...] = (g * sigmoid(g) * u).astype(bf16)


def gate_up_back_kernel(*refs):
    parts, (weight, gate, up, dffn, out) = refs[:-5], refs[-5:]
    rows = joined(parts)
    dffn[...] = rows
    dact = dot_nn(rows, weight[...])
    g = gate[...]
    sig = sigmoid(g)
    out[:, :512] = (dact * up[...] * sig * (1.0 + g * (1.0 - sig))).astype(bf16)
    out[:, 512:] = (dact * g * sig).astype(bf16)


def natural_kernel(flags, p0, p1, p2, p3, p4, p5, p6, p7, out):
    local = joined((p0, p1, p2, p3, p4, p5, p6, p7)).astype(out.dtype)
    for block in range(8):
        out[pl.ds(pl.multiple_of(flags[24 + block] * SHARE, SHARE), SHARE), :] = local[
            SHARE * block : SHARE * (block + 1), :
        ]


def add_norm_kernel(hidden, part0, part1, part2, part3, gain, out_kept, normed, inverse):
    total = hidden[...] + part0[...] + (
        part1[...].astype(f32) + part2[...].astype(f32) + part3[...].astype(f32)
    )
    out_kept[...] = total
    scale = lax.rsqrt(jnp.mean(total * total, axis=1, keepdims=True) + norm_eps)
    inverse[...] = jnp.broadcast_to(scale, inverse.shape)
    normed[...] = (total * scale * gain[...]).astype(bf16)


def add_norm(hidden, parts, gain):
    shape = hidden.shape
    return run_kernel(
        add_norm_kernel,
        [kept(shape), shape_of(shape, bf16), kept((shape[0], 128))],
        None, stored(hidden), *summands(parts), gain[None],
    )


def output_kernel(hidden, part0, part1, part2, part3, out):
    total = hidden[...] + part0[...] + (
        part1[...].astype(f32) + part2[...].astype(f32) + part3[...].astype(f32)
    )
    out[...] = total.astype(bf16)


def norm_back_kernel(grad, part0, part1, part2, part3, hidden, inverse, gain, out, rounded, ggain):
    received = part0[...] + (part1[...].astype(f32) + part2[...].astype(f32) + part3[...].astype(f32))
    scale = inverse[:, 0:1]
    unit = hidden[...] * scale
    scaled = received * gain[...]
    ggain[...] = jnp.sum(received * unit, axis=0, keepdims=True)
    total = grad[...] + scale * (scaled - unit * jnp.mean(scaled * unit, axis=1, keepdims=True))
    out[...] = total
    rounded[...] = total.astype(bf16)


def norm_back(grad, parts, hidden, inverse, gain):
    shape = hidden.shape
    return run_kernel(
        norm_back_kernel,
        [kept(shape), shape_of(shape, bf16), kept((1, shape[1]))],
        None, stored(grad), *summands(parts), stored(hidden), stored(inverse), gain[None],
    )


def gradient_kernel(pairs, *refs):
    out, at = refs[-1], 0
    for index in range(pairs):
        left, right = refs[2 * index], refs[2 * index + 1]
        width = right.shape[1]
        out[:, at : at + width] = dot_tn(left[...], right[...]).astype(bf16)
        at += width
    if at < out.shape[1]:
        out[:, at:] = jnp.zeros((out.shape[0], out.shape[1] - at), bf16)


def weight_gradients(pairs, total, block, index, buffer=None):
    rows, model = pairs[0][0].shape
    width = sum(right.shape[1] for _, right in pairs)
    specs, args = [], []
    for left, right in pairs:
        specs += [
            pl.BlockSpec((rows, 512), lambda i: (0, i)),
            pl.BlockSpec(right.shape, lambda i: (0, 0)),
        ]
        args += [left, right]
    aliases = {}
    kernel = partial(gradient_kernel, len(pairs))
    if buffer is not None:
        aliases = {len(args): 0}
        specs.append(pl.BlockSpec(memory_space=pltpu.HBM))
        args.append(buffer)

        def kernel(*refs):
            gradient_kernel(len(pairs), *refs[:-2], refs[-1])

    return pl.pallas_call(
        kernel,
        grid=(model // 512,),
        out_shape=pltpu.HBM((model, total), bf16),
        in_specs=specs,
        out_specs=pl.BlockSpec((512, block), lambda i: (i, index)),
        input_output_aliases=aliases,
        compiler_params=pltpu.CompilerParams(vmem_limit_bytes=VMEM_LIMIT),
        cost_estimate=pl.CostEstimate(
            flops=2 * rows * model * width, bytes_accessed=model * width * 2, transcendentals=0
        ),
    )(*args)


def owned_kernel(pairs, *refs):
    out, at = refs[-1], 0
    for pair in range(pairs):
        left, right = refs[2 * pair], refs[2 * pair + 1]
        result = dot_tn(left[...], right[...]).astype(bf16)
        width = right.shape[1]
        for index in range(2):
            out[index, :, at : at + width] = result[128 * index : 128 * (index + 1)]
        at += width
    if at < out.shape[2]:
        for index in range(2):
            out[index, :, at:] = refs[2 * pairs][...]


def owned_gradients(pairs, small=None):
    rows, model = pairs[0][0].shape
    width = sum(right.shape[1] for _, right in pairs)
    specs, args = [], []
    for left, right in pairs:
        specs += [pl.BlockSpec((rows, 256), lambda i: (0, i)), pl.BlockSpec(right.shape, lambda i: (0, 0))]
        args += [left, right]
    if small is not None:
        specs.append(pl.BlockSpec(small.shape, lambda i: (0, 0)))
        args.append(small)
        width += small.shape[1]
    return pl.pallas_call(
        partial(owned_kernel, len(pairs)),
        grid=(model // 256,),
        out_shape=pltpu.HBM((16, model // 16, width), bf16),
        in_specs=specs,
        out_specs=pl.BlockSpec((2, model // 16, width), lambda i: (i, 0, 0)),
        compiler_params=pltpu.CompilerParams(vmem_limit_bytes=VMEM_LIMIT),
        cost_estimate=pl.CostEstimate(
            flops=2 * rows * model * width, bytes_accessed=model * width * 2, transcendentals=0
        ),
    )(*args)


def small_kernel(gain1, gain2, conv_sh, conv_x, heads, skip, out):
    out[...] = jnp.zeros(out.shape, bf16)
    for row in range(16):
        own = slice(128 * row, 128 * row + 128)
        out[row : row + 1, :] = gain1[:, own].astype(bf16)
        out[16 + row : 17 + row, :] = gain2[:, own].astype(bf16)
    out[32:37, :] = conv_sh[0:5, :].astype(bf16)
    for tap in range(CONV + 1):
        for pair in range(PAIRS):
            row = 37 + PAIRS * tap + pair
            out[row : row + 1, :] = conv_x[tap : tap + 1, lanes_of(pair)].astype(bf16)
    out[52:54, :] = heads[0:2, :].astype(bf16)
    lanes = lane_index((1, 128))
    sums = jnp.zeros((1, 128), f32)
    for pair in range(PAIRS):
        part = skip[:, lanes_of(pair)]
        for half in range(2):
            mine = (lanes < HP) if half == 0 else (lanes >= HP)
            total = jnp.sum(jnp.where(mine, part, 0.0), axis=1, keepdims=True)
            sums = sums + jnp.where(lanes == 2 * pair + half, total, 0.0)
    out[54:55, :] = sums.astype(bf16)


def owner_sum(values):
    total = values[0].astype(f32)
    for index in range(1, 16):
        total = total + values[index].astype(f32)
    return total


def block_sum_kernel(values, over_tp, late, conv_x, heads):
    whole = owner_sum(values)
    late[...] = whole[:, 0:LATE]
    total = whole[:, LATE : LATE + 128]
    over_tp[0:128, :] = whole[:, XLOC:512].astype(bf16)
    over_tp[128:224, :] = jnp.zeros((96, 128), bf16)
    for layer in range(2):
        first = 64 * layer
        over_tp[128 + 48 * layer : 165 + 48 * layer, :] = total[first : first + 37, :].astype(bf16)
        for tap in range(CONV + 1):
            for pair in range(PAIRS):
                row = first + 37 + PAIRS * tap + pair
                conv_x[5 * layer + tap : 5 * layer + tap + 1, lanes_of(pair)] = total[row : row + 1, :]
        heads[3 * layer : 3 * layer + 3, :] = total[first + 52 : first + 55, :]


def early_outputs_kernel(lower, upper, attn, ssm, gate, up, down, query, z):
    for layer, ref in ((0, lower), (1, upper)):
        for index, out in enumerate((gate, up, down)):
            out[layer] = ref[:, 512 * index : 512 * (index + 1)].astype(f32)
        attn[layer] = ref[:, 1536:1664].astype(f32)
        ssm[layer] = ref[:, 1664:2048].astype(f32)
        z[layer] = ref[:, 2048:2432].astype(f32)
        query[layer] = ref[:, 2432:2560].astype(f32)


def last_outputs_kernel(flags, *refs):
    parts, other, (late, upper_late, z) = refs[:8], refs[8:16], refs[16:19]
    zx, dt, shared, gains1, gains2, conv_bc, every = refs[19:]
    zx[0, :, 0, :] = z[0]
    zx[1, :, 0, :] = z[1]
    zx[0, :, 1, :] = late[:, 0:XLOC]
    zx[1, :, 1, :] = upper_late[:, 0:XLOC].astype(f32)
    dt[0] = late[:, 512 : 512 + HLOC]
    dt[1] = upper_late[:, 512 : 512 + HLOC].astype(f32)
    total = jnp.zeros((96, 128), f32)
    for index, part in enumerate(parts):
        every[index] = part[...].astype(f32)
        total = total + part[128:224, :].astype(f32)
    for index, part in enumerate(other):
        every[8 + index, 0:128, :] = part[...].astype(f32)
    for rank in range(8):
        own = slice(128 * rank, 128 * rank + 128)
        shared[0, :, own] = every[flags[16 + rank], 0:128, :]
        shared[1, :, own] = every[8 + flags[16 + rank], 0:128, :]
    for layer in range(2):
        for row in range(16):
            own = slice(128 * row, 128 * row + 128)
            at = 48 * layer + row
            gains1[layer : layer + 1, own] = total[at : at + 1, :]
            gains2[layer : layer + 1, own] = total[at + 16 : at + 17, :]
        for rank in range(4):
            part = every[flags[20 + rank], 160 + 48 * layer : 168 + 48 * layer, :]
            conv_bc[5 * layer : 5 * layer + 5, 128 * rank : 128 * rank + 128] = part[0:5, :]


def body(
    inputs, cotangent, segment_ids, w_query, w_shared, w_zx, w_dt, w_attn_out, w_ssm_out, w_gate, w_up, w_down,
    gains, conv_x, conv_bc, head_params,
):
    layers = w_query.shape[0]
    rank, ctx = lax.axis_index("tp"), lax.axis_index("ctx")
    y, core = rank // 2, rank % 2
    model = inputs.shape[2]

    def local_of(block_y, block_core):
        return jnp.where(block_core == core, 0, 4) + (block_y - y) % 4

    seg_all = segment_ids[0]
    first_row = ctx * ROWS
    padded = jnp.concatenate([jnp.full((CONV - 1,), -1, i32), seg_all])
    seg_ext = lax.dynamic_slice_in_dim(padded, first_row, ROWS + CONV - 1)
    seg_own = seg_ext[CONV - 1 :]
    blocks = seg_all.reshape(SEQ_BLOCKS, ROWS)
    seg_rows = jnp.stack(
        [
            jnp.where(ctx >= back, lax.dynamic_index_in_dim(blocks, jnp.maximum(ctx - back, 0), 0, False), -1)
            for back in range(SEQ_BLOCKS)
        ]
        + [jnp.full((ROWS,), -1, i32)] * 4
    ).astype(f32)
    naturals = jnp.arange(8, dtype=i32)
    flags = jnp.concatenate(
        [
            jnp.stack([rank, y, core, ctx, seg_ext[CONV - 2], seg_own[-1], rank, rank]).astype(i32),
            local_of(naturals % 4, naturals // 4).astype(i32),
            local_of(naturals // 2, naturals % 2).astype(i32),
            (jnp.where(naturals < 4, core, 1 - core) * 4 + (y + naturals) % 4).astype(i32),
        ]
    )

    half_width = HD // 2
    frequency = rope_base ** (-jnp.arange(half_width, dtype=f32) / half_width)
    places = (first_row + jnp.arange(ROWS, dtype=i32)).astype(f32)
    angles = places[:, None] * frequency[None, :]
    cosine, sine = jnp.cos(angles), jnp.sin(angles)
    marks = [seg_ext[tap : tap + ROWS] == seg_own for tap in range(CONV - 1)]
    marks += [seg_own, seg_own == seg_ext[CONV - 2], seg_own == seg_own[-1]]
    marks = jnp.pad(jnp.stack([mark.astype(f32) for mark in marks], axis=1), ((0, 0), (0, 122)))
    table = jnp.concatenate([cosine, cosine, -sine, sine, marks], axis=1)

    own_conv = jnp.maximum(rank - 4, 0) * 128
    small = []
    for layer in range(layers):
        rows = [conv_x[layer], lax.dynamic_slice_in_dim(conv_bc[layer], own_conv, 128, 1)]
        rows.append(jnp.pad(head_params[layer], ((0, 2), (0, 128 - HLOC))))
        small.append(jnp.pad(jnp.concatenate(rows, axis=1), ((0, 3), (0, 0))))

    def packed(*members):
        width = sum(
            {4: 2 * XLOC}.get(member.ndim, 128 if member.shape[2] in (1024, HLOC) else member.shape[2])
            for member, _ in members
        )
        (columns,) = run_kernel(
            pack_kernel,
            [shape_of((w_query.shape[1], width), bf16)],
            rank.astype(i32).reshape(1),
            *(Layer(member, layer) for member, layer in members),
        )
        return lax.all_gather(columns, ("fsdp", "ctx"), axis=0, tiled=True)

    def proj_members(layer):
        return [(member, layer) for member in (w_zx, w_query, w_shared, w_dt)]

    weight_a = packed(*proj_members(0), (w_attn_out, 0), (w_ssm_out, 0))
    weight_b = packed(*proj_members(1), (w_gate, 0), (w_up, 0), (w_down, 0))
    weight_c = packed((w_gate, 1), (w_up, 1), (w_down, 1), (w_attn_out, 1), (w_ssm_out, 1))
    proj_place = [(weight_a, 0, PROJ), (weight_b, 0, PROJ)]
    out_place = [(weight_a, PROJ, 512), (weight_c, 1536, 512)]
    gate_up_place = [(weight_b, PROJ, 1024), (weight_c, 0, 1024)]
    down_place = [(weight_b, PROJ + 1024, 512), (weight_c, 1024, 512)]

    def together(*values):
        return lax.optimization_barrier(values)

    weight_a, table, seg_rows, small = together(weight_a, table, seg_rows, small)
    normed_shape = shape_of((ROWS, model), bf16)
    normed_kept = kept((ROWS, model), bf16)
    normed_b, inverse1, hidden, dffn_b, grad_hidden = run_kernel(
        first_kernel,
        [normed_shape, kept((SHARE, 128)), kept((SHARE, model)), normed_kept, kept((SHARE, model))],
        flags, inputs, cotangent, gains[0],
    )
    weight_a, normed_b = together(weight_a, normed_b)
    proj_place[0] = (weight_a, 0, PROJ)
    out_place[0] = (weight_a, PROJ, 512)
    normed_parts, dffn_parts = (normed_b,), (dffn_b,)
    saved = []
    wide = shape_of((ROWS, 512))
    proj_weight = fetched("proj_0", *proj_place[0])
    for layer in range(layers):
        normed_b, z, z_kept, xs, query, query_kept, dtn, dtn_kept = run_kernel(
            proj_kernel,
            [
                normed_kept, shape_of((ROWS, XLOC)), kept((ROWS, XLOC)), wide, shape_of((ROWS, HD), bf16),
                kept((ROWS, HD), bf16), shape_of((ROWS, 128)), kept((ROWS, 128)),
            ],
            flags, *(passed(normed_parts) if layer > 0 else normed_parts), proj_weight, table,
            scratch=[pltpu.VMEM((ROWS, PROJ), f32)],
        )
        halo = along_ctx(xs[ROWS - 8 :], 1)
        shared_own, shared_ext = run_kernel(
            shared_kernel,
            [shape_of((ROWS, 128), bf16), kept((264, 128))],
            flags, xs, Columns(halo), table, small[layer],
        )
        shared_parts = from_all(shared_own)
        x_ext, xc, xc_kept, rates, rates_kept, rates_t, rates_t_kept = run_kernel(
            prep_kernel,
            [
                kept((264, XLOC)), shape_of((ROWS, XLOC)), kept((ROWS, XLOC)), shape_of((ROWS, 256)),
                kept((ROWS, 256)), shape_of((16, ROWS)), kept((16, ROWS)),
            ],
            None, xs, dtn, Columns(halo), table, small[layer],
        )
        message, shared, shared_kept = run_kernel(
            state_kernel,
            [shape_of((KV + MSG, NSTATE), bf16), shape_of((8 * ROWS, 128), bf16), kept((8 * ROWS, 128), bf16)],
            flags, *passed(shared_parts), xc, rates, rates_t, table,
        )
        earlier = tuple(along_ctx(message, back) for back in (1, 2, 3))
        (intra,) = run_kernel(
            intra_kernel, [shape_of((ROWS, XLOC))],
            flags, shared, xc, rates, rates_t, table, seg_rows, small[layer],
        )
        earlier, intra = together(earlier, intra)
        halves = [Columns(part, 0, NSTATE, rows=KV) for part in earlier]
        (swapped,) = run_kernel(halves_kernel, [shape_of((3 * KV, NSTATE), bf16)], None, *halves)
        swapped, out_weight = together(other_core(swapped), fetched(f"out_{layer}", *out_place[layer]))
        attn, log_total, pairs = run_kernel(
            attention_kernel,
            [shape_of((ROWS, HD), bf16), kept((ROWS, HD)), kept((SEQ_BLOCKS * ROWS, 2 * HD), bf16)],
            flags, query, shared, *halves, Columns(swapped), table, seg_rows,
        )
        state, ssm_y, cat, cat_kept = run_kernel(
            carry_kernel,
            [kept((XLOC, NSTATE)), kept((ROWS, XLOC)), shape_of((ROWS, 512), bf16), kept((ROWS, 512), bf16)],
            flags, *passed(earlier), shared, rates, table, intra, z, attn,
        )
        parts = summed_rows([cat], out_weight)
        if layer > 0:
            parts, gate_up_weight = together(parts, fetched(f"gate_up_{layer}", *gate_up_place[layer]))
        hidden1, normed2, inverse2 = add_norm(hidden, parts, gains[layer, 1])
        if layer > 0:
            normed_parts, down_weight = from_all(normed2, fetched("down_1", *down_place[layer]))
        else:
            normed_parts = from_all(normed2)
            gate_up_weight, down_weight = fetched_all("ffn_0", [gate_up_place[layer], down_place[layer]])
        wide_kept = kept((ROWS, 512))
        normed2_b, gate, up, act_b, act_kept = run_kernel(
            gate_up_kernel, [normed_kept, wide_kept, wide_kept, shape_of((ROWS, 512), bf16), kept((ROWS, 512), bf16)],
            None, *passed(normed_parts), gate_up_weight,
        )
        saved.append(
            (
                hidden, normed_b, inverse1, shared_ext, shared_kept, query_kept, x_ext, xc_kept, z_kept, dtn_kept,
                rates_kept, rates_t_kept, pairs, log_total, state, ssm_y, cat_kept, hidden1, inverse2, normed2_b,
                gate, up, act_kept,
            )
        )
        if layer + 1 < layers:
            hidden, next_normed, inverse1 = add_norm(
                hidden1, summed_rows([act_b], down_weight), gains[layer + 1, 0]
            )
            normed_parts, proj_weight = from_all(next_normed, fetched("proj_1", *proj_place[layer + 1]))

    weight_sums = [None] * layers
    small_parts = [None] * layers
    inner = None
    for layer in reversed(range(layers)):
        (
            hidden, normed_b, inverse1, shared_ext, shared, query, x_ext, xc, z, dtn, rates, rates_t,
            pairs, log_total, state, ssm_y, cat, hidden1, inverse2, normed2_b, gate, up, act_b,
        ) = saved[layer]
        last = layer == 0
        dffn_b, dgate_up = run_kernel(
            gate_up_back_kernel, [normed_kept, shape_of((ROWS, 1024), bf16)],
            None, *passed(dffn_parts), down_weight, stored(gate), stored(up),
        )
        parts = summed_rows([dgate_up], gate_up_weight)
        outer = weight_gradients([(normed2_b, dgate_up), (dffn_b, act_b)], 3200 if last else 2560, 1536, 0, inner)
        parts, outer = lax.optimization_barrier((parts, outer))
        grad_mid, dmix, ggain2 = norm_back(grad_hidden, parts, hidden1, inverse2, gains[layer, 1])
        dmix_parts = from_all(dmix)
        dmix_parts, fetch = from_all(
            dmix,
            fetched_all(
                f"mixer_{layer}",
                [out_place[layer]]
                + [(array, 0, array.shape[1]) for array in (z, ssm_y, shared, rates, rates_t, xc, query, pairs, state)],
            ),
        )
        out_weight, z, ssm_y, shared, rates, rates_t, xc, query, pairs, state = fetch
        dmix_b, dattn, dy, dz, message = run_kernel(
            gate_back_kernel,
            [
                normed_kept, shape_of((ROWS, HD), bf16), shape_of((ROWS, XLOC)), shape_of((ROWS, XLOC), bf16),
                shape_of((MSG, NSTATE), bf16),
            ],
            flags, *passed(dmix_parts), out_weight, z, ssm_y, shared, rates, rates_t, table,
            scratch=[pltpu.VMEM((ROWS, XLOC), f32), pltpu.VMEM((ROWS, 512), f32)],
        )
        after = tuple(along_ctx(message, -ahead) for ahead in (1, 2, 3))
        early, mine, theirs = run_kernel(
            attention_back_kernel,
            [kept((ROWS, 512), bf16), shape_of((4 * ROWS, HD)), shape_of((4 * ROWS, HD), bf16)],
            flags, dattn, dz, query, pairs, stored(log_total), table, seg_rows,
        )
        got = other_core(theirs)
        dx, dshared, drates, dskip = run_kernel(
            intra_back_kernel,
            [kept((ROWS, XLOC)), kept((ROWS, 2 * NSTATE)), kept((ROWS, 256)), kept((1, XLOC))],
            flags, dy, xc, shared, rates, rates_t, table, seg_rows, state, small[layer],
            scratch=[pltpu.VMEM((128, ROWS), f32), pltpu.VMEM((ROWS, 128), f32)],
        )
        got, dx = lax.optimization_barrier((got, dx))
        dkv = parts_from(mine, got, along_ctx, -1)
        outer = weight_gradients([(dmix_b, cat)], outer.shape[1], 512, 3, outer)
        outer = weight_gradients([(normed_b, early)], outer.shape[1], 512, 4, outer)
        if last:
            after, dkv, outer, weight_sums[1] = together(after, dkv, outer, weight_sums[1])
        else:
            after, dkv, outer = together(after, dkv, outer)
        weight_sums[layer] = lax.psum_scatter(outer, ("fsdp", "ctx"), scatter_dimension=0, tiled=True)
        packed_grads, dxpre, edge_x, gconv_x, ddt, gheads = run_kernel(
            state_back_kernel,
            [
                shape_of((8 * ROWS, 128), bf16), kept((ROWS, XLOC)), shape_of((8, XLOC)), kept((8, XLOC)),
                kept((ROWS, 128)), kept((8, 128)),
            ],
            flags, *passed(after), shared, xc, rates, rates_t, table, state, small[layer], stored(dtn), stored(dx), stored(dshared), stored(drates), *summands(dkv), stored(x_ext),
            scratch=[pltpu.VMEM((272, XLOC), f32), pltpu.VMEM((ROWS, XLOC), f32), pltpu.VMEM((ROWS, 128), f32)],
        )
        edge_x = along_ctx(edge_x, -1)
        dshared_parts = parts_of_sum(packed_grads[: 4 * ROWS], packed_grads[4 * ROWS :], along_y, 1)
        dsh, edge_sh, gconv_sh = run_kernel(
            shared_back_kernel,
            [shape_of((ROWS, 128)), shape_of((8, 128)), kept((8, 128))],
            flags, *summands(dshared_parts), stored(shared_ext), table, small[layer],
            scratch=[pltpu.VMEM((272, 128), f32)],
        )
        edge_sh, proj_weight = together(
            along_ctx(edge_sh, -1), fetched(f"proj_again_{layer}", *proj_place[layer])
        )
        (late,) = run_kernel(
            late_kernel, [shape_of((ROWS, LATE), bf16)], flags, stored(dxpre), Columns(edge_x), dsh,
            Columns(edge_sh), stored(ddt),
        )
        parts = summed_rows([early, late], proj_weight)
        if not last:
            inner = weight_gradients([(normed_b, late)], 3200, LATE, 4)
            parts, inner = together(parts, inner)
        grad_hidden, rounded, ggain1 = norm_back(grad_mid, parts, hidden, inverse1, gains[layer, 0])
        if last:
            dffn_parts = from_all(rounded)
        else:
            dffn_parts, (down_weight, gate_up_weight) = from_all(
                rounded, fetched_all("ffn_again", [down_place[layer - 1], gate_up_place[layer - 1]])
            )
            last_hidden1, last_act = hidden1, act_b
        (small_parts[layer],) = run_kernel(
            small_kernel, [shape_of((64, 128), bf16)],
            None, *map(stored, (ggain1, ggain2, gconv_sh, gconv_x, gheads, dskip)),
        )
    small_all = jnp.concatenate(small_parts, axis=0)
    owned = owned_gradients([(normed_b, late)], small_all)
    owned = lax.all_to_all(owned, ("fsdp", "ctx"), 0, 0, tiled=True)
    (input_grad,) = run_kernel(natural_kernel, [kept((ROWS, model))], flags, *passed(dffn_parts))
    last_act, down_weight, _ = together(last_act, fetched("down_last", *down_place[1]), small_parts[0])
    (layer_out,) = run_kernel(
        output_kernel, [shape_of((SHARE, model), bf16)], None,
        stored(last_hidden1), *summands(summed_rows([last_act], down_weight)),
    )
    (layer_out,) = run_kernel(natural_kernel, [normed_kept], flags, *passed(from_all(layer_out)))
    lower, upper = weight_sums

    def pair_of(width):
        return shape_of((layers, model // 16, width))

    owned, layer_out, input_grad = together(owned, layer_out, input_grad)
    over_tp, late_sum, gconv_x, gheads = run_kernel(
        block_sum_kernel,
        [
            shape_of((224, 128), bf16), shape_of((model // 16, LATE)), shape_of((layers * (CONV + 1), XLOC)),
            shape_of((8, 128)),
        ],
        None, Columns(owned),
    )
    over_tp = from_all(over_tp)
    lower, over_tp = together(lower, over_tp)
    upper_late = lower[:, 2560:3200]
    upper_shared = from_all(upper_late[:, XLOC:512])
    grad_attn, grad_ssm, grad_gate, grad_up, grad_down, grad_query, grad_z = run_kernel(
        early_outputs_kernel,
        [
            *(kept((layers, model // 16, width)) for width in (128, 384, 512, 512, 512, 128)),
            pair_of(XLOC),
        ],
        None, Columns(lower), Columns(upper),
    )
    grad_zx, grad_dt, grad_shared, ggains1, ggains2, gconv_bc = run_kernel(
        last_outputs_kernel,
        [
            shape_of((layers, model // 16, 2, XLOC)), pair_of(HLOC), pair_of(1024), shape_of((layers, model)),
            shape_of((layers, model)), shape_of((layers * (CONV + 1), 512)),
        ],
        flags, *passed(over_tp), *passed(upper_shared), late_sum, Columns(upper_late), grad_z,
        scratch=[pltpu.VMEM((16, 224, 128), f32)],
    )
    gconv_x = gconv_x.reshape(layers, CONV + 1, XLOC)
    gconv_bc = gconv_bc.reshape(layers, CONV + 1, 512)
    gheads = gheads[: 3 * layers].reshape(layers, 3, 128)[:, :, :HLOC]
    return (
        layer_out[None],
        input_grad[None],
        grad_query,
        grad_shared,
        grad_zx,
        grad_dt,
        grad_attn,
        grad_ssm,
        grad_gate,
        grad_up,
        grad_down,
        ggains1,
        gconv_x,
        gconv_bc,
        gheads[:, :2],
        ggains2,
        gheads[:, 2],
    )


def solution(mesh):
    columns = P(None, ("fsdp", "ctx"), "tp")
    rows = P("fsdp", "ctx", None)
    return jax.shard_map(
        body,
        mesh=mesh,
        in_specs=(
            rows, rows, P("fsdp", None), columns, P(None, ("fsdp", "ctx"), None),
            P(None, ("fsdp", "ctx"), None, "tp"), columns, columns, columns, columns, columns, columns,
            P(), P(None, None, "tp"), P(), P(None, None, "tp"),
        ),
        out_specs=(
            rows, rows, columns, P(None, ("fsdp", "ctx"), None), P(None, ("fsdp", "ctx"), None, "tp"),
            columns, columns, columns, columns, columns, columns,
            P(), P(None, None, "tp"), P(), P(None, None, "tp"), P(), P(None, "tp"),
        ),
        check_vma=False,
    )
```

```python
import math
from functools import partial

import jax
import jax.numpy as jnp
from jax import lax
from jax.experimental import pallas as pl
from jax.experimental.pallas import tpu as pltpu
from jax.sharding import PartitionSpec as P

HD = 128
HP = 64
NSTATE = 256
CONV = 4
ROWS = 256
SHARE = 32
XLOC = 384
PROJ = 1152
LATE = 640
HLOC = 6
PAIRS = 3
SEQ_BLOCKS = 4
MSG = XLOC + 16
KV = 128
VMEM_LIMIT = 16 * 1024 * 1024

norm_eps = 1e-05
rope_base = 100000000000.0
bf16 = jnp.bfloat16
f32 = jnp.float32
i32 = jnp.int32


def along_y(value, steps):
    pairs = [(i, ((i // 2 + steps) % 4) * 2 + i % 2) for i in range(8)]
    return lax.ppermute(value, "tp", pairs)


def other_core(value):
    return lax.ppermute(value, "tp", [(i, i ^ 1) for i in range(8)])


def along_ctx(value, steps):
    first, last = max(0, -steps), min(4, 4 - steps)
    return lax.ppermute(value, "ctx", [(i, i + steps) for i in range(first, last)])


def ring(value, axis, steps):
    return lax.ppermute(value, axis, [(i, (i + steps) % 4) for i in range(4)])


def from_all(value, beside=None):
    half = [value] + [along_y(value, -k) for k in (1, 2, 3)]
    if beside is not None:
        half[1], beside = lax.optimization_barrier((half[1], beside))
    parts = tuple(half + [other_core(part) for part in half])
    return parts if beside is None else (parts, beside)


def dot_nn(a, b):
    return jnp.dot(a, b, preferred_element_type=f32)


def dot_nt(a, b):
    return lax.dot_general(a, b, (((1,), (1,)), ((), ())), preferred_element_type=f32)


def dot_tn(a, b):
    return lax.dot_general(a, b, (((0,), (0,)), ((), ())), preferred_element_type=f32)


def shape_of(shape, dtype=f32):
    return jax.ShapeDtypeStruct(shape, dtype)


class Columns:
    def __init__(self, array, block=0, width=None, rows=None, keep=False):
        self.array, self.block, self.keep = array, block, keep
        self.shape = (rows or array.shape[0],) + array.shape[1:-1] + (width or array.shape[-1],)

    def spec(self):
        place = (0,) * (len(self.shape) - 1) + (self.block,)
        return pl.BlockSpec(self.shape, lambda i: place, pipeline_mode=pl.Buffered(1))


class Layer:
    def __init__(self, array, layer):
        self.array, self.layer, self.keep = array, layer, True
        self.shape = (1,) + array.shape[1:]

    def spec(self):
        place = (self.layer,) + (0,) * (len(self.shape) - 1)
        return pl.BlockSpec(self.shape, lambda i: place, pipeline_mode=pl.Buffered(1))


def stored(array):
    return Columns(array, keep=True)


def summands(parts):
    return [stored(parts[0])] + passed(parts[1:])


def passed(arrays):
    return [Columns(array) for array in arrays]


def kept(shape, dtype=f32):
    return pltpu.HBM(shape, dtype)


def fetch_kernel(places, *refs):
    count = len(places)
    sources, outs, sems = refs[:count], refs[count : 2 * count], refs[-1]
    copies = []
    for (start, pieces), source, out in zip(places, sources, outs):
        rows, width = out.shape[0] // pieces, out.shape[1]
        for index in range(pieces):
            own = pl.ds(rows * index, rows)
            copies.append(
                pltpu.make_async_copy(
                    source.at[own, pl.ds(start, width)], out.at[own, :], sems.at[len(copies)]
                )
            )
    for copy in copies:
        copy.start()
    for copy in copies:
        copy.wait()


def fetched_all(name, sources):
    places = [(start, 4 if array.shape[0] == 2048 and width > 128 else 1) for array, start, width in sources]
    whole = pl.BlockSpec(memory_space=pltpu.VMEM)
    return pl.pallas_call(
        partial(fetch_kernel, places),
        name=name,
        out_shape=tuple(pltpu.VMEM((array.shape[0], width), array.dtype) for array, _, width in sources),
        in_specs=[pl.BlockSpec(memory_space=pltpu.HBM)] * len(sources),
        out_specs=tuple(whole for _ in sources),
        scratch_shapes=[pltpu.SemaphoreType.DMA((sum(pieces for _, pieces in places),))],
        compiler_params=pltpu.CompilerParams(vmem_limit_bytes=VMEM_LIMIT),
        cost_estimate=pl.CostEstimate(
            flops=0, bytes_accessed=sum(2 * array.shape[0] * width for array, _, width in sources), transcendentals=0
        ),
    )(*(pltpu.with_memory_space_constraint(array, pltpu.HBM) for array, _, _ in sources))


def fetched(name, array, start, width):
    return fetched_all(name, [(array, start, width)])[0]


def restored(name, arrays):
    return fetched_all(name, [(array, 0, array.shape[1]) for array in arrays])


def run_kernel(kernel, outs, flags, *args, scratch=(), flops=50_000_000):
    whole = pl.BlockSpec(memory_space=pltpu.VMEM)
    own = [isinstance(arg, (Columns, Layer)) for arg in args]
    specs, arrays, out_specs = [], [], []
    for arg, copied in zip(args, own):
        specs.append(arg.spec() if copied else whole)
        array = arg.array if copied else arg
        arrays.append(pltpu.with_memory_space_constraint(array, pltpu.HBM) if copied and arg.keep else array)
    for out in outs:
        in_vmem = isinstance(out, jax.ShapeDtypeStruct)
        out_specs.append(whole if in_vmem else pl.BlockSpec(out.shape, lambda i, n=len(out.shape): (0,) * n))
        own.append(not in_vmem)
    moved = sum(2 * math.prod(arg.shape) for arg in args) + sum(2 * math.prod(o.shape) for o in outs)
    if flags is not None:
        specs = [pl.BlockSpec(memory_space=pltpu.SMEM)] + specs
        arrays = [flags] + arrays
    return pl.pallas_call(
        kernel,
        grid=(1,) if any(own) else (),
        out_shape=tuple(outs),
        in_specs=specs,
        out_specs=tuple(out_specs),
        scratch_shapes=list(scratch),
        compiler_params=pltpu.CompilerParams(vmem_limit_bytes=VMEM_LIMIT),
        cost_estimate=pl.CostEstimate(flops=flops, bytes_accessed=moved, transcendentals=0),
    )(*arrays)


def local_block(flags, natural):
    return pl.multiple_of(flags[8 + natural] * SHARE, SHARE)


def rank_block(flags, rank):
    return pl.multiple_of(flags[16 + rank] * ROWS, ROWS)


def lane_index(shape):
    return lax.broadcasted_iota(i32, shape, len(shape) - 1)


def spread(columns, pair):
    low = lane_index((1, 128)) < HP
    return jnp.where(low, columns[:, 2 * pair : 2 * pair + 1], columns[:, 2 * pair + 1 : 2 * pair + 2])


def lanes_of(pair):
    return slice(128 * pair, 128 * pair + 128)


def turned(value, table, sign):
    return value * table[:, 0:128] + sign * (pltpu.roll(value, 64, 1) * table[:, 128:256])


def segments(table):
    return table[:, 259:260]


def sigmoid(v):
    return 1.0 / (1.0 + jnp.exp(-v))


def softplus(v):
    return jnp.maximum(v, 0.0) + jnp.log1p(jnp.exp(-jnp.abs(v)))


def conv_sum(ext, table, weight):
    total = weight[CONV : CONV + 1, :] + ext[8 : 8 + ROWS, :] * weight[3:4, :]
    for tap in range(CONV - 1):
        total = total + table[:, 256 + tap : 257 + tap] * ext[5 + tap : 5 + tap + ROWS, :] * weight[tap : tap + 1, :]
    return total


def conv_back(grad_out, ext, table, weight, work, grad_ref, edge_ref, gweight_ref):
    total = conv_sum(ext, table, weight)
    sig = sigmoid(total)
    grad = grad_out * sig * (1.0 + total * (1.0 - sig))
    width = grad.shape[1]
    gweight_ref[...] = jnp.zeros((8, width), f32)
    gweight_ref[CONV : CONV + 1, :] = jnp.sum(grad, axis=0, keepdims=True)
    gweight_ref[3:4, :] = jnp.sum(grad * ext[8 : 8 + ROWS, :], axis=0, keepdims=True)
    work[0:8, :] = jnp.zeros((8, width), f32)
    work[264:272, :] = jnp.zeros((8, width), f32)
    own = grad * weight[3:4, :]
    edge = jnp.zeros((8, width), f32)
    for tap in range(CONV - 1):
        part = grad * table[:, 256 + tap : 257 + tap]
        gweight_ref[tap : tap + 1, :] = jnp.sum(
            part * ext[5 + tap : 5 + tap + ROWS, :], axis=0, keepdims=True
        )
        work[8:264, :] = part * weight[tap : tap + 1, :]
        own = own + work[11 - tap : 11 - tap + ROWS, :]
        edge = edge + work[3 - tap : 11 - tap, :]
    grad_ref[...] = own
    edge_ref[...] = edge


def pack_kernel(place, *refs):
    out, at, index = refs[-1], 0, 0
    while index < len(refs) - 1:
        ref = refs[index]
        if len(ref.shape) == 4:
            out[:, at : at + XLOC] = ref[0, :, 0, :]
            out[:, at + XLOC : at + 512] = refs[index + 1][0]
            out[:, at + 512 : at + 896] = ref[0, :, 1, :]
            at, index = at + 896, index + 2
            continue
        width = min(ref.shape[2], 512)
        if width == HLOC:
            out[:, at : at + 128] = jnp.zeros((out.shape[0], 128), bf16)
            out[:, at : at + HLOC] = ref[0]
            width = 128
        elif ref.shape[2] == 1024:
            width = 128
            out[:, at : at + width] = ref[0, :, pl.ds(pl.multiple_of(place[0] * 128, 128), 128)]
        else:
            out[:, at : at + width] = ref[0]
        at, index = at + width, index + 1


def first_kernel(flags, rows, cotangent, gain, normed, inverse, hidden_kept, grads, grad):
    for block in range(8):
        own = slice(SHARE * block, SHARE * (block + 1))
        from_rows = pl.ds(pl.multiple_of(flags[24 + block] * SHARE, SHARE), SHARE)
        wide = rows[0, from_rows, :].astype(f32)
        scale = lax.rsqrt(jnp.mean(wide * wide, axis=1, keepdims=True) + norm_eps)
        normed[own, :] = (wide * scale * gain[0:1, :]).astype(bf16)
        grads[own, :] = cotangent[0, from_rows, :]
        if block == 0:
            hidden_kept[...] = wide
            inverse[...] = jnp.broadcast_to(scale, inverse.shape)
            grad[...] = cotangent[0, from_rows, :].astype(f32)


def joined(parts):
    return parts[0][...] if len(parts) == 1 else jnp.concatenate([part[...] for part in parts], axis=0)


def proj_kernel(flags, *refs):
    parts, (weight, table, normed, z, z_kept, xs, query, query_kept, dtn, dtn_kept, work) = refs[:-11], refs[-11:]
    rows = joined(parts)
    normed[...] = rows
    work[...] = dot_nn(rows, weight[...])
    for block in range(8):
        own = slice(SHARE * block, SHARE * (block + 1))
        from_rows = pl.ds(local_block(flags, block), SHARE)
        for out in (z, z_kept):
            out[own, :] = work[from_rows, 0:XLOC]
        xs[own, :] = work[from_rows, 512:1024]
        head = turned(work[from_rows, XLOC:512], table[own, :], 1.0).astype(bf16)
        for out in (query, query_kept):
            out[own, :] = head
        for out in (dtn, dtn_kept):
            out[own, :] = work[from_rows, 1024:PROJ]


def shared_kernel(flags, xs, halo, table, small, out, ext):
    own = xs[:, XLOC:512]
    ext[0:8, :] = halo[:, XLOC:512]
    ext[8 : 8 + ROWS, :] = own
    total = conv_sum(ext, table, small[:, XLOC:512])
    rank = flags[0]
    out[...] = jnp.where(
        rank < 2, turned(own, table, 1.0), jnp.where(rank < 4, own, total * sigmoid(total))
    ).astype(bf16)


def prep_kernel(xs, dtn, halo, table, small, ext, xc, xc_kept, rates, rates_kept, rates_t, rates_t_kept):
    ext[0:8, :] = halo[:, 0:XLOC]
    ext[8 : 8 + ROWS, :] = xs[:, 0:XLOC]
    total = conv_sum(ext, table, small[:, 0:XLOC])
    for out in (xc, xc_kept):
        out[...] = total * sigmoid(total)
    params = small[:, 512:640]
    rate = softplus(dtn[...] + params[1:2, :])
    logs = -jnp.exp(params[0:1, :]) * rate
    rows = lax.broadcasted_iota(i32, (ROWS, ROWS), 0)
    lower = (rows >= lane_index((ROWS, ROWS))).astype(f32)
    running = jnp.dot(lower, logs, precision=lax.Precision.HIGHEST, preferred_element_type=f32)
    for out in (rates, rates_kept):
        out[:, 0:128] = rate
        out[:, 128:256] = running
    rate_t, running_t = rate.T[0:8, :], running.T[0:8, :]
    for out in (rates_t, rates_t_kept):
        out[0:8, :] = rate_t
        out[8:16, :] = running_t


def block_decays(flags, rates_t):
    kept = jnp.where(flags[4] == flags[5], 1.0, 0.0)
    return jnp.exp(rates_t[8:16, ROWS - 1 : ROWS]) * kept


def decay_rows(flags, rates_t):
    rows = jnp.broadcast_to(block_decays(flags, rates_t), (8, NSTATE))
    return jnp.concatenate([rows, jnp.zeros((8, NSTATE), f32)], axis=0).astype(bf16)


def weights_in(rates, table):
    last = rates[ROWS - 1 : ROWS, 128:256]
    gap = jnp.exp(last - rates[:, 128:256]) * table[:, 261:262]
    return gap, gap * rates[:, 0:128]


def rank_columns(flags, shared, first):
    return jnp.concatenate(
        [shared[pl.ds(rank_block(flags, rank), ROWS), :] for rank in (first, first + 1)], axis=1
    )


def inject_of(flags, shared):
    return rank_columns(flags, shared, 4)


def readout_of(flags, shared):
    return rank_columns(flags, shared, 6)


def carry_of(rates, table):
    return jnp.exp(rates[:, 128:256]) * table[:, 260:261]


def state_kernel(flags, s0, s1, s2, s3, s4, s5, s6, s7, xc, rates, rates_t, table, out, shared, shared_kept):
    for index, part in enumerate((s0, s1, s2, s3, s4, s5, s6, s7)):
        shared[ROWS * index : ROWS * (index + 1), :] = part[...]
        shared_kept[ROWS * index : ROWS * (index + 1), :] = part[...]
    inject = inject_of(flags, shared)
    _, weight = weights_in(rates, table)
    for pair in range(PAIRS):
        weighted = (xc[:, lanes_of(pair)] * spread(weight, pair)).astype(bf16)
        out[KV + 128 * pair : KV + 128 * (pair + 1), :] = dot_tn(weighted, inject).astype(bf16)
    out[KV + XLOC : KV + MSG, :] = decay_rows(flags, rates_t)
    half = shared[pl.ds(rank_block(flags, 2 * flags[2] + flags[1] // 2), ROWS), :]
    out[0:KV, :] = jnp.concatenate([half[0:128], half[128:256]], axis=1)


def halves_kernel(msg1, msg2, msg3, out):
    for index, msg in enumerate((msg1, msg2, msg3)):
        out[KV * index : KV * (index + 1), :] = msg[...]


def allowed_pairs(table, seg_rows):
    rows = lax.broadcasted_iota(i32, (ROWS, ROWS), 0)
    return (rows >= lane_index((ROWS, ROWS))) & (segments(table) == seg_rows[0:1, :])


def head_decay(allowed, rates, rates_t, head):
    gap = rates[:, 128 + head : 129 + head] - rates_t[8 + head : 9 + head, :]
    return jnp.where(allowed, jnp.exp(jnp.where(allowed, gap, 0.0)), 0.0)


def intra_kernel(flags, shared, xc, rates, rates_t, table, seg_rows, small, out):
    inject, readout = inject_of(flags, shared), readout_of(flags, shared)
    both = dot_nt(readout, inject)
    allowed = allowed_pairs(table, seg_rows)
    low = lane_index((1, 128)) < HP
    for pair in range(PAIRS):
        x = xc[:, lanes_of(pair)]
        xb = x.astype(bf16)
        heads = []
        for head in (2 * pair, 2 * pair + 1):
            decay = head_decay(allowed, rates, rates_t, head)
            heads.append(dot_nn((both * decay * rates_t[head : head + 1, :]).astype(bf16), xb))
        out[:, lanes_of(pair)] = jnp.where(low, heads[0], heads[1]) + spread(small[2:3, 512:640], pair) * x


def keys_values(flags, shared, halves, swapped):
    head, first = flags[1] // 2, flags[2] == 0
    pairs = [
        (
            shared[pl.ds(rank_block(flags, head), ROWS), :],
            shared[pl.ds(rank_block(flags, 2 + head), ROWS), :],
        )
    ]
    for index, half in enumerate(halves):
        packed = half[...], swapped[KV * index : KV * (index + 1), :]
        mine, theirs = (jnp.concatenate([part[:, 0:128], part[:, 128:256]], axis=0) for part in packed)
        pairs.append((jnp.where(first, mine, theirs), jnp.where(first, theirs, mine)))
    return pairs


def masked_scores(query, pairs, table, seg_rows):
    parts = []
    for block, (keys, _) in enumerate(pairs):
        score = dot_nt(query, keys) * HD ** (-0.5)
        keep = segments(table) == seg_rows[block : block + 1, :]
        if block == 0:
            rows = lax.broadcasted_iota(i32, (ROWS, ROWS), 0)
            keep = keep & (rows >= lane_index((ROWS, ROWS)))
        parts.append(jnp.where(keep, score, -1e30))
    return parts


def attention_kernel(flags, query, shared, h1, h2, h3, swapped, table, seg_rows, out, log_total, kept):
    pairs = keys_values(flags, shared, (h1, h2, h3), swapped)
    for block, (keys, values) in enumerate(pairs):
        kept[ROWS * block : ROWS * (block + 1), 0:HD] = keys
        kept[ROWS * block : ROWS * (block + 1), HD : 2 * HD] = values
    parts = masked_scores(query[...], pairs, table, seg_rows)
    top = parts[0].max(axis=1, keepdims=True)
    for part in parts[1:]:
        top = jnp.maximum(top, part.max(axis=1, keepdims=True))
    parts = [jnp.exp(part - top) for part in parts]
    total = sum(part.sum(axis=1, keepdims=True) for part in parts)
    inverse = 1.0 / total
    result = jnp.zeros((ROWS, HD), f32)
    for part, (_, values) in zip(parts, pairs):
        result = result + dot_nn((part * inverse).astype(bf16), values)
    out[...] = result.astype(bf16)
    log_total[...] = jnp.broadcast_to(top + jnp.log(total), (ROWS, HD))


def chained(first, second, third, base):
    rows1 = first[base + XLOC : base + MSG, :].astype(f32)
    rows2 = second[base + XLOC : base + MSG, :].astype(f32)
    parts = []
    for head in range(HLOC):
        own = slice(base + HP * head, base + HP * head + HP)
        older = second[own, :].astype(f32) + rows2[head : head + 1, :] * third[own, :].astype(f32)
        parts.append(first[own, :].astype(f32) + rows1[head : head + 1, :] * older)
    return jnp.concatenate(parts, axis=0)


def carry_kernel(flags, msg1, msg2, msg3, shared, rates, table, intra, z, attn, state, ssm_y, cat, cat_kept):
    entering = chained(msg1, msg2, msg3, KV)
    state[...] = entering
    from_state = dot_nt(readout_of(flags, shared), entering.astype(bf16))
    carry = carry_of(rates, table)
    for pair in range(PAIRS):
        own = lanes_of(pair)
        y = intra[:, own] + spread(carry, pair) * from_state[:, own]
        ssm_y[:, own] = y
        gate = z[:, own]
        gated = (y * gate * sigmoid(gate)).astype(bf16)
        for block in range(8):
            for out in (cat, cat_kept):
                out[pl.ds(local_block(flags, block), SHARE), 128 + 128 * pair : 256 + 128 * pair] = gated[
                    SHARE * block : SHARE * (block + 1), :
                ]
    for block in range(8):
        for out in (cat, cat_kept):
            out[pl.ds(local_block(flags, block), SHARE), 0:128] = attn[SHARE * block : SHARE * (block + 1), :]


def gate_back_kernel(
    flags, p0, p1, p2, p3, p4, p5, p6, p7, weight, z, ssm_y, shared, rates, rates_t, table,
    dmix, dattn, dy, dz, msg, work, local,
):
    rows = joined((p0, p1, p2, p3, p4, p5, p6, p7))
    dmix[...] = rows
    local[...] = dot_nn(rows, weight[...])
    for block in range(8):
        own = slice(SHARE * block, SHARE * (block + 1))
        from_rows = pl.ds(local_block(flags, block), SHARE)
        dattn[own, :] = local[from_rows, 0:128].astype(bf16)
        work[own, :] = local[from_rows, 128:512]
    readout = readout_of(flags, shared)
    carry = carry_of(rates, table)
    for pair in range(PAIRS):
        own = lanes_of(pair)
        gate, grad = z[:, own], work[:, own]
        sig = sigmoid(gate)
        y_grad = grad * gate * sig
        dy[:, own] = y_grad
        dz[:, own] = (grad * ssm_y[:, own] * sig * (1.0 + gate * (1.0 - sig))).astype(bf16)
        msg[own, :] = dot_tn((y_grad * spread(carry, pair)).astype(bf16), readout).astype(bf16)
    msg[XLOC:MSG, :] = decay_rows(flags, rates_t)


def attention_back_kernel(
    flags, dattn, dz, query, kept, log_total, table, seg_rows,
    early, mine, theirs,
):
    pairs = []
    for block in range(SEQ_BLOCKS):
        own = slice(ROWS * block, ROWS * (block + 1))
        pairs.append((kept[own, 0:HD], kept[own, HD : 2 * HD]))
    first = flags[2] == 0
    q = query[...]
    grad = dattn[...]
    parts = masked_scores(q, pairs, table, seg_rows)
    logs = log_total[:, 0:1]
    probs = [jnp.exp(part - logs) for part in parts]
    grads = [dot_nt(grad, values) for _, values in pairs]
    inner = sum((p * g).sum(axis=1, keepdims=True) for p, g in zip(probs, grads))
    total = jnp.zeros((ROWS, HD), f32)
    for block, (p, g, (keys, _)) in enumerate(zip(probs, grads, pairs)):
        own = slice(ROWS * block, ROWS * (block + 1))
        score = (p * (g - inner)).astype(bf16)
        total = total + dot_nn(score, keys)
        dkeys = dot_tn(score, q) * HD ** (-0.5)
        dvalues = dot_tn(p.astype(bf16), grad)
        mine[own, :] = jnp.where(first, dkeys, dvalues)
        theirs[own, :] = jnp.where(first, dvalues, dkeys).astype(bf16)
    total = total * HD ** (-0.5)
    dq = turned(total, table, -1.0).astype(bf16)
    for block in range(8):
        own = slice(SHARE * block, SHARE * (block + 1))
        to_rows = pl.ds(local_block(flags, block), SHARE)
        early[to_rows, 0:XLOC] = dz[own, :]
        early[to_rows, XLOC:512] = dq[own, :]


def intra_back_kernel(
    flags, dy, xc, shared, rates, rates_t, table, seg_rows, state, small,
    dx, dshared, drates, dskip, row_sums, dcum,
):
    inject, readout = inject_of(flags, shared), readout_of(flags, shared)
    both = dot_nt(readout, inject)
    allowed = allowed_pairs(table, seg_rows)
    low = lane_index((1, 128)) < HP
    carry = carry_of(rates, table)
    entering = state[...].astype(bf16)
    from_state = dot_nt(readout, entering)
    dboth = jnp.zeros((ROWS, ROWS), f32)
    row_sums[...] = jnp.zeros((128, ROWS), f32)
    dcum[...] = jnp.zeros((ROWS, 128), f32)
    carried = []
    for pair in range(PAIRS):
        own = lanes_of(pair)
        x = xc[:, own]
        xb = x.astype(bf16)
        grad = dy[:, own]
        dskip[:, own] = jnp.sum(grad * x, axis=0, keepdims=True)
        carried.append((grad * spread(carry, pair)).astype(bf16))
        through = grad * from_state[:, own]
        total = spread(small[2:3, 512:640], pair) * grad
        for head in (2 * pair, 2 * pair + 1):
            mine = low if head % 2 == 0 else jnp.logical_not(low)
            decay = head_decay(allowed, rates, rates_t, head)
            steps = rates_t[head : head + 1, :]
            head_grad = jnp.where(mine, grad, 0.0).astype(bf16)
            dmix = dot_nt(head_grad, xb)
            kept = dmix * decay
            dboth = dboth + kept * steps
            mixed = both * decay
            total = total + dot_tn((mixed * steps).astype(bf16), head_grad)
            passed = dmix * mixed
            row_sums[head : head + 1, :] = jnp.sum(passed, axis=0, keepdims=True)
            dcum[:, head : head + 1] = jnp.sum(passed * steps, axis=1, keepdims=True) + carry[
                :, head : head + 1
            ] * jnp.sum(jnp.where(mine, through, 0.0), axis=1, keepdims=True)
        dx[:, own] = total
    columns = row_sums[...].T
    drates[:, 0:128] = columns
    drates[:, 128:256] = dcum[...] - rates[:, 0:128] * columns
    dboth_b = dboth.astype(bf16)
    dshared[:, NSTATE:] = dot_nn(dboth_b, inject) + dot_nn(jnp.concatenate(carried, axis=1), entering)
    dshared[:, 0:NSTATE] = dot_tn(dboth_b, readout)


def state_back_kernel(
    flags, msg1, msg2, msg3, shared, xc, rates, rates_t, table, state, small, dtn,
    dx, dshared, drates, kv0, kv1, kv2, kv3, ext,
    packed, dxpre, edge, gweight, ddt, heads, work, dconv, sums,
):
    later = chained(msg1, msg2, msg3, 0)
    later_b = later.astype(bf16)
    inject = inject_of(flags, shared)
    low = lane_index((1, 128)) < HP
    params = small[:, 512:640]
    gap, weights = weights_in(rates, table)
    from_later = dot_nt(inject, later_b)
    products = later * state[...]
    decays = block_decays(flags, rates_t)
    sums[...] = jnp.zeros((ROWS, 128), f32)
    weighted = []
    for pair in range(PAIRS):
        own = lanes_of(pair)
        x = xc[:, own]
        scale = spread(weights, pair)
        weighted.append((x * scale).astype(bf16))
        dconv[:, own] = dx[:, own] + scale * from_later[:, own]
        through = x * from_later[:, own]
        for head in (2 * pair, 2 * pair + 1):
            mine = low if head % 2 == 0 else jnp.logical_not(low)
            sums[:, head : head + 1] = jnp.sum(jnp.where(mine, through, 0.0), axis=1, keepdims=True)
    dweights = sums[...]
    moved = dweights * weights
    last = jnp.sum(moved, axis=0, keepdims=True)
    lanes = lane_index((1, 128))
    for head in range(HLOC):
        total = jnp.sum(
            jnp.sum(products[HP * head : HP * head + HP, :], axis=0, keepdims=True), axis=1, keepdims=True
        )
        last = last + jnp.where(lanes == head, total * decays[head : head + 1, :], 0.0)
    rows = lax.broadcasted_iota(i32, (ROWS, 128), 0)
    dcums = drates[:, 128:256] - moved + jnp.where(rows == ROWS - 1, last, 0.0)
    square = lax.broadcasted_iota(i32, (ROWS, ROWS), 0)
    upper = (square <= lane_index((ROWS, ROWS))).astype(f32)
    dlogs = jnp.dot(upper, dcums, precision=lax.Precision.HIGHEST, preferred_element_type=f32)
    rate = -jnp.exp(params[0:1, :])
    dsteps = drates[:, 0:128] + dweights * gap + dlogs * rate
    ddts = dsteps * sigmoid(dtn[...] + params[1:2, :])
    ddt[...] = ddts
    heads[...] = jnp.zeros((8, 128), f32)
    heads[0:1, :] = jnp.sum(dlogs * rate * rates[:, 0:128], axis=0, keepdims=True)
    heads[1:2, :] = jnp.sum(ddts, axis=0, keepdims=True)
    dinject_all = (dshared[:, 0:NSTATE] + dot_nn(jnp.concatenate(weighted, axis=1), later_b)).astype(bf16)
    dreadout_all = dshared[:, NSTATE:].astype(bf16)
    packed[...] = jnp.zeros((8 * ROWS, 128), bf16)
    grads = kv0[...] + kv1[...].astype(f32) + kv2[...].astype(f32) + kv3[...].astype(f32)
    owner = 2 * flags[2] + flags[1] // 2
    packed[pl.ds(rank_block(flags, owner), ROWS), :] = grads.astype(bf16)
    packed[pl.ds(rank_block(flags, 4), ROWS), :] = dinject_all[:, 0:128]
    packed[pl.ds(rank_block(flags, 5), ROWS), :] = dinject_all[:, 128:256]
    packed[pl.ds(rank_block(flags, 6), ROWS), :] = dreadout_all[:, 0:128]
    packed[pl.ds(rank_block(flags, 7), ROWS), :] = dreadout_all[:, 128:256]
    conv_back(dconv[...], ext, table, small[:, 0:XLOC], work, dxpre, edge, gweight)


def shared_back_kernel(flags, part0, part1, part2, part3, ext, table, small, out, edge, gweight, work):
    grad = part0[...] + part1[...].astype(f32) + part2[...].astype(f32) + part3[...].astype(f32)
    conv_back(grad, ext, table, small[:, XLOC:512], work, out, edge, gweight)
    rank = flags[0]
    of_conv = jnp.where(rank < 4, 0.0, 1.0)
    edge[...] = edge[...] * of_conv
    gweight[...] = gweight[...] * of_conv
    out[...] = jnp.where(rank < 2, turned(grad, table, -1.0), jnp.where(rank < 4, grad, out[...]))


def late_kernel(flags, dxpre, edge_x, dsh, edge_sh, ddt, out):
    for block in range(8):
        own = slice(SHARE * block, SHARE * (block + 1))
        to_rows = pl.ds(local_block(flags, block), SHARE)
        x, sh = dxpre[own, :], dsh[own, :]
        if block == 7:
            pad = jnp.zeros((SHARE - 8, 128), f32)
            sh = sh + jnp.concatenate([pad, edge_sh[...]], axis=0)
            x = x + jnp.concatenate([jnp.zeros((SHARE - 8, XLOC), f32), edge_x[...]], axis=0)
        out[to_rows, 0:XLOC] = x.astype(bf16)
        out[to_rows, XLOC:512] = sh.astype(bf16)
        out[to_rows, 512:LATE] = jnp.where(lane_index((1, 128)) < HLOC, ddt[own, :], 0.0).astype(bf16)


def half_sum_kernel(own, other, keep, send1, send2, send3):
    rows = own.shape[0] // 4
    keep[...] = own[0:rows, :] + other[0:rows, :].astype(f32)
    for index, send in ((1, send1), (2, send2), (3, send3)):
        part = slice(rows * index, rows * (index + 1))
        send[...] = (own[part, :].astype(f32) + other[part, :].astype(f32)).astype(bf16)


def parts_of_sum(own, other, along, sign):
    return parts_from(own, other_core(other), along, sign)


def parts_from(own, got, along, sign):
    rows, width = own.shape[0] // 4, own.shape[1]
    sent = shape_of((rows, width), bf16)
    keep, *sends = run_kernel(half_sum_kernel, [kept((rows, width)), sent, sent, sent], None, own, Columns(got))
    return (keep,) + tuple(along(send, sign * k) for k, send in zip((1, 2, 3), sends))


def split_kernel(*refs):
    lefts, weight, own, other = refs[:-3], refs[-3], refs[-2], refs[-1]
    left = lefts[0][...] if len(lefts) == 1 else jnp.concatenate([ref[...] for ref in lefts], axis=1)
    result = dot_nt(left, weight[...])
    own[...] = result[: ROWS // 2]
    other[...] = result[ROWS // 2 :].astype(bf16)


def summed_rows(lefts, weight):
    model, width = weight.shape
    own, other = pl.pallas_call(
        split_kernel,
        grid=(model // 512,),
        out_shape=(shape_of((ROWS // 2, model)), shape_of((ROWS // 2, model), bf16)),
        in_specs=[pl.BlockSpec(left.shape, lambda i: (0, 0)) for left in lefts]
        + [pl.BlockSpec((512, width), lambda i: (i, 0))],
        out_specs=(
            pl.BlockSpec((ROWS // 2, 512), lambda i: (0, i)),
            pl.BlockSpec((ROWS // 2, 512), lambda i: (0, i)),
        ),
        compiler_params=pltpu.CompilerParams(vmem_limit_bytes=VMEM_LIMIT),
        cost_estimate=pl.CostEstimate(
            flops=2 * ROWS * model * width, bytes_accessed=2 * model * width, transcendentals=0
        ),
    )(*lefts, weight)
    return parts_of_sum(own, other, along_y, 1)


def gate_up_kernel(p0, p1, p2, p3, p4, p5, p6, p7, weight, normed, gate, up, act, act_kept):
    rows = joined((p0, p1, p2, p3, p4, p5, p6, p7))
    normed[...] = rows
    result = dot_nn(rows, weight[...])
    g, u = result[:, :512], result[:, 512:]
    gate[...] = g
    up[...] = u
    for out in (act, act_kept):
        out[...] = (g * sigmoid(g) * u).astype(bf16)


def gate_up_back_kernel(*refs):
    parts, (weight, gate, up, dffn, out) = refs[:-5], refs[-5:]
    rows = joined(parts)
    dffn[...] = rows
    dact = dot_nn(rows, weight[...])
    g = gate[...]
    sig = sigmoid(g)
    out[:, :512] = (dact * up[...] * sig * (1.0 + g * (1.0 - sig))).astype(bf16)
    out[:, 512:] = (dact * g * sig).astype(bf16)


def natural_kernel(flags, p0, p1, p2, p3, p4, p5, p6, p7, out):
    local = joined((p0, p1, p2, p3, p4, p5, p6, p7)).astype(out.dtype)
    for block in range(8):
        out[pl.ds(pl.multiple_of(flags[24 + block] * SHARE, SHARE), SHARE), :] = local[
            SHARE * block : SHARE * (block + 1), :
        ]


def add_norm_kernel(hidden, part0, part1, part2, part3, gain, out_kept, normed, inverse):
    total = hidden[...] + part0[...] + (
        part1[...].astype(f32) + part2[...].astype(f32) + part3[...].astype(f32)
    )
    out_kept[...] = total
    scale = lax.rsqrt(jnp.mean(total * total, axis=1, keepdims=True) + norm_eps)
    inverse[...] = jnp.broadcast_to(scale, inverse.shape)
    normed[...] = (total * scale * gain[...]).astype(bf16)


def add_norm(hidden, parts, gain):
    shape = hidden.shape
    return run_kernel(
        add_norm_kernel,
        [kept(shape), shape_of(shape, bf16), kept((shape[0], 128))],
        None, stored(hidden), *summands(parts), gain[None],
    )


def output_kernel(hidden, part0, part1, part2, part3, out):
    total = hidden[...] + part0[...] + (
        part1[...].astype(f32) + part2[...].astype(f32) + part3[...].astype(f32)
    )
    out[...] = total.astype(bf16)


def norm_back_kernel(grad, part0, part1, part2, part3, hidden, inverse, gain, out, rounded, ggain):
    received = part0[...] + (part1[...].astype(f32) + part2[...].astype(f32) + part3[...].astype(f32))
    scale = inverse[:, 0:1]
    unit = hidden[...] * scale
    scaled = received * gain[...]
    ggain[...] = jnp.sum(received * unit, axis=0, keepdims=True)
    total = grad[...] + scale * (scaled - unit * jnp.mean(scaled * unit, axis=1, keepdims=True))
    out[...] = total
    rounded[...] = total.astype(bf16)


def norm_back(parts, grad, hidden, inverse, gain):
    shape = hidden.shape
    return run_kernel(
        norm_back_kernel,
        [kept(shape), shape_of(shape, bf16), kept((1, shape[1]))],
        None, grad, *summands(parts), hidden, inverse, gain[None],
    )


def gradient_kernel(pairs, *refs):
    out, at = refs[-1], 0
    for index in range(pairs):
        left, right = refs[2 * index], refs[2 * index + 1]
        width = right.shape[1]
        out[:, at : at + width] = dot_tn(left[...], right[...]).astype(bf16)
        at += width
    if at < out.shape[1]:
        out[:, at:] = jnp.zeros((out.shape[0], out.shape[1] - at), bf16)


def weight_gradients(pairs, total, block, index, buffer=None):
    rows, model = pairs[0][0].shape
    width = sum(right.shape[1] for _, right in pairs)
    specs, args = [], []
    for left, right in pairs:
        specs += [
            pl.BlockSpec((rows, 512), lambda i: (0, i)),
            pl.BlockSpec(right.shape, lambda i: (0, 0)),
        ]
        args += [left, right]
    aliases = {}
    kernel = partial(gradient_kernel, len(pairs))
    if buffer is not None:
        aliases = {len(args): 0}
        specs.append(pl.BlockSpec(memory_space=pltpu.HBM))
        args.append(buffer)

        def kernel(*refs):
            gradient_kernel(len(pairs), *refs[:-2], refs[-1])

    return pl.pallas_call(
        kernel,
        grid=(model // 512,),
        out_shape=pltpu.HBM((model, total), bf16),
        in_specs=specs,
        out_specs=pl.BlockSpec((512, block), lambda i: (i, index)),
        input_output_aliases=aliases,
        compiler_params=pltpu.CompilerParams(vmem_limit_bytes=VMEM_LIMIT),
        cost_estimate=pl.CostEstimate(
            flops=2 * rows * model * width, bytes_accessed=model * width * 2, transcendentals=0
        ),
    )(*args)


def owned_kernel(pairs, *refs):
    out, at = refs[-1], 0
    for pair in range(pairs):
        left, right = refs[2 * pair], refs[2 * pair + 1]
        result = dot_tn(left[...], right[...]).astype(bf16)
        width = right.shape[1]
        for index in range(2):
            out[index, :, at : at + width] = result[128 * index : 128 * (index + 1)]
        at += width
    if at < out.shape[2]:
        for index in range(2):
            out[index, :, at:] = refs[2 * pairs][...]


def owned_gradients(pairs, small=None):
    rows, model = pairs[0][0].shape
    width = sum(right.shape[1] for _, right in pairs)
    specs, args = [], []
    for left, right in pairs:
        specs += [pl.BlockSpec((rows, 256), lambda i: (0, i)), pl.BlockSpec(right.shape, lambda i: (0, 0))]
        args += [left, right]
    if small is not None:
        specs.append(pl.BlockSpec(small.shape, lambda i: (0, 0)))
        args.append(small)
        width += small.shape[1]
    return pl.pallas_call(
        partial(owned_kernel, len(pairs)),
        grid=(model // 256,),
        out_shape=pltpu.HBM((16, model // 16, width), bf16),
        in_specs=specs,
        out_specs=pl.BlockSpec((2, model // 16, width), lambda i: (i, 0, 0)),
        compiler_params=pltpu.CompilerParams(vmem_limit_bytes=VMEM_LIMIT),
        cost_estimate=pl.CostEstimate(
            flops=2 * rows * model * width, bytes_accessed=model * width * 2, transcendentals=0
        ),
    )(*args)


def small_kernel(gain1, gain2, conv_sh, conv_x, heads, skip, out):
    out[...] = jnp.zeros(out.shape, bf16)
    for row in range(16):
        own = slice(128 * row, 128 * row + 128)
        out[row : row + 1, :] = gain1[:, own].astype(bf16)
        out[16 + row : 17 + row, :] = gain2[:, own].astype(bf16)
    out[32:37, :] = conv_sh[0:5, :].astype(bf16)
    for tap in range(CONV + 1):
        for pair in range(PAIRS):
            row = 37 + PAIRS * tap + pair
            out[row : row + 1, :] = conv_x[tap : tap + 1, lanes_of(pair)].astype(bf16)
    out[52:54, :] = heads[0:2, :].astype(bf16)
    lanes = lane_index((1, 128))
    sums = jnp.zeros((1, 128), f32)
    for pair in range(PAIRS):
        part = skip[:, lanes_of(pair)]
        for half in range(2):
            mine = (lanes < HP) if half == 0 else (lanes >= HP)
            total = jnp.sum(jnp.where(mine, part, 0.0), axis=1, keepdims=True)
            sums = sums + jnp.where(lanes == 2 * pair + half, total, 0.0)
    out[54:55, :] = sums.astype(bf16)


def owner_sum(values):
    total = values[0].astype(f32)
    for index in range(1, 16):
        total = total + values[index].astype(f32)
    return total


def block_sum_kernel(values, over_tp, late, conv_x, heads):
    whole = owner_sum(values)
    late[...] = whole[:, 0:LATE]
    total = whole[:, LATE : LATE + 128]
    over_tp[0:128, :] = whole[:, XLOC:512].astype(bf16)
    over_tp[128:224, :] = jnp.zeros((96, 128), bf16)
    for layer in range(2):
        first = 64 * layer
        over_tp[128 + 48 * layer : 165 + 48 * layer, :] = total[first : first + 37, :].astype(bf16)
        for tap in range(CONV + 1):
            for pair in range(PAIRS):
                row = first + 37 + PAIRS * tap + pair
                conv_x[5 * layer + tap : 5 * layer + tap + 1, lanes_of(pair)] = total[row : row + 1, :]
        heads[3 * layer : 3 * layer + 3, :] = total[first + 52 : first + 55, :]


def early_outputs_kernel(lower, upper_ffn, upper_mixer, attn, ssm, gate, up, down, query, z):
    for layer, ref in ((0, lower), (1, upper_ffn)):
        for index, out in enumerate((gate, up, down)):
            out[layer] = ref[:, 512 * index : 512 * (index + 1)].astype(f32)
    for layer, ref, at in ((0, lower, 1536), (1, upper_mixer, 1024)):
        attn[layer] = ref[:, at : at + 128].astype(f32)
        ssm[layer] = ref[:, at + 128 : at + 512].astype(f32)
        z[layer] = ref[:, at + 512 : at + 896].astype(f32)
        query[layer] = ref[:, at + 896 : at + 1024].astype(f32)


def last_outputs_kernel(flags, *refs):
    parts, other, (late, upper_late, z) = refs[:8], refs[8:16], refs[16:19]
    zx, dt, shared, gains1, gains2, conv_bc, every = refs[19:]
    zx[0, :, 0, :] = z[0]
    zx[1, :, 0, :] = z[1]
    zx[0, :, 1, :] = late[:, 0:XLOC]
    zx[1, :, 1, :] = upper_late[:, 0:XLOC].astype(f32)
    dt[0] = late[:, 512 : 512 + HLOC]
    dt[1] = upper_late[:, 512 : 512 + HLOC].astype(f32)
    total = jnp.zeros((96, 128), f32)
    for index, part in enumerate(parts):
        every[index] = part[...].astype(f32)
        total = total + part[128:224, :].astype(f32)
    for index, part in enumerate(other):
        every[8 + index, 0:128, :] = part[...].astype(f32)
    for rank in range(8):
        own = slice(128 * rank, 128 * rank + 128)
        shared[0, :, own] = every[flags[16 + rank], 0:128, :]
        shared[1, :, own] = every[8 + flags[16 + rank], 0:128, :]
    for layer in range(2):
        for row in range(16):
            own = slice(128 * row, 128 * row + 128)
            at = 48 * layer + row
            gains1[layer : layer + 1, own] = total[at : at + 1, :]
            gains2[layer : layer + 1, own] = total[at + 16 : at + 17, :]
        for rank in range(4):
            part = every[flags[20 + rank], 160 + 48 * layer : 168 + 48 * layer, :]
            conv_bc[5 * layer : 5 * layer + 5, 128 * rank : 128 * rank + 128] = part[0:5, :]


def body(
    inputs, cotangent, segment_ids, w_query, w_shared, w_zx, w_dt, w_attn_out, w_ssm_out, w_gate, w_up, w_down,
    gains, conv_x, conv_bc, head_params,
):
    layers = w_query.shape[0]
    rank, ctx = lax.axis_index("tp"), lax.axis_index("ctx")
    y, core = rank // 2, rank % 2
    model = inputs.shape[2]

    def local_of(block_y, block_core):
        return jnp.where(block_core == core, 0, 4) + (block_y - y) % 4

    seg_all = segment_ids[0]
    first_row = ctx * ROWS
    padded = jnp.concatenate([jnp.full((CONV - 1,), -1, i32), seg_all])
    seg_ext = lax.dynamic_slice_in_dim(padded, first_row, ROWS + CONV - 1)
    seg_own = seg_ext[CONV - 1 :]
    blocks = seg_all.reshape(SEQ_BLOCKS, ROWS)
    seg_rows = jnp.stack(
        [
            jnp.where(ctx >= back, lax.dynamic_index_in_dim(blocks, jnp.maximum(ctx - back, 0), 0, False), -1)
            for back in range(SEQ_BLOCKS)
        ]
        + [jnp.full((ROWS,), -1, i32)] * 4
    ).astype(f32)
    naturals = jnp.arange(8, dtype=i32)
    flags = jnp.concatenate(
        [
            jnp.stack([rank, y, core, ctx, seg_ext[CONV - 2], seg_own[-1], rank, rank]).astype(i32),
            local_of(naturals % 4, naturals // 4).astype(i32),
            local_of(naturals // 2, naturals % 2).astype(i32),
            (jnp.where(naturals < 4, core, 1 - core) * 4 + (y + naturals) % 4).astype(i32),
        ]
    )

    half_width = HD // 2
    frequency = rope_base ** (-jnp.arange(half_width, dtype=f32) / half_width)
    places = (first_row + jnp.arange(ROWS, dtype=i32)).astype(f32)
    angles = places[:, None] * frequency[None, :]
    cosine, sine = jnp.cos(angles), jnp.sin(angles)
    marks = [seg_ext[tap : tap + ROWS] == seg_own for tap in range(CONV - 1)]
    marks += [seg_own, seg_own == seg_ext[CONV - 2], seg_own == seg_own[-1]]
    marks = jnp.pad(jnp.stack([mark.astype(f32) for mark in marks], axis=1), ((0, 0), (0, 122)))
    table = jnp.concatenate([cosine, cosine, -sine, sine, marks], axis=1)

    own_conv = jnp.maximum(rank - 4, 0) * 128
    small = []
    for layer in range(layers):
        rows = [conv_x[layer], lax.dynamic_slice_in_dim(conv_bc[layer], own_conv, 128, 1)]
        rows.append(jnp.pad(head_params[layer], ((0, 2), (0, 128 - HLOC))))
        small.append(jnp.pad(jnp.concatenate(rows, axis=1), ((0, 3), (0, 0))))

    def packed(*members):
        width = sum(
            {4: 2 * XLOC}.get(member.ndim, 128 if member.shape[2] in (1024, HLOC) else member.shape[2])
            for member, _ in members
        )
        (columns,) = run_kernel(
            pack_kernel,
            [shape_of((w_query.shape[1], width), bf16)],
            rank.astype(i32).reshape(1),
            *(Layer(member, layer) for member, layer in members),
        )
        return lax.all_gather(columns, ("fsdp", "ctx"), axis=0, tiled=True)

    def proj_members(layer):
        return [(member, layer) for member in (w_zx, w_query, w_shared, w_dt)]

    weight_a = packed(*proj_members(0), (w_attn_out, 0), (w_ssm_out, 0))
    weight_b = packed(*proj_members(1), (w_gate, 0), (w_up, 0), (w_down, 0))
    weight_c = packed((w_gate, 1), (w_up, 1), (w_down, 1), (w_attn_out, 1), (w_ssm_out, 1))
    proj_place = [(weight_a, 0, PROJ), (weight_b, 0, PROJ)]
    out_place = [(weight_a, PROJ, 512), (weight_c, 1536, 512)]
    gate_up_place = [(weight_b, PROJ, 1024), (weight_c, 0, 1024)]
    down_place = [(weight_b, PROJ + 1024, 512), (weight_c, 1024, 512)]

    def together(*values):
        return lax.optimization_barrier(values)

    weight_a, table, seg_rows, small = together(weight_a, table, seg_rows, small)
    normed_shape = shape_of((ROWS, model), bf16)
    normed_kept = kept((ROWS, model), bf16)
    normed_b, inverse1, hidden, dffn_b, grad_hidden = run_kernel(
        first_kernel,
        [normed_shape, kept((SHARE, 128)), kept((SHARE, model)), normed_kept, kept((SHARE, model))],
        flags, inputs, cotangent, gains[0],
    )
    weight_a, normed_b = together(weight_a, normed_b)
    proj_place[0] = (weight_a, 0, PROJ)
    out_place[0] = (weight_a, PROJ, 512)
    normed_parts, dffn_parts = (normed_b,), (dffn_b,)
    saved = []
    wide = shape_of((ROWS, 512))
    proj_weight = fetched("proj_0", *proj_place[0])
    for layer in range(layers):
        normed_b, z, z_kept, xs, query, query_kept, dtn, dtn_kept = run_kernel(
            proj_kernel,
            [
                normed_kept, shape_of((ROWS, XLOC)), kept((ROWS, XLOC)), wide, shape_of((ROWS, HD), bf16),
                kept((ROWS, HD), bf16), shape_of((ROWS, 128)), kept((ROWS, 128)),
            ],
            flags, *(passed(normed_parts) if layer > 0 else normed_parts), proj_weight, table,
            scratch=[pltpu.VMEM((ROWS, PROJ), f32)],
        )
        halo = along_ctx(xs[ROWS - 8 :], 1)
        shared_own, shared_ext = run_kernel(
            shared_kernel,
            [shape_of((ROWS, 128), bf16), kept((264, 128))],
            flags, xs, Columns(halo), table, small[layer],
        )
        shared_parts = from_all(shared_own)
        x_ext, xc, xc_kept, rates, rates_kept, rates_t, rates_t_kept = run_kernel(
            prep_kernel,
            [
                kept((264, XLOC)), shape_of((ROWS, XLOC)), kept((ROWS, XLOC)), shape_of((ROWS, 256)),
                kept((ROWS, 256)), shape_of((16, ROWS)), kept((16, ROWS)),
            ],
            None, xs, dtn, Columns(halo), table, small[layer],
        )
        message, shared, shared_kept = run_kernel(
            state_kernel,
            [shape_of((KV + MSG, NSTATE), bf16), shape_of((8 * ROWS, 128), bf16), kept((8 * ROWS, 128), bf16)],
            flags, *passed(shared_parts), xc, rates, rates_t, table,
        )
        earlier = tuple(along_ctx(message, back) for back in (1, 2, 3))
        (intra,) = run_kernel(
            intra_kernel, [shape_of((ROWS, XLOC))],
            flags, shared, xc, rates, rates_t, table, seg_rows, small[layer],
        )
        earlier, intra = together(earlier, intra)
        halves = [Columns(part, 0, NSTATE, rows=KV) for part in earlier]
        (swapped,) = run_kernel(halves_kernel, [shape_of((3 * KV, NSTATE), bf16)], None, *halves)
        swapped, out_weight = together(other_core(swapped), fetched(f"out_{layer}", *out_place[layer]))
        attn, log_total, pairs = run_kernel(
            attention_kernel,
            [shape_of((ROWS, HD), bf16), kept((ROWS, HD)), kept((SEQ_BLOCKS * ROWS, 2 * HD), bf16)],
            flags, query, shared, *halves, Columns(swapped), table, seg_rows,
        )
        state, ssm_y, cat, cat_kept = run_kernel(
            carry_kernel,
            [kept((XLOC, NSTATE)), kept((ROWS, XLOC)), shape_of((ROWS, 512), bf16), kept((ROWS, 512), bf16)],
            flags, *passed(earlier), shared, rates, table, intra, z, attn,
        )
        parts = summed_rows([cat], out_weight)
        if layer > 0:
            parts, gate_up_weight = together(parts, fetched(f"gate_up_{layer}", *gate_up_place[layer]))
        hidden1, normed2, inverse2 = add_norm(hidden, parts, gains[layer, 1])
        if layer > 0:
            normed_parts, down_weight = from_all(normed2, fetched("down_1", *down_place[layer]))
        else:
            normed_parts = from_all(normed2)
            gate_up_weight, down_weight = fetched_all("ffn_0", [gate_up_place[layer], down_place[layer]])
        wide_kept = kept((ROWS, 512))
        normed2_b, gate, up, act_b, act_kept = run_kernel(
            gate_up_kernel, [normed_kept, wide_kept, wide_kept, shape_of((ROWS, 512), bf16), kept((ROWS, 512), bf16)],
            None, *passed(normed_parts), gate_up_weight,
        )
        saved.append(
            (
                hidden, normed_b, inverse1, shared_ext, shared_kept, query_kept, x_ext, xc_kept, z_kept, dtn_kept,
                rates_kept, rates_t_kept, pairs, log_total, state, ssm_y, cat_kept, hidden1, inverse2, normed2_b,
                gate, up, act_kept,
            )
        )
        if layer + 1 < layers:
            hidden, next_normed, inverse1 = add_norm(
                hidden1, summed_rows([act_b], down_weight), gains[layer + 1, 0]
            )
            normed_parts, proj_weight = from_all(next_normed, fetched("proj_1", *proj_place[layer + 1]))

    small_parts = [None] * layers
    for layer in reversed(range(layers)):
        (
            hidden, normed_b, inverse1, shared_ext, shared, query, x_ext, xc, z, dtn, rates, rates_t,
            pairs, log_total, state, ssm_y, cat, hidden1, inverse2, normed2_b, gate, up, act_b,
        ) = saved[layer]
        last = layer == 0
        dffn_b, dgate_up = run_kernel(
            gate_up_back_kernel, [normed_kept, shape_of((ROWS, 1024), bf16)],
            None, *passed(dffn_parts), down_weight, stored(gate), stored(up),
        )
        parts = summed_rows([dgate_up], gate_up_weight)
        outer = weight_gradients([(normed2_b, dgate_up), (dffn_b, act_b)], 2560 if last else 1536, 1536, 0)
        parts, outer = lax.optimization_barrier((parts, outer))
        parts, kept_rows = together(parts, restored(f"norm2_{layer}", [grad_hidden, hidden1, inverse2]))
        grad_mid, dmix, ggain2 = norm_back(parts, *kept_rows, gains[layer, 1])
        if not last:
            ffn_sum = lax.psum_scatter(outer, ("fsdp", "ctx"), scatter_dimension=0, tiled=True)
        dmix_parts = from_all(dmix)
        dmix_parts, fetch = from_all(
            dmix,
            fetched_all(
                f"mixer_{layer}",
                [out_place[layer]]
                + [(array, 0, array.shape[1]) for array in (z, ssm_y, shared, rates, rates_t, xc, query, pairs, state)],
            ),
        )
        rates_t_kept = rates_t
        out_weight, z, ssm_y, shared, rates, rates_t, xc, query, pairs, state = fetch
        dmix_b, dattn, dy, dz, message = run_kernel(
            gate_back_kernel,
            [
                normed_kept, shape_of((ROWS, HD), bf16), shape_of((ROWS, XLOC)), shape_of((ROWS, XLOC), bf16),
                shape_of((MSG, NSTATE), bf16),
            ],
            flags, *passed(dmix_parts), out_weight, z, ssm_y, shared, rates, rates_t, table,
            scratch=[pltpu.VMEM((ROWS, XLOC), f32), pltpu.VMEM((ROWS, 512), f32)],
        )
        after = tuple(along_ctx(message, -ahead) for ahead in (1, 2, 3))
        early, mine, theirs = run_kernel(
            attention_back_kernel,
            [kept((ROWS, 512), bf16), shape_of((4 * ROWS, HD)), shape_of((4 * ROWS, HD), bf16)],
            flags, dattn, dz, query, pairs, stored(log_total), table, seg_rows,
        )
        got = other_core(theirs)
        dx, dshared, drates, dskip = run_kernel(
            intra_back_kernel,
            [kept((ROWS, XLOC)), kept((ROWS, 2 * NSTATE)), kept((ROWS, 256)), kept((1, XLOC))],
            flags, dy, xc, shared, rates, rates_t, table, seg_rows, state, small[layer],
            scratch=[pltpu.VMEM((128, ROWS), f32), pltpu.VMEM((ROWS, 128), f32)],
        )
        got, dx = lax.optimization_barrier((got, dx))
        dkv = parts_from(mine, got, along_ctx, -1)
        if last:
            outer = weight_gradients([(dmix_b, cat)], 2560, 512, 3, outer)
            outer = weight_gradients([(normed_b, early)], 2560, 512, 4, outer)
            after, dkv, outer, ffn_sum = together(after, dkv, outer, ffn_sum)
            lower = lax.psum_scatter(outer, ("fsdp", "ctx"), scatter_dimension=0, tiled=True)
        else:
            outer = weight_gradients([(dmix_b, cat), (normed_b, early)], 2048, 1024, 1)
            after, dkv, outer = together(after, dkv, outer)
        packed_grads, dxpre, edge_x, gconv_x, ddt, gheads = run_kernel(
            state_back_kernel,
            [
                shape_of((8 * ROWS, 128), bf16), kept((ROWS, XLOC)), shape_of((8, XLOC)), kept((8, XLOC)),
                kept((ROWS, 128)), kept((8, 128)),
            ],
            flags, *map(stored, after), shared, xc, rates, stored(rates_t_kept), table, state, stored(small[layer]), stored(dtn), stored(dx), stored(dshared), stored(drates), *map(stored, dkv), stored(x_ext),
            scratch=[pltpu.VMEM((272, XLOC), f32), pltpu.VMEM((ROWS, XLOC), f32), pltpu.VMEM((ROWS, 128), f32)],
        )
        edge_x = along_ctx(edge_x, -1)
        dshared_parts = parts_of_sum(packed_grads[: 4 * ROWS], packed_grads[4 * ROWS :], along_y, 1)
        dsh, edge_sh, gconv_sh = run_kernel(
            shared_back_kernel,
            [shape_of((ROWS, 128)), shape_of((8, 128)), kept((8, 128))],
            flags, *summands(dshared_parts), stored(shared_ext), table, small[layer],
            scratch=[pltpu.VMEM((272, 128), f32)],
        )
        edge_sh, proj_weight = together(
            along_ctx(edge_sh, -1), fetched(f"proj_again_{layer}", *proj_place[layer])
        )
        (late,) = run_kernel(
            late_kernel, [shape_of((ROWS, LATE), bf16)], flags, stored(dxpre), Columns(edge_x), dsh,
            Columns(edge_sh), stored(ddt),
        )
        parts = summed_rows([early, late], proj_weight)
        if not last:
            outer = weight_gradients([(normed_b, late)], 2048, LATE, 0, outer)
            parts, outer = together(parts, outer)
            mixer_sum = lax.psum_scatter(outer, ("fsdp", "ctx"), scatter_dimension=0, tiled=True)
        else:
            parts, mixer_sum = together(parts, mixer_sum)
        parts, kept_rows = together(parts, restored(f"norm1_{layer}", [grad_mid, hidden, inverse1]))
        grad_hidden, rounded, ggain1 = norm_back(parts, *kept_rows, gains[layer, 0])
        if last:
            dffn_parts = from_all(rounded)
        else:
            dffn_parts, (down_weight, gate_up_weight) = from_all(
                rounded, fetched_all("ffn_again", [down_place[layer - 1], gate_up_place[layer - 1]])
            )
            last_hidden1, last_act = hidden1, act_b
        (small_parts[layer],) = run_kernel(
            small_kernel, [shape_of((64, 128), bf16)],
            None, *map(stored, (ggain1, ggain2, gconv_sh, gconv_x, gheads, dskip)),
        )
    small_all = jnp.concatenate(small_parts, axis=0)
    owned = owned_gradients([(normed_b, late)], small_all)
    owned = lax.all_to_all(owned, ("fsdp", "ctx"), 0, 0, tiled=True)
    (input_grad,) = run_kernel(natural_kernel, [kept((ROWS, model))], flags, *passed(dffn_parts))
    last_act, down_weight, _ = together(last_act, fetched("down_last", *down_place[1]), small_parts[0])
    (layer_out,) = run_kernel(
        output_kernel, [shape_of((SHARE, model), bf16)], None,
        stored(last_hidden1), *summands(summed_rows([last_act], down_weight)),
    )
    (layer_out,) = run_kernel(natural_kernel, [normed_kept], flags, *passed(from_all(layer_out)))
    def pair_of(width):
        return shape_of((layers, model // 16, width))

    upper_late = mixer_sum[:, 0:LATE]
    upper_shared = from_all(mixer_sum[:, XLOC:512])
    owned, layer_out, input_grad, upper_shared = together(owned, layer_out, input_grad, upper_shared)
    over_tp, late_sum, gconv_x, gheads = run_kernel(
        block_sum_kernel,
        [
            shape_of((224, 128), bf16), shape_of((model // 16, LATE)), shape_of((layers * (CONV + 1), XLOC)),
            shape_of((8, 128)),
        ],
        None, Columns(owned),
    )
    over_tp = from_all(over_tp)
    lower, over_tp = together(lower, over_tp)
    grad_attn, grad_ssm, grad_gate, grad_up, grad_down, grad_query, grad_z = run_kernel(
        early_outputs_kernel,
        [
            *(kept((layers, model // 16, width)) for width in (128, 384, 512, 512, 512, 128)),
            pair_of(XLOC),
        ],
        None, Columns(lower), Columns(ffn_sum), Columns(mixer_sum),
    )
    grad_zx, grad_dt, grad_shared, ggains1, ggains2, gconv_bc = run_kernel(
        last_outputs_kernel,
        [
            shape_of((layers, model // 16, 2, XLOC)), pair_of(HLOC), pair_of(1024), shape_of((layers, model)),
            shape_of((layers, model)), shape_of((layers * (CONV + 1), 512)),
        ],
        flags, *passed(over_tp), *passed(upper_shared), late_sum, Columns(upper_late), grad_z,
        scratch=[pltpu.VMEM((16, 224, 128), f32)],
    )
    gconv_x = gconv_x.reshape(layers, CONV + 1, XLOC)
    gconv_bc = gconv_bc.reshape(layers, CONV + 1, 512)
    gheads = gheads[: 3 * layers].reshape(layers, 3, 128)[:, :, :HLOC]
    return (
        layer_out[None],
        input_grad[None],
        grad_query,
        grad_shared,
        grad_zx,
        grad_dt,
        grad_attn,
        grad_ssm,
        grad_gate,
        grad_up,
        grad_down,
        ggains1,
        gconv_x,
        gconv_bc,
        gheads[:, :2],
        ggains2,
        gheads[:, 2],
    )


def solution(mesh):
    columns = P(None, ("fsdp", "ctx"), "tp")
    rows = P("fsdp", "ctx", None)
    return jax.shard_map(
        body,
        mesh=mesh,
        in_specs=(
            rows, rows, P("fsdp", None), columns, P(None, ("fsdp", "ctx"), None),
            P(None, ("fsdp", "ctx"), None, "tp"), columns, columns, columns, columns, columns, columns,
            P(), P(None, None, "tp"), P(), P(None, None, "tp"),
        ),
        out_specs=(
            rows, rows, columns, P(None, ("fsdp", "ctx"), None), P(None, ("fsdp", "ctx"), None, "tp"),
            columns, columns, columns, columns, columns, columns,
            P(), P(None, None, "tp"), P(), P(None, None, "tp"), P(), P(None, "tp"),
        ),
        check_vma=False,
    )
```

```python
import math
from functools import partial

import jax
import jax.numpy as jnp
from jax import lax
from jax.experimental import pallas as pl
from jax.experimental.pallas import tpu as pltpu
from jax.sharding import PartitionSpec as P

HD = 128
HP = 64
NSTATE = 256
CONV = 4
ROWS = 256
SHARE = 32
XLOC = 384
PROJ = 1152
LATE = 640
HLOC = 6
PAIRS = 3
SEQ_BLOCKS = 4
MSG = XLOC + 16
KV = 128
VMEM_LIMIT = 16 * 1024 * 1024

norm_eps = 1e-05
rope_base = 100000000000.0
bf16 = jnp.bfloat16
f32 = jnp.float32
i32 = jnp.int32


def along_y(value, steps):
    pairs = [(i, ((i // 2 + steps) % 4) * 2 + i % 2) for i in range(8)]
    return lax.ppermute(value, "tp", pairs)


def other_core(value):
    return lax.ppermute(value, "tp", [(i, i ^ 1) for i in range(8)])


def along_ctx(value, steps):
    first, last = max(0, -steps), min(4, 4 - steps)
    return lax.ppermute(value, "ctx", [(i, i + steps) for i in range(first, last)])


def ring(value, axis, steps):
    return lax.ppermute(value, axis, [(i, (i + steps) % 4) for i in range(4)])


def from_all(value, beside=None):
    half = [value] + [along_y(value, -k) for k in (1, 2, 3)]
    if beside is not None:
        half[1], beside = lax.optimization_barrier((half[1], beside))
    parts = tuple(half + [other_core(part) for part in half])
    return parts if beside is None else (parts, beside)


def dot_nn(a, b):
    return jnp.dot(a, b, preferred_element_type=f32)


def dot_nt(a, b):
    return lax.dot_general(a, b, (((1,), (1,)), ((), ())), preferred_element_type=f32)


def dot_tn(a, b):
    return lax.dot_general(a, b, (((0,), (0,)), ((), ())), preferred_element_type=f32)


def shape_of(shape, dtype=f32):
    return jax.ShapeDtypeStruct(shape, dtype)


class Columns:
    def __init__(self, array, block=0, width=None, rows=None, keep=False):
        self.array, self.block, self.keep = array, block, keep
        self.shape = (rows or array.shape[0],) + array.shape[1:-1] + (width or array.shape[-1],)

    def spec(self):
        place = (0,) * (len(self.shape) - 1) + (self.block,)
        return pl.BlockSpec(self.shape, lambda i: place, pipeline_mode=pl.Buffered(1))


class Layer:
    def __init__(self, array, layer):
        self.array, self.layer, self.keep = array, layer, True
        self.shape = (1,) + array.shape[1:]

    def spec(self):
        place = (self.layer,) + (0,) * (len(self.shape) - 1)
        return pl.BlockSpec(self.shape, lambda i: place, pipeline_mode=pl.Buffered(1))


def stored(array):
    return Columns(array, keep=True)


def summands(parts):
    return [stored(parts[0])] + passed(parts[1:])


def passed(arrays):
    return [Columns(array) for array in arrays]


def kept(shape, dtype=f32):
    return pltpu.HBM(shape, dtype)


def fetch_kernel(places, *refs):
    count = len(places)
    sources, outs, sems = refs[:count], refs[count : 2 * count], refs[-1]
    copies = []
    for (start, pieces), source, out in zip(places, sources, outs):
        rows, width = out.shape[0] // pieces, out.shape[1]
        for index in range(pieces):
            own = pl.ds(rows * index, rows)
            copies.append(
                pltpu.make_async_copy(
                    source.at[own, pl.ds(start, width)], out.at[own, :], sems.at[len(copies)]
                )
            )
    for copy in copies:
        copy.start()
    for copy in copies:
        copy.wait()


def fetched_all(name, sources):
    places = [(start, 4 if array.shape[0] == 2048 and width > 128 else 1) for array, start, width in sources]
    whole = pl.BlockSpec(memory_space=pltpu.VMEM)
    return pl.pallas_call(
        partial(fetch_kernel, places),
        name=name,
        out_shape=tuple(pltpu.VMEM((array.shape[0], width), array.dtype) for array, _, width in sources),
        in_specs=[pl.BlockSpec(memory_space=pltpu.HBM)] * len(sources),
        out_specs=tuple(whole for _ in sources),
        scratch_shapes=[pltpu.SemaphoreType.DMA((sum(pieces for _, pieces in places),))],
        compiler_params=pltpu.CompilerParams(vmem_limit_bytes=VMEM_LIMIT),
        cost_estimate=pl.CostEstimate(
            flops=0, bytes_accessed=sum(2 * array.shape[0] * width for array, _, width in sources), transcendentals=0
        ),
    )(*(pltpu.with_memory_space_constraint(array, pltpu.HBM) for array, _, _ in sources))


def fetched(name, array, start, width):
    return fetched_all(name, [(array, start, width)])[0]


def restored(name, arrays):
    return fetched_all(name, [(array, 0, array.shape[1]) for array in arrays])


def run_kernel(kernel, outs, flags, *args, scratch=(), us=1.0):
    whole = pl.BlockSpec(memory_space=pltpu.VMEM)
    own = [isinstance(arg, (Columns, Layer)) for arg in args]
    specs, arrays, out_specs = [], [], []
    for arg, copied in zip(args, own):
        specs.append(arg.spec() if copied else whole)
        array = arg.array if copied else arg
        arrays.append(pltpu.with_memory_space_constraint(array, pltpu.HBM) if copied and arg.keep else array)
    for out in outs:
        in_vmem = isinstance(out, jax.ShapeDtypeStruct)
        out_specs.append(whole if in_vmem else pl.BlockSpec(out.shape, lambda i, n=len(out.shape): (0,) * n))
        own.append(not in_vmem)
    moved = sum(2 * math.prod(arg.shape) for arg in args) + sum(2 * math.prod(o.shape) for o in outs)
    if flags is not None:
        specs = [pl.BlockSpec(memory_space=pltpu.SMEM)] + specs
        arrays = [flags] + arrays
    return pl.pallas_call(
        kernel,
        grid=(1,) if any(own) else (),
        out_shape=tuple(outs),
        in_specs=specs,
        out_specs=tuple(out_specs),
        scratch_shapes=list(scratch),
        compiler_params=pltpu.CompilerParams(vmem_limit_bytes=VMEM_LIMIT),
        cost_estimate=pl.CostEstimate(flops=int(us * 1e9), bytes_accessed=moved, transcendentals=0),
    )(*arrays)


def local_block(flags, natural):
    return pl.multiple_of(flags[8 + natural] * SHARE, SHARE)


def rank_block(flags, rank):
    return pl.multiple_of(flags[16 + rank] * ROWS, ROWS)


def lane_index(shape):
    return lax.broadcasted_iota(i32, shape, len(shape) - 1)


def spread(columns, pair):
    low = lane_index((1, 128)) < HP
    return jnp.where(low, columns[:, 2 * pair : 2 * pair + 1], columns[:, 2 * pair + 1 : 2 * pair + 2])


def lanes_of(pair):
    return slice(128 * pair, 128 * pair + 128)


def turned(value, table, sign):
    return value * table[:, 0:128] + sign * (pltpu.roll(value, 64, 1) * table[:, 128:256])


def segments(table):
    return table[:, 259:260]


def sigmoid(v):
    return 1.0 / (1.0 + jnp.exp(-v))


def softplus(v):
    return jnp.maximum(v, 0.0) + jnp.log1p(jnp.exp(-jnp.abs(v)))


def conv_sum(ext, table, weight):
    total = weight[CONV : CONV + 1, :] + ext[8 : 8 + ROWS, :] * weight[3:4, :]
    for tap in range(CONV - 1):
        total = total + table[:, 256 + tap : 257 + tap] * ext[5 + tap : 5 + tap + ROWS, :] * weight[tap : tap + 1, :]
    return total


def conv_back(grad_out, ext, table, weight, work, grad_ref, edge_ref, gweight_ref):
    total = conv_sum(ext, table, weight)
    sig = sigmoid(total)
    grad = grad_out * sig * (1.0 + total * (1.0 - sig))
    width = grad.shape[1]
    gweight_ref[...] = jnp.zeros((8, width), f32)
    gweight_ref[CONV : CONV + 1, :] = jnp.sum(grad, axis=0, keepdims=True)
    gweight_ref[3:4, :] = jnp.sum(grad * ext[8 : 8 + ROWS, :], axis=0, keepdims=True)
    work[0:8, :] = jnp.zeros((8, width), f32)
    work[264:272, :] = jnp.zeros((8, width), f32)
    own = grad * weight[3:4, :]
    edge = jnp.zeros((8, width), f32)
    for tap in range(CONV - 1):
        part = grad * table[:, 256 + tap : 257 + tap]
        gweight_ref[tap : tap + 1, :] = jnp.sum(
            part * ext[5 + tap : 5 + tap + ROWS, :], axis=0, keepdims=True
        )
        work[8:264, :] = part * weight[tap : tap + 1, :]
        own = own + work[11 - tap : 11 - tap + ROWS, :]
        edge = edge + work[3 - tap : 11 - tap, :]
    grad_ref[...] = own
    edge_ref[...] = edge


def pack_kernel(place, *refs):
    out, at, index = refs[-1], 0, 0
    while index < len(refs) - 1:
        ref = refs[index]
        if len(ref.shape) == 4:
            out[:, at : at + XLOC] = ref[0, :, 0, :]
            out[:, at + XLOC : at + 512] = refs[index + 1][0]
            out[:, at + 512 : at + 896] = ref[0, :, 1, :]
            at, index = at + 896, index + 2
            continue
        width = min(ref.shape[2], 512)
        if width == HLOC:
            out[:, at : at + 128] = jnp.zeros((out.shape[0], 128), bf16)
            out[:, at : at + HLOC] = ref[0]
            width = 128
        elif ref.shape[2] == 1024:
            width = 128
            out[:, at : at + width] = ref[0, :, pl.ds(pl.multiple_of(place[0] * 128, 128), 128)]
        else:
            out[:, at : at + width] = ref[0]
        at, index = at + width, index + 1


def first_kernel(flags, rows, cotangent, gain, normed, inverse, hidden_kept, grads, grad):
    for block in range(8):
        own = slice(SHARE * block, SHARE * (block + 1))
        from_rows = pl.ds(pl.multiple_of(flags[24 + block] * SHARE, SHARE), SHARE)
        wide = rows[0, from_rows, :].astype(f32)
        scale = lax.rsqrt(jnp.mean(wide * wide, axis=1, keepdims=True) + norm_eps)
        normed[own, :] = (wide * scale * gain[0:1, :]).astype(bf16)
        grads[own, :] = cotangent[0, from_rows, :]
        if block == 0:
            hidden_kept[...] = wide
            inverse[...] = jnp.broadcast_to(scale, inverse.shape)
            grad[...] = cotangent[0, from_rows, :].astype(f32)


def joined(parts):
    return parts[0][...] if len(parts) == 1 else jnp.concatenate([part[...] for part in parts], axis=0)


def proj_kernel(flags, *refs):
    parts, (weight, table, normed, z, z_kept, xs, query, query_kept, dtn, dtn_kept, work) = refs[:-11], refs[-11:]
    rows = joined(parts)
    normed[...] = rows
    work[...] = dot_nn(rows, weight[...])
    for block in range(8):
        own = slice(SHARE * block, SHARE * (block + 1))
        from_rows = pl.ds(local_block(flags, block), SHARE)
        for out in (z, z_kept):
            out[own, :] = work[from_rows, 0:XLOC]
        xs[own, :] = work[from_rows, 512:1024]
        head = turned(work[from_rows, XLOC:512], table[own, :], 1.0).astype(bf16)
        for out in (query, query_kept):
            out[own, :] = head
        for out in (dtn, dtn_kept):
            out[own, :] = work[from_rows, 1024:PROJ]


def shared_kernel(flags, xs, halo, table, small, out, ext):
    own = xs[:, XLOC:512]
    ext[0:8, :] = halo[:, XLOC:512]
    ext[8 : 8 + ROWS, :] = own
    total = conv_sum(ext, table, small[:, XLOC:512])
    rank = flags[0]
    out[...] = jnp.where(
        rank < 2, turned(own, table, 1.0), jnp.where(rank < 4, own, total * sigmoid(total))
    ).astype(bf16)


def prep_kernel(xs, dtn, halo, table, small, ext, xc, xc_kept, rates, rates_kept, rates_t, rates_t_kept):
    ext[0:8, :] = halo[:, 0:XLOC]
    ext[8 : 8 + ROWS, :] = xs[:, 0:XLOC]
    total = conv_sum(ext, table, small[:, 0:XLOC])
    for out in (xc, xc_kept):
        out[...] = total * sigmoid(total)
    params = small[:, 512:640]
    rate = softplus(dtn[...] + params[1:2, :])
    logs = -jnp.exp(params[0:1, :]) * rate
    rows = lax.broadcasted_iota(i32, (ROWS, ROWS), 0)
    lower = (rows >= lane_index((ROWS, ROWS))).astype(f32)
    running = jnp.dot(lower, logs, precision=lax.Precision.HIGHEST, preferred_element_type=f32)
    for out in (rates, rates_kept):
        out[:, 0:128] = rate
        out[:, 128:256] = running
    rate_t, running_t = rate.T[0:8, :], running.T[0:8, :]
    for out in (rates_t, rates_t_kept):
        out[0:8, :] = rate_t
        out[8:16, :] = running_t


def block_decays(flags, rates_t):
    kept = jnp.where(flags[4] == flags[5], 1.0, 0.0)
    return jnp.exp(rates_t[8:16, ROWS - 1 : ROWS]) * kept


def decay_rows(flags, rates_t):
    rows = jnp.broadcast_to(block_decays(flags, rates_t), (8, NSTATE))
    return jnp.concatenate([rows, jnp.zeros((8, NSTATE), f32)], axis=0).astype(bf16)


def weights_in(rates, table):
    last = rates[ROWS - 1 : ROWS, 128:256]
    gap = jnp.exp(last - rates[:, 128:256]) * table[:, 261:262]
    return gap, gap * rates[:, 0:128]


def rank_columns(flags, shared, first):
    return jnp.concatenate(
        [shared[pl.ds(rank_block(flags, rank), ROWS), :] for rank in (first, first + 1)], axis=1
    )


def inject_of(flags, shared):
    return rank_columns(flags, shared, 4)


def readout_of(flags, shared):
    return rank_columns(flags, shared, 6)


def carry_of(rates, table):
    return jnp.exp(rates[:, 128:256]) * table[:, 260:261]


def state_kernel(flags, s0, s1, s2, s3, s4, s5, s6, s7, xc, rates, rates_t, table, out, shared, shared_kept):
    for index, part in enumerate((s0, s1, s2, s3, s4, s5, s6, s7)):
        shared[ROWS * index : ROWS * (index + 1), :] = part[...]
        shared_kept[ROWS * index : ROWS * (index + 1), :] = part[...]
    inject = inject_of(flags, shared)
    _, weight = weights_in(rates, table)
    for pair in range(PAIRS):
        weighted = (xc[:, lanes_of(pair)] * spread(weight, pair)).astype(bf16)
        out[KV + 128 * pair : KV + 128 * (pair + 1), :] = dot_tn(weighted, inject).astype(bf16)
    out[KV + XLOC : KV + MSG, :] = decay_rows(flags, rates_t)
    half = shared[pl.ds(rank_block(flags, 2 * flags[2] + flags[1] // 2), ROWS), :]
    out[0:KV, :] = jnp.concatenate([half[0:128], half[128:256]], axis=1)


def halves_kernel(msg1, msg2, msg3, out):
    for index, msg in enumerate((msg1, msg2, msg3)):
        out[KV * index : KV * (index + 1), :] = msg[...]


def allowed_pairs(table, seg_rows):
    rows = lax.broadcasted_iota(i32, (ROWS, ROWS), 0)
    return (rows >= lane_index((ROWS, ROWS))) & (segments(table) == seg_rows[0:1, :])


def head_decay(allowed, rates, rates_t, head):
    gap = rates[:, 128 + head : 129 + head] - rates_t[8 + head : 9 + head, :]
    return jnp.where(allowed, jnp.exp(jnp.where(allowed, gap, 0.0)), 0.0)


def intra_kernel(flags, shared, xc, rates, rates_t, table, seg_rows, small, out):
    inject, readout = inject_of(flags, shared), readout_of(flags, shared)
    both = dot_nt(readout, inject)
    allowed = allowed_pairs(table, seg_rows)
    low = lane_index((1, 128)) < HP
    for pair in range(PAIRS):
        x = xc[:, lanes_of(pair)]
        xb = x.astype(bf16)
        heads = []
        for head in (2 * pair, 2 * pair + 1):
            decay = head_decay(allowed, rates, rates_t, head)
            heads.append(dot_nn((both * decay * rates_t[head : head + 1, :]).astype(bf16), xb))
        out[:, lanes_of(pair)] = jnp.where(low, heads[0], heads[1]) + spread(small[2:3, 512:640], pair) * x


def keys_values(flags, shared, halves, swapped):
    head, first = flags[1] // 2, flags[2] == 0
    pairs = [
        (
            shared[pl.ds(rank_block(flags, head), ROWS), :],
            shared[pl.ds(rank_block(flags, 2 + head), ROWS), :],
        )
    ]
    for index, half in enumerate(halves):
        packed = half[...], swapped[KV * index : KV * (index + 1), :]
        mine, theirs = (jnp.concatenate([part[:, 0:128], part[:, 128:256]], axis=0) for part in packed)
        pairs.append((jnp.where(first, mine, theirs), jnp.where(first, theirs, mine)))
    return pairs


def masked_scores(query, pairs, table, seg_rows):
    parts = []
    for block, (keys, _) in enumerate(pairs):
        score = dot_nt(query, keys) * HD ** (-0.5)
        keep = segments(table) == seg_rows[block : block + 1, :]
        if block == 0:
            rows = lax.broadcasted_iota(i32, (ROWS, ROWS), 0)
            keep = keep & (rows >= lane_index((ROWS, ROWS)))
        parts.append(jnp.where(keep, score, -1e30))
    return parts


def attention_kernel(flags, query, shared, h1, h2, h3, swapped, table, seg_rows, out, out_kept, log_total, kept):
    pairs = keys_values(flags, shared, (h1, h2, h3), swapped)
    for block, (keys, values) in enumerate(pairs):
        kept[ROWS * block : ROWS * (block + 1), 0:HD] = keys
        kept[ROWS * block : ROWS * (block + 1), HD : 2 * HD] = values
    parts = masked_scores(query[...], pairs, table, seg_rows)
    top = parts[0].max(axis=1, keepdims=True)
    for part in parts[1:]:
        top = jnp.maximum(top, part.max(axis=1, keepdims=True))
    parts = [jnp.exp(part - top) for part in parts]
    total = sum(part.sum(axis=1, keepdims=True) for part in parts)
    inverse = 1.0 / total
    result = jnp.zeros((ROWS, HD), f32)
    for part, (_, values) in zip(parts, pairs):
        result = result + dot_nn((part * inverse).astype(bf16), values)
    rounded = result.astype(bf16)
    for block in range(8):
        for ref in (out, out_kept):
            ref[pl.ds(local_block(flags, block), SHARE), :] = rounded[SHARE * block : SHARE * (block + 1), :]
    log_total[...] = jnp.broadcast_to(top + jnp.log(total), (ROWS, HD))


def chained(first, second, third, base):
    rows1 = first[base + XLOC : base + MSG, :].astype(f32)
    rows2 = second[base + XLOC : base + MSG, :].astype(f32)
    parts = []
    for head in range(HLOC):
        own = slice(base + HP * head, base + HP * head + HP)
        older = second[own, :].astype(f32) + rows2[head : head + 1, :] * third[own, :].astype(f32)
        parts.append(first[own, :].astype(f32) + rows1[head : head + 1, :] * older)
    return jnp.concatenate(parts, axis=0)


def carry_kernel(flags, msg1, msg2, msg3, shared, rates, table, intra, z, state, ssm_y, cat, cat_kept):
    entering = chained(msg1, msg2, msg3, KV)
    state[...] = entering
    from_state = dot_nt(readout_of(flags, shared), entering.astype(bf16))
    carry = carry_of(rates, table)
    for pair in range(PAIRS):
        own = lanes_of(pair)
        y = intra[:, own] + spread(carry, pair) * from_state[:, own]
        ssm_y[:, own] = y
        gate = z[:, own]
        gated = (y * gate * sigmoid(gate)).astype(bf16)
        for block in range(8):
            for out in (cat, cat_kept):
                out[pl.ds(local_block(flags, block), SHARE), 128 * pair : 128 * (pair + 1)] = gated[
                    SHARE * block : SHARE * (block + 1), :
                ]


def gate_back_kernel(
    flags, p0, p1, p2, p3, p4, p5, p6, p7, weight, z, ssm_y, shared, rates, rates_t, table,
    dmix, dattn, dy, dz, msg, work, local,
):
    rows = joined((p0, p1, p2, p3, p4, p5, p6, p7))
    dmix[...] = rows
    local[...] = dot_nn(rows, weight[...])
    for block in range(8):
        own = slice(SHARE * block, SHARE * (block + 1))
        from_rows = pl.ds(local_block(flags, block), SHARE)
        dattn[own, :] = local[from_rows, 0:128].astype(bf16)
        work[own, :] = local[from_rows, 128:512]
    readout = readout_of(flags, shared)
    carry = carry_of(rates, table)
    for pair in range(PAIRS):
        own = lanes_of(pair)
        gate, grad = z[:, own], work[:, own]
        sig = sigmoid(gate)
        y_grad = grad * gate * sig
        dy[:, own] = y_grad
        dz[:, own] = (grad * ssm_y[:, own] * sig * (1.0 + gate * (1.0 - sig))).astype(bf16)
        msg[own, :] = dot_tn((y_grad * spread(carry, pair)).astype(bf16), readout).astype(bf16)
    msg[XLOC:MSG, :] = decay_rows(flags, rates_t)


def attention_back_kernel(
    flags, dattn, dz, query, kept, log_total, table, seg_rows,
    early, mine, theirs,
):
    pairs = []
    for block in range(SEQ_BLOCKS):
        own = slice(ROWS * block, ROWS * (block + 1))
        pairs.append((kept[own, 0:HD], kept[own, HD : 2 * HD]))
    first = flags[2] == 0
    q = query[...]
    grad = dattn[...]
    parts = masked_scores(q, pairs, table, seg_rows)
    logs = log_total[:, 0:1]
    probs = [jnp.exp(part - logs) for part in parts]
    grads = [dot_nt(grad, values) for _, values in pairs]
    inner = sum((p * g).sum(axis=1, keepdims=True) for p, g in zip(probs, grads))
    total = jnp.zeros((ROWS, HD), f32)
    for block, (p, g, (keys, _)) in enumerate(zip(probs, grads, pairs)):
        own = slice(ROWS * block, ROWS * (block + 1))
        score = (p * (g - inner)).astype(bf16)
        total = total + dot_nn(score, keys)
        dkeys = dot_tn(score, q) * HD ** (-0.5)
        dvalues = dot_tn(p.astype(bf16), grad)
        mine[own, :] = jnp.where(first, dkeys, dvalues)
        theirs[own, :] = jnp.where(first, dvalues, dkeys).astype(bf16)
    total = total * HD ** (-0.5)
    dq = turned(total, table, -1.0).astype(bf16)
    for block in range(8):
        own = slice(SHARE * block, SHARE * (block + 1))
        to_rows = pl.ds(local_block(flags, block), SHARE)
        early[to_rows, 0:XLOC] = dz[own, :]
        early[to_rows, XLOC:512] = dq[own, :]


def intra_back_kernel(
    flags, dy, xc, shared, rates, rates_t, table, seg_rows, state, small,
    dx, dshared, drates, dskip, row_sums, dcum,
):
    inject, readout = inject_of(flags, shared), readout_of(flags, shared)
    both = dot_nt(readout, inject)
    allowed = allowed_pairs(table, seg_rows)
    low = lane_index((1, 128)) < HP
    carry = carry_of(rates, table)
    entering = state[...].astype(bf16)
    from_state = dot_nt(readout, entering)
    dboth = jnp.zeros((ROWS, ROWS), f32)
    row_sums[...] = jnp.zeros((128, ROWS), f32)
    dcum[...] = jnp.zeros((ROWS, 128), f32)
    carried = []
    for pair in range(PAIRS):
        own = lanes_of(pair)
        x = xc[:, own]
        xb = x.astype(bf16)
        grad = dy[:, own]
        dskip[:, own] = jnp.sum(grad * x, axis=0, keepdims=True)
        carried.append((grad * spread(carry, pair)).astype(bf16))
        through = grad * from_state[:, own]
        total = spread(small[2:3, 512:640], pair) * grad
        for head in (2 * pair, 2 * pair + 1):
            mine = low if head % 2 == 0 else jnp.logical_not(low)
            decay = head_decay(allowed, rates, rates_t, head)
            steps = rates_t[head : head + 1, :]
            head_grad = jnp.where(mine, grad, 0.0).astype(bf16)
            dmix = dot_nt(head_grad, xb)
            kept = dmix * decay
            dboth = dboth + kept * steps
            mixed = both * decay
            total = total + dot_tn((mixed * steps).astype(bf16), head_grad)
            passed = dmix * mixed
            row_sums[head : head + 1, :] = jnp.sum(passed, axis=0, keepdims=True)
            dcum[:, head : head + 1] = jnp.sum(passed * steps, axis=1, keepdims=True) + carry[
                :, head : head + 1
            ] * jnp.sum(jnp.where(mine, through, 0.0), axis=1, keepdims=True)
        dx[:, own] = total
    columns = row_sums[...].T
    drates[:, 0:128] = columns
    drates[:, 128:256] = dcum[...] - rates[:, 0:128] * columns
    dboth_b = dboth.astype(bf16)
    dshared[:, NSTATE:] = dot_nn(dboth_b, inject) + dot_nn(jnp.concatenate(carried, axis=1), entering)
    dshared[:, 0:NSTATE] = dot_tn(dboth_b, readout)


def packed_back_kernel(
    flags, msg1, msg2, msg3, shared, xc, rates, table, dshared, kv0, kv1, kv2, kv3, packed, state_grad,
):
    later = chained(msg1, msg2, msg3, 0)
    state_grad[...] = later
    _, weights = weights_in(rates, table)
    weighted = [(xc[:, lanes_of(pair)] * spread(weights, pair)).astype(bf16) for pair in range(PAIRS)]
    weighted = jnp.concatenate(weighted, axis=1)
    dinject = (dshared[:, 0:NSTATE] + dot_nn(weighted, later.astype(bf16))).astype(bf16)
    dreadout = dshared[:, NSTATE:].astype(bf16)
    packed[...] = jnp.zeros((8 * ROWS, 128), bf16)
    grads = kv0[...] + kv1[...].astype(f32) + kv2[...].astype(f32) + kv3[...].astype(f32)
    owner = 2 * flags[2] + flags[1] // 2
    packed[pl.ds(rank_block(flags, owner), ROWS), :] = grads.astype(bf16)
    packed[pl.ds(rank_block(flags, 4), ROWS), :] = dinject[:, 0:128]
    packed[pl.ds(rank_block(flags, 5), ROWS), :] = dinject[:, 128:256]
    packed[pl.ds(rank_block(flags, 6), ROWS), :] = dreadout[:, 0:128]
    packed[pl.ds(rank_block(flags, 7), ROWS), :] = dreadout[:, 128:256]


def state_back_kernel(
    flags, later, shared, xc, rates, rates_t, table, state, small, dtn, dx, drates, ext,
    dxpre, edge, gweight, ddt, heads, work, dconv, sums,
):
    inject = inject_of(flags, shared)
    low = lane_index((1, 128)) < HP
    params = small[:, 512:640]
    gap, weights = weights_in(rates, table)
    from_later = dot_nt(inject, later[...].astype(bf16))
    products = later[...] * state[...]
    decays = block_decays(flags, rates_t)
    sums[...] = jnp.zeros((ROWS, 128), f32)
    for pair in range(PAIRS):
        own = lanes_of(pair)
        dconv[:, own] = dx[:, own] + spread(weights, pair) * from_later[:, own]
        through = xc[:, own] * from_later[:, own]
        for head in (2 * pair, 2 * pair + 1):
            mine = low if head % 2 == 0 else jnp.logical_not(low)
            sums[:, head : head + 1] = jnp.sum(jnp.where(mine, through, 0.0), axis=1, keepdims=True)
    dweights = sums[...]
    moved = dweights * weights
    last = jnp.sum(moved, axis=0, keepdims=True)
    lanes = lane_index((1, 128))
    for head in range(HLOC):
        total = jnp.sum(
            jnp.sum(products[HP * head : HP * head + HP, :], axis=0, keepdims=True), axis=1, keepdims=True
        )
        last = last + jnp.where(lanes == head, total * decays[head : head + 1, :], 0.0)
    rows = lax.broadcasted_iota(i32, (ROWS, 128), 0)
    dcums = drates[:, 128:256] - moved + jnp.where(rows == ROWS - 1, last, 0.0)
    square = lax.broadcasted_iota(i32, (ROWS, ROWS), 0)
    upper = (square <= lane_index((ROWS, ROWS))).astype(f32)
    dlogs = jnp.dot(upper, dcums, precision=lax.Precision.HIGHEST, preferred_element_type=f32)
    rate = -jnp.exp(params[0:1, :])
    dsteps = drates[:, 0:128] + dweights * gap + dlogs * rate
    ddts = dsteps * sigmoid(dtn[...] + params[1:2, :])
    ddt[...] = ddts
    heads[...] = jnp.zeros((8, 128), f32)
    heads[0:1, :] = jnp.sum(dlogs * rate * rates[:, 0:128], axis=0, keepdims=True)
    heads[1:2, :] = jnp.sum(ddts, axis=0, keepdims=True)
    conv_back(dconv[...], ext, table, small[:, 0:XLOC], work, dxpre, edge, gweight)


def shared_back_kernel(flags, part0, part1, part2, part3, ext, table, small, out, edge, gweight, work):
    grad = part0[...] + part1[...].astype(f32) + part2[...].astype(f32) + part3[...].astype(f32)
    conv_back(grad, ext, table, small[:, XLOC:512], work, out, edge, gweight)
    rank = flags[0]
    of_conv = jnp.where(rank < 4, 0.0, 1.0)
    edge[...] = edge[...] * of_conv
    gweight[...] = gweight[...] * of_conv
    out[...] = jnp.where(rank < 2, turned(grad, table, -1.0), jnp.where(rank < 4, grad, out[...]))


def late_kernel(flags, dxpre, edge_x, dsh, edge_sh, ddt, out):
    for block in range(8):
        own = slice(SHARE * block, SHARE * (block + 1))
        to_rows = pl.ds(local_block(flags, block), SHARE)
        x, sh = dxpre[own, :], dsh[own, :]
        if block == 7:
            pad = jnp.zeros((SHARE - 8, 128), f32)
            sh = sh + jnp.concatenate([pad, edge_sh[...]], axis=0)
            x = x + jnp.concatenate([jnp.zeros((SHARE - 8, XLOC), f32), edge_x[...]], axis=0)
        out[to_rows, 0:XLOC] = x.astype(bf16)
        out[to_rows, XLOC:512] = sh.astype(bf16)
        out[to_rows, 512:LATE] = jnp.where(lane_index((1, 128)) < HLOC, ddt[own, :], 0.0).astype(bf16)


def half_sum_kernel(own, other, keep, send1, send2, send3):
    rows = own.shape[0] // 4
    keep[...] = own[0:rows, :] + other[0:rows, :].astype(f32)
    for index, send in ((1, send1), (2, send2), (3, send3)):
        part = slice(rows * index, rows * (index + 1))
        send[...] = (own[part, :].astype(f32) + other[part, :].astype(f32)).astype(bf16)


def parts_of_sum(own, other, along, sign):
    return parts_from(own, other_core(other), along, sign)


def parts_from(own, got, along, sign):
    rows, width = own.shape[0] // 4, own.shape[1]
    sent = shape_of((rows, width), bf16)
    keep, *sends = run_kernel(half_sum_kernel, [kept((rows, width)), sent, sent, sent], None, own, Columns(got))
    return (keep,) + tuple(along(send, sign * k) for k, send in zip((1, 2, 3), sends))


def split_kernel(*refs):
    lefts, weight, own, other = refs[:-3], refs[-3], refs[-2], refs[-1]
    left = lefts[0][...] if len(lefts) == 1 else jnp.concatenate([ref[...] for ref in lefts], axis=1)
    result = dot_nt(left, weight[...])
    own[...] = result[: ROWS // 2]
    other[...] = result[ROWS // 2 :].astype(bf16)


def summed_rows(lefts, weight):
    model, width = weight.shape
    own, other = pl.pallas_call(
        split_kernel,
        grid=(model // 512,),
        out_shape=(shape_of((ROWS // 2, model)), shape_of((ROWS // 2, model), bf16)),
        in_specs=[pl.BlockSpec(left.shape, lambda i: (0, 0)) for left in lefts]
        + [pl.BlockSpec((512, width), lambda i: (i, 0))],
        out_specs=(
            pl.BlockSpec((ROWS // 2, 512), lambda i: (0, i)),
            pl.BlockSpec((ROWS // 2, 512), lambda i: (0, i)),
        ),
        compiler_params=pltpu.CompilerParams(vmem_limit_bytes=VMEM_LIMIT),
        cost_estimate=pl.CostEstimate(
            flops=2 * ROWS * model * width, bytes_accessed=2 * model * width, transcendentals=0
        ),
    )(*lefts, weight)
    return parts_of_sum(own, other, along_y, 1)


def gate_up_kernel(p0, p1, p2, p3, p4, p5, p6, p7, weight, normed, gate, up, act, act_kept):
    rows = joined((p0, p1, p2, p3, p4, p5, p6, p7))
    normed[...] = rows
    result = dot_nn(rows, weight[...])
    g, u = result[:, :512], result[:, 512:]
    gate[...] = g
    up[...] = u
    for out in (act, act_kept):
        out[...] = (g * sigmoid(g) * u).astype(bf16)


def gate_up_back_kernel(*refs):
    parts, (weight, gate, up, dffn, out) = refs[:-5], refs[-5:]
    rows = joined(parts)
    dffn[...] = rows
    dact = dot_nn(rows, weight[...])
    g = gate[...]
    sig = sigmoid(g)
    out[:, :512] = (dact * up[...] * sig * (1.0 + g * (1.0 - sig))).astype(bf16)
    out[:, 512:] = (dact * g * sig).astype(bf16)


def natural_kernel(flags, p0, p1, p2, p3, p4, p5, p6, p7, out):
    local = joined((p0, p1, p2, p3, p4, p5, p6, p7)).astype(out.dtype)
    for block in range(8):
        out[pl.ds(pl.multiple_of(flags[24 + block] * SHARE, SHARE), SHARE), :] = local[
            SHARE * block : SHARE * (block + 1), :
        ]


def add_norm_kernel(hidden, part0, part1, part2, part3, gain, out_kept, normed, inverse):
    total = hidden[...] + part0[...] + (
        part1[...].astype(f32) + part2[...].astype(f32) + part3[...].astype(f32)
    )
    out_kept[...] = total
    scale = lax.rsqrt(jnp.mean(total * total, axis=1, keepdims=True) + norm_eps)
    inverse[...] = jnp.broadcast_to(scale, inverse.shape)
    normed[...] = (total * scale * gain[...]).astype(bf16)


def add_norm(hidden, parts, gain):
    shape = hidden.shape
    return run_kernel(
        add_norm_kernel,
        [kept(shape), shape_of(shape, bf16), kept((shape[0], 128))],
        None, hidden, *summands(parts), gain[None],
    )


def output_kernel(hidden, part0, part1, part2, part3, out):
    total = hidden[...] + part0[...] + (
        part1[...].astype(f32) + part2[...].astype(f32) + part3[...].astype(f32)
    )
    out[...] = total.astype(bf16)


def norm_back_kernel(grad, part0, part1, part2, part3, hidden, inverse, gain, out, rounded, ggain):
    received = part0[...] + (part1[...].astype(f32) + part2[...].astype(f32) + part3[...].astype(f32))
    scale = inverse[:, 0:1]
    unit = hidden[...] * scale
    scaled = received * gain[...]
    ggain[...] = jnp.sum(received * unit, axis=0, keepdims=True)
    total = grad[...] + scale * (scaled - unit * jnp.mean(scaled * unit, axis=1, keepdims=True))
    out[...] = total
    rounded[...] = total.astype(bf16)


def norm_back(parts, grad, hidden, inverse, gain):
    shape = hidden.shape
    return run_kernel(
        norm_back_kernel,
        [kept(shape), shape_of(shape, bf16), kept((1, shape[1]))],
        None, grad, *summands(parts), hidden, inverse, gain[None],
    )


def gradient_kernel(pairs, *refs):
    out, at = refs[-1], 0
    for index in range(pairs):
        left, right = refs[2 * index], refs[2 * index + 1]
        width = right.shape[1]
        out[:, at : at + width] = dot_tn(left[...], right[...]).astype(bf16)
        at += width
    if at < out.shape[1]:
        out[:, at:] = jnp.zeros((out.shape[0], out.shape[1] - at), bf16)


def weight_gradients(pairs, total, block, index, buffer=None):
    rows, model = pairs[0][0].shape
    width = sum(right.shape[1] for _, right in pairs)
    specs, args = [], []
    for left, right in pairs:
        specs += [
            pl.BlockSpec((rows, 512), lambda i: (0, i)),
            pl.BlockSpec(right.shape, lambda i: (0, 0)),
        ]
        args += [left, right]
    aliases = {}
    kernel = partial(gradient_kernel, len(pairs))
    if buffer is not None:
        aliases = {len(args): 0}
        specs.append(pl.BlockSpec(memory_space=pltpu.HBM))
        args.append(buffer)

        def kernel(*refs):
            gradient_kernel(len(pairs), *refs[:-2], refs[-1])

    return pl.pallas_call(
        kernel,
        grid=(model // 512,),
        out_shape=pltpu.HBM((model, total), bf16),
        in_specs=specs,
        out_specs=pl.BlockSpec((512, block), lambda i: (i, index)),
        input_output_aliases=aliases,
        compiler_params=pltpu.CompilerParams(vmem_limit_bytes=VMEM_LIMIT),
        cost_estimate=pl.CostEstimate(
            flops=2 * rows * model * width, bytes_accessed=model * width * 2, transcendentals=0
        ),
    )(*args)


def owned_kernel(pairs, *refs):
    out, at = refs[-1], 0
    for pair in range(pairs):
        left, right = refs[2 * pair], refs[2 * pair + 1]
        result = dot_tn(left[...], right[...]).astype(bf16)
        width = right.shape[1]
        for index in range(2):
            out[index, :, at : at + width] = result[128 * index : 128 * (index + 1)]
        at += width
    if at < out.shape[2]:
        for index in range(2):
            out[index, :, at:] = refs[2 * pairs][...]


def owned_gradients(pairs, small=None):
    rows, model = pairs[0][0].shape
    width = sum(right.shape[1] for _, right in pairs)
    specs, args = [], []
    for left, right in pairs:
        block = right.block if isinstance(right, Columns) else 0
        specs += [
            pl.BlockSpec((rows, 256), lambda i: (0, i)),
            pl.BlockSpec(right.shape, lambda i, block=block: (0, block)),
        ]
        args += [left, right.array if isinstance(right, Columns) else right]
    if small is not None:
        specs.append(pl.BlockSpec(small.shape, lambda i: (0, 0)))
        args.append(small)
        width += small.shape[1]
    return pl.pallas_call(
        partial(owned_kernel, len(pairs)),
        grid=(model // 256,),
        out_shape=pltpu.HBM((16, model // 16, width), bf16),
        in_specs=specs,
        out_specs=pl.BlockSpec((2, model // 16, width), lambda i: (i, 0, 0)),
        compiler_params=pltpu.CompilerParams(vmem_limit_bytes=VMEM_LIMIT),
        cost_estimate=pl.CostEstimate(
            flops=2 * rows * model * width, bytes_accessed=model * width * 2, transcendentals=0
        ),
    )(*args)


def small_kernel(gain1, gain2, conv_sh, conv_x, heads, skip, out):
    out[...] = jnp.zeros(out.shape, bf16)
    for row in range(16):
        own = slice(128 * row, 128 * row + 128)
        out[row : row + 1, :] = gain1[:, own].astype(bf16)
        out[16 + row : 17 + row, :] = gain2[:, own].astype(bf16)
    out[32:37, :] = conv_sh[0:5, :].astype(bf16)
    for tap in range(CONV + 1):
        for pair in range(PAIRS):
            row = 37 + PAIRS * tap + pair
            out[row : row + 1, :] = conv_x[tap : tap + 1, lanes_of(pair)].astype(bf16)
    out[52:54, :] = heads[0:2, :].astype(bf16)
    lanes = lane_index((1, 128))
    sums = jnp.zeros((1, 128), f32)
    for pair in range(PAIRS):
        part = skip[:, lanes_of(pair)]
        for half in range(2):
            mine = (lanes < HP) if half == 0 else (lanes >= HP)
            total = jnp.sum(jnp.where(mine, part, 0.0), axis=1, keepdims=True)
            sums = sums + jnp.where(lanes == 2 * pair + half, total, 0.0)
    out[54:55, :] = sums.astype(bf16)


def owner_sum(values):
    total = values[0].astype(f32)
    for index in range(1, 16):
        total = total + values[index].astype(f32)
    return total


def block_sum_kernel(values, over_tp, late, conv_x, heads):
    whole = owner_sum(values)
    late[...] = whole[:, 0:LATE]
    total = whole[:, LATE + 128 : LATE + 256]
    over_tp[0:128, :] = whole[:, XLOC:512].astype(bf16)
    over_tp[128:256, :] = whole[:, LATE : LATE + 128].astype(bf16)
    over_tp[256:352, :] = jnp.zeros((96, 128), bf16)
    for layer in range(2):
        first = 64 * layer
        over_tp[256 + 48 * layer : 293 + 48 * layer, :] = total[first : first + 37, :].astype(bf16)
        for tap in range(CONV + 1):
            for pair in range(PAIRS):
                row = first + 37 + PAIRS * tap + pair
                conv_x[5 * layer + tap : 5 * layer + tap + 1, lanes_of(pair)] = total[row : row + 1, :]
        heads[3 * layer : 3 * layer + 3, :] = total[first + 52 : first + 55, :]


def weight_outputs_kernel(lower, upper, late, attn, ssm, gate, up, down, query, zx, dt):
    for layer, ref in ((0, lower), (1, upper)):
        for index, out in enumerate((gate, up, down)):
            out[layer] = ref[:, 512 * index : 512 * (index + 1)].astype(f32)
        attn[layer] = ref[:, 1536:1664].astype(f32)
        ssm[layer] = ref[:, 1664:2048].astype(f32)
        zx[layer, :, 0, :] = ref[:, 2048:2432].astype(f32)
        query[layer] = ref[:, 2432:2560].astype(f32)
    zx[0, :, 1, :] = late[:, 0:XLOC]
    zx[1, :, 1, :] = lower[:, 2560:2944].astype(f32)
    dt[0] = late[:, 512 : 512 + HLOC]
    dt[1] = lower[:, 3072 : 3072 + HLOC].astype(f32)


def tp_outputs_kernel(flags, *refs):
    parts, (shared, gains1, gains2, conv_bc, every) = refs[:8], refs[8:]
    total = jnp.zeros((96, 128), f32)
    for index, part in enumerate(parts):
        every[index] = part[...].astype(f32)
        total = total + part[256:352, :].astype(f32)
    for layer in range(2):
        for rank in range(8):
            own = slice(128 * rank, 128 * rank + 128)
            shared[layer, :, own] = every[flags[16 + rank], 128 * layer : 128 * layer + 128, :]
        for row in range(16):
            own = slice(128 * row, 128 * row + 128)
            at = 48 * layer + row
            gains1[layer : layer + 1, own] = total[at : at + 1, :]
            gains2[layer : layer + 1, own] = total[at + 16 : at + 17, :]
        for rank in range(4):
            part = every[flags[20 + rank], 288 + 48 * layer : 296 + 48 * layer, :]
            conv_bc[5 * layer : 5 * layer + 5, 128 * rank : 128 * rank + 128] = part[0:5, :]


def body(
    inputs, cotangent, segment_ids, w_query, w_shared, w_zx, w_dt, w_attn_out, w_ssm_out, w_gate, w_up, w_down,
    gains, conv_x, conv_bc, head_params,
):
    layers = w_query.shape[0]
    rank, ctx = lax.axis_index("tp"), lax.axis_index("ctx")
    y, core = rank // 2, rank % 2
    model = inputs.shape[2]

    def local_of(block_y, block_core):
        return jnp.where(block_core == core, 0, 4) + (block_y - y) % 4

    seg_all = segment_ids[0]
    first_row = ctx * ROWS
    padded = jnp.concatenate([jnp.full((CONV - 1,), -1, i32), seg_all])
    seg_ext = lax.dynamic_slice_in_dim(padded, first_row, ROWS + CONV - 1)
    seg_own = seg_ext[CONV - 1 :]
    blocks = seg_all.reshape(SEQ_BLOCKS, ROWS)
    seg_rows = jnp.stack(
        [
            jnp.where(ctx >= back, lax.dynamic_index_in_dim(blocks, jnp.maximum(ctx - back, 0), 0, False), -1)
            for back in range(SEQ_BLOCKS)
        ]
        + [jnp.full((ROWS,), -1, i32)] * 4
    ).astype(f32)
    naturals = jnp.arange(8, dtype=i32)
    flags = jnp.concatenate(
        [
            jnp.stack([rank, y, core, ctx, seg_ext[CONV - 2], seg_own[-1], rank, rank]).astype(i32),
            local_of(naturals % 4, naturals // 4).astype(i32),
            local_of(naturals // 2, naturals % 2).astype(i32),
            (jnp.where(naturals < 4, core, 1 - core) * 4 + (y + naturals) % 4).astype(i32),
        ]
    )

    half_width = HD // 2
    frequency = rope_base ** (-jnp.arange(half_width, dtype=f32) / half_width)
    places = (first_row + jnp.arange(ROWS, dtype=i32)).astype(f32)
    angles = places[:, None] * frequency[None, :]
    cosine, sine = jnp.cos(angles), jnp.sin(angles)
    marks = [seg_ext[tap : tap + ROWS] == seg_own for tap in range(CONV - 1)]
    marks += [seg_own, seg_own == seg_ext[CONV - 2], seg_own == seg_own[-1]]
    marks = jnp.pad(jnp.stack([mark.astype(f32) for mark in marks], axis=1), ((0, 0), (0, 122)))
    table = jnp.concatenate([cosine, cosine, -sine, sine, marks], axis=1)

    own_conv = jnp.maximum(rank - 4, 0) * 128
    small = []
    for layer in range(layers):
        rows = [conv_x[layer], lax.dynamic_slice_in_dim(conv_bc[layer], own_conv, 128, 1)]
        rows.append(jnp.pad(head_params[layer], ((0, 2), (0, 128 - HLOC))))
        small.append(jnp.pad(jnp.concatenate(rows, axis=1), ((0, 3), (0, 0))))

    def packed(*members):
        width = sum(
            {4: 2 * XLOC}.get(member.ndim, 128 if member.shape[2] in (1024, HLOC) else member.shape[2])
            for member, _ in members
        )
        (columns,) = run_kernel(
            pack_kernel,
            [shape_of((w_query.shape[1], width), bf16)],
            rank.astype(i32).reshape(1),
            *(Layer(member, layer) for member, layer in members),
        )
        return lax.all_gather(columns, ("fsdp", "ctx"), axis=0, tiled=True)

    def proj_members(layer):
        return [(member, layer) for member in (w_zx, w_query, w_shared, w_dt)]

    weight_a = packed(*proj_members(0), (w_attn_out, 0), (w_ssm_out, 0))
    weight_b = packed(*proj_members(1), (w_gate, 0), (w_up, 0), (w_down, 0))
    weight_c = packed((w_gate, 1), (w_up, 1), (w_down, 1), (w_attn_out, 1), (w_ssm_out, 1))
    proj_place = [(weight_a, 0, PROJ), (weight_b, 0, PROJ)]
    out_place = [(weight_a, PROJ, 512), (weight_c, 1536, 512)]
    gate_up_place = [(weight_b, PROJ, 1024), (weight_c, 0, 1024)]
    down_place = [(weight_b, PROJ + 1024, 512), (weight_c, 1024, 512)]

    def together(*values):
        return lax.optimization_barrier(values)

    weight_a, table, seg_rows, small = together(weight_a, table, seg_rows, small)
    normed_shape = shape_of((ROWS, model), bf16)
    normed_kept = kept((ROWS, model), bf16)
    normed_b, inverse1, hidden, dffn_b, grad_hidden = run_kernel(
        first_kernel,
        [normed_shape, kept((SHARE, 128)), kept((SHARE, model)), normed_kept, kept((SHARE, model))],
        flags, inputs, cotangent, gains[0],
    )
    weight_a, normed_b = together(weight_a, normed_b)
    proj_place[0] = (weight_a, 0, PROJ)
    out_place[0] = (weight_a, PROJ, 512)
    normed_parts, dffn_parts = (normed_b,), (dffn_b,)
    saved = []
    wide = shape_of((ROWS, 512))
    proj_weight = fetched("proj_0", *proj_place[0])
    for layer in range(layers):
        normed_b, z, z_kept, xs, query, query_kept, dtn, dtn_kept = run_kernel(
            proj_kernel,
            [
                normed_kept, shape_of((ROWS, XLOC)), kept((ROWS, XLOC)), wide, shape_of((ROWS, HD), bf16),
                kept((ROWS, HD), bf16), shape_of((ROWS, 128)), kept((ROWS, 128)),
            ],
            flags, *(passed(normed_parts) if layer > 0 else normed_parts), proj_weight, table,
            scratch=[pltpu.VMEM((ROWS, PROJ), f32)], us=3.3,
        )
        halo = along_ctx(xs[ROWS - 8 :], 1)
        shared_own, shared_ext = run_kernel(
            shared_kernel,
            [shape_of((ROWS, 128), bf16), kept((264, 128))],
            flags, xs, Columns(halo), table, small[layer],
        )
        prepared = run_kernel(
            prep_kernel,
            [
                kept((264, XLOC)), shape_of((ROWS, XLOC)), kept((ROWS, XLOC)), shape_of((ROWS, 256)),
                kept((ROWS, 256)), shape_of((16, ROWS)), kept((16, ROWS)),
            ],
            None, xs, dtn, Columns(halo), table, small[layer], us=1.5,
        )
        shared_parts, prepared = from_all(shared_own, prepared)
        x_ext, xc, xc_kept, rates, rates_kept, rates_t, rates_t_kept = prepared
        message, shared, shared_kept = run_kernel(
            state_kernel,
            [shape_of((KV + MSG, NSTATE), bf16), shape_of((8 * ROWS, 128), bf16), kept((8 * ROWS, 128), bf16)],
            flags, *passed(shared_parts), xc, rates, rates_t, table, us=1.9,
        )
        earlier = tuple(along_ctx(message, back) for back in (1, 2, 3))
        (intra,) = run_kernel(
            intra_kernel, [shape_of((ROWS, XLOC))],
            flags, shared, xc, rates, rates_t, table, seg_rows, small[layer], us=1.3,
        )
        if layer > 0:
            earlier, intra = together(earlier, intra)
        else:
            earlier, intra, out_weight = together(earlier, intra, fetched(f"out_{layer}", *out_place[layer]))
        halves = [Columns(part, 0, NSTATE, rows=KV) for part in earlier]
        (swapped,) = run_kernel(halves_kernel, [shape_of((3 * KV, NSTATE), bf16)], None, *halves)
        state, ssm_y, gated, gated_kept = run_kernel(
            carry_kernel,
            [kept((XLOC, NSTATE)), kept((ROWS, XLOC)), shape_of((ROWS, XLOC), bf16), kept((ROWS, XLOC), bf16)],
            flags, *passed(earlier), shared, rates, table, intra, z, us=1.9,
        )
        swapped, gated = together(other_core(swapped), gated)
        attn, attn_kept, log_total, pairs = run_kernel(
            attention_kernel,
            [
                shape_of((ROWS, HD), bf16), kept((ROWS, HD), bf16), kept((ROWS, HD)),
                kept((SEQ_BLOCKS * ROWS, 2 * HD), bf16),
            ],
            flags, query, shared, *halves, Columns(swapped), table, seg_rows, us=2.0,
        )
        if layer > 0:
            out_weight = fetched(f"out_{layer}", *out_place[layer])
        parts = summed_rows([attn, gated], out_weight)
        if layer > 0:
            parts, gate_up_weight = together(parts, fetched(f"gate_up_{layer}", *gate_up_place[layer]))
        parts, (rows,) = together(parts, restored(f"hidden_{layer}", [hidden]))
        hidden1, normed2, inverse2 = add_norm(rows, parts, gains[layer, 1])
        if layer > 0:
            normed_parts, down_weight = from_all(normed2, fetched("down_1", *down_place[layer]))
        else:
            normed_parts = from_all(normed2)
            gate_up_weight, down_weight = fetched_all("ffn_0", [gate_up_place[layer], down_place[layer]])
        wide_kept = kept((ROWS, 512))
        normed2_b, gate, up, act_b, act_kept = run_kernel(
            gate_up_kernel, [normed_kept, wide_kept, wide_kept, shape_of((ROWS, 512), bf16), kept((ROWS, 512), bf16)],
            None, *passed(normed_parts), gate_up_weight, us=2.3,
        )
        saved.append(
            (
                hidden, normed_b, inverse1, shared_ext, shared_kept, query_kept, x_ext, xc_kept, z_kept, dtn_kept,
                rates_kept, rates_t_kept, pairs, log_total, state, ssm_y, attn_kept, gated_kept, hidden1, inverse2, normed2_b,
                gate, up, act_kept,
            )
        )
        if layer + 1 < layers:
            parts, (rows,) = together(summed_rows([act_b], down_weight), restored(f"hidden1_{layer}", [hidden1]))
            hidden, next_normed, inverse1 = add_norm(rows, parts, gains[layer + 1, 0])
            normed_parts, proj_weight = from_all(next_normed, fetched("proj_1", *proj_place[layer + 1]))

    small_parts = [None] * layers
    inner = None
    for layer in reversed(range(layers)):
        (
            hidden, normed_b, inverse1, shared_ext, shared, query, x_ext, xc, z, dtn, rates, rates_t,
            pairs, log_total, state, ssm_y, attn, gated, hidden1, inverse2, normed2_b, gate, up, act_b,
        ) = saved[layer]
        last = layer == 0
        dffn_b, dgate_up = run_kernel(
            gate_up_back_kernel, [normed_kept, shape_of((ROWS, 1024), bf16)],
            None, *passed(dffn_parts), down_weight, stored(gate), stored(up), us=2.7,
        )
        parts = summed_rows([dgate_up], gate_up_weight)
        outer = weight_gradients(
            [(normed2_b, dgate_up), (dffn_b, act_b)], 3200 if last else 2560, 1536, 0, inner
        )
        parts, outer = lax.optimization_barrier((parts, outer))
        parts, kept_rows = together(parts, restored(f"norm2_{layer}", [grad_hidden, hidden1, inverse2]))
        grad_mid, dmix, ggain2 = norm_back(parts, *kept_rows, gains[layer, 1])
        dmix_parts = from_all(dmix)
        dmix_parts, fetch = from_all(
            dmix,
            fetched_all(
                f"mixer_{layer}",
                [out_place[layer]]
                + [(array, 0, array.shape[1]) for array in (z, ssm_y, shared, rates, rates_t, xc, query, pairs, state)],
            ),
        )
        rates_t_kept = rates_t
        out_weight, z, ssm_y, shared, rates, rates_t, xc, query, pairs, state = fetch
        dmix_b, dattn, dy, dz, message = run_kernel(
            gate_back_kernel,
            [
                normed_kept, shape_of((ROWS, HD), bf16), shape_of((ROWS, XLOC)), shape_of((ROWS, XLOC), bf16),
                shape_of((MSG, NSTATE), bf16),
            ],
            flags, *passed(dmix_parts), out_weight, z, ssm_y, shared, rates, rates_t, table, us=2.6,
            scratch=[pltpu.VMEM((ROWS, XLOC), f32), pltpu.VMEM((ROWS, 512), f32)],
        )
        after = tuple(along_ctx(message, -ahead) for ahead in (1, 2, 3))
        early, mine, theirs = run_kernel(
            attention_back_kernel,
            [kept((ROWS, 512), bf16), shape_of((4 * ROWS, HD)), shape_of((4 * ROWS, HD), bf16)],
            flags, dattn, dz, query, pairs, stored(log_total), table, seg_rows, us=2.9,
        )
        got = other_core(theirs)
        dx, dshared, drates, dskip = run_kernel(
            intra_back_kernel,
            [kept((ROWS, XLOC)), kept((ROWS, 2 * NSTATE)), kept((ROWS, 256)), kept((1, XLOC))],
            flags, dy, xc, shared, rates, rates_t, table, seg_rows, state, small[layer], us=3.6,
            scratch=[pltpu.VMEM((128, ROWS), f32), pltpu.VMEM((ROWS, 128), f32)],
        )
        got, dx = lax.optimization_barrier((got, dx))
        dkv = parts_from(mine, got, along_ctx, -1)
        width = outer.shape[1]
        outer = weight_gradients([(dmix_b, attn), (dmix_b, gated)], width, 512, 3, outer)
        outer = weight_gradients([(normed_b, early)], width, 512, 4, outer)
        if last:
            after, dkv, outer, upper = together(after, dkv, outer, upper)
            lower = lax.psum_scatter(outer, ("fsdp", "ctx"), scatter_dimension=0, tiled=True)
        else:
            after, dkv, outer = together(after, dkv, outer)
            upper = lax.psum_scatter(outer, ("fsdp", "ctx"), scatter_dimension=0, tiled=True)
        packed_grads, state_grad = run_kernel(
            packed_back_kernel, [shape_of((8 * ROWS, 128), bf16), kept((XLOC, NSTATE))],
            flags, *map(stored, after), shared, xc, rates, table, stored(dshared), *map(stored, dkv), us=2.5,
        )
        dshared_parts = parts_of_sum(packed_grads[: 4 * ROWS], packed_grads[4 * ROWS :], along_y, 1)
        dxpre, edge_x, gconv_x, ddt, gheads = run_kernel(
            state_back_kernel,
            [kept((ROWS, XLOC)), shape_of((8, XLOC)), kept((8, XLOC)), kept((ROWS, 128)), kept((8, 128))],
            flags, stored(state_grad), shared, xc, rates, stored(rates_t_kept), table, state, stored(small[layer]),
            stored(dtn), stored(dx), stored(drates), stored(x_ext),
            scratch=[pltpu.VMEM((272, XLOC), f32), pltpu.VMEM((ROWS, XLOC), f32), pltpu.VMEM((ROWS, 128), f32)],
            us=3.5,
        )
        dshared_parts, edge_x = together(dshared_parts, edge_x)
        edge_x = along_ctx(edge_x, -1)
        dsh, edge_sh, gconv_sh = run_kernel(
            shared_back_kernel,
            [shape_of((ROWS, 128)), shape_of((8, 128)), kept((8, 128))],
            flags, *summands(dshared_parts), stored(shared_ext), table, small[layer],
            scratch=[pltpu.VMEM((272, 128), f32)],
        )
        edge_sh, proj_weight = together(
            along_ctx(edge_sh, -1), fetched(f"proj_again_{layer}", *proj_place[layer])
        )
        (late,) = run_kernel(
            late_kernel, [shape_of((ROWS, LATE), bf16)], flags, stored(dxpre), Columns(edge_x), dsh,
            Columns(edge_sh), stored(ddt),
        )
        parts = summed_rows([early, late], proj_weight)
        if not last:
            inner = weight_gradients([(normed_b, late)], 3200, LATE, 4)
            parts, inner = together(parts, inner)
            upper_pair = (normed_b, Columns(late, 3, 128))
        parts, kept_rows = together(parts, restored(f"norm1_{layer}", [grad_mid, hidden, inverse1]))
        grad_hidden, rounded, ggain1 = norm_back(parts, *kept_rows, gains[layer, 0])
        if last:
            dffn_parts = from_all(rounded)
        else:
            dffn_parts, (down_weight, gate_up_weight) = from_all(
                rounded, fetched_all("ffn_again", [down_place[layer - 1], gate_up_place[layer - 1]])
            )
            last_hidden1, last_act = hidden1, act_b
        (small_parts[layer],) = run_kernel(
            small_kernel, [shape_of((64, 128), bf16)],
            None, *map(stored, (ggain1, ggain2, gconv_sh, gconv_x, gheads, dskip)),
        )
    small_all = jnp.concatenate(small_parts, axis=0)
    owned = owned_gradients([(normed_b, late), upper_pair], small_all)
    owned = lax.all_to_all(owned, ("fsdp", "ctx"), 0, 0, tiled=True)
    (input_grad,) = run_kernel(natural_kernel, [kept((ROWS, model))], flags, *passed(dffn_parts))
    last_act, down_weight, _ = together(last_act, fetched("down_last", *down_place[1]), small_parts[0])
    (layer_out,) = run_kernel(
        output_kernel, [shape_of((SHARE, model), bf16)], None,
        stored(last_hidden1), *summands(summed_rows([last_act], down_weight)),
    )
    (layer_out,) = run_kernel(natural_kernel, [normed_kept], flags, *passed(from_all(layer_out)))
    def pair_of(width):
        return shape_of((layers, model // 16, width))

    owned, layer_out, input_grad = together(owned, layer_out, input_grad)
    over_tp, late_sum, gconv_x, gheads = run_kernel(
        block_sum_kernel,
        [
            shape_of((352, 128), bf16), kept((model // 16, LATE)), shape_of((layers * (CONV + 1), XLOC)),
            shape_of((8, 128)),
        ],
        None, Columns(owned),
    )
    grad_shared, ggains1, ggains2, gconv_bc = run_kernel(
        tp_outputs_kernel,
        [
            pair_of(1024), shape_of((layers, model)), shape_of((layers, model)),
            shape_of((layers * (CONV + 1), 512)),
        ],
        flags, *passed(from_all(over_tp)),
        scratch=[pltpu.VMEM((8, 352, 128), f32)], us=2.0,
    )
    lower, grad_shared = together(lower, grad_shared)
    grad_attn, grad_ssm, grad_gate, grad_up, grad_down, grad_query, grad_zx, grad_dt = run_kernel(
        weight_outputs_kernel,
        [
            *(kept((layers, model // 16, width)) for width in (128, 384, 512, 512, 512, 128)),
            shape_of((layers, model // 16, 2, XLOC)), pair_of(HLOC),
        ],
        None, stored(lower), stored(upper), stored(late_sum), us=3.0,
    )
    gconv_x = gconv_x.reshape(layers, CONV + 1, XLOC)
    gconv_bc = gconv_bc.reshape(layers, CONV + 1, 512)
    gheads = gheads[: 3 * layers].reshape(layers, 3, 128)[:, :, :HLOC]
    return (
        layer_out[None],
        input_grad[None],
        grad_query,
        grad_shared,
        grad_zx,
        grad_dt,
        grad_attn,
        grad_ssm,
        grad_gate,
        grad_up,
        grad_down,
        ggains1,
        gconv_x,
        gconv_bc,
        gheads[:, :2],
        ggains2,
        gheads[:, 2],
    )


def solution(mesh):
    columns = P(None, ("fsdp", "ctx"), "tp")
    rows = P("fsdp", "ctx", None)
    return jax.shard_map(
        body,
        mesh=mesh,
        in_specs=(
            rows, rows, P("fsdp", None), columns, P(None, ("fsdp", "ctx"), None),
            P(None, ("fsdp", "ctx"), None, "tp"), columns, columns, columns, columns, columns, columns,
            P(), P(None, None, "tp"), P(), P(None, None, "tp"),
        ),
        out_specs=(
            rows, rows, columns, P(None, ("fsdp", "ctx"), None), P(None, ("fsdp", "ctx"), None, "tp"),
            columns, columns, columns, columns, columns, columns,
            P(), P(None, None, "tp"), P(), P(None, None, "tp"), P(), P(None, "tp"),
        ),
        check_vma=False,
    )
```

```python
import math
from functools import partial

import jax
import jax.numpy as jnp
from jax import lax
from jax.experimental import pallas as pl
from jax.experimental.pallas import tpu as pltpu
from jax.sharding import PartitionSpec as P

HD = 128
HP = 64
NSTATE = 256
CONV = 4
ROWS = 256
SHARE = 32
XLOC = 384
PROJ = 1152
LATE = 640
HLOC = 6
PAIRS = 3
SEQ_BLOCKS = 4
MSG = XLOC + 16
KV = 128
VMEM_LIMIT = 16 * 1024 * 1024

norm_eps = 1e-05
rope_base = 100000000000.0
bf16 = jnp.bfloat16
f32 = jnp.float32
i32 = jnp.int32


def along_y(value, steps):
    pairs = [(i, ((i // 2 + steps) % 4) * 2 + i % 2) for i in range(8)]
    return lax.ppermute(value, "tp", pairs)


def other_core(value):
    return lax.ppermute(value, "tp", [(i, i ^ 1) for i in range(8)])


def along_ctx(value, steps):
    first, last = max(0, -steps), min(4, 4 - steps)
    return lax.ppermute(value, "ctx", [(i, i + steps) for i in range(first, last)])


def ring(value, axis, steps):
    return lax.ppermute(value, axis, [(i, (i + steps) % 4) for i in range(4)])


def from_all(value, beside=None):
    half = [value] + [along_y(value, -k) for k in (1, 2, 3)]
    if beside is not None:
        half[1], beside = lax.optimization_barrier((half[1], beside))
    parts = tuple(half + [other_core(part) for part in half])
    return parts if beside is None else (parts, beside)


def dot_nn(a, b):
    return jnp.dot(a, b, preferred_element_type=f32)


def dot_nt(a, b):
    return lax.dot_general(a, b, (((1,), (1,)), ((), ())), preferred_element_type=f32)


def dot_tn(a, b):
    return lax.dot_general(a, b, (((0,), (0,)), ((), ())), preferred_element_type=f32)


def shape_of(shape, dtype=f32):
    return jax.ShapeDtypeStruct(shape, dtype)


class Columns:
    def __init__(self, array, block=0, width=None, rows=None, keep=False):
        self.array, self.block, self.keep = array, block, keep
        self.shape = (rows or array.shape[0],) + array.shape[1:-1] + (width or array.shape[-1],)

    def spec(self):
        place = (0,) * (len(self.shape) - 1) + (self.block,)
        return pl.BlockSpec(self.shape, lambda i: place, pipeline_mode=pl.Buffered(1))


class Layer:
    def __init__(self, array, layer):
        self.array, self.layer, self.keep = array, layer, True
        self.shape = (1,) + array.shape[1:]

    def spec(self):
        place = (self.layer,) + (0,) * (len(self.shape) - 1)
        return pl.BlockSpec(self.shape, lambda i: place, pipeline_mode=pl.Buffered(1))


def stored(array):
    return Columns(array, keep=True)


def summands(parts):
    return [stored(parts[0])] + passed(parts[1:])


def passed(arrays):
    return [Columns(array) for array in arrays]


def kept(shape, dtype=f32):
    return pltpu.HBM(shape, dtype)


def fetch_kernel(places, *refs):
    count = len(places)
    sources, outs, sems = refs[:count], refs[count : 2 * count], refs[-1]
    copies = []
    for (start, pieces), source, out in zip(places, sources, outs):
        rows, width = out.shape[0] // pieces, out.shape[1]
        for index in range(pieces):
            own = pl.ds(rows * index, rows)
            copies.append(
                pltpu.make_async_copy(
                    source.at[own, pl.ds(start, width)], out.at[own, :], sems.at[len(copies)]
                )
            )
    for copy in copies:
        copy.start()
    for copy in copies:
        copy.wait()


def fetched_all(name, sources):
    places = [(start, 4 if array.shape[0] == 2048 and width > 128 else 1) for array, start, width in sources]
    whole = pl.BlockSpec(memory_space=pltpu.VMEM)
    return pl.pallas_call(
        partial(fetch_kernel, places),
        name=name,
        out_shape=tuple(pltpu.VMEM((array.shape[0], width), array.dtype) for array, _, width in sources),
        in_specs=[pl.BlockSpec(memory_space=pltpu.HBM)] * len(sources),
        out_specs=tuple(whole for _ in sources),
        scratch_shapes=[pltpu.SemaphoreType.DMA((sum(pieces for _, pieces in places),))],
        compiler_params=pltpu.CompilerParams(vmem_limit_bytes=VMEM_LIMIT),
        cost_estimate=pl.CostEstimate(
            flops=0, bytes_accessed=sum(2 * array.shape[0] * width for array, _, width in sources), transcendentals=0
        ),
    )(*(pltpu.with_memory_space_constraint(array, pltpu.HBM) for array, _, _ in sources))


def fetched(name, array, start, width):
    return fetched_all(name, [(array, start, width)])[0]


def restored(name, arrays):
    return fetched_all(name, [(array, 0, array.shape[1]) for array in arrays])


def run_kernel(kernel, outs, flags, *args, scratch=(), us=1.0):
    whole = pl.BlockSpec(memory_space=pltpu.VMEM)
    own = [isinstance(arg, (Columns, Layer)) for arg in args]
    specs, arrays, out_specs = [], [], []
    for arg, copied in zip(args, own):
        specs.append(arg.spec() if copied else whole)
        array = arg.array if copied else arg
        arrays.append(pltpu.with_memory_space_constraint(array, pltpu.HBM) if copied and arg.keep else array)
    for out in outs:
        in_vmem = isinstance(out, jax.ShapeDtypeStruct)
        out_specs.append(whole if in_vmem else pl.BlockSpec(out.shape, lambda i, n=len(out.shape): (0,) * n))
        own.append(not in_vmem)
    moved = sum(2 * math.prod(arg.shape) for arg in args) + sum(2 * math.prod(o.shape) for o in outs)
    if flags is not None:
        specs = [pl.BlockSpec(memory_space=pltpu.SMEM)] + specs
        arrays = [flags] + arrays
    return pl.pallas_call(
        kernel,
        grid=(1,) if any(own) else (),
        out_shape=tuple(outs),
        in_specs=specs,
        out_specs=tuple(out_specs),
        scratch_shapes=list(scratch),
        compiler_params=pltpu.CompilerParams(vmem_limit_bytes=VMEM_LIMIT),
        cost_estimate=pl.CostEstimate(flops=int(us * 1e9), bytes_accessed=moved, transcendentals=0),
    )(*arrays)


def local_block(flags, natural):
    return pl.multiple_of(flags[8 + natural] * SHARE, SHARE)


def rank_block(flags, rank):
    return pl.multiple_of(flags[16 + rank] * ROWS, ROWS)


def lane_index(shape):
    return lax.broadcasted_iota(i32, shape, len(shape) - 1)


def spread(columns, pair):
    low = lane_index((1, 128)) < HP
    return jnp.where(low, columns[:, 2 * pair : 2 * pair + 1], columns[:, 2 * pair + 1 : 2 * pair + 2])


def lanes_of(pair):
    return slice(128 * pair, 128 * pair + 128)


def turned(value, table, sign):
    return value * table[:, 0:128] + sign * (pltpu.roll(value, 64, 1) * table[:, 128:256])


def segments(table):
    return table[:, 259:260]


def sigmoid(v):
    return 1.0 / (1.0 + jnp.exp(-v))


def softplus(v):
    return jnp.maximum(v, 0.0) + jnp.log1p(jnp.exp(-jnp.abs(v)))


def conv_sum(ext, table, weight):
    total = weight[CONV : CONV + 1, :] + ext[8 : 8 + ROWS, :] * weight[3:4, :]
    for tap in range(CONV - 1):
        total = total + table[:, 256 + tap : 257 + tap] * ext[5 + tap : 5 + tap + ROWS, :] * weight[tap : tap + 1, :]
    return total


def conv_back(grad_out, ext, table, weight, work, grad_ref, edge_ref, gweight_ref):
    total = conv_sum(ext, table, weight)
    sig = sigmoid(total)
    grad = grad_out * sig * (1.0 + total * (1.0 - sig))
    width = grad.shape[1]
    gweight_ref[...] = jnp.zeros((8, width), f32)
    gweight_ref[CONV : CONV + 1, :] = jnp.sum(grad, axis=0, keepdims=True)
    gweight_ref[3:4, :] = jnp.sum(grad * ext[8 : 8 + ROWS, :], axis=0, keepdims=True)
    work[0:8, :] = jnp.zeros((8, width), f32)
    work[264:272, :] = jnp.zeros((8, width), f32)
    own = grad * weight[3:4, :]
    edge = jnp.zeros((8, width), f32)
    for tap in range(CONV - 1):
        part = grad * table[:, 256 + tap : 257 + tap]
        gweight_ref[tap : tap + 1, :] = jnp.sum(
            part * ext[5 + tap : 5 + tap + ROWS, :], axis=0, keepdims=True
        )
        work[8:264, :] = part * weight[tap : tap + 1, :]
        own = own + work[11 - tap : 11 - tap + ROWS, :]
        edge = edge + work[3 - tap : 11 - tap, :]
    grad_ref[...] = own
    edge_ref[...] = edge


def pack_kernel(place, *refs):
    out, at, index = refs[-1], 0, 0
    while index < len(refs) - 1:
        ref = refs[index]
        if len(ref.shape) == 4:
            out[:, at : at + XLOC] = ref[0, :, 0, :]
            out[:, at + XLOC : at + 512] = refs[index + 1][0]
            out[:, at + 512 : at + 896] = ref[0, :, 1, :]
            at, index = at + 896, index + 2
            continue
        width = min(ref.shape[2], 512)
        if width == HLOC:
            out[:, at : at + 128] = jnp.zeros((out.shape[0], 128), bf16)
            out[:, at : at + HLOC] = ref[0]
            width = 128
        elif ref.shape[2] == 1024:
            width = 128
            out[:, at : at + width] = ref[0, :, pl.ds(pl.multiple_of(place[0] * 128, 128), 128)]
        else:
            out[:, at : at + width] = ref[0]
        at, index = at + width, index + 1


def first_kernel(flags, rows, cotangent, gain, normed, inverse, hidden_kept, grads, grad):
    for block in range(8):
        own = slice(SHARE * block, SHARE * (block + 1))
        from_rows = pl.ds(pl.multiple_of(flags[24 + block] * SHARE, SHARE), SHARE)
        wide = rows[0, from_rows, :].astype(f32)
        scale = lax.rsqrt(jnp.mean(wide * wide, axis=1, keepdims=True) + norm_eps)
        normed[own, :] = (wide * scale * gain[0:1, :]).astype(bf16)
        grads[own, :] = cotangent[0, from_rows, :]
        if block == 0:
            hidden_kept[...] = wide
            inverse[...] = jnp.broadcast_to(scale, inverse.shape)
            grad[...] = cotangent[0, from_rows, :].astype(f32)


def joined(parts):
    return parts[0][...] if len(parts) == 1 else jnp.concatenate([part[...] for part in parts], axis=0)


def proj_kernel(flags, *refs):
    parts, (weight, table, normed, z, z_kept, xs, query, query_kept, dtn, dtn_kept, work) = refs[:-11], refs[-11:]
    rows = joined(parts)
    normed[...] = rows
    work[...] = dot_nn(rows, weight[...])
    for block in range(8):
        own = slice(SHARE * block, SHARE * (block + 1))
        from_rows = pl.ds(local_block(flags, block), SHARE)
        for out in (z, z_kept):
            out[own, :] = work[from_rows, 0:XLOC]
        xs[own, 0:XLOC] = work[from_rows, 512:896]
        xs[own, XLOC:512] = work[from_rows, 1024:PROJ]
        head = turned(work[from_rows, XLOC:512], table[own, :], 1.0).astype(bf16)
        for out in (query, query_kept):
            out[own, :] = head
        for out in (dtn, dtn_kept):
            out[own, :] = work[from_rows, 896:1024]


def shared_kernel(flags, xs, halo, table, small, out, ext):
    own = xs[:, XLOC:512]
    ext[0:8, :] = halo[:, XLOC:512]
    ext[8 : 8 + ROWS, :] = own
    total = conv_sum(ext, table, small[:, XLOC:512])
    rank = flags[0]
    out[...] = jnp.where(
        rank < 2, turned(own, table, 1.0), jnp.where(rank < 4, own, total * sigmoid(total))
    ).astype(bf16)


def prep_kernel(xs, dtn, halo, table, small, ext, xc, xc_kept, rates, rates_kept, rates_t, rates_t_kept):
    ext[0:8, :] = halo[:, 0:XLOC]
    ext[8 : 8 + ROWS, :] = xs[:, 0:XLOC]
    total = conv_sum(ext, table, small[:, 0:XLOC])
    for out in (xc, xc_kept):
        out[...] = total * sigmoid(total)
    params = small[:, 512:640]
    rate = softplus(dtn[...] + params[1:2, :])
    logs = -jnp.exp(params[0:1, :]) * rate
    rows = lax.broadcasted_iota(i32, (ROWS, ROWS), 0)
    lower = (rows >= lane_index((ROWS, ROWS))).astype(f32)
    running = jnp.dot(lower, logs, precision=lax.Precision.HIGHEST, preferred_element_type=f32)
    for out in (rates, rates_kept):
        out[:, 0:128] = rate
        out[:, 128:256] = running
    rate_t, running_t = rate.T[0:8, :], running.T[0:8, :]
    for out in (rates_t, rates_t_kept):
        out[0:8, :] = rate_t
        out[8:16, :] = running_t


def block_decays(flags, rates_t):
    kept = jnp.where(flags[4] == flags[5], 1.0, 0.0)
    return jnp.exp(rates_t[8:16, ROWS - 1 : ROWS]) * kept


def decay_rows(flags, rates_t):
    rows = jnp.broadcast_to(block_decays(flags, rates_t), (8, NSTATE))
    return jnp.concatenate([rows, jnp.zeros((8, NSTATE), f32)], axis=0).astype(bf16)


def weights_in(rates, table):
    last = rates[ROWS - 1 : ROWS, 128:256]
    gap = jnp.exp(last - rates[:, 128:256]) * table[:, 261:262]
    return gap, gap * rates[:, 0:128]


def rank_columns(flags, shared, first):
    return jnp.concatenate(
        [shared[pl.ds(rank_block(flags, rank), ROWS), :] for rank in (first, first + 1)], axis=1
    )


def inject_of(flags, shared):
    return rank_columns(flags, shared, 4)


def readout_of(flags, shared):
    return rank_columns(flags, shared, 6)


def carry_of(rates, table):
    return jnp.exp(rates[:, 128:256]) * table[:, 260:261]


def state_kernel(flags, s0, s1, s2, s3, s4, s5, s6, s7, xc, rates, rates_t, table, out, shared, shared_kept):
    for index, part in enumerate((s0, s1, s2, s3, s4, s5, s6, s7)):
        shared[ROWS * index : ROWS * (index + 1), :] = part[...]
        shared_kept[ROWS * index : ROWS * (index + 1), :] = part[...]
    inject = inject_of(flags, shared)
    _, weight = weights_in(rates, table)
    for pair in range(PAIRS):
        weighted = (xc[:, lanes_of(pair)] * spread(weight, pair)).astype(bf16)
        out[KV + 128 * pair : KV + 128 * (pair + 1), :] = dot_tn(weighted, inject).astype(bf16)
    out[KV + XLOC : KV + MSG, :] = decay_rows(flags, rates_t)
    half = shared[pl.ds(rank_block(flags, 2 * flags[2] + flags[1] // 2), ROWS), :]
    out[0:KV, :] = jnp.concatenate([half[0:128], half[128:256]], axis=1)


def halves_kernel(msg1, msg2, msg3, out):
    for index, msg in enumerate((msg1, msg2, msg3)):
        out[KV * index : KV * (index + 1), :] = msg[...]


def allowed_pairs(table, seg_rows):
    rows = lax.broadcasted_iota(i32, (ROWS, ROWS), 0)
    return (rows >= lane_index((ROWS, ROWS))) & (segments(table) == seg_rows[0:1, :])


def head_decay(allowed, rates, rates_t, head):
    gap = rates[:, 128 + head : 129 + head] - rates_t[8 + head : 9 + head, :]
    return jnp.where(allowed, jnp.exp(jnp.where(allowed, gap, 0.0)), 0.0)


def intra_kernel(flags, shared, xc, rates, rates_t, table, seg_rows, small, out):
    inject, readout = inject_of(flags, shared), readout_of(flags, shared)
    both = dot_nt(readout, inject)
    allowed = allowed_pairs(table, seg_rows)
    low = lane_index((1, 128)) < HP
    for pair in range(PAIRS):
        x = xc[:, lanes_of(pair)]
        xb = x.astype(bf16)
        heads = []
        for head in (2 * pair, 2 * pair + 1):
            decay = head_decay(allowed, rates, rates_t, head)
            heads.append(dot_nn((both * decay * rates_t[head : head + 1, :]).astype(bf16), xb))
        out[:, lanes_of(pair)] = jnp.where(low, heads[0], heads[1]) + spread(small[2:3, 512:640], pair) * x


def keys_values(flags, shared, halves, swapped):
    head, first = flags[1] // 2, flags[2] == 0
    pairs = [
        (
            shared[pl.ds(rank_block(flags, head), ROWS), :],
            shared[pl.ds(rank_block(flags, 2 + head), ROWS), :],
        )
    ]
    for index, half in enumerate(halves):
        packed = half[...], swapped[KV * index : KV * (index + 1), :]
        mine, theirs = (jnp.concatenate([part[:, 0:128], part[:, 128:256]], axis=0) for part in packed)
        pairs.append((jnp.where(first, mine, theirs), jnp.where(first, theirs, mine)))
    return pairs


def masked_scores(query, pairs, table, seg_rows):
    parts = []
    for block, (keys, _) in enumerate(pairs):
        score = dot_nt(query, keys) * HD ** (-0.5)
        keep = segments(table) == seg_rows[block : block + 1, :]
        if block == 0:
            rows = lax.broadcasted_iota(i32, (ROWS, ROWS), 0)
            keep = keep & (rows >= lane_index((ROWS, ROWS)))
        parts.append(jnp.where(keep, score, -1e30))
    return parts


def attention_kernel(flags, query, shared, h1, h2, h3, swapped, table, seg_rows, out, out_kept, log_total, kept):
    pairs = keys_values(flags, shared, (h1, h2, h3), swapped)
    for block, (keys, values) in enumerate(pairs):
        kept[ROWS * block : ROWS * (block + 1), 0:HD] = keys
        kept[ROWS * block : ROWS * (block + 1), HD : 2 * HD] = values
    parts = masked_scores(query[...], pairs, table, seg_rows)
    top = parts[0].max(axis=1, keepdims=True)
    for part in parts[1:]:
        top = jnp.maximum(top, part.max(axis=1, keepdims=True))
    parts = [jnp.exp(part - top) for part in parts]
    total = sum(part.sum(axis=1, keepdims=True) for part in parts)
    inverse = 1.0 / total
    result = jnp.zeros((ROWS, HD), f32)
    for part, (_, values) in zip(parts, pairs):
        result = result + dot_nn((part * inverse).astype(bf16), values)
    rounded = result.astype(bf16)
    for block in range(8):
        for ref in (out, out_kept):
            ref[pl.ds(local_block(flags, block), SHARE), :] = rounded[SHARE * block : SHARE * (block + 1), :]
    log_total[...] = jnp.broadcast_to(top + jnp.log(total), (ROWS, HD))


def chained(first, second, third, base):
    rows1 = first[base + XLOC : base + MSG, :].astype(f32)
    rows2 = second[base + XLOC : base + MSG, :].astype(f32)
    parts = []
    for head in range(HLOC):
        own = slice(base + HP * head, base + HP * head + HP)
        older = second[own, :].astype(f32) + rows2[head : head + 1, :] * third[own, :].astype(f32)
        parts.append(first[own, :].astype(f32) + rows1[head : head + 1, :] * older)
    return jnp.concatenate(parts, axis=0)


def carry_kernel(flags, msg1, msg2, msg3, shared, rates, table, intra, z, state, ssm_y, cat, cat_kept):
    entering = chained(msg1, msg2, msg3, KV)
    state[...] = entering
    from_state = dot_nt(readout_of(flags, shared), entering.astype(bf16))
    carry = carry_of(rates, table)
    for pair in range(PAIRS):
        own = lanes_of(pair)
        y = intra[:, own] + spread(carry, pair) * from_state[:, own]
        ssm_y[:, own] = y
        gate = z[:, own]
        gated = (y * gate * sigmoid(gate)).astype(bf16)
        for block in range(8):
            for out in (cat, cat_kept):
                out[pl.ds(local_block(flags, block), SHARE), 128 * pair : 128 * (pair + 1)] = gated[
                    SHARE * block : SHARE * (block + 1), :
                ]


def gate_back_kernel(
    flags, p0, p1, p2, p3, p4, p5, p6, p7, weight, z, ssm_y, shared, rates, rates_t, table,
    dmix, dattn, dy, dz, msg, work, local,
):
    rows = joined((p0, p1, p2, p3, p4, p5, p6, p7))
    dmix[...] = rows
    local[...] = dot_nn(rows, weight[...])
    for block in range(8):
        own = slice(SHARE * block, SHARE * (block + 1))
        from_rows = pl.ds(local_block(flags, block), SHARE)
        dattn[own, :] = local[from_rows, 0:128].astype(bf16)
        work[own, :] = local[from_rows, 128:512]
    readout = readout_of(flags, shared)
    carry = carry_of(rates, table)
    for pair in range(PAIRS):
        own = lanes_of(pair)
        gate, grad = z[:, own], work[:, own]
        sig = sigmoid(gate)
        y_grad = grad * gate * sig
        dy[:, own] = y_grad
        dz[:, own] = (grad * ssm_y[:, own] * sig * (1.0 + gate * (1.0 - sig))).astype(bf16)
        msg[own, :] = dot_tn((y_grad * spread(carry, pair)).astype(bf16), readout).astype(bf16)
    msg[XLOC:MSG, :] = decay_rows(flags, rates_t)


def attention_back_kernel(
    flags, dattn, dz, query, kept, log_total, table, seg_rows,
    early, mine, theirs,
):
    pairs = []
    for block in range(SEQ_BLOCKS):
        own = slice(ROWS * block, ROWS * (block + 1))
        pairs.append((kept[own, 0:HD], kept[own, HD : 2 * HD]))
    first = flags[2] == 0
    q = query[...]
    grad = dattn[...]
    parts = masked_scores(q, pairs, table, seg_rows)
    logs = log_total[:, 0:1]
    probs = [jnp.exp(part - logs) for part in parts]
    grads = [dot_nt(grad, values) for _, values in pairs]
    inner = sum((p * g).sum(axis=1, keepdims=True) for p, g in zip(probs, grads))
    total = jnp.zeros((ROWS, HD), f32)
    for block, (p, g, (keys, _)) in enumerate(zip(probs, grads, pairs)):
        own = slice(ROWS * block, ROWS * (block + 1))
        score = (p * (g - inner)).astype(bf16)
        total = total + dot_nn(score, keys)
        dkeys = dot_tn(score, q) * HD ** (-0.5)
        dvalues = dot_tn(p.astype(bf16), grad)
        mine[own, :] = jnp.where(first, dkeys, dvalues)
        theirs[own, :] = jnp.where(first, dvalues, dkeys).astype(bf16)
    total = total * HD ** (-0.5)
    dq = turned(total, table, -1.0).astype(bf16)
    for block in range(8):
        own = slice(SHARE * block, SHARE * (block + 1))
        to_rows = pl.ds(local_block(flags, block), SHARE)
        early[to_rows, 0:XLOC] = dz[own, :]
        early[to_rows, XLOC:512] = dq[own, :]


def intra_back_kernel(
    flags, dy, xc, shared, rates, rates_t, table, seg_rows, state, small,
    dx, dshared, drates, dskip, row_sums, dcum,
):
    inject, readout = inject_of(flags, shared), readout_of(flags, shared)
    both = dot_nt(readout, inject)
    allowed = allowed_pairs(table, seg_rows)
    low = lane_index((1, 128)) < HP
    carry = carry_of(rates, table)
    entering = state[...].astype(bf16)
    from_state = dot_nt(readout, entering)
    dboth = jnp.zeros((ROWS, ROWS), f32)
    row_sums[...] = jnp.zeros((128, ROWS), f32)
    dcum[...] = jnp.zeros((ROWS, 128), f32)
    carried = []
    for pair in range(PAIRS):
        own = lanes_of(pair)
        x = xc[:, own]
        xb = x.astype(bf16)
        grad = dy[:, own]
        dskip[:, own] = jnp.sum(grad * x, axis=0, keepdims=True)
        carried.append((grad * spread(carry, pair)).astype(bf16))
        through = grad * from_state[:, own]
        total = spread(small[2:3, 512:640], pair) * grad
        for head in (2 * pair, 2 * pair + 1):
            mine = low if head % 2 == 0 else jnp.logical_not(low)
            decay = head_decay(allowed, rates, rates_t, head)
            steps = rates_t[head : head + 1, :]
            head_grad = jnp.where(mine, grad, 0.0).astype(bf16)
            dmix = dot_nt(head_grad, xb)
            kept = dmix * decay
            dboth = dboth + kept * steps
            mixed = both * decay
            total = total + dot_tn((mixed * steps).astype(bf16), head_grad)
            passed = dmix * mixed
            row_sums[head : head + 1, :] = jnp.sum(passed, axis=0, keepdims=True)
            dcum[:, head : head + 1] = jnp.sum(passed * steps, axis=1, keepdims=True) + carry[
                :, head : head + 1
            ] * jnp.sum(jnp.where(mine, through, 0.0), axis=1, keepdims=True)
        dx[:, own] = total
    columns = row_sums[...].T
    drates[:, 0:128] = columns
    drates[:, 128:256] = dcum[...] - rates[:, 0:128] * columns
    dboth_b = dboth.astype(bf16)
    dshared[:, NSTATE:] = dot_nn(dboth_b, inject) + dot_nn(jnp.concatenate(carried, axis=1), entering)
    dshared[:, 0:NSTATE] = dot_tn(dboth_b, readout)


def packed_back_kernel(
    flags, msg1, msg2, msg3, shared, xc, rates, table, dshared, kv0, kv1, kv2, kv3, packed, state_grad,
):
    later = chained(msg1, msg2, msg3, 0)
    state_grad[...] = later
    _, weights = weights_in(rates, table)
    weighted = [(xc[:, lanes_of(pair)] * spread(weights, pair)).astype(bf16) for pair in range(PAIRS)]
    weighted = jnp.concatenate(weighted, axis=1)
    dinject = (dshared[:, 0:NSTATE] + dot_nn(weighted, later.astype(bf16))).astype(bf16)
    dreadout = dshared[:, NSTATE:].astype(bf16)
    packed[...] = jnp.zeros((8 * ROWS, 128), bf16)
    grads = kv0[...] + kv1[...].astype(f32) + kv2[...].astype(f32) + kv3[...].astype(f32)
    owner = 2 * flags[2] + flags[1] // 2
    packed[pl.ds(rank_block(flags, owner), ROWS), :] = grads.astype(bf16)
    packed[pl.ds(rank_block(flags, 4), ROWS), :] = dinject[:, 0:128]
    packed[pl.ds(rank_block(flags, 5), ROWS), :] = dinject[:, 128:256]
    packed[pl.ds(rank_block(flags, 6), ROWS), :] = dreadout[:, 0:128]
    packed[pl.ds(rank_block(flags, 7), ROWS), :] = dreadout[:, 128:256]


def state_back_kernel(
    flags, later, shared, xc, rates, rates_t, table, state, small, dtn, dx, drates, ext,
    dxpre, edge, gweight, ddt, heads, work, dconv, sums,
):
    inject = inject_of(flags, shared)
    low = lane_index((1, 128)) < HP
    params = small[:, 512:640]
    gap, weights = weights_in(rates, table)
    from_later = dot_nt(inject, later[...].astype(bf16))
    products = later[...] * state[...]
    decays = block_decays(flags, rates_t)
    sums[...] = jnp.zeros((ROWS, 128), f32)
    for pair in range(PAIRS):
        own = lanes_of(pair)
        dconv[:, own] = dx[:, own] + spread(weights, pair) * from_later[:, own]
        through = xc[:, own] * from_later[:, own]
        for head in (2 * pair, 2 * pair + 1):
            mine = low if head % 2 == 0 else jnp.logical_not(low)
            sums[:, head : head + 1] = jnp.sum(jnp.where(mine, through, 0.0), axis=1, keepdims=True)
    dweights = sums[...]
    moved = dweights * weights
    last = jnp.sum(moved, axis=0, keepdims=True)
    lanes = lane_index((1, 128))
    for head in range(HLOC):
        total = jnp.sum(
            jnp.sum(products[HP * head : HP * head + HP, :], axis=0, keepdims=True), axis=1, keepdims=True
        )
        last = last + jnp.where(lanes == head, total * decays[head : head + 1, :], 0.0)
    rows = lax.broadcasted_iota(i32, (ROWS, 128), 0)
    dcums = drates[:, 128:256] - moved + jnp.where(rows == ROWS - 1, last, 0.0)
    square = lax.broadcasted_iota(i32, (ROWS, ROWS), 0)
    upper = (square <= lane_index((ROWS, ROWS))).astype(f32)
    dlogs = jnp.dot(upper, dcums, precision=lax.Precision.HIGHEST, preferred_element_type=f32)
    rate = -jnp.exp(params[0:1, :])
    dsteps = drates[:, 0:128] + dweights * gap + dlogs * rate
    ddts = dsteps * sigmoid(dtn[...] + params[1:2, :])
    ddt[...] = ddts
    heads[...] = jnp.zeros((8, 128), f32)
    heads[0:1, :] = jnp.sum(dlogs * rate * rates[:, 0:128], axis=0, keepdims=True)
    heads[1:2, :] = jnp.sum(ddts, axis=0, keepdims=True)
    conv_back(dconv[...], ext, table, small[:, 0:XLOC], work, dxpre, edge, gweight)


def shared_back_kernel(flags, part0, part1, part2, part3, ext, table, small, out, edge, gweight, work):
    grad = part0[...] + part1[...].astype(f32) + part2[...].astype(f32) + part3[...].astype(f32)
    conv_back(grad, ext, table, small[:, XLOC:512], work, out, edge, gweight)
    rank = flags[0]
    of_conv = jnp.where(rank < 4, 0.0, 1.0)
    edge[...] = edge[...] * of_conv
    gweight[...] = gweight[...] * of_conv
    out[...] = jnp.where(rank < 2, turned(grad, table, -1.0), jnp.where(rank < 4, grad, out[...]))


def late_kernel(flags, dxpre, edge_x, dsh, edge_sh, ddt, out):
    for block in range(8):
        own = slice(SHARE * block, SHARE * (block + 1))
        to_rows = pl.ds(local_block(flags, block), SHARE)
        x, sh = dxpre[own, :], dsh[own, :]
        if block == 7:
            pad = jnp.zeros((SHARE - 8, 128), f32)
            sh = sh + jnp.concatenate([pad, edge_sh[...]], axis=0)
            x = x + jnp.concatenate([jnp.zeros((SHARE - 8, XLOC), f32), edge_x[...]], axis=0)
        out[to_rows, 0:XLOC] = x.astype(bf16)
        out[to_rows, 512:LATE] = sh.astype(bf16)
        out[to_rows, XLOC:512] = jnp.where(lane_index((1, 128)) < HLOC, ddt[own, :], 0.0).astype(bf16)


def half_sum_kernel(own, other, keep, send1, send2, send3):
    rows = own.shape[0] // 4
    keep[...] = own[0:rows, :] + other[0:rows, :].astype(f32)
    for index, send in ((1, send1), (2, send2), (3, send3)):
        part = slice(rows * index, rows * (index + 1))
        send[...] = (own[part, :].astype(f32) + other[part, :].astype(f32)).astype(bf16)


def parts_of_sum(own, other, along, sign):
    return parts_from(own, other_core(other), along, sign)


def parts_from(own, got, along, sign):
    rows, width = own.shape[0] // 4, own.shape[1]
    sent = shape_of((rows, width), bf16)
    keep, *sends = run_kernel(half_sum_kernel, [kept((rows, width)), sent, sent, sent], None, own, Columns(got))
    return (keep,) + tuple(along(send, sign * k) for k, send in zip((1, 2, 3), sends))


def split_kernel(*refs):
    lefts, weight, own, other = refs[:-3], refs[-3], refs[-2], refs[-1]
    left = lefts[0][...] if len(lefts) == 1 else jnp.concatenate([ref[...] for ref in lefts], axis=1)
    result = dot_nt(left, weight[...])
    own[...] = result[: ROWS // 2]
    other[...] = result[ROWS // 2 :].astype(bf16)


def summed_rows(lefts, weight):
    model, width = weight.shape
    own, other = pl.pallas_call(
        split_kernel,
        grid=(model // 512,),
        out_shape=(shape_of((ROWS // 2, model)), shape_of((ROWS // 2, model), bf16)),
        in_specs=[pl.BlockSpec(left.shape, lambda i: (0, 0)) for left in lefts]
        + [pl.BlockSpec((512, width), lambda i: (i, 0))],
        out_specs=(
            pl.BlockSpec((ROWS // 2, 512), lambda i: (0, i)),
            pl.BlockSpec((ROWS // 2, 512), lambda i: (0, i)),
        ),
        compiler_params=pltpu.CompilerParams(vmem_limit_bytes=VMEM_LIMIT),
        cost_estimate=pl.CostEstimate(
            flops=2 * ROWS * model * width, bytes_accessed=2 * model * width, transcendentals=0
        ),
    )(*lefts, weight)
    return parts_of_sum(own, other, along_y, 1)


def gate_up_kernel(p0, p1, p2, p3, p4, p5, p6, p7, weight, normed, gate, up, act, act_kept):
    rows = joined((p0, p1, p2, p3, p4, p5, p6, p7))
    normed[...] = rows
    result = dot_nn(rows, weight[...])
    g, u = result[:, :512], result[:, 512:]
    gate[...] = g
    up[...] = u
    for out in (act, act_kept):
        out[...] = (g * sigmoid(g) * u).astype(bf16)


def gate_up_back_kernel(*refs):
    parts, (weight, gate, up, dffn, out) = refs[:-5], refs[-5:]
    rows = joined(parts)
    dffn[...] = rows
    dact = dot_nn(rows, weight[...])
    g = gate[...]
    sig = sigmoid(g)
    out[:, :512] = (dact * up[...] * sig * (1.0 + g * (1.0 - sig))).astype(bf16)
    out[:, 512:] = (dact * g * sig).astype(bf16)


def natural_kernel(flags, p0, p1, p2, p3, p4, p5, p6, p7, out):
    local = joined((p0, p1, p2, p3, p4, p5, p6, p7)).astype(out.dtype)
    for block in range(8):
        out[pl.ds(pl.multiple_of(flags[24 + block] * SHARE, SHARE), SHARE), :] = local[
            SHARE * block : SHARE * (block + 1), :
        ]


def add_norm_kernel(hidden, part0, part1, part2, part3, gain, out_kept, normed, inverse):
    total = hidden[...] + part0[...] + (
        part1[...].astype(f32) + part2[...].astype(f32) + part3[...].astype(f32)
    )
    out_kept[...] = total
    scale = lax.rsqrt(jnp.mean(total * total, axis=1, keepdims=True) + norm_eps)
    inverse[...] = jnp.broadcast_to(scale, inverse.shape)
    normed[...] = (total * scale * gain[...]).astype(bf16)


def add_norm(hidden, parts, gain):
    shape = hidden.shape
    return run_kernel(
        add_norm_kernel,
        [kept(shape), shape_of(shape, bf16), kept((shape[0], 128))],
        None, hidden, *summands(parts), gain[None],
    )


def output_kernel(hidden, part0, part1, part2, part3, out):
    total = hidden[...] + part0[...] + (
        part1[...].astype(f32) + part2[...].astype(f32) + part3[...].astype(f32)
    )
    out[...] = total.astype(bf16)


def norm_back_kernel(grad, part0, part1, part2, part3, hidden, inverse, gain, out, rounded, ggain):
    received = part0[...] + (part1[...].astype(f32) + part2[...].astype(f32) + part3[...].astype(f32))
    scale = inverse[:, 0:1]
    unit = hidden[...] * scale
    scaled = received * gain[...]
    ggain[...] = jnp.sum(received * unit, axis=0, keepdims=True)
    total = grad[...] + scale * (scaled - unit * jnp.mean(scaled * unit, axis=1, keepdims=True))
    out[...] = total
    rounded[...] = total.astype(bf16)


def norm_back(parts, grad, hidden, inverse, gain):
    shape = hidden.shape
    return run_kernel(
        norm_back_kernel,
        [kept(shape), shape_of(shape, bf16), kept((1, shape[1]))],
        None, grad, *summands(parts), hidden, inverse, gain[None],
    )


def gradient_kernel(pairs, *refs):
    out, at = refs[-1], 0
    for index in range(pairs):
        left, right = refs[2 * index], refs[2 * index + 1]
        width = right.shape[1]
        out[:, at : at + width] = dot_tn(left[...], right[...]).astype(bf16)
        at += width
    if at < out.shape[1]:
        out[:, at:] = jnp.zeros((out.shape[0], out.shape[1] - at), bf16)


def weight_gradients(pairs, total, block, index, buffer=None):
    rows, model = pairs[0][0].shape
    width = sum(right.shape[1] for _, right in pairs)
    specs, args = [], []
    for left, right in pairs:
        block_right = right.block if isinstance(right, Columns) else 0
        specs += [
            pl.BlockSpec((rows, 512), lambda i: (0, i)),
            pl.BlockSpec(right.shape, lambda i, block=block_right: (0, block)),
        ]
        args += [left, right.array if isinstance(right, Columns) else right]
    aliases = {}
    kernel = partial(gradient_kernel, len(pairs))
    if buffer is not None:
        aliases = {len(args): 0}
        specs.append(pl.BlockSpec(memory_space=pltpu.HBM))
        args.append(buffer)

        def kernel(*refs):
            gradient_kernel(len(pairs), *refs[:-2], refs[-1])

    return pl.pallas_call(
        kernel,
        grid=(model // 512,),
        out_shape=pltpu.HBM((model, total), bf16),
        in_specs=specs,
        out_specs=pl.BlockSpec((512, block), lambda i: (i, index)),
        input_output_aliases=aliases,
        compiler_params=pltpu.CompilerParams(vmem_limit_bytes=VMEM_LIMIT),
        cost_estimate=pl.CostEstimate(
            flops=2 * rows * model * width, bytes_accessed=model * width * 2, transcendentals=0
        ),
    )(*args)


def owned_kernel(pairs, small, *refs):
    out, at = refs[-1], 0
    for pair in range(pairs):
        left, right = refs[2 * pair], refs[2 * pair + 1]
        result = dot_tn(left[...], right[...]).astype(bf16)
        width = right.shape[1]
        for index in range(2):
            out[index, :, at : at + width] = result[128 * index : 128 * (index + 1)]
        at += width
    if small:
        mine = lane_index((1, 128)) < HLOC
        for index in range(2):
            out[index, :, XLOC:512] = jnp.where(mine, out[index, :, XLOC:512], refs[2 * pairs][...])


def owned_gradients(pairs, small=None):
    rows, model = pairs[0][0].shape
    width = sum(right.shape[1] for _, right in pairs)
    specs, args = [], []
    for left, right in pairs:
        block = right.block if isinstance(right, Columns) else 0
        specs += [
            pl.BlockSpec((rows, 256), lambda i: (0, i)),
            pl.BlockSpec(right.shape, lambda i, block=block: (0, block)),
        ]
        args += [left, right.array if isinstance(right, Columns) else right]
    if small is not None:
        specs.append(pl.BlockSpec(small.shape, lambda i: (0, 0)))
        args.append(small)
    return pl.pallas_call(
        partial(owned_kernel, len(pairs), small is not None),
        grid=(model // 256,),
        out_shape=pltpu.HBM((16, model // 16, width), bf16),
        in_specs=specs,
        out_specs=pl.BlockSpec((2, model // 16, width), lambda i: (i, 0, 0)),
        compiler_params=pltpu.CompilerParams(vmem_limit_bytes=VMEM_LIMIT),
        cost_estimate=pl.CostEstimate(
            flops=2 * rows * model * width, bytes_accessed=model * width * 2, transcendentals=0
        ),
    )(*args)


def small_kernel(gain1, gain2, conv_sh, conv_x, heads, skip, out):
    out[...] = jnp.zeros(out.shape, bf16)
    for row in range(16):
        own = slice(128 * row, 128 * row + 128)
        out[row : row + 1, :] = gain1[:, own].astype(bf16)
        out[16 + row : 17 + row, :] = gain2[:, own].astype(bf16)
    out[32:37, :] = conv_sh[0:5, :].astype(bf16)
    for tap in range(CONV + 1):
        for pair in range(PAIRS):
            row = 37 + PAIRS * tap + pair
            out[row : row + 1, :] = conv_x[tap : tap + 1, lanes_of(pair)].astype(bf16)
    out[52:54, :] = heads[0:2, :].astype(bf16)
    lanes = lane_index((1, 128))
    sums = jnp.zeros((1, 128), f32)
    for pair in range(PAIRS):
        part = skip[:, lanes_of(pair)]
        for half in range(2):
            mine = (lanes < HP) if half == 0 else (lanes >= HP)
            total = jnp.sum(jnp.where(mine, part, 0.0), axis=1, keepdims=True)
            sums = sums + jnp.where(lanes == 2 * pair + half, total, 0.0)
    out[54:55, :] = sums.astype(bf16)


def spread_kernel(small, out, work):
    work[...] = small[...].astype(f32)
    columns = work[...].T
    work[56:62, :] = columns[122:128, :]
    out[...] = pltpu.roll(work[...], HLOC, 1).astype(bf16)


def gathered_back(packed, work):
    rolled = pltpu.roll(packed, 128 - HLOC, 1)
    work[...] = jnp.zeros((128, 128), f32)
    work[122:128, :] = rolled[56:62, :]
    return jnp.where(lane_index((1, 128)) < 128 - HLOC, rolled, work[...].T)


def owner_sum(values):
    total = values[0].astype(f32)
    for index in range(1, 16):
        total = total + values[index].astype(f32)
    return total


def block_sum_kernel(values, over_tp, late, conv_x, heads, work):
    whole = owner_sum(values)
    late[...] = whole[:, 0:LATE]
    total = gathered_back(whole[:, XLOC:512], work)
    over_tp[0:128, :] = whole[:, 512:LATE].astype(bf16)
    over_tp[128:256, :] = whole[:, LATE : LATE + 128].astype(bf16)
    over_tp[256:352, :] = jnp.zeros((96, 128), bf16)
    for layer in range(2):
        first = 64 * layer
        over_tp[256 + 48 * layer : 293 + 48 * layer, :] = total[first : first + 37, :].astype(bf16)
        for tap in range(CONV + 1):
            for pair in range(PAIRS):
                row = first + 37 + PAIRS * tap + pair
                conv_x[5 * layer + tap : 5 * layer + tap + 1, lanes_of(pair)] = total[row : row + 1, :]
        heads[3 * layer : 3 * layer + 3, :] = total[first + 52 : first + 55, :]


def weight_outputs_kernel(lower, upper, late, attn, ssm, gate, up, down, query, zx, dt):
    for layer, ref in ((0, lower), (1, upper)):
        for index, out in enumerate((gate, up, down)):
            out[layer] = ref[:, 512 * index : 512 * (index + 1)].astype(f32)
        attn[layer] = ref[:, 1536:1664].astype(f32)
        ssm[layer] = ref[:, 1664:2048].astype(f32)
        zx[layer, :, 0, :] = ref[:, 2048:2432].astype(f32)
        query[layer] = ref[:, 2432:2560].astype(f32)
    zx[0, :, 1, :] = late[:, 0:XLOC]
    zx[1, :, 1, :] = lower[:, 2560:2944].astype(f32)
    dt[0] = late[:, XLOC : XLOC + HLOC]
    dt[1] = lower[:, 2944 : 2944 + HLOC].astype(f32)


def tp_outputs_kernel(flags, *refs):
    parts, (shared, gains1, gains2, conv_bc, every) = refs[:8], refs[8:]
    total = jnp.zeros((96, 128), f32)
    for index, part in enumerate(parts):
        every[index] = part[...].astype(f32)
        total = total + part[256:352, :].astype(f32)
    for layer in range(2):
        for rank in range(8):
            own = slice(128 * rank, 128 * rank + 128)
            shared[layer, :, own] = every[flags[16 + rank], 128 * layer : 128 * layer + 128, :]
        for row in range(16):
            own = slice(128 * row, 128 * row + 128)
            at = 48 * layer + row
            gains1[layer : layer + 1, own] = total[at : at + 1, :]
            gains2[layer : layer + 1, own] = total[at + 16 : at + 17, :]
        for rank in range(4):
            part = every[flags[20 + rank], 288 + 48 * layer : 296 + 48 * layer, :]
            conv_bc[5 * layer : 5 * layer + 5, 128 * rank : 128 * rank + 128] = part[0:5, :]


def body(
    inputs, cotangent, segment_ids, w_query, w_shared, w_zx, w_dt, w_attn_out, w_ssm_out, w_gate, w_up, w_down,
    gains, conv_x, conv_bc, head_params,
):
    layers = w_query.shape[0]
    rank, ctx = lax.axis_index("tp"), lax.axis_index("ctx")
    y, core = rank // 2, rank % 2
    model = inputs.shape[2]

    def local_of(block_y, block_core):
        return jnp.where(block_core == core, 0, 4) + (block_y - y) % 4

    seg_all = segment_ids[0]
    first_row = ctx * ROWS
    padded = jnp.concatenate([jnp.full((CONV - 1,), -1, i32), seg_all])
    seg_ext = lax.dynamic_slice_in_dim(padded, first_row, ROWS + CONV - 1)
    seg_own = seg_ext[CONV - 1 :]
    blocks = seg_all.reshape(SEQ_BLOCKS, ROWS)
    seg_rows = jnp.stack(
        [
            jnp.where(ctx >= back, lax.dynamic_index_in_dim(blocks, jnp.maximum(ctx - back, 0), 0, False), -1)
            for back in range(SEQ_BLOCKS)
        ]
        + [jnp.full((ROWS,), -1, i32)] * 4
    ).astype(f32)
    naturals = jnp.arange(8, dtype=i32)
    flags = jnp.concatenate(
        [
            jnp.stack([rank, y, core, ctx, seg_ext[CONV - 2], seg_own[-1], rank, rank]).astype(i32),
            local_of(naturals % 4, naturals // 4).astype(i32),
            local_of(naturals // 2, naturals % 2).astype(i32),
            (jnp.where(naturals < 4, core, 1 - core) * 4 + (y + naturals) % 4).astype(i32),
        ]
    )

    half_width = HD // 2
    frequency = rope_base ** (-jnp.arange(half_width, dtype=f32) / half_width)
    places = (first_row + jnp.arange(ROWS, dtype=i32)).astype(f32)
    angles = places[:, None] * frequency[None, :]
    cosine, sine = jnp.cos(angles), jnp.sin(angles)
    marks = [seg_ext[tap : tap + ROWS] == seg_own for tap in range(CONV - 1)]
    marks += [seg_own, seg_own == seg_ext[CONV - 2], seg_own == seg_own[-1]]
    marks = jnp.pad(jnp.stack([mark.astype(f32) for mark in marks], axis=1), ((0, 0), (0, 122)))
    table = jnp.concatenate([cosine, cosine, -sine, sine, marks], axis=1)

    own_conv = jnp.maximum(rank - 4, 0) * 128
    small = []
    for layer in range(layers):
        rows = [conv_x[layer], lax.dynamic_slice_in_dim(conv_bc[layer], own_conv, 128, 1)]
        rows.append(jnp.pad(head_params[layer], ((0, 2), (0, 128 - HLOC))))
        small.append(jnp.pad(jnp.concatenate(rows, axis=1), ((0, 3), (0, 0))))

    def packed(*members):
        width = sum(
            {4: 2 * XLOC}.get(member.ndim, 128 if member.shape[2] in (1024, HLOC) else member.shape[2])
            for member, _ in members
        )
        (columns,) = run_kernel(
            pack_kernel,
            [shape_of((w_query.shape[1], width), bf16)],
            rank.astype(i32).reshape(1),
            *(Layer(member, layer) for member, layer in members),
        )
        return lax.all_gather(columns, ("fsdp", "ctx"), axis=0, tiled=True)

    def proj_members(layer):
        return [(member, layer) for member in (w_zx, w_query, w_dt, w_shared)]

    weight_a = packed(*proj_members(0), (w_attn_out, 0), (w_ssm_out, 0))
    weight_b = packed(*proj_members(1), (w_gate, 0), (w_up, 0), (w_down, 0))
    weight_c = packed((w_gate, 1), (w_up, 1), (w_down, 1), (w_attn_out, 1), (w_ssm_out, 1))
    proj_place = [(weight_a, 0, PROJ), (weight_b, 0, PROJ)]
    out_place = [(weight_a, PROJ, 512), (weight_c, 1536, 512)]
    gate_up_place = [(weight_b, PROJ, 1024), (weight_c, 0, 1024)]
    down_place = [(weight_b, PROJ + 1024, 512), (weight_c, 1024, 512)]

    def together(*values):
        return lax.optimization_barrier(values)

    weight_a, table, seg_rows, small = together(weight_a, table, seg_rows, small)
    normed_shape = shape_of((ROWS, model), bf16)
    normed_kept = kept((ROWS, model), bf16)
    normed_b, inverse1, hidden, dffn_b, grad_hidden = run_kernel(
        first_kernel,
        [normed_shape, kept((SHARE, 128)), kept((SHARE, model)), normed_kept, kept((SHARE, model))],
        flags, inputs, cotangent, gains[0],
    )
    weight_a, normed_b = together(weight_a, normed_b)
    proj_place[0] = (weight_a, 0, PROJ)
    out_place[0] = (weight_a, PROJ, 512)
    normed_parts, dffn_parts = (normed_b,), (dffn_b,)
    saved = []
    wide = shape_of((ROWS, 512))
    proj_weight = fetched("proj_0", *proj_place[0])
    for layer in range(layers):
        normed_b, z, z_kept, xs, query, query_kept, dtn, dtn_kept = run_kernel(
            proj_kernel,
            [
                normed_kept, shape_of((ROWS, XLOC)), kept((ROWS, XLOC)), wide, shape_of((ROWS, HD), bf16),
                kept((ROWS, HD), bf16), shape_of((ROWS, 128)), kept((ROWS, 128)),
            ],
            flags, *(passed(normed_parts) if layer > 0 else normed_parts), proj_weight, table,
            scratch=[pltpu.VMEM((ROWS, PROJ), f32)], us=3.3,
        )
        halo = along_ctx(xs[ROWS - 8 :], 1)
        shared_own, shared_ext = run_kernel(
            shared_kernel,
            [shape_of((ROWS, 128), bf16), kept((264, 128))],
            flags, xs, Columns(halo), table, small[layer],
        )
        prepared = run_kernel(
            prep_kernel,
            [
                kept((264, XLOC)), shape_of((ROWS, XLOC)), kept((ROWS, XLOC)), shape_of((ROWS, 256)),
                kept((ROWS, 256)), shape_of((16, ROWS)), kept((16, ROWS)),
            ],
            None, xs, dtn, Columns(halo), table, small[layer], us=1.5,
        )
        shared_parts, prepared = from_all(shared_own, prepared)
        x_ext, xc, xc_kept, rates, rates_kept, rates_t, rates_t_kept = prepared
        message, shared, shared_kept = run_kernel(
            state_kernel,
            [shape_of((KV + MSG, NSTATE), bf16), shape_of((8 * ROWS, 128), bf16), kept((8 * ROWS, 128), bf16)],
            flags, *passed(shared_parts), xc, rates, rates_t, table, us=1.9,
        )
        earlier = tuple(along_ctx(message, back) for back in (1, 2, 3))
        (intra,) = run_kernel(
            intra_kernel, [shape_of((ROWS, XLOC))],
            flags, shared, xc, rates, rates_t, table, seg_rows, small[layer], us=1.3,
        )
        if layer > 0:
            earlier, intra = together(earlier, intra)
        else:
            earlier, intra, out_weight = together(earlier, intra, fetched(f"out_{layer}", *out_place[layer]))
        halves = [Columns(part, 0, NSTATE, rows=KV) for part in earlier]
        (swapped,) = run_kernel(halves_kernel, [shape_of((3 * KV, NSTATE), bf16)], None, *halves)
        state, ssm_y, gated, gated_kept = run_kernel(
            carry_kernel,
            [kept((XLOC, NSTATE)), kept((ROWS, XLOC)), shape_of((ROWS, XLOC), bf16), kept((ROWS, XLOC), bf16)],
            flags, *passed(earlier), shared, rates, table, intra, z, us=1.9,
        )
        swapped, gated = together(other_core(swapped), gated)
        attn, attn_kept, log_total, pairs = run_kernel(
            attention_kernel,
            [
                shape_of((ROWS, HD), bf16), kept((ROWS, HD), bf16), kept((ROWS, HD)),
                kept((SEQ_BLOCKS * ROWS, 2 * HD), bf16),
            ],
            flags, query, shared, *halves, Columns(swapped), table, seg_rows, us=2.0,
        )
        if layer > 0:
            out_weight = fetched(f"out_{layer}", *out_place[layer])
        parts = summed_rows([attn, gated], out_weight)
        if layer > 0:
            parts, gate_up_weight = together(parts, fetched(f"gate_up_{layer}", *gate_up_place[layer]))
        parts, (rows,) = together(parts, restored(f"hidden_{layer}", [hidden]))
        hidden1, normed2, inverse2 = add_norm(rows, parts, gains[layer, 1])
        if layer > 0:
            normed_parts, down_weight = from_all(normed2, fetched("down_1", *down_place[layer]))
        else:
            normed_parts = from_all(normed2)
            gate_up_weight, down_weight = fetched_all("ffn_0", [gate_up_place[layer], down_place[layer]])
        wide_kept = kept((ROWS, 512))
        normed2_b, gate, up, act_b, act_kept = run_kernel(
            gate_up_kernel, [normed_kept, wide_kept, wide_kept, shape_of((ROWS, 512), bf16), kept((ROWS, 512), bf16)],
            None, *passed(normed_parts), gate_up_weight, us=2.3,
        )
        saved.append(
            (
                hidden, normed_b, inverse1, shared_ext, shared_kept, query_kept, x_ext, xc_kept, z_kept, dtn_kept,
                rates_kept, rates_t_kept, pairs, log_total, state, ssm_y, attn_kept, gated_kept, hidden1, inverse2, normed2_b,
                gate, up, act_kept,
            )
        )
        if layer + 1 < layers:
            parts, (rows,) = together(summed_rows([act_b], down_weight), restored(f"hidden1_{layer}", [hidden1]))
            hidden, next_normed, inverse1 = add_norm(rows, parts, gains[layer + 1, 0])
            normed_parts, proj_weight = from_all(next_normed, fetched("proj_1", *proj_place[layer + 1]))

    small_parts = [None] * layers
    inner = None
    for layer in reversed(range(layers)):
        (
            hidden, normed_b, inverse1, shared_ext, shared, query, x_ext, xc, z, dtn, rates, rates_t,
            pairs, log_total, state, ssm_y, attn, gated, hidden1, inverse2, normed2_b, gate, up, act_b,
        ) = saved[layer]
        last = layer == 0
        dffn_b, dgate_up = run_kernel(
            gate_up_back_kernel, [normed_kept, shape_of((ROWS, 1024), bf16)],
            None, *passed(dffn_parts), down_weight, stored(gate), stored(up), us=2.7,
        )
        parts = summed_rows([dgate_up], gate_up_weight)
        outer = weight_gradients(
            [(normed2_b, dgate_up), (dffn_b, act_b)], 3072 if last else 2560, 1536, 0, inner
        )
        parts, outer = lax.optimization_barrier((parts, outer))
        parts, kept_rows = together(parts, restored(f"norm2_{layer}", [grad_hidden, hidden1, inverse2]))
        grad_mid, dmix, ggain2 = norm_back(parts, *kept_rows, gains[layer, 1])
        dmix_parts = from_all(dmix)
        dmix_parts, fetch = from_all(
            dmix,
            fetched_all(
                f"mixer_{layer}",
                [out_place[layer]]
                + [(array, 0, array.shape[1]) for array in (z, ssm_y, shared, rates, rates_t, xc, query, pairs, state)],
            ),
        )
        from_kept = [stored(array) for array in (shared, xc, rates, rates_t, state)]
        out_weight, z, ssm_y, shared, rates, rates_t, xc, query, pairs, state = fetch
        dmix_b, dattn, dy, dz, message = run_kernel(
            gate_back_kernel,
            [
                normed_kept, shape_of((ROWS, HD), bf16), shape_of((ROWS, XLOC)), shape_of((ROWS, XLOC), bf16),
                shape_of((MSG, NSTATE), bf16),
            ],
            flags, *passed(dmix_parts), out_weight, z, ssm_y, shared, rates, rates_t, table, us=2.6,
            scratch=[pltpu.VMEM((ROWS, XLOC), f32), pltpu.VMEM((ROWS, 512), f32)],
        )
        after = tuple(along_ctx(message, -ahead) for ahead in (1, 2, 3))
        early, mine, theirs = run_kernel(
            attention_back_kernel,
            [kept((ROWS, 512), bf16), shape_of((4 * ROWS, HD)), shape_of((4 * ROWS, HD), bf16)],
            flags, dattn, dz, query, pairs, stored(log_total), table, seg_rows, us=2.9,
        )
        got = other_core(theirs)
        dx, dshared, drates, dskip = run_kernel(
            intra_back_kernel,
            [kept((ROWS, XLOC)), kept((ROWS, 2 * NSTATE)), kept((ROWS, 256)), kept((1, XLOC))],
            flags, dy, xc, shared, rates, rates_t, table, seg_rows, state, small[layer], us=3.6,
            scratch=[pltpu.VMEM((128, ROWS), f32), pltpu.VMEM((ROWS, 128), f32)],
        )
        dkv = parts_from(mine, got, along_ctx, -1)
        width = outer.shape[1]
        outer = weight_gradients([(dmix_b, attn), (dmix_b, gated)], width, 512, 3, outer)
        outer = weight_gradients([(normed_b, early)], width, 512, 4, outer)
        if last:
            after, dkv, outer, upper = together(after, dkv, outer, upper)
            lower = lax.psum_scatter(outer, ("fsdp", "ctx"), scatter_dimension=0, tiled=True)
        else:
            after, dkv, outer = together(after, dkv, outer)
            upper = lax.psum_scatter(outer, ("fsdp", "ctx"), scatter_dimension=0, tiled=True)
        packed_grads, state_grad = run_kernel(
            packed_back_kernel, [shape_of((8 * ROWS, 128), bf16), kept((XLOC, NSTATE))],
            flags, *map(stored, after), *from_kept[:3], table, stored(dshared), *map(stored, dkv), us=2.5,
        )
        dshared_parts = parts_of_sum(packed_grads[: 4 * ROWS], packed_grads[4 * ROWS :], along_y, 1)
        dxpre, edge_x, gconv_x, ddt, gheads = run_kernel(
            state_back_kernel,
            [kept((ROWS, XLOC)), shape_of((8, XLOC)), kept((8, XLOC)), kept((ROWS, 128)), kept((8, 128))],
            flags, stored(state_grad), *from_kept[:4], table, from_kept[4], stored(small[layer]),
            stored(dtn), stored(dx), stored(drates), stored(x_ext),
            scratch=[pltpu.VMEM((272, XLOC), f32), pltpu.VMEM((ROWS, XLOC), f32), pltpu.VMEM((ROWS, 128), f32)],
            us=3.5,
        )
        dshared_parts, edge_x = together(dshared_parts, edge_x)
        edge_x = along_ctx(edge_x, -1)
        dsh, edge_sh, gconv_sh = run_kernel(
            shared_back_kernel,
            [shape_of((ROWS, 128)), shape_of((8, 128)), kept((8, 128))],
            flags, *summands(dshared_parts), stored(shared_ext), table, small[layer],
            scratch=[pltpu.VMEM((272, 128), f32)],
        )
        edge_sh, proj_weight = together(
            along_ctx(edge_sh, -1), fetched(f"proj_again_{layer}", *proj_place[layer])
        )
        (late,) = run_kernel(
            late_kernel, [shape_of((ROWS, LATE), bf16)], flags, stored(dxpre), Columns(edge_x), dsh,
            Columns(edge_sh), stored(ddt),
        )
        parts = summed_rows([early, late], proj_weight)
        if not last:
            inner = weight_gradients([(normed_b, Columns(late, 0, 512))], 3072, 512, 5)
            parts, inner = together(parts, inner)
            upper_pair = (normed_b, Columns(late, 4, 128))
        parts, kept_rows = together(parts, restored(f"norm1_{layer}", [grad_mid, hidden, inverse1]))
        grad_hidden, rounded, ggain1 = norm_back(parts, *kept_rows, gains[layer, 0])
        if last:
            dffn_parts = from_all(rounded)
        else:
            dffn_parts, (down_weight, gate_up_weight) = from_all(
                rounded, fetched_all("ffn_again", [down_place[layer - 1], gate_up_place[layer - 1]])
            )
            last_hidden1, last_act = hidden1, act_b
        (small_parts[layer],) = run_kernel(
            small_kernel, [shape_of((64, 128), bf16)],
            None, *map(stored, (ggain1, ggain2, gconv_sh, gconv_x, gheads, dskip)),
        )
    (small_all,) = run_kernel(
        spread_kernel, [shape_of((128, 128), bf16)], None, jnp.concatenate(small_parts, axis=0),
        scratch=[pltpu.VMEM((128, 128), f32)],
    )
    owned = owned_gradients([(normed_b, late), upper_pair], small_all)
    owned = lax.all_to_all(owned, ("fsdp", "ctx"), 0, 0, tiled=True)
    (input_grad,) = run_kernel(natural_kernel, [kept((ROWS, model))], flags, *passed(dffn_parts))
    last_act, down_weight, _ = together(last_act, fetched("down_last", *down_place[1]), small_parts[0])
    (layer_out,) = run_kernel(
        output_kernel, [shape_of((SHARE, model), bf16)], None,
        stored(last_hidden1), *summands(summed_rows([last_act], down_weight)),
    )
    (layer_out,) = run_kernel(natural_kernel, [normed_kept], flags, *passed(from_all(layer_out)))
    def pair_of(width):
        return shape_of((layers, model // 16, width))

    owned, layer_out, input_grad = together(owned, layer_out, input_grad)
    over_tp, late_sum, gconv_x, gheads = run_kernel(
        block_sum_kernel,
        [
            shape_of((352, 128), bf16), kept((model // 16, LATE)), shape_of((layers * (CONV + 1), XLOC)),
            shape_of((8, 128)),
        ],
        None, Columns(owned),
        scratch=[pltpu.VMEM((128, 128), f32)],
    )
    grad_shared, ggains1, ggains2, gconv_bc = run_kernel(
        tp_outputs_kernel,
        [
            pair_of(1024), shape_of((layers, model)), shape_of((layers, model)),
            shape_of((layers * (CONV + 1), 512)),
        ],
        flags, *passed(from_all(over_tp)),
        scratch=[pltpu.VMEM((8, 352, 128), f32)], us=2.0,
    )
    lower, grad_shared = together(lower, grad_shared)
    grad_attn, grad_ssm, grad_gate, grad_up, grad_down, grad_query, grad_zx, grad_dt = run_kernel(
        weight_outputs_kernel,
        [
            *(kept((layers, model // 16, width)) for width in (128, 384, 512, 512, 512, 128)),
            shape_of((layers, model // 16, 2, XLOC)), pair_of(HLOC),
        ],
        None, stored(lower), stored(upper), stored(late_sum), us=3.0,
    )
    gconv_x = gconv_x.reshape(layers, CONV + 1, XLOC)
    gconv_bc = gconv_bc.reshape(layers, CONV + 1, 512)
    gheads = gheads[: 3 * layers].reshape(layers, 3, 128)[:, :, :HLOC]
    return (
        layer_out[None],
        input_grad[None],
        grad_query,
        grad_shared,
        grad_zx,
        grad_dt,
        grad_attn,
        grad_ssm,
        grad_gate,
        grad_up,
        grad_down,
        ggains1,
        gconv_x,
        gconv_bc,
        gheads[:, :2],
        ggains2,
        gheads[:, 2],
    )


def solution(mesh):
    columns = P(None, ("fsdp", "ctx"), "tp")
    rows = P("fsdp", "ctx", None)
    return jax.shard_map(
        body,
        mesh=mesh,
        in_specs=(
            rows, rows, P("fsdp", None), columns, P(None, ("fsdp", "ctx"), None),
            P(None, ("fsdp", "ctx"), None, "tp"), columns, columns, columns, columns, columns, columns,
            P(), P(None, None, "tp"), P(), P(None, None, "tp"),
        ),
        out_specs=(
            rows, rows, columns, P(None, ("fsdp", "ctx"), None), P(None, ("fsdp", "ctx"), None, "tp"),
            columns, columns, columns, columns, columns, columns,
            P(), P(None, None, "tp"), P(), P(None, None, "tp"), P(), P(None, "tp"),
        ),
        check_vma=False,
    )
```

```python
import math
from functools import partial

import jax
import jax.numpy as jnp
from jax import lax
from jax.experimental import pallas as pl
from jax.experimental.pallas import tpu as pltpu
from jax.sharding import PartitionSpec as P

HD = 128
HP = 64
NSTATE = 256
CONV = 4
ROWS = 256
SHARE = 32
XLOC = 384
PROJ = 1152
LATE = 640
HLOC = 6
PAIRS = 3
SEQ_BLOCKS = 4
MSG = XLOC + 16
KV = 128
VMEM_LIMIT = 16 * 1024 * 1024

norm_eps = 1e-05
rope_base = 100000000000.0
bf16 = jnp.bfloat16
f32 = jnp.float32
i32 = jnp.int32


def along_y(value, steps):
    pairs = [(i, ((i // 2 + steps) % 4) * 2 + i % 2) for i in range(8)]
    return lax.ppermute(value, "tp", pairs)


def other_core(value):
    return lax.ppermute(value, "tp", [(i, i ^ 1) for i in range(8)])


def along_ctx(value, steps):
    first, last = max(0, -steps), min(4, 4 - steps)
    return lax.ppermute(value, "ctx", [(i, i + steps) for i in range(first, last)])


def ring(value, axis, steps):
    return lax.ppermute(value, axis, [(i, (i + steps) % 4) for i in range(4)])


def from_all(value, beside=None):
    half = [value] + [along_y(value, -k) for k in (1, 2, 3)]
    if beside is not None:
        half[1], beside = lax.optimization_barrier((half[1], beside))
    parts = tuple(half + [other_core(part) for part in half])
    return parts if beside is None else (parts, beside)


def dot_nn(a, b):
    return jnp.dot(a, b, preferred_element_type=f32)


def dot_nt(a, b):
    return lax.dot_general(a, b, (((1,), (1,)), ((), ())), preferred_element_type=f32)


def dot_tn(a, b):
    return lax.dot_general(a, b, (((0,), (0,)), ((), ())), preferred_element_type=f32)


def shape_of(shape, dtype=f32):
    return jax.ShapeDtypeStruct(shape, dtype)


class Columns:
    def __init__(self, array, block=0, width=None, rows=None, keep=False):
        self.array, self.block, self.keep = array, block, keep
        self.shape = (rows or array.shape[0],) + array.shape[1:-1] + (width or array.shape[-1],)

    def spec(self):
        place = (0,) * (len(self.shape) - 1) + (self.block,)
        return pl.BlockSpec(self.shape, lambda i: place, pipeline_mode=pl.Buffered(1))


class Layer:
    def __init__(self, array, layer):
        self.array, self.layer, self.keep = array, layer, True
        self.shape = (1,) + array.shape[1:]

    def spec(self):
        place = (self.layer,) + (0,) * (len(self.shape) - 1)
        return pl.BlockSpec(self.shape, lambda i: place, pipeline_mode=pl.Buffered(1))


def stored(array):
    return Columns(array, keep=True)


def summands(parts):
    return [stored(parts[0])] + passed(parts[1:])


def passed(arrays):
    return [Columns(array) for array in arrays]


def kept(shape, dtype=f32):
    return pltpu.HBM(shape, dtype)


def fetch_kernel(places, *refs):
    count = len(places)
    sources, outs, sems = refs[:count], refs[count : 2 * count], refs[-1]
    copies = []
    for (start, pieces), source, out in zip(places, sources, outs):
        rows, width = out.shape[0] // pieces, out.shape[1]
        for index in range(pieces):
            own = pl.ds(rows * index, rows)
            copies.append(
                pltpu.make_async_copy(
                    source.at[own, pl.ds(start, width)], out.at[own, :], sems.at[len(copies)]
                )
            )
    for copy in copies:
        copy.start()
    for copy in copies:
        copy.wait()


def fetched_all(name, sources):
    places = [(start, 4 if array.shape[0] == 2048 and width > 128 else 1) for array, start, width in sources]
    whole = pl.BlockSpec(memory_space=pltpu.VMEM)
    return pl.pallas_call(
        partial(fetch_kernel, places),
        name=name,
        out_shape=tuple(pltpu.VMEM((array.shape[0], width), array.dtype) for array, _, width in sources),
        in_specs=[pl.BlockSpec(memory_space=pltpu.HBM)] * len(sources),
        out_specs=tuple(whole for _ in sources),
        scratch_shapes=[pltpu.SemaphoreType.DMA((sum(pieces for _, pieces in places),))],
        compiler_params=pltpu.CompilerParams(vmem_limit_bytes=VMEM_LIMIT),
        cost_estimate=pl.CostEstimate(
            flops=0, bytes_accessed=sum(2 * array.shape[0] * width for array, _, width in sources), transcendentals=0
        ),
    )(*(pltpu.with_memory_space_constraint(array, pltpu.HBM) for array, _, _ in sources))


def fetched(name, array, start, width):
    return fetched_all(name, [(array, start, width)])[0]


def restored(name, arrays):
    return fetched_all(name, [(array, 0, array.shape[1]) for array in arrays])


def run_kernel(kernel, outs, flags, *args, scratch=(), us=1.0):
    whole = pl.BlockSpec(memory_space=pltpu.VMEM)
    own = [isinstance(arg, (Columns, Layer)) for arg in args]
    specs, arrays, out_specs = [], [], []
    for arg, copied in zip(args, own):
        specs.append(arg.spec() if copied else whole)
        array = arg.array if copied else arg
        arrays.append(pltpu.with_memory_space_constraint(array, pltpu.HBM) if copied and arg.keep else array)
    for out in outs:
        in_vmem = isinstance(out, jax.ShapeDtypeStruct)
        out_specs.append(whole if in_vmem else pl.BlockSpec(out.shape, lambda i, n=len(out.shape): (0,) * n))
        own.append(not in_vmem)
    moved = sum(2 * math.prod(arg.shape) for arg in args) + sum(2 * math.prod(o.shape) for o in outs)
    if flags is not None:
        specs = [pl.BlockSpec(memory_space=pltpu.SMEM)] + specs
        arrays = [flags] + arrays
    return pl.pallas_call(
        kernel,
        grid=(1,) if any(own) else (),
        out_shape=tuple(outs),
        in_specs=specs,
        out_specs=tuple(out_specs),
        scratch_shapes=list(scratch),
        compiler_params=pltpu.CompilerParams(vmem_limit_bytes=VMEM_LIMIT),
        cost_estimate=pl.CostEstimate(flops=int(us * 1e9), bytes_accessed=moved, transcendentals=0),
    )(*arrays)


def local_block(flags, natural):
    return pl.multiple_of(flags[8 + natural] * SHARE, SHARE)


def rank_block(flags, rank):
    return pl.multiple_of(flags[16 + rank] * ROWS, ROWS)


def lane_index(shape):
    return lax.broadcasted_iota(i32, shape, len(shape) - 1)


def spread(columns, pair):
    low = lane_index((1, 128)) < HP
    return jnp.where(low, columns[:, 2 * pair : 2 * pair + 1], columns[:, 2 * pair + 1 : 2 * pair + 2])


def lanes_of(pair):
    return slice(128 * pair, 128 * pair + 128)


def turned(value, table, sign):
    return value * table[:, 0:128] + sign * (pltpu.roll(value, 64, 1) * table[:, 128:256])


def segments(table):
    return table[:, 259:260]


def sigmoid(v):
    return 1.0 / (1.0 + jnp.exp(-v))


def softplus(v):
    return jnp.maximum(v, 0.0) + jnp.log1p(jnp.exp(-jnp.abs(v)))


def conv_sum(ext, table, weight):
    total = weight[CONV : CONV + 1, :] + ext[8 : 8 + ROWS, :] * weight[3:4, :]
    for tap in range(CONV - 1):
        total = total + table[:, 256 + tap : 257 + tap] * ext[5 + tap : 5 + tap + ROWS, :] * weight[tap : tap + 1, :]
    return total


def conv_back(grad_out, ext, table, weight, work, grad_ref, edge_ref, gweight_ref):
    total = conv_sum(ext, table, weight)
    sig = sigmoid(total)
    grad = grad_out * sig * (1.0 + total * (1.0 - sig))
    width = grad.shape[1]
    gweight_ref[...] = jnp.zeros((8, width), f32)
    gweight_ref[CONV : CONV + 1, :] = jnp.sum(grad, axis=0, keepdims=True)
    gweight_ref[3:4, :] = jnp.sum(grad * ext[8 : 8 + ROWS, :], axis=0, keepdims=True)
    work[0:8, :] = jnp.zeros((8, width), f32)
    work[264:272, :] = jnp.zeros((8, width), f32)
    own = grad * weight[3:4, :]
    edge = jnp.zeros((8, width), f32)
    for tap in range(CONV - 1):
        part = grad * table[:, 256 + tap : 257 + tap]
        gweight_ref[tap : tap + 1, :] = jnp.sum(
            part * ext[5 + tap : 5 + tap + ROWS, :], axis=0, keepdims=True
        )
        work[8:264, :] = part * weight[tap : tap + 1, :]
        own = own + work[11 - tap : 11 - tap + ROWS, :]
        edge = edge + work[3 - tap : 11 - tap, :]
    grad_ref[...] = own
    edge_ref[...] = edge


def pack_kernel(place, *refs):
    out, at, index = refs[-1], 0, 0
    while index < len(refs) - 1:
        ref = refs[index]
        if len(ref.shape) == 4:
            out[:, at : at + XLOC] = ref[0, :, 0, :]
            out[:, at + XLOC : at + 512] = refs[index + 1][0]
            out[:, at + 512 : at + 896] = ref[0, :, 1, :]
            at, index = at + 896, index + 2
            continue
        width = min(ref.shape[2], 512)
        if width == HLOC:
            out[:, at : at + 128] = jnp.zeros((out.shape[0], 128), bf16)
            out[:, at : at + HLOC] = ref[0]
            width = 128
        elif ref.shape[2] == 1024:
            width = 128
            out[:, at : at + width] = ref[0, :, pl.ds(pl.multiple_of(place[0] * 128, 128), 128)]
        else:
            out[:, at : at + width] = ref[0]
        at, index = at + width, index + 1


def first_kernel(flags, rows, cotangent, gain, normed, inverse, hidden_kept, grads, grad):
    for block in range(8):
        own = slice(SHARE * block, SHARE * (block + 1))
        from_rows = pl.ds(pl.multiple_of(flags[24 + block] * SHARE, SHARE), SHARE)
        wide = rows[0, from_rows, :].astype(f32)
        scale = lax.rsqrt(jnp.mean(wide * wide, axis=1, keepdims=True) + norm_eps)
        normed[own, :] = (wide * scale * gain[0:1, :]).astype(bf16)
        grads[own, :] = cotangent[0, from_rows, :]
        if block == 0:
            hidden_kept[...] = wide
            inverse[...] = jnp.broadcast_to(scale, inverse.shape)
            grad[...] = cotangent[0, from_rows, :].astype(f32)


def joined(parts):
    return parts[0][...] if len(parts) == 1 else jnp.concatenate([part[...] for part in parts], axis=0)


def projections(flags, work, table, z, z_kept, xs, query, query_kept, dtn, dtn_kept):
    for block in range(8):
        own = slice(SHARE * block, SHARE * (block + 1))
        from_rows = pl.ds(local_block(flags, block), SHARE)
        for out in (z, z_kept):
            out[own, :] = work[from_rows, 0:XLOC]
        xs[own, 0:XLOC] = work[from_rows, 512:896]
        xs[own, XLOC:512] = work[from_rows, 1024:PROJ]
        head = turned(work[from_rows, XLOC:512], table[own, :], 1.0).astype(bf16)
        for out in (query, query_kept):
            out[own, :] = head
        for out in (dtn, dtn_kept):
            out[own, :] = work[from_rows, 896:1024]


def proj_kernel(flags, p0, p1, p2, p3, p4, p5, p6, p7, weight, table, normed, *refs):
    rows = joined((p0, p1, p2, p3, p4, p5, p6, p7))
    normed[...] = rows
    work = refs[-1]
    work[...] = dot_nn(rows, weight[...])
    projections(flags, work, table, *refs[:-1])


def first_proj_kernel(flags, rows, weight, table, z, z_kept, xs, query, query_kept, dtn, dtn_kept, work):
    step = pl.program_id(0)
    part = dot_nn(rows[...], weight[...])

    @pl.when(step == 0)
    def _():
        work[...] = part

    @pl.when(step > 0)
    def _():
        work[...] = work[...] + part

    @pl.when(step == 3)
    def _():
        projections(flags, work, table, z, z_kept, xs, query, query_kept, dtn, dtn_kept)


def first_projections(flags, normed, weight, table):
    model = normed.shape[1]
    whole = pl.BlockSpec(memory_space=pltpu.VMEM)
    outs = [
        shape_of((ROWS, XLOC)), kept((ROWS, XLOC)), shape_of((ROWS, 512)), shape_of((ROWS, HD), bf16),
        kept((ROWS, HD), bf16), shape_of((ROWS, 128)), kept((ROWS, 128)),
    ]
    return pl.pallas_call(
        first_proj_kernel,
        grid=(4,),
        out_shape=tuple(outs),
        in_specs=[
            pl.BlockSpec(memory_space=pltpu.SMEM),
            pl.BlockSpec((ROWS, model // 4), lambda i: (0, i)),
            pl.BlockSpec((model // 4, PROJ), lambda i: (i, 0)),
            whole,
        ],
        out_specs=tuple(
            whole if isinstance(out, jax.ShapeDtypeStruct) else pl.BlockSpec(out.shape, lambda i: (0, 0))
            for out in outs
        ),
        scratch_shapes=[pltpu.VMEM((ROWS, PROJ), f32)],
        compiler_params=pltpu.CompilerParams(vmem_limit_bytes=VMEM_LIMIT),
        cost_estimate=pl.CostEstimate(flops=4 * 10**9, bytes_accessed=2 * model * PROJ, transcendentals=0),
    )(flags, normed, pltpu.with_memory_space_constraint(weight, pltpu.HBM), table)


def shared_kernel(flags, xs, halo, table, small, out, ext):
    own = xs[:, XLOC:512]
    ext[0:8, :] = halo[:, XLOC:512]
    ext[8 : 8 + ROWS, :] = own
    total = conv_sum(ext, table, small[:, XLOC:512])
    rank = flags[0]
    out[...] = jnp.where(
        rank < 2, turned(own, table, 1.0), jnp.where(rank < 4, own, total * sigmoid(total))
    ).astype(bf16)


def prep_kernel(xs, dtn, halo, table, small, ext, xc, xc_kept, rates, rates_kept, rates_t, rates_t_kept):
    ext[0:8, :] = halo[:, 0:XLOC]
    ext[8 : 8 + ROWS, :] = xs[:, 0:XLOC]
    total = conv_sum(ext, table, small[:, 0:XLOC])
    for out in (xc, xc_kept):
        out[...] = total * sigmoid(total)
    params = small[:, 512:640]
    rate = softplus(dtn[...] + params[1:2, :])
    logs = -jnp.exp(params[0:1, :]) * rate
    rows = lax.broadcasted_iota(i32, (ROWS, ROWS), 0)
    lower = (rows >= lane_index((ROWS, ROWS))).astype(f32)
    running = jnp.dot(lower, logs, precision=lax.Precision.HIGHEST, preferred_element_type=f32)
    for out in (rates, rates_kept):
        out[:, 0:128] = rate
        out[:, 128:256] = running
    rate_t, running_t = rate.T[0:8, :], running.T[0:8, :]
    for out in (rates_t, rates_t_kept):
        out[0:8, :] = rate_t
        out[8:16, :] = running_t


def block_decays(flags, rates_t):
    kept = jnp.where(flags[4] == flags[5], 1.0, 0.0)
    return jnp.exp(rates_t[8:16, ROWS - 1 : ROWS]) * kept


def decay_rows(flags, rates_t):
    rows = jnp.broadcast_to(block_decays(flags, rates_t), (8, NSTATE))
    return jnp.concatenate([rows, jnp.zeros((8, NSTATE), f32)], axis=0).astype(bf16)


def weights_in(rates, table):
    last = rates[ROWS - 1 : ROWS, 128:256]
    gap = jnp.exp(last - rates[:, 128:256]) * table[:, 261:262]
    return gap, gap * rates[:, 0:128]


def rank_columns(flags, shared, first):
    return jnp.concatenate(
        [shared[pl.ds(rank_block(flags, rank), ROWS), :] for rank in (first, first + 1)], axis=1
    )


def inject_of(flags, shared):
    return rank_columns(flags, shared, 4)


def readout_of(flags, shared):
    return rank_columns(flags, shared, 6)


def carry_of(rates, table):
    return jnp.exp(rates[:, 128:256]) * table[:, 260:261]


def state_kernel(flags, s0, s1, s2, s3, s4, s5, s6, s7, xc, rates, rates_t, table, out, shared, shared_kept):
    for index, part in enumerate((s0, s1, s2, s3, s4, s5, s6, s7)):
        shared[ROWS * index : ROWS * (index + 1), :] = part[...]
        shared_kept[ROWS * index : ROWS * (index + 1), :] = part[...]
    inject = inject_of(flags, shared)
    _, weight = weights_in(rates, table)
    for pair in range(PAIRS):
        weighted = (xc[:, lanes_of(pair)] * spread(weight, pair)).astype(bf16)
        out[KV + 128 * pair : KV + 128 * (pair + 1), :] = dot_tn(weighted, inject).astype(bf16)
    out[KV + XLOC : KV + MSG, :] = decay_rows(flags, rates_t)
    half = shared[pl.ds(rank_block(flags, 2 * flags[2] + flags[1] // 2), ROWS), :]
    out[0:KV, :] = jnp.concatenate([half[0:128], half[128:256]], axis=1)


def halves_kernel(msg1, msg2, msg3, out):
    for index, msg in enumerate((msg1, msg2, msg3)):
        out[KV * index : KV * (index + 1), :] = msg[...]


def allowed_pairs(table, seg_rows):
    rows = lax.broadcasted_iota(i32, (ROWS, ROWS), 0)
    return (rows >= lane_index((ROWS, ROWS))) & (segments(table) == seg_rows[0:1, :])


def head_decay(allowed, rates, rates_t, head):
    gap = rates[:, 128 + head : 129 + head] - rates_t[8 + head : 9 + head, :]
    return jnp.where(allowed, jnp.exp(jnp.where(allowed, gap, 0.0)), 0.0)


def intra_kernel(flags, shared, xc, rates, rates_t, table, seg_rows, small, out):
    inject, readout = inject_of(flags, shared), readout_of(flags, shared)
    both = dot_nt(readout, inject)
    allowed = allowed_pairs(table, seg_rows)
    low = lane_index((1, 128)) < HP
    for pair in range(PAIRS):
        x = xc[:, lanes_of(pair)]
        xb = x.astype(bf16)
        heads = []
        for head in (2 * pair, 2 * pair + 1):
            decay = head_decay(allowed, rates, rates_t, head)
            heads.append(dot_nn((both * decay * rates_t[head : head + 1, :]).astype(bf16), xb))
        out[:, lanes_of(pair)] = jnp.where(low, heads[0], heads[1]) + spread(small[2:3, 512:640], pair) * x


def keys_values(flags, shared, halves, swapped):
    head, first = flags[1] // 2, flags[2] == 0
    pairs = [
        (
            shared[pl.ds(rank_block(flags, head), ROWS), :],
            shared[pl.ds(rank_block(flags, 2 + head), ROWS), :],
        )
    ]
    for index, half in enumerate(halves):
        packed = half[...], swapped[KV * index : KV * (index + 1), :]
        mine, theirs = (jnp.concatenate([part[:, 0:128], part[:, 128:256]], axis=0) for part in packed)
        pairs.append((jnp.where(first, mine, theirs), jnp.where(first, theirs, mine)))
    return pairs


def masked_scores(query, pairs, table, seg_rows):
    parts = []
    for block, (keys, _) in enumerate(pairs):
        score = dot_nt(query, keys) * HD ** (-0.5)
        keep = segments(table) == seg_rows[block : block + 1, :]
        if block == 0:
            rows = lax.broadcasted_iota(i32, (ROWS, ROWS), 0)
            keep = keep & (rows >= lane_index((ROWS, ROWS)))
        parts.append(jnp.where(keep, score, -1e30))
    return parts


def attention_kernel(flags, query, shared, h1, h2, h3, swapped, table, seg_rows, out, out_kept, log_total, kept):
    pairs = keys_values(flags, shared, (h1, h2, h3), swapped)
    for block, (keys, values) in enumerate(pairs):
        kept[ROWS * block : ROWS * (block + 1), 0:HD] = keys
        kept[ROWS * block : ROWS * (block + 1), HD : 2 * HD] = values
    parts = masked_scores(query[...], pairs, table, seg_rows)
    top = parts[0].max(axis=1, keepdims=True)
    for part in parts[1:]:
        top = jnp.maximum(top, part.max(axis=1, keepdims=True))
    parts = [jnp.exp(part - top) for part in parts]
    total = sum(part.sum(axis=1, keepdims=True) for part in parts)
    inverse = 1.0 / total
    result = jnp.zeros((ROWS, HD), f32)
    for part, (_, values) in zip(parts, pairs):
        result = result + dot_nn((part * inverse).astype(bf16), values)
    rounded = result.astype(bf16)
    for block in range(8):
        for ref in (out, out_kept):
            ref[pl.ds(local_block(flags, block), SHARE), :] = rounded[SHARE * block : SHARE * (block + 1), :]
    log_total[...] = jnp.broadcast_to(top + jnp.log(total), (ROWS, HD))


def chained(first, second, third, base):
    rows1 = first[base + XLOC : base + MSG, :].astype(f32)
    rows2 = second[base + XLOC : base + MSG, :].astype(f32)
    parts = []
    for head in range(HLOC):
        own = slice(base + HP * head, base + HP * head + HP)
        older = second[own, :].astype(f32) + rows2[head : head + 1, :] * third[own, :].astype(f32)
        parts.append(first[own, :].astype(f32) + rows1[head : head + 1, :] * older)
    return jnp.concatenate(parts, axis=0)


def carry_kernel(flags, msg1, msg2, msg3, shared, rates, table, intra, z, state, ssm_y, cat, cat_kept):
    entering = chained(msg1, msg2, msg3, KV)
    state[...] = entering
    from_state = dot_nt(readout_of(flags, shared), entering.astype(bf16))
    carry = carry_of(rates, table)
    for pair in range(PAIRS):
        own = lanes_of(pair)
        y = intra[:, own] + spread(carry, pair) * from_state[:, own]
        ssm_y[:, own] = y
        gate = z[:, own]
        gated = (y * gate * sigmoid(gate)).astype(bf16)
        for block in range(8):
            for out in (cat, cat_kept):
                out[pl.ds(local_block(flags, block), SHARE), 128 * pair : 128 * (pair + 1)] = gated[
                    SHARE * block : SHARE * (block + 1), :
                ]


def gate_back_kernel(
    flags, p0, p1, p2, p3, p4, p5, p6, p7, weight, z, ssm_y, shared, rates, rates_t, table,
    dmix, dattn, dy, dz, msg, work, local,
):
    rows = joined((p0, p1, p2, p3, p4, p5, p6, p7))
    dmix[...] = rows
    local[...] = dot_nn(rows, weight[...])
    for block in range(8):
        own = slice(SHARE * block, SHARE * (block + 1))
        from_rows = pl.ds(local_block(flags, block), SHARE)
        dattn[own, :] = local[from_rows, 0:128].astype(bf16)
        work[own, :] = local[from_rows, 128:512]
    readout = readout_of(flags, shared)
    carry = carry_of(rates, table)
    for pair in range(PAIRS):
        own = lanes_of(pair)
        gate, grad = z[:, own], work[:, own]
        sig = sigmoid(gate)
        y_grad = grad * gate * sig
        dy[:, own] = y_grad
        dz[:, own] = (grad * ssm_y[:, own] * sig * (1.0 + gate * (1.0 - sig))).astype(bf16)
        msg[own, :] = dot_tn((y_grad * spread(carry, pair)).astype(bf16), readout).astype(bf16)
    msg[XLOC:MSG, :] = decay_rows(flags, rates_t)


def attention_back_kernel(
    flags, dattn, dz, query, kept, log_total, table, seg_rows,
    early, mine, theirs,
):
    pairs = []
    for block in range(SEQ_BLOCKS):
        own = slice(ROWS * block, ROWS * (block + 1))
        pairs.append((kept[own, 0:HD], kept[own, HD : 2 * HD]))
    first = flags[2] == 0
    q = query[...]
    grad = dattn[...]
    parts = masked_scores(q, pairs, table, seg_rows)
    logs = log_total[:, 0:1]
    probs = [jnp.exp(part - logs) for part in parts]
    grads = [dot_nt(grad, values) for _, values in pairs]
    inner = sum((p * g).sum(axis=1, keepdims=True) for p, g in zip(probs, grads))
    total = jnp.zeros((ROWS, HD), f32)
    for block, (p, g, (keys, _)) in enumerate(zip(probs, grads, pairs)):
        own = slice(ROWS * block, ROWS * (block + 1))
        score = (p * (g - inner)).astype(bf16)
        total = total + dot_nn(score, keys)
        dkeys = dot_tn(score, q) * HD ** (-0.5)
        dvalues = dot_tn(p.astype(bf16), grad)
        mine[own, :] = jnp.where(first, dkeys, dvalues)
        theirs[own, :] = jnp.where(first, dvalues, dkeys).astype(bf16)
    total = total * HD ** (-0.5)
    dq = turned(total, table, -1.0).astype(bf16)
    for block in range(8):
        own = slice(SHARE * block, SHARE * (block + 1))
        to_rows = pl.ds(local_block(flags, block), SHARE)
        early[to_rows, 0:XLOC] = dz[own, :]
        early[to_rows, XLOC:512] = dq[own, :]


def intra_back_kernel(
    flags, dy, xc, shared, rates, rates_t, table, seg_rows, state, small,
    dx, dshared, drates, dskip, row_sums, dcum,
):
    inject, readout = inject_of(flags, shared), readout_of(flags, shared)
    both = dot_nt(readout, inject)
    allowed = allowed_pairs(table, seg_rows)
    low = lane_index((1, 128)) < HP
    carry = carry_of(rates, table)
    entering = state[...].astype(bf16)
    from_state = dot_nt(readout, entering)
    dboth = jnp.zeros((ROWS, ROWS), f32)
    row_sums[...] = jnp.zeros((128, ROWS), f32)
    dcum[...] = jnp.zeros((ROWS, 128), f32)
    carried = []
    for pair in range(PAIRS):
        own = lanes_of(pair)
        x = xc[:, own]
        xb = x.astype(bf16)
        grad = dy[:, own]
        dskip[:, own] = jnp.sum(grad * x, axis=0, keepdims=True)
        carried.append((grad * spread(carry, pair)).astype(bf16))
        through = grad * from_state[:, own]
        total = spread(small[2:3, 512:640], pair) * grad
        for head in (2 * pair, 2 * pair + 1):
            mine = low if head % 2 == 0 else jnp.logical_not(low)
            decay = head_decay(allowed, rates, rates_t, head)
            steps = rates_t[head : head + 1, :]
            head_grad = jnp.where(mine, grad, 0.0).astype(bf16)
            dmix = dot_nt(head_grad, xb)
            kept = dmix * decay
            dboth = dboth + kept * steps
            mixed = both * decay
            total = total + dot_tn((mixed * steps).astype(bf16), head_grad)
            passed = dmix * mixed
            row_sums[head : head + 1, :] = jnp.sum(passed, axis=0, keepdims=True)
            dcum[:, head : head + 1] = jnp.sum(passed * steps, axis=1, keepdims=True) + carry[
                :, head : head + 1
            ] * jnp.sum(jnp.where(mine, through, 0.0), axis=1, keepdims=True)
        dx[:, own] = total
    columns = row_sums[...].T
    drates[:, 0:128] = columns
    drates[:, 128:256] = dcum[...] - rates[:, 0:128] * columns
    dboth_b = dboth.astype(bf16)
    dshared[:, NSTATE:] = dot_nn(dboth_b, inject) + dot_nn(jnp.concatenate(carried, axis=1), entering)
    dshared[:, 0:NSTATE] = dot_tn(dboth_b, readout)


def packed_back_kernel(
    flags, msg1, msg2, msg3, shared, xc, rates, table, dshared, kv0, kv1, kv2, kv3, packed, state_grad,
):
    later = chained(msg1, msg2, msg3, 0)
    state_grad[...] = later
    _, weights = weights_in(rates, table)
    weighted = [(xc[:, lanes_of(pair)] * spread(weights, pair)).astype(bf16) for pair in range(PAIRS)]
    weighted = jnp.concatenate(weighted, axis=1)
    dinject = (dshared[:, 0:NSTATE] + dot_nn(weighted, later.astype(bf16))).astype(bf16)
    dreadout = dshared[:, NSTATE:].astype(bf16)
    packed[...] = jnp.zeros((8 * ROWS, 128), bf16)
    grads = kv0[...] + kv1[...].astype(f32) + kv2[...].astype(f32) + kv3[...].astype(f32)
    owner = 2 * flags[2] + flags[1] // 2
    packed[pl.ds(rank_block(flags, owner), ROWS), :] = grads.astype(bf16)
    packed[pl.ds(rank_block(flags, 4), ROWS), :] = dinject[:, 0:128]
    packed[pl.ds(rank_block(flags, 5), ROWS), :] = dinject[:, 128:256]
    packed[pl.ds(rank_block(flags, 6), ROWS), :] = dreadout[:, 0:128]
    packed[pl.ds(rank_block(flags, 7), ROWS), :] = dreadout[:, 128:256]


def state_back_kernel(
    flags, later, shared, xc, rates, rates_t, table, state, small, dtn, dx, drates, ext,
    dxpre, edge, gweight, ddt, heads, work, dconv, sums,
):
    inject = inject_of(flags, shared)
    low = lane_index((1, 128)) < HP
    params = small[:, 512:640]
    gap, weights = weights_in(rates, table)
    from_later = dot_nt(inject, later[...].astype(bf16))
    products = later[...] * state[...]
    decays = block_decays(flags, rates_t)
    sums[...] = jnp.zeros((ROWS, 128), f32)
    for pair in range(PAIRS):
        own = lanes_of(pair)
        dconv[:, own] = dx[:, own] + spread(weights, pair) * from_later[:, own]
        through = xc[:, own] * from_later[:, own]
        for head in (2 * pair, 2 * pair + 1):
            mine = low if head % 2 == 0 else jnp.logical_not(low)
            sums[:, head : head + 1] = jnp.sum(jnp.where(mine, through, 0.0), axis=1, keepdims=True)
    dweights = sums[...]
    moved = dweights * weights
    last = jnp.sum(moved, axis=0, keepdims=True)
    lanes = lane_index((1, 128))
    for head in range(HLOC):
        total = jnp.sum(
            jnp.sum(products[HP * head : HP * head + HP, :], axis=0, keepdims=True), axis=1, keepdims=True
        )
        last = last + jnp.where(lanes == head, total * decays[head : head + 1, :], 0.0)
    rows = lax.broadcasted_iota(i32, (ROWS, 128), 0)
    dcums = drates[:, 128:256] - moved + jnp.where(rows == ROWS - 1, last, 0.0)
    square = lax.broadcasted_iota(i32, (ROWS, ROWS), 0)
    upper = (square <= lane_index((ROWS, ROWS))).astype(f32)
    dlogs = jnp.dot(upper, dcums, precision=lax.Precision.HIGHEST, preferred_element_type=f32)
    rate = -jnp.exp(params[0:1, :])
    dsteps = drates[:, 0:128] + dweights * gap + dlogs * rate
    ddts = dsteps * sigmoid(dtn[...] + params[1:2, :])
    ddt[...] = ddts
    heads[...] = jnp.zeros((8, 128), f32)
    heads[0:1, :] = jnp.sum(dlogs * rate * rates[:, 0:128], axis=0, keepdims=True)
    heads[1:2, :] = jnp.sum(ddts, axis=0, keepdims=True)
    conv_back(dconv[...], ext, table, small[:, 0:XLOC], work, dxpre, edge, gweight)


def shared_back_kernel(flags, part0, part1, part2, part3, ext, table, small, out, edge, gweight, work):
    grad = part0[...] + part1[...].astype(f32) + part2[...].astype(f32) + part3[...].astype(f32)
    conv_back(grad, ext, table, small[:, XLOC:512], work, out, edge, gweight)
    rank = flags[0]
    of_conv = jnp.where(rank < 4, 0.0, 1.0)
    edge[...] = edge[...] * of_conv
    gweight[...] = gweight[...] * of_conv
    out[...] = jnp.where(rank < 2, turned(grad, table, -1.0), jnp.where(rank < 4, grad, out[...]))


def late_kernel(flags, dxpre, edge_x, dsh, edge_sh, ddt, out):
    for block in range(8):
        own = slice(SHARE * block, SHARE * (block + 1))
        to_rows = pl.ds(local_block(flags, block), SHARE)
        x, sh = dxpre[own, :], dsh[own, :]
        if block == 7:
            pad = jnp.zeros((SHARE - 8, 128), f32)
            sh = sh + jnp.concatenate([pad, edge_sh[...]], axis=0)
            x = x + jnp.concatenate([jnp.zeros((SHARE - 8, XLOC), f32), edge_x[...]], axis=0)
        out[to_rows, 0:XLOC] = x.astype(bf16)
        out[to_rows, 512:LATE] = sh.astype(bf16)
        out[to_rows, XLOC:512] = jnp.where(lane_index((1, 128)) < HLOC, ddt[own, :], 0.0).astype(bf16)


def half_sum_kernel(own, other, keep, send1, send2, send3):
    rows = own.shape[0] // 4
    keep[...] = own[0:rows, :] + other[0:rows, :].astype(f32)
    for index, send in ((1, send1), (2, send2), (3, send3)):
        part = slice(rows * index, rows * (index + 1))
        send[...] = (own[part, :].astype(f32) + other[part, :].astype(f32)).astype(bf16)


def parts_of_sum(own, other, along, sign):
    return parts_from(own, other_core(other), along, sign)


def parts_from(own, got, along, sign):
    rows, width = own.shape[0] // 4, own.shape[1]
    sent = shape_of((rows, width), bf16)
    keep, *sends = run_kernel(half_sum_kernel, [kept((rows, width)), sent, sent, sent], None, own, Columns(got))
    return (keep,) + tuple(along(send, sign * k) for k, send in zip((1, 2, 3), sends))


def split_kernel(*refs):
    lefts, weight, own, other = refs[:-3], refs[-3], refs[-2], refs[-1]
    left = lefts[0][...] if len(lefts) == 1 else jnp.concatenate([ref[...] for ref in lefts], axis=1)
    result = dot_nt(left, weight[...])
    own[...] = result[: ROWS // 2]
    other[...] = result[ROWS // 2 :].astype(bf16)


def summed_rows(lefts, weight):
    model, width = weight.shape
    own, other = pl.pallas_call(
        split_kernel,
        grid=(model // 512,),
        out_shape=(shape_of((ROWS // 2, model)), shape_of((ROWS // 2, model), bf16)),
        in_specs=[pl.BlockSpec(left.shape, lambda i: (0, 0)) for left in lefts]
        + [pl.BlockSpec((512, width), lambda i: (i, 0))],
        out_specs=(
            pl.BlockSpec((ROWS // 2, 512), lambda i: (0, i)),
            pl.BlockSpec((ROWS // 2, 512), lambda i: (0, i)),
        ),
        compiler_params=pltpu.CompilerParams(vmem_limit_bytes=VMEM_LIMIT),
        cost_estimate=pl.CostEstimate(
            flops=2 * ROWS * model * width, bytes_accessed=2 * model * width, transcendentals=0
        ),
    )(*lefts, weight)
    return parts_of_sum(own, other, along_y, 1)


def gate_up_kernel(p0, p1, p2, p3, p4, p5, p6, p7, weight, normed, gate, up, act, act_kept):
    rows = joined((p0, p1, p2, p3, p4, p5, p6, p7))
    normed[...] = rows
    result = dot_nn(rows, weight[...])
    g, u = result[:, :512], result[:, 512:]
    gate[...] = g
    up[...] = u
    for out in (act, act_kept):
        out[...] = (g * sigmoid(g) * u).astype(bf16)


def gate_up_back_kernel(*refs):
    parts, (weight, gate, up, dffn, out) = refs[:-5], refs[-5:]
    rows = joined(parts)
    dffn[...] = rows
    dact = dot_nn(rows, weight[...])
    g = gate[...]
    sig = sigmoid(g)
    out[:, :512] = (dact * up[...] * sig * (1.0 + g * (1.0 - sig))).astype(bf16)
    out[:, 512:] = (dact * g * sig).astype(bf16)


def natural_kernel(flags, p0, p1, p2, p3, p4, p5, p6, p7, out):
    local = joined((p0, p1, p2, p3, p4, p5, p6, p7)).astype(out.dtype)
    for block in range(8):
        out[pl.ds(pl.multiple_of(flags[24 + block] * SHARE, SHARE), SHARE), :] = local[
            SHARE * block : SHARE * (block + 1), :
        ]


def add_norm_kernel(hidden, part0, part1, part2, part3, gain, out_kept, normed, inverse):
    total = hidden[...] + part0[...] + (
        part1[...].astype(f32) + part2[...].astype(f32) + part3[...].astype(f32)
    )
    out_kept[...] = total
    scale = lax.rsqrt(jnp.mean(total * total, axis=1, keepdims=True) + norm_eps)
    inverse[...] = jnp.broadcast_to(scale, inverse.shape)
    normed[...] = (total * scale * gain[...]).astype(bf16)


def add_norm(hidden, parts, gain):
    shape = hidden.shape
    return run_kernel(
        add_norm_kernel,
        [kept(shape), shape_of(shape, bf16), kept((shape[0], 128))],
        None, hidden, *summands(parts), gain[None],
    )


def output_kernel(hidden, part0, part1, part2, part3, out):
    total = hidden[...] + part0[...] + (
        part1[...].astype(f32) + part2[...].astype(f32) + part3[...].astype(f32)
    )
    out[...] = total.astype(bf16)


def norm_back_kernel(grad, part0, part1, part2, part3, hidden, inverse, gain, out, rounded, ggain):
    received = part0[...] + (part1[...].astype(f32) + part2[...].astype(f32) + part3[...].astype(f32))
    scale = inverse[:, 0:1]
    unit = hidden[...] * scale
    scaled = received * gain[...]
    ggain[...] = jnp.sum(received * unit, axis=0, keepdims=True)
    total = grad[...] + scale * (scaled - unit * jnp.mean(scaled * unit, axis=1, keepdims=True))
    out[...] = total
    rounded[...] = total.astype(bf16)


def norm_back(parts, grad, hidden, inverse, gain):
    shape = hidden.shape
    return run_kernel(
        norm_back_kernel,
        [kept(shape), shape_of(shape, bf16), kept((1, shape[1]))],
        None, grad, *summands(parts), hidden, inverse, gain[None],
    )


def gradient_kernel(pairs, *refs):
    out, at = refs[-1], 0
    for index in range(pairs):
        left, right = refs[2 * index], refs[2 * index + 1]
        width = right.shape[1]
        out[:, at : at + width] = dot_tn(left[...], right[...]).astype(bf16)
        at += width
    if at < out.shape[1]:
        out[:, at:] = jnp.zeros((out.shape[0], out.shape[1] - at), bf16)


def weight_gradients(pairs, total, block, index, buffer=None):
    rows, model = pairs[0][0].shape
    width = sum(right.shape[1] for _, right in pairs)
    specs, args = [], []
    for left, right in pairs:
        block_right = right.block if isinstance(right, Columns) else 0
        specs += [
            pl.BlockSpec((rows, 512), lambda i: (0, i)),
            pl.BlockSpec(right.shape, lambda i, block=block_right: (0, block)),
        ]
        args += [left, right.array if isinstance(right, Columns) else right]
    aliases = {}
    kernel = partial(gradient_kernel, len(pairs))
    if buffer is not None:
        aliases = {len(args): 0}
        specs.append(pl.BlockSpec(memory_space=pltpu.HBM))
        args.append(buffer)

        def kernel(*refs):
            gradient_kernel(len(pairs), *refs[:-2], refs[-1])

    return pl.pallas_call(
        kernel,
        grid=(model // 512,),
        out_shape=pltpu.HBM((model, total), bf16),
        in_specs=specs,
        out_specs=pl.BlockSpec((512, block), lambda i: (i, index)),
        input_output_aliases=aliases,
        compiler_params=pltpu.CompilerParams(vmem_limit_bytes=VMEM_LIMIT),
        cost_estimate=pl.CostEstimate(
            flops=2 * rows * model * width, bytes_accessed=model * width * 2, transcendentals=0
        ),
    )(*args)


def owned_kernel(pairs, *refs):
    out, at = refs[-1], 0
    for pair in range(pairs):
        left, right = refs[2 * pair], refs[2 * pair + 1]
        result = dot_tn(left[...], right[...]).astype(bf16)
        width = right.shape[1]
        for index in range(2):
            out[index, :, at : at + width] = result[128 * index : 128 * (index + 1)]
        at += width


def insert_kernel(small, block, out):
    mine = lane_index((1, 1, 128)) < HLOC
    out[...] = jnp.where(mine, block[...], small[...][None])


def with_small(owned, small):
    spec = pl.BlockSpec((16, 128, 128), lambda i: (0, 0, XLOC // 128))
    return pl.pallas_call(
        insert_kernel,
        grid=(1,),
        out_shape=pltpu.HBM(owned.shape, bf16),
        in_specs=[pl.BlockSpec((128, 128), lambda i: (0, 0)), spec],
        out_specs=spec,
        input_output_aliases={1: 0},
        compiler_params=pltpu.CompilerParams(vmem_limit_bytes=VMEM_LIMIT),
        cost_estimate=pl.CostEstimate(flops=10**9, bytes_accessed=10**6, transcendentals=0),
    )(small, owned)


def owned_gradients(pairs):
    rows, model = pairs[0][0].shape
    width = sum(right.shape[1] for _, right in pairs)
    specs, args = [], []
    for left, right in pairs:
        block = right.block if isinstance(right, Columns) else 0
        specs += [
            pl.BlockSpec((rows, 256), lambda i: (0, i)),
            pl.BlockSpec(right.shape, lambda i, block=block: (0, block)),
        ]
        args += [left, right.array if isinstance(right, Columns) else right]
    return pl.pallas_call(
        partial(owned_kernel, len(pairs)),
        grid=(model // 256,),
        out_shape=pltpu.HBM((16, model // 16, width), bf16),
        in_specs=specs,
        out_specs=pl.BlockSpec((2, model // 16, width), lambda i: (i, 0, 0)),
        compiler_params=pltpu.CompilerParams(vmem_limit_bytes=VMEM_LIMIT),
        cost_estimate=pl.CostEstimate(
            flops=2 * rows * model * width, bytes_accessed=model * width * 2, transcendentals=0
        ),
    )(*args)


def small_kernel(gain1, gain2, conv_sh, conv_x, heads, skip, out):
    out[...] = jnp.zeros(out.shape, bf16)
    for row in range(16):
        own = slice(128 * row, 128 * row + 128)
        out[row : row + 1, :] = gain1[:, own].astype(bf16)
        out[16 + row : 17 + row, :] = gain2[:, own].astype(bf16)
    out[32:37, :] = conv_sh[0:5, :].astype(bf16)
    for tap in range(CONV + 1):
        for pair in range(PAIRS):
            row = 37 + PAIRS * tap + pair
            out[row : row + 1, :] = conv_x[tap : tap + 1, lanes_of(pair)].astype(bf16)
    out[52:54, :] = heads[0:2, :].astype(bf16)
    lanes = lane_index((1, 128))
    sums = jnp.zeros((1, 128), f32)
    for pair in range(PAIRS):
        part = skip[:, lanes_of(pair)]
        for half in range(2):
            mine = (lanes < HP) if half == 0 else (lanes >= HP)
            total = jnp.sum(jnp.where(mine, part, 0.0), axis=1, keepdims=True)
            sums = sums + jnp.where(lanes == 2 * pair + half, total, 0.0)
    out[54:55, :] = sums.astype(bf16)


def spread_kernel(small, out, work):
    work[...] = small[...].astype(f32)
    columns = work[...].T
    work[56:62, :] = columns[122:128, :]
    out[...] = pltpu.roll(work[...], HLOC, 1).astype(bf16)


def gathered_back(packed, work):
    rolled = pltpu.roll(packed, 128 - HLOC, 1)
    work[...] = jnp.zeros((128, 128), f32)
    work[122:128, :] = rolled[56:62, :]
    return jnp.where(lane_index((1, 128)) < 128 - HLOC, rolled, work[...].T)


def owner_sum(values):
    total = values[0].astype(f32)
    for index in range(1, 16):
        total = total + values[index].astype(f32)
    return total


def block_sum_kernel(values, over_tp, late, conv_x, heads, work):
    whole = owner_sum(values)
    late[...] = whole[:, 0:LATE]
    total = gathered_back(whole[:, XLOC:512], work)
    over_tp[0:128, :] = whole[:, 512:LATE].astype(bf16)
    over_tp[128:256, :] = whole[:, LATE : LATE + 128].astype(bf16)
    over_tp[256:352, :] = jnp.zeros((96, 128), bf16)
    for layer in range(2):
        first = 64 * layer
        over_tp[256 + 48 * layer : 293 + 48 * layer, :] = total[first : first + 37, :].astype(bf16)
        for tap in range(CONV + 1):
            for pair in range(PAIRS):
                row = first + 37 + PAIRS * tap + pair
                conv_x[5 * layer + tap : 5 * layer + tap + 1, lanes_of(pair)] = total[row : row + 1, :]
        heads[3 * layer : 3 * layer + 3, :] = total[first + 52 : first + 55, :]


def weight_outputs_kernel(lower, upper, late, attn, ssm, gate, up, down, query, zx, dt):
    for layer, ref in ((0, lower), (1, upper)):
        for index, out in enumerate((gate, up, down)):
            out[layer] = ref[:, 512 * index : 512 * (index + 1)].astype(f32)
        attn[layer] = ref[:, 1536:1664].astype(f32)
        ssm[layer] = ref[:, 1664:2048].astype(f32)
        zx[layer, :, 0, :] = ref[:, 2048:2432].astype(f32)
        query[layer] = ref[:, 2432:2560].astype(f32)
    zx[0, :, 1, :] = late[:, 0:XLOC]
    zx[1, :, 1, :] = lower[:, 2560:2944].astype(f32)
    dt[0] = late[:, XLOC : XLOC + HLOC]
    dt[1] = lower[:, 2944 : 2944 + HLOC].astype(f32)


def tp_outputs_kernel(flags, *refs):
    parts, (shared, gains1, gains2, conv_bc, every) = refs[:8], refs[8:]
    total = jnp.zeros((96, 128), f32)
    for index, part in enumerate(parts):
        every[index] = part[...].astype(f32)
        total = total + part[256:352, :].astype(f32)
    for layer in range(2):
        for rank in range(8):
            own = slice(128 * rank, 128 * rank + 128)
            shared[layer, :, own] = every[flags[16 + rank], 128 * layer : 128 * layer + 128, :]
        for row in range(16):
            own = slice(128 * row, 128 * row + 128)
            at = 48 * layer + row
            gains1[layer : layer + 1, own] = total[at : at + 1, :]
            gains2[layer : layer + 1, own] = total[at + 16 : at + 17, :]
        for rank in range(4):
            part = every[flags[20 + rank], 288 + 48 * layer : 296 + 48 * layer, :]
            conv_bc[5 * layer : 5 * layer + 5, 128 * rank : 128 * rank + 128] = part[0:5, :]


def body(
    inputs, cotangent, segment_ids, w_query, w_shared, w_zx, w_dt, w_attn_out, w_ssm_out, w_gate, w_up, w_down,
    gains, conv_x, conv_bc, head_params,
):
    layers = w_query.shape[0]
    rank, ctx = lax.axis_index("tp"), lax.axis_index("ctx")
    y, core = rank // 2, rank % 2
    model = inputs.shape[2]

    def local_of(block_y, block_core):
        return jnp.where(block_core == core, 0, 4) + (block_y - y) % 4

    seg_all = segment_ids[0]
    first_row = ctx * ROWS
    padded = jnp.concatenate([jnp.full((CONV - 1,), -1, i32), seg_all])
    seg_ext = lax.dynamic_slice_in_dim(padded, first_row, ROWS + CONV - 1)
    seg_own = seg_ext[CONV - 1 :]
    blocks = seg_all.reshape(SEQ_BLOCKS, ROWS)
    seg_rows = jnp.stack(
        [
            jnp.where(ctx >= back, lax.dynamic_index_in_dim(blocks, jnp.maximum(ctx - back, 0), 0, False), -1)
            for back in range(SEQ_BLOCKS)
        ]
        + [jnp.full((ROWS,), -1, i32)] * 4
    ).astype(f32)
    naturals = jnp.arange(8, dtype=i32)
    flags = jnp.concatenate(
        [
            jnp.stack([rank, y, core, ctx, seg_ext[CONV - 2], seg_own[-1], rank, rank]).astype(i32),
            local_of(naturals % 4, naturals // 4).astype(i32),
            local_of(naturals // 2, naturals % 2).astype(i32),
            (jnp.where(naturals < 4, core, 1 - core) * 4 + (y + naturals) % 4).astype(i32),
        ]
    )

    half_width = HD // 2
    frequency = rope_base ** (-jnp.arange(half_width, dtype=f32) / half_width)
    places = (first_row + jnp.arange(ROWS, dtype=i32)).astype(f32)
    angles = places[:, None] * frequency[None, :]
    cosine, sine = jnp.cos(angles), jnp.sin(angles)
    marks = [seg_ext[tap : tap + ROWS] == seg_own for tap in range(CONV - 1)]
    marks += [seg_own, seg_own == seg_ext[CONV - 2], seg_own == seg_own[-1]]
    marks = jnp.pad(jnp.stack([mark.astype(f32) for mark in marks], axis=1), ((0, 0), (0, 122)))
    table = jnp.concatenate([cosine, cosine, -sine, sine, marks], axis=1)

    own_conv = jnp.maximum(rank - 4, 0) * 128
    small = []
    for layer in range(layers):
        rows = [conv_x[layer], lax.dynamic_slice_in_dim(conv_bc[layer], own_conv, 128, 1)]
        rows.append(jnp.pad(head_params[layer], ((0, 2), (0, 128 - HLOC))))
        small.append(jnp.pad(jnp.concatenate(rows, axis=1), ((0, 3), (0, 0))))

    def packed(*members):
        width = sum(
            {4: 2 * XLOC}.get(member.ndim, 128 if member.shape[2] in (1024, HLOC) else member.shape[2])
            for member, _ in members
        )
        (columns,) = run_kernel(
            pack_kernel,
            [shape_of((w_query.shape[1], width), bf16)],
            rank.astype(i32).reshape(1),
            *(Layer(member, layer) for member, layer in members),
        )
        return lax.all_gather(columns, ("fsdp", "ctx"), axis=0, tiled=True)

    def proj_members(layer):
        return [(member, layer) for member in (w_zx, w_query, w_dt, w_shared)]

    weight_a = packed(*proj_members(0), (w_attn_out, 0), (w_ssm_out, 0))
    weight_b = packed(*proj_members(1), (w_gate, 0), (w_up, 0), (w_down, 0))
    weight_c = packed((w_gate, 1), (w_up, 1), (w_down, 1), (w_attn_out, 1), (w_ssm_out, 1))
    proj_place = [(weight_a, 0, PROJ), (weight_b, 0, PROJ)]
    out_place = [(weight_a, PROJ, 512), (weight_c, 1536, 512)]
    gate_up_place = [(weight_b, PROJ, 1024), (weight_c, 0, 1024)]
    down_place = [(weight_b, PROJ + 1024, 512), (weight_c, 1024, 512)]

    def together(*values):
        return lax.optimization_barrier(values)

    weight_a, table, seg_rows, small = together(weight_a, table, seg_rows, small)
    normed_shape = shape_of((ROWS, model), bf16)
    normed_kept = kept((ROWS, model), bf16)
    normed_b, inverse1, hidden, dffn_b, grad_hidden = run_kernel(
        first_kernel,
        [normed_kept, kept((SHARE, 128)), kept((SHARE, model)), normed_kept, kept((SHARE, model))],
        flags, inputs, cotangent, gains[0],
    )
    weight_a, normed_b = together(weight_a, normed_b)
    proj_place[0] = (weight_a, 0, PROJ)
    out_place[0] = (weight_a, PROJ, 512)
    dffn_parts = (dffn_b,)
    saved = []
    wide = shape_of((ROWS, 512))
    for layer in range(layers):
        if layer == 0:
            z, z_kept, xs, query, query_kept, dtn, dtn_kept = first_projections(flags, normed_b, weight_a, table)
        else:
            normed_b, z, z_kept, xs, query, query_kept, dtn, dtn_kept = run_kernel(
                proj_kernel,
                [
                    normed_kept, shape_of((ROWS, XLOC)), kept((ROWS, XLOC)), wide, shape_of((ROWS, HD), bf16),
                    kept((ROWS, HD), bf16), shape_of((ROWS, 128)), kept((ROWS, 128)),
                ],
                flags, *passed(normed_parts), proj_weight, table,
                scratch=[pltpu.VMEM((ROWS, PROJ), f32)], us=3.3,
            )
        halo = along_ctx(xs[ROWS - 8 :], 1)
        shared_own, shared_ext = run_kernel(
            shared_kernel,
            [shape_of((ROWS, 128), bf16), kept((264, 128))],
            flags, xs, Columns(halo), table, small[layer],
        )
        prepared = run_kernel(
            prep_kernel,
            [
                kept((264, XLOC)), shape_of((ROWS, XLOC)), kept((ROWS, XLOC)), shape_of((ROWS, 256)),
                kept((ROWS, 256)), shape_of((16, ROWS)), kept((16, ROWS)),
            ],
            None, xs, dtn, Columns(halo), table, small[layer], us=1.5,
        )
        shared_parts, prepared = from_all(shared_own, prepared)
        x_ext, xc, xc_kept, rates, rates_kept, rates_t, rates_t_kept = prepared
        message, shared, shared_kept = run_kernel(
            state_kernel,
            [shape_of((KV + MSG, NSTATE), bf16), shape_of((8 * ROWS, 128), bf16), kept((8 * ROWS, 128), bf16)],
            flags, *passed(shared_parts), xc, rates, rates_t, table, us=1.9,
        )
        earlier = tuple(along_ctx(message, back) for back in (1, 2, 3))
        (intra,) = run_kernel(
            intra_kernel, [shape_of((ROWS, XLOC))],
            flags, shared, xc, rates, rates_t, table, seg_rows, small[layer], us=1.3,
        )
        if layer > 0:
            earlier, intra = together(earlier, intra)
        else:
            earlier, intra, out_weight = together(earlier, intra, fetched(f"out_{layer}", *out_place[layer]))
        halves = [Columns(part, 0, NSTATE, rows=KV) for part in earlier]
        (swapped,) = run_kernel(halves_kernel, [shape_of((3 * KV, NSTATE), bf16)], None, *halves)
        state, ssm_y, gated, gated_kept = run_kernel(
            carry_kernel,
            [kept((XLOC, NSTATE)), kept((ROWS, XLOC)), shape_of((ROWS, XLOC), bf16), kept((ROWS, XLOC), bf16)],
            flags, *passed(earlier), shared, rates, table, intra, z, us=1.9,
        )
        swapped, gated = together(other_core(swapped), gated)
        attn, attn_kept, log_total, pairs = run_kernel(
            attention_kernel,
            [
                shape_of((ROWS, HD), bf16), kept((ROWS, HD), bf16), kept((ROWS, HD)),
                kept((SEQ_BLOCKS * ROWS, 2 * HD), bf16),
            ],
            flags, query, shared, *halves, Columns(swapped), table, seg_rows, us=2.0,
        )
        if layer > 0:
            out_weight = fetched(f"out_{layer}", *out_place[layer])
        parts = summed_rows([attn, gated], out_weight)
        if layer > 0:
            parts, gate_up_weight = together(parts, fetched(f"gate_up_{layer}", *gate_up_place[layer]))
        parts, (rows,) = together(parts, restored(f"hidden_{layer}", [hidden]))
        hidden1, normed2, inverse2 = add_norm(rows, parts, gains[layer, 1])
        if layer > 0:
            normed_parts, down_weight = from_all(normed2, fetched("down_1", *down_place[layer]))
        else:
            normed_parts = from_all(normed2)
            gate_up_weight, down_weight = fetched_all("ffn_0", [gate_up_place[layer], down_place[layer]])
        wide_kept = kept((ROWS, 512))
        normed2_b, gate, up, act_b, act_kept = run_kernel(
            gate_up_kernel, [normed_kept, wide_kept, wide_kept, shape_of((ROWS, 512), bf16), kept((ROWS, 512), bf16)],
            None, *passed(normed_parts), gate_up_weight, us=2.3,
        )
        saved.append(
            (
                hidden, normed_b, inverse1, shared_ext, shared_kept, query_kept, x_ext, xc_kept, z_kept, dtn_kept,
                rates_kept, rates_t_kept, pairs, log_total, state, ssm_y, attn_kept, gated_kept, hidden1, inverse2, normed2_b,
                gate, up, act_kept,
            )
        )
        if layer + 1 < layers:
            parts, (rows,) = together(summed_rows([act_b], down_weight), restored(f"hidden1_{layer}", [hidden1]))
            hidden, next_normed, inverse1 = add_norm(rows, parts, gains[layer + 1, 0])
            normed_parts, proj_weight = from_all(next_normed, fetched("proj_1", *proj_place[layer + 1]))

    small_parts = [None] * layers
    inner = None
    for layer in reversed(range(layers)):
        (
            hidden, normed_b, inverse1, shared_ext, shared, query, x_ext, xc, z, dtn, rates, rates_t,
            pairs, log_total, state, ssm_y, attn, gated, hidden1, inverse2, normed2_b, gate, up, act_b,
        ) = saved[layer]
        last = layer == 0
        dffn_b, dgate_up = run_kernel(
            gate_up_back_kernel, [normed_kept, shape_of((ROWS, 1024), bf16)],
            None, *passed(dffn_parts), down_weight, stored(gate), stored(up), us=2.7,
        )
        parts = summed_rows([dgate_up], gate_up_weight)
        outer = weight_gradients(
            [(normed2_b, dgate_up), (dffn_b, act_b)], 3072 if last else 2560, 1536, 0, inner
        )
        parts, outer = lax.optimization_barrier((parts, outer))
        parts, kept_rows = together(parts, restored(f"norm2_{layer}", [grad_hidden, hidden1, inverse2]))
        grad_mid, dmix, ggain2 = norm_back(parts, *kept_rows, gains[layer, 1])
        dmix_parts = from_all(dmix)
        dmix_parts, fetch = from_all(
            dmix,
            fetched_all(
                f"mixer_{layer}",
                [out_place[layer]]
                + [(array, 0, array.shape[1]) for array in (z, ssm_y, shared, rates, rates_t, xc, query, pairs, state)],
            ),
        )
        from_kept = [stored(array) for array in (shared, xc, rates, rates_t, state)]
        out_weight, z, ssm_y, shared, rates, rates_t, xc, query, pairs, state = fetch
        dmix_b, dattn, dy, dz, message = run_kernel(
            gate_back_kernel,
            [
                normed_kept, shape_of((ROWS, HD), bf16), shape_of((ROWS, XLOC)), shape_of((ROWS, XLOC), bf16),
                shape_of((MSG, NSTATE), bf16),
            ],
            flags, *passed(dmix_parts), out_weight, z, ssm_y, shared, rates, rates_t, table, us=2.6,
            scratch=[pltpu.VMEM((ROWS, XLOC), f32), pltpu.VMEM((ROWS, 512), f32)],
        )
        after = tuple(along_ctx(message, -ahead) for ahead in (1, 2, 3))
        early, mine, theirs = run_kernel(
            attention_back_kernel,
            [kept((ROWS, 512), bf16), shape_of((4 * ROWS, HD)), shape_of((4 * ROWS, HD), bf16)],
            flags, dattn, dz, query, pairs, stored(log_total), table, seg_rows, us=2.9,
        )
        got = other_core(theirs)
        dx, dshared, drates, dskip = run_kernel(
            intra_back_kernel,
            [kept((ROWS, XLOC)), kept((ROWS, 2 * NSTATE)), kept((ROWS, 256)), kept((1, XLOC))],
            flags, dy, xc, shared, rates, rates_t, table, seg_rows, state, small[layer], us=3.6,
            scratch=[pltpu.VMEM((128, ROWS), f32), pltpu.VMEM((ROWS, 128), f32)],
        )
        dkv = parts_from(mine, got, along_ctx, -1)
        width = outer.shape[1]
        outer = weight_gradients([(dmix_b, attn), (dmix_b, gated)], width, 512, 3, outer)
        outer = weight_gradients([(normed_b, early)], width, 512, 4, outer)
        if last:
            after, dkv, outer, dx, upper = together(after, dkv, outer, dx, upper)
            lower = lax.psum_scatter(outer, ("fsdp", "ctx"), scatter_dimension=0, tiled=True)
        else:
            after, dkv, outer, dx = together(after, dkv, outer, dx)
            upper = lax.psum_scatter(outer, ("fsdp", "ctx"), scatter_dimension=0, tiled=True)
        packed_grads, state_grad = run_kernel(
            packed_back_kernel, [shape_of((8 * ROWS, 128), bf16), kept((XLOC, NSTATE))],
            flags, *map(stored, after), *from_kept[:3], table, stored(dshared), *map(stored, dkv), us=2.5,
        )
        dshared_parts = parts_of_sum(packed_grads[: 4 * ROWS], packed_grads[4 * ROWS :], along_y, 1)
        dxpre, edge_x, gconv_x, ddt, gheads = run_kernel(
            state_back_kernel,
            [kept((ROWS, XLOC)), shape_of((8, XLOC)), kept((8, XLOC)), kept((ROWS, 128)), kept((8, 128))],
            flags, stored(state_grad), *from_kept[:4], table, from_kept[4], stored(small[layer]),
            stored(dtn), stored(dx), stored(drates), stored(x_ext),
            scratch=[pltpu.VMEM((272, XLOC), f32), pltpu.VMEM((ROWS, XLOC), f32), pltpu.VMEM((ROWS, 128), f32)],
            us=3.5,
        )
        dshared_parts, edge_x = together(dshared_parts, edge_x)
        edge_x = along_ctx(edge_x, -1)
        dsh, edge_sh, gconv_sh = run_kernel(
            shared_back_kernel,
            [shape_of((ROWS, 128)), shape_of((8, 128)), kept((8, 128))],
            flags, *summands(dshared_parts), stored(shared_ext), table, small[layer],
            scratch=[pltpu.VMEM((272, 128), f32)],
        )
        edge_sh, proj_weight = together(
            along_ctx(edge_sh, -1), fetched(f"proj_again_{layer}", *proj_place[layer])
        )
        (late,) = run_kernel(
            late_kernel, [shape_of((ROWS, LATE), bf16)], flags, stored(dxpre), Columns(edge_x), dsh,
            Columns(edge_sh), stored(ddt),
        )
        parts = summed_rows([early, late], proj_weight)
        if not last:
            inner = weight_gradients([(normed_b, Columns(late, 0, 512))], 3072, 512, 5)
            parts, inner = together(parts, inner)
            upper_pair = (normed_b, Columns(late, 4, 128))
        else:
            parts, owned = together(parts, owned_gradients([(normed_b, late), upper_pair]))
        parts, kept_rows = together(parts, restored(f"norm1_{layer}", [grad_mid, hidden, inverse1]))
        grad_hidden, rounded, ggain1 = norm_back(parts, *kept_rows, gains[layer, 0])
        if last:
            dffn_parts = from_all(rounded)
        else:
            dffn_parts, (down_weight, gate_up_weight) = from_all(
                rounded, fetched_all("ffn_again", [down_place[layer - 1], gate_up_place[layer - 1]])
            )
            last_hidden1, last_act = hidden1, act_b
        (small_parts[layer],) = run_kernel(
            small_kernel, [shape_of((64, 128), bf16)],
            None, *map(stored, (ggain1, ggain2, gconv_sh, gconv_x, gheads, dskip)),
        )
    (small_all,) = run_kernel(
        spread_kernel, [shape_of((128, 128), bf16)], None, jnp.concatenate(small_parts, axis=0),
        scratch=[pltpu.VMEM((128, 128), f32)],
    )
    owned = lax.all_to_all(with_small(owned, small_all), ("fsdp", "ctx"), 0, 0, tiled=True)
    (input_grad,) = run_kernel(natural_kernel, [kept((ROWS, model))], flags, *passed(dffn_parts))
    last_act, down_weight, _ = together(last_act, fetched("down_last", *down_place[1]), small_parts[0])
    (layer_out,) = run_kernel(
        output_kernel, [shape_of((SHARE, model), bf16)], None,
        stored(last_hidden1), *summands(summed_rows([last_act], down_weight)),
    )
    (layer_out,) = run_kernel(natural_kernel, [normed_kept], flags, *passed(from_all(layer_out)))
    def pair_of(width):
        return shape_of((layers, model // 16, width))

    owned, layer_out, input_grad = together(owned, layer_out, input_grad)
    over_tp, late_sum, gconv_x, gheads = run_kernel(
        block_sum_kernel,
        [
            shape_of((352, 128), bf16), kept((model // 16, LATE)), shape_of((layers * (CONV + 1), XLOC)),
            shape_of((8, 128)),
        ],
        None, Columns(owned),
        scratch=[pltpu.VMEM((128, 128), f32)],
    )
    grad_shared, ggains1, ggains2, gconv_bc = run_kernel(
        tp_outputs_kernel,
        [
            pair_of(1024), shape_of((layers, model)), shape_of((layers, model)),
            shape_of((layers * (CONV + 1), 512)),
        ],
        flags, *passed(from_all(over_tp)),
        scratch=[pltpu.VMEM((8, 352, 128), f32)], us=2.0,
    )
    lower, grad_shared = together(lower, grad_shared)
    grad_attn, grad_ssm, grad_gate, grad_up, grad_down, grad_query, grad_zx, grad_dt = run_kernel(
        weight_outputs_kernel,
        [
            *(kept((layers, model // 16, width)) for width in (128, 384, 512, 512, 512, 128)),
            shape_of((layers, model // 16, 2, XLOC)), pair_of(HLOC),
        ],
        None, stored(lower), stored(upper), stored(late_sum), us=3.0,
    )
    gconv_x = gconv_x.reshape(layers, CONV + 1, XLOC)
    gconv_bc = gconv_bc.reshape(layers, CONV + 1, 512)
    gheads = gheads[: 3 * layers].reshape(layers, 3, 128)[:, :, :HLOC]
    return (
        layer_out[None],
        input_grad[None],
        grad_query,
        grad_shared,
        grad_zx,
        grad_dt,
        grad_attn,
        grad_ssm,
        grad_gate,
        grad_up,
        grad_down,
        ggains1,
        gconv_x,
        gconv_bc,
        gheads[:, :2],
        ggains2,
        gheads[:, 2],
    )


def solution(mesh):
    columns = P(None, ("fsdp", "ctx"), "tp")
    rows = P("fsdp", "ctx", None)
    return jax.shard_map(
        body,
        mesh=mesh,
        in_specs=(
            rows, rows, P("fsdp", None), columns, P(None, ("fsdp", "ctx"), None),
            P(None, ("fsdp", "ctx"), None, "tp"), columns, columns, columns, columns, columns, columns,
            P(), P(None, None, "tp"), P(), P(None, None, "tp"),
        ),
        out_specs=(
            rows, rows, columns, P(None, ("fsdp", "ctx"), None), P(None, ("fsdp", "ctx"), None, "tp"),
            columns, columns, columns, columns, columns, columns,
            P(), P(None, None, "tp"), P(), P(None, None, "tp"), P(), P(None, "tp"),
        ),
        check_vma=False,
    )
```

```python
import math
from functools import partial

import jax
import jax.numpy as jnp
from jax import lax
from jax.experimental import pallas as pl
from jax.experimental.pallas import tpu as pltpu
from jax.sharding import PartitionSpec as P

HD = 128
HP = 64
NSTATE = 256
CONV = 4
ROWS = 256
SHARE = 32
XLOC = 384
PROJ = 1152
LATE = 640
HLOC = 6
PAIRS = 3
SEQ_BLOCKS = 4
MSG = XLOC + 16
KV = 128
VMEM_LIMIT = 16 * 1024 * 1024

norm_eps = 1e-05
rope_base = 100000000000.0
bf16 = jnp.bfloat16
f32 = jnp.float32
i32 = jnp.int32


def along_y(value, steps):
    pairs = [(i, ((i // 2 + steps) % 4) * 2 + i % 2) for i in range(8)]
    return lax.ppermute(value, "tp", pairs)


def other_core(value):
    return lax.ppermute(value, "tp", [(i, i ^ 1) for i in range(8)])


def along_ctx(value, steps):
    first, last = max(0, -steps), min(4, 4 - steps)
    return lax.ppermute(value, "ctx", [(i, i + steps) for i in range(first, last)])


def ring(value, axis, steps):
    return lax.ppermute(value, axis, [(i, (i + steps) % 4) for i in range(4)])


def from_all(value, beside=None):
    half = [value] + [along_y(value, -k) for k in (1, 2, 3)]
    if beside is not None:
        half[1], beside = lax.optimization_barrier((half[1], beside))
    parts = tuple(half + [other_core(part) for part in half])
    return parts if beside is None else (parts, beside)


def dot_nn(a, b):
    return jnp.dot(a, b, preferred_element_type=f32)


def dot_nt(a, b):
    return lax.dot_general(a, b, (((1,), (1,)), ((), ())), preferred_element_type=f32)


def dot_tn(a, b):
    return lax.dot_general(a, b, (((0,), (0,)), ((), ())), preferred_element_type=f32)


def shape_of(shape, dtype=f32):
    return jax.ShapeDtypeStruct(shape, dtype)


class Columns:
    def __init__(self, array, block=0, width=None, rows=None, keep=False):
        self.array, self.block, self.keep = array, block, keep
        self.shape = (rows or array.shape[0],) + array.shape[1:-1] + (width or array.shape[-1],)

    def spec(self):
        place = (0,) * (len(self.shape) - 1) + (self.block,)
        return pl.BlockSpec(self.shape, lambda i: place, pipeline_mode=pl.Buffered(1))


class Layer:
    def __init__(self, array, layer):
        self.array, self.layer, self.keep = array, layer, True
        self.shape = (1,) + array.shape[1:]

    def spec(self):
        place = (self.layer,) + (0,) * (len(self.shape) - 1)
        return pl.BlockSpec(self.shape, lambda i: place, pipeline_mode=pl.Buffered(1))


def stored(array):
    return Columns(array, keep=True)


def summands(parts):
    return [stored(parts[0])] + passed(parts[1:])


def passed(arrays):
    return [Columns(array) for array in arrays]


def kept(shape, dtype=f32):
    return pltpu.HBM(shape, dtype)


def fetch_kernel(places, *refs):
    count = len(places)
    sources, outs, sems = refs[:count], refs[count : 2 * count], refs[-1]
    copies = []
    for (start, pieces), source, out in zip(places, sources, outs):
        rows, width = out.shape[0] // pieces, out.shape[1]
        for index in range(pieces):
            own = pl.ds(rows * index, rows)
            copies.append(
                pltpu.make_async_copy(
                    source.at[own, pl.ds(start, width)], out.at[own, :], sems.at[len(copies)]
                )
            )
    for copy in copies:
        copy.start()
    for copy in copies:
        copy.wait()


def fetched_all(name, sources):
    places = [(start, 4 if array.shape[0] == 2048 and width > 128 else 1) for array, start, width in sources]
    whole = pl.BlockSpec(memory_space=pltpu.VMEM)
    return pl.pallas_call(
        partial(fetch_kernel, places),
        name=name,
        out_shape=tuple(pltpu.VMEM((array.shape[0], width), array.dtype) for array, _, width in sources),
        in_specs=[pl.BlockSpec(memory_space=pltpu.HBM)] * len(sources),
        out_specs=tuple(whole for _ in sources),
        scratch_shapes=[pltpu.SemaphoreType.DMA((sum(pieces for _, pieces in places),))],
        compiler_params=pltpu.CompilerParams(vmem_limit_bytes=VMEM_LIMIT),
        cost_estimate=pl.CostEstimate(
            flops=0, bytes_accessed=sum(2 * array.shape[0] * width for array, _, width in sources), transcendentals=0
        ),
    )(*(pltpu.with_memory_space_constraint(array, pltpu.HBM) for array, _, _ in sources))


def fetched(name, array, start, width):
    return fetched_all(name, [(array, start, width)])[0]


def restored(name, arrays):
    return fetched_all(name, [(array, 0, array.shape[1]) for array in arrays])


def stash_kernel(*refs):
    count = len(refs) // 2
    sems = refs[-1]
    copies = [pltpu.make_async_copy(refs[k], refs[count + k], sems.at[k]) for k in range(count)]
    for copy in copies:
        copy.start()
    for copy in copies:
        copy.wait()


def stashed(name, arrays):
    return pl.pallas_call(
        stash_kernel,
        name=name,
        out_shape=tuple(pltpu.HBM(array.shape, array.dtype) for array in arrays),
        in_specs=[pl.BlockSpec(memory_space=pltpu.VMEM)] * len(arrays),
        out_specs=tuple(pl.BlockSpec(memory_space=pltpu.HBM) for _ in arrays),
        scratch_shapes=[pltpu.SemaphoreType.DMA((len(arrays),))],
        compiler_params=pltpu.CompilerParams(vmem_limit_bytes=VMEM_LIMIT),
        cost_estimate=pl.CostEstimate(flops=10**9, bytes_accessed=10**6, transcendentals=0),
    )(*arrays)


def run_kernel(kernel, outs, flags, *args, scratch=(), us=1.0):
    whole = pl.BlockSpec(memory_space=pltpu.VMEM)
    own = [isinstance(arg, (Columns, Layer)) for arg in args]
    specs, arrays, out_specs = [], [], []
    for arg, copied in zip(args, own):
        specs.append(arg.spec() if copied else whole)
        array = arg.array if copied else arg
        arrays.append(pltpu.with_memory_space_constraint(array, pltpu.HBM) if copied and arg.keep else array)
    for out in outs:
        in_vmem = isinstance(out, jax.ShapeDtypeStruct)
        out_specs.append(whole if in_vmem else pl.BlockSpec(out.shape, lambda i, n=len(out.shape): (0,) * n))
        own.append(not in_vmem)
    moved = sum(2 * math.prod(arg.shape) for arg in args) + sum(2 * math.prod(o.shape) for o in outs)
    if flags is not None:
        specs = [pl.BlockSpec(memory_space=pltpu.SMEM)] + specs
        arrays = [flags] + arrays
    return pl.pallas_call(
        kernel,
        grid=(1,) if any(own) else (),
        out_shape=tuple(outs),
        in_specs=specs,
        out_specs=tuple(out_specs),
        scratch_shapes=list(scratch),
        compiler_params=pltpu.CompilerParams(vmem_limit_bytes=VMEM_LIMIT),
        cost_estimate=pl.CostEstimate(flops=int(us * 1e9), bytes_accessed=moved, transcendentals=0),
    )(*arrays)


def local_block(flags, natural):
    return pl.multiple_of(flags[8 + natural] * SHARE, SHARE)


def rank_block(flags, rank):
    return pl.multiple_of(flags[16 + rank] * ROWS, ROWS)


def lane_index(shape):
    return lax.broadcasted_iota(i32, shape, len(shape) - 1)


def spread(columns, pair):
    low = lane_index((1, 128)) < HP
    return jnp.where(low, columns[:, 2 * pair : 2 * pair + 1], columns[:, 2 * pair + 1 : 2 * pair + 2])


def lanes_of(pair):
    return slice(128 * pair, 128 * pair + 128)


def turned(value, table, sign):
    return value * table[:, 0:128] + sign * (pltpu.roll(value, 64, 1) * table[:, 128:256])


def segments(table):
    return table[:, 259:260]


def sigmoid(v):
    return 1.0 / (1.0 + jnp.exp(-v))


def softplus(v):
    return jnp.maximum(v, 0.0) + jnp.log1p(jnp.exp(-jnp.abs(v)))


def conv_sum(ext, table, weight):
    total = weight[CONV : CONV + 1, :] + ext[8 : 8 + ROWS, :] * weight[3:4, :]
    for tap in range(CONV - 1):
        total = total + table[:, 256 + tap : 257 + tap] * ext[5 + tap : 5 + tap + ROWS, :] * weight[tap : tap + 1, :]
    return total


def conv_back(grad_out, ext, table, weight, work, grad_ref, edge_ref, gweight_ref):
    total = conv_sum(ext, table, weight)
    sig = sigmoid(total)
    grad = grad_out * sig * (1.0 + total * (1.0 - sig))
    width = grad.shape[1]
    gweight_ref[...] = jnp.zeros((8, width), f32)
    gweight_ref[CONV : CONV + 1, :] = jnp.sum(grad, axis=0, keepdims=True)
    gweight_ref[3:4, :] = jnp.sum(grad * ext[8 : 8 + ROWS, :], axis=0, keepdims=True)
    work[0:8, :] = jnp.zeros((8, width), f32)
    work[264:272, :] = jnp.zeros((8, width), f32)
    own = grad * weight[3:4, :]
    edge = jnp.zeros((8, width), f32)
    for tap in range(CONV - 1):
        part = grad * table[:, 256 + tap : 257 + tap]
        gweight_ref[tap : tap + 1, :] = jnp.sum(
            part * ext[5 + tap : 5 + tap + ROWS, :], axis=0, keepdims=True
        )
        work[8:264, :] = part * weight[tap : tap + 1, :]
        own = own + work[11 - tap : 11 - tap + ROWS, :]
        edge = edge + work[3 - tap : 11 - tap, :]
    grad_ref[...] = own
    edge_ref[...] = edge


def pack_kernel(place, *refs):
    out, at, index = refs[-1], 0, 0
    while index < len(refs) - 1:
        ref = refs[index]
        if len(ref.shape) == 4:
            out[:, at : at + XLOC] = ref[0, :, 0, :]
            out[:, at + XLOC : at + 512] = refs[index + 1][0]
            out[:, at + 512 : at + 896] = ref[0, :, 1, :]
            at, index = at + 896, index + 2
            continue
        width = min(ref.shape[2], 512)
        if width == HLOC:
            out[:, at : at + 128] = jnp.zeros((out.shape[0], 128), bf16)
            out[:, at : at + HLOC] = ref[0]
            width = 128
        elif ref.shape[2] == 1024:
            width = 128
            out[:, at : at + width] = ref[0, :, pl.ds(pl.multiple_of(place[0] * 128, 128), 128)]
        else:
            out[:, at : at + width] = ref[0]
        at, index = at + width, index + 1


def first_kernel(flags, rows, cotangent, gain, normed, inverse, hidden_kept, grads, grad):
    for block in range(8):
        own = slice(SHARE * block, SHARE * (block + 1))
        from_rows = pl.ds(pl.multiple_of(flags[24 + block] * SHARE, SHARE), SHARE)
        wide = rows[0, from_rows, :].astype(f32)
        scale = lax.rsqrt(jnp.mean(wide * wide, axis=1, keepdims=True) + norm_eps)
        normed[own, :] = (wide * scale * gain[0:1, :]).astype(bf16)
        grads[own, :] = cotangent[0, from_rows, :]
        if block == 0:
            hidden_kept[...] = wide
            inverse[...] = jnp.broadcast_to(scale, inverse.shape)
            grad[...] = cotangent[0, from_rows, :].astype(f32)


def joined(parts):
    return parts[0][...] if len(parts) == 1 else jnp.concatenate([part[...] for part in parts], axis=0)


def projections(flags, work, table, z, z_kept, xs, query, query_kept, dtn, dtn_kept):
    for block in range(8):
        own = slice(SHARE * block, SHARE * (block + 1))
        from_rows = pl.ds(local_block(flags, block), SHARE)
        for out in (z, z_kept):
            out[own, :] = work[from_rows, 0:XLOC]
        xs[own, 0:XLOC] = work[from_rows, 512:896]
        xs[own, XLOC:512] = work[from_rows, 1024:PROJ]
        head = turned(work[from_rows, XLOC:512], table[own, :], 1.0).astype(bf16)
        for out in (query, query_kept):
            out[own, :] = head
        for out in (dtn, dtn_kept):
            out[own, :] = work[from_rows, 896:1024]


def proj_kernel(flags, p0, p1, p2, p3, p4, p5, p6, p7, weight, table, normed, *refs):
    rows = joined((p0, p1, p2, p3, p4, p5, p6, p7))
    normed[...] = rows
    work = refs[-1]
    work[...] = dot_nn(rows, weight[...])
    projections(flags, work, table, *refs[:-1])


def first_proj_kernel(flags, rows, weight, table, z, z_kept, xs, query, query_kept, dtn, dtn_kept, work):
    step = pl.program_id(0)
    part = dot_nn(rows[...], weight[...])

    @pl.when(step == 0)
    def _():
        work[...] = part

    @pl.when(step > 0)
    def _():
        work[...] = work[...] + part

    @pl.when(step == 3)
    def _():
        projections(flags, work, table, z, z_kept, xs, query, query_kept, dtn, dtn_kept)


def first_projections(flags, normed, weight, table):
    model = normed.shape[1]
    whole = pl.BlockSpec(memory_space=pltpu.VMEM)
    outs = [
        shape_of((ROWS, XLOC)), kept((ROWS, XLOC)), shape_of((ROWS, 512)), shape_of((ROWS, HD), bf16),
        kept((ROWS, HD), bf16), shape_of((ROWS, 128)), kept((ROWS, 128)),
    ]
    return pl.pallas_call(
        first_proj_kernel,
        grid=(4,),
        out_shape=tuple(outs),
        in_specs=[
            pl.BlockSpec(memory_space=pltpu.SMEM),
            pl.BlockSpec((ROWS, model // 4), lambda i: (0, i)),
            pl.BlockSpec((model // 4, PROJ), lambda i: (i, 0)),
            whole,
        ],
        out_specs=tuple(
            whole if isinstance(out, jax.ShapeDtypeStruct) else pl.BlockSpec(out.shape, lambda i: (0, 0))
            for out in outs
        ),
        scratch_shapes=[pltpu.VMEM((ROWS, PROJ), f32)],
        compiler_params=pltpu.CompilerParams(vmem_limit_bytes=VMEM_LIMIT),
        cost_estimate=pl.CostEstimate(flops=4 * 10**9, bytes_accessed=2 * model * PROJ, transcendentals=0),
    )(flags, normed, pltpu.with_memory_space_constraint(weight, pltpu.HBM), table)


def shared_kernel(flags, xs, halo, table, small, out, ext):
    own = xs[:, XLOC:512]
    ext[0:8, :] = halo[:, XLOC:512]
    ext[8 : 8 + ROWS, :] = own
    total = conv_sum(ext, table, small[:, XLOC:512])
    rank = flags[0]
    out[...] = jnp.where(
        rank < 2, turned(own, table, 1.0), jnp.where(rank < 4, own, total * sigmoid(total))
    ).astype(bf16)


def prep_kernel(xs, dtn, halo, table, small, ext, xc, xc_kept, rates, rates_kept, rates_t, rates_t_kept):
    ext[0:8, :] = halo[:, 0:XLOC]
    ext[8 : 8 + ROWS, :] = xs[:, 0:XLOC]
    total = conv_sum(ext, table, small[:, 0:XLOC])
    for out in (xc, xc_kept):
        out[...] = total * sigmoid(total)
    params = small[:, 512:640]
    rate = softplus(dtn[...] + params[1:2, :])
    logs = -jnp.exp(params[0:1, :]) * rate
    rows = lax.broadcasted_iota(i32, (ROWS, ROWS), 0)
    lower = (rows >= lane_index((ROWS, ROWS))).astype(f32)
    running = jnp.dot(lower, logs, precision=lax.Precision.HIGHEST, preferred_element_type=f32)
    for out in (rates, rates_kept):
        out[:, 0:128] = rate
        out[:, 128:256] = running
    rate_t, running_t = rate.T[0:8, :], running.T[0:8, :]
    for out in (rates_t, rates_t_kept):
        out[0:8, :] = rate_t
        out[8:16, :] = running_t


def block_decays(flags, rates_t):
    kept = jnp.where(flags[4] == flags[5], 1.0, 0.0)
    return jnp.exp(rates_t[8:16, ROWS - 1 : ROWS]) * kept


def decay_rows(flags, rates_t):
    rows = jnp.broadcast_to(block_decays(flags, rates_t), (8, NSTATE))
    return jnp.concatenate([rows, jnp.zeros((8, NSTATE), f32)], axis=0).astype(bf16)


def weights_in(rates, table):
    last = rates[ROWS - 1 : ROWS, 128:256]
    gap = jnp.exp(last - rates[:, 128:256]) * table[:, 261:262]
    return gap, gap * rates[:, 0:128]


def rank_columns(flags, shared, first):
    return jnp.concatenate(
        [shared[pl.ds(rank_block(flags, rank), ROWS), :] for rank in (first, first + 1)], axis=1
    )


def inject_of(flags, shared):
    return rank_columns(flags, shared, 4)


def readout_of(flags, shared):
    return rank_columns(flags, shared, 6)


def carry_of(rates, table):
    return jnp.exp(rates[:, 128:256]) * table[:, 260:261]


def state_kernel(flags, s0, s1, s2, s3, s4, s5, s6, s7, xc, rates, rates_t, table, out, shared, shared_kept):
    for index, part in enumerate((s0, s1, s2, s3, s4, s5, s6, s7)):
        shared[ROWS * index : ROWS * (index + 1), :] = part[...]
        shared_kept[ROWS * index : ROWS * (index + 1), :] = part[...]
    inject = inject_of(flags, shared)
    _, weight = weights_in(rates, table)
    for pair in range(PAIRS):
        weighted = (xc[:, lanes_of(pair)] * spread(weight, pair)).astype(bf16)
        out[KV + 128 * pair : KV + 128 * (pair + 1), :] = dot_tn(weighted, inject).astype(bf16)
    out[KV + XLOC : KV + MSG, :] = decay_rows(flags, rates_t)
    half = shared[pl.ds(rank_block(flags, 2 * flags[2] + flags[1] // 2), ROWS), :]
    out[0:KV, :] = jnp.concatenate([half[0:128], half[128:256]], axis=1)


def halves_kernel(msg1, msg2, msg3, out):
    for index, msg in enumerate((msg1, msg2, msg3)):
        out[KV * index : KV * (index + 1), :] = msg[...]


def allowed_pairs(table, seg_rows):
    rows = lax.broadcasted_iota(i32, (ROWS, ROWS), 0)
    return (rows >= lane_index((ROWS, ROWS))) & (segments(table) == seg_rows[0:1, :])


def head_decay(allowed, rates, rates_t, head):
    gap = rates[:, 128 + head : 129 + head] - rates_t[8 + head : 9 + head, :]
    return jnp.where(allowed, jnp.exp(jnp.where(allowed, gap, 0.0)), 0.0)


def intra_kernel(flags, shared, xc, rates, rates_t, table, seg_rows, small, out):
    inject, readout = inject_of(flags, shared), readout_of(flags, shared)
    both = dot_nt(readout, inject)
    allowed = allowed_pairs(table, seg_rows)
    low = lane_index((1, 128)) < HP
    for pair in range(PAIRS):
        x = xc[:, lanes_of(pair)]
        xb = x.astype(bf16)
        heads = []
        for head in (2 * pair, 2 * pair + 1):
            decay = head_decay(allowed, rates, rates_t, head)
            heads.append(dot_nn((both * decay * rates_t[head : head + 1, :]).astype(bf16), xb))
        out[:, lanes_of(pair)] = jnp.where(low, heads[0], heads[1]) + spread(small[2:3, 512:640], pair) * x


def keys_values(flags, shared, halves, swapped):
    head, first = flags[1] // 2, flags[2] == 0
    pairs = [
        (
            shared[pl.ds(rank_block(flags, head), ROWS), :],
            shared[pl.ds(rank_block(flags, 2 + head), ROWS), :],
        )
    ]
    for index, half in enumerate(halves):
        packed = half[...], swapped[KV * index : KV * (index + 1), :]
        mine, theirs = (jnp.concatenate([part[:, 0:128], part[:, 128:256]], axis=0) for part in packed)
        pairs.append((jnp.where(first, mine, theirs), jnp.where(first, theirs, mine)))
    return pairs


def masked_scores(query, pairs, table, seg_rows):
    parts = []
    for block, (keys, _) in enumerate(pairs):
        score = dot_nt(query, keys) * HD ** (-0.5)
        keep = segments(table) == seg_rows[block : block + 1, :]
        if block == 0:
            rows = lax.broadcasted_iota(i32, (ROWS, ROWS), 0)
            keep = keep & (rows >= lane_index((ROWS, ROWS)))
        parts.append(jnp.where(keep, score, -1e30))
    return parts


def attention_kernel(flags, query, shared, h1, h2, h3, swapped, table, seg_rows, out, out_kept, log_total, kept):
    pairs = keys_values(flags, shared, (h1, h2, h3), swapped)
    for block, (keys, values) in enumerate(pairs):
        kept[ROWS * block : ROWS * (block + 1), 0:HD] = keys
        kept[ROWS * block : ROWS * (block + 1), HD : 2 * HD] = values
    parts = masked_scores(query[...], pairs, table, seg_rows)
    top = parts[0].max(axis=1, keepdims=True)
    for part in parts[1:]:
        top = jnp.maximum(top, part.max(axis=1, keepdims=True))
    parts = [jnp.exp(part - top) for part in parts]
    total = sum(part.sum(axis=1, keepdims=True) for part in parts)
    inverse = 1.0 / total
    result = jnp.zeros((ROWS, HD), f32)
    for part, (_, values) in zip(parts, pairs):
        result = result + dot_nn((part * inverse).astype(bf16), values)
    rounded = result.astype(bf16)
    for block in range(8):
        for ref in (out, out_kept):
            ref[pl.ds(local_block(flags, block), SHARE), :] = rounded[SHARE * block : SHARE * (block + 1), :]
    log_total[...] = jnp.broadcast_to(top + jnp.log(total), (ROWS, HD))


def chained(first, second, third, base):
    rows1 = first[base + XLOC : base + MSG, :].astype(f32)
    rows2 = second[base + XLOC : base + MSG, :].astype(f32)
    parts = []
    for head in range(HLOC):
        own = slice(base + HP * head, base + HP * head + HP)
        older = second[own, :].astype(f32) + rows2[head : head + 1, :] * third[own, :].astype(f32)
        parts.append(first[own, :].astype(f32) + rows1[head : head + 1, :] * older)
    return jnp.concatenate(parts, axis=0)


def carry_kernel(flags, msg1, msg2, msg3, shared, rates, table, intra, z, state, ssm_y, cat, cat_kept):
    entering = chained(msg1, msg2, msg3, KV)
    state[...] = entering
    from_state = dot_nt(readout_of(flags, shared), entering.astype(bf16))
    carry = carry_of(rates, table)
    for pair in range(PAIRS):
        own = lanes_of(pair)
        y = intra[:, own] + spread(carry, pair) * from_state[:, own]
        ssm_y[:, own] = y
        gate = z[:, own]
        gated = (y * gate * sigmoid(gate)).astype(bf16)
        for block in range(8):
            for out in (cat, cat_kept):
                out[pl.ds(local_block(flags, block), SHARE), 128 * pair : 128 * (pair + 1)] = gated[
                    SHARE * block : SHARE * (block + 1), :
                ]


def gate_back_kernel(
    flags, p0, p1, p2, p3, p4, p5, p6, p7, weight, z, ssm_y, shared, rates, rates_t, table,
    dmix, dattn, dy, dz, msg, work, local,
):
    rows = joined((p0, p1, p2, p3, p4, p5, p6, p7))
    dmix[...] = rows
    local[...] = dot_nn(rows, weight[...])
    for block in range(8):
        own = slice(SHARE * block, SHARE * (block + 1))
        from_rows = pl.ds(local_block(flags, block), SHARE)
        dattn[own, :] = local[from_rows, 0:128].astype(bf16)
        work[own, :] = local[from_rows, 128:512]
    readout = readout_of(flags, shared)
    carry = carry_of(rates, table)
    for pair in range(PAIRS):
        own = lanes_of(pair)
        gate, grad = z[:, own], work[:, own]
        sig = sigmoid(gate)
        y_grad = grad * gate * sig
        dy[:, own] = y_grad
        dz[:, own] = (grad * ssm_y[:, own] * sig * (1.0 + gate * (1.0 - sig))).astype(bf16)
        msg[own, :] = dot_tn((y_grad * spread(carry, pair)).astype(bf16), readout).astype(bf16)
    msg[XLOC:MSG, :] = decay_rows(flags, rates_t)


def attention_back_kernel(
    flags, dattn, dz, query, kept, log_total, table, seg_rows,
    early, mine, theirs,
):
    pairs = []
    for block in range(SEQ_BLOCKS):
        own = slice(ROWS * block, ROWS * (block + 1))
        pairs.append((kept[own, 0:HD], kept[own, HD : 2 * HD]))
    first = flags[2] == 0
    q = query[...]
    grad = dattn[...]
    parts = masked_scores(q, pairs, table, seg_rows)
    logs = log_total[:, 0:1]
    probs = [jnp.exp(part - logs) for part in parts]
    grads = [dot_nt(grad, values) for _, values in pairs]
    inner = sum((p * g).sum(axis=1, keepdims=True) for p, g in zip(probs, grads))
    total = jnp.zeros((ROWS, HD), f32)
    for block, (p, g, (keys, _)) in enumerate(zip(probs, grads, pairs)):
        own = slice(ROWS * block, ROWS * (block + 1))
        score = (p * (g - inner)).astype(bf16)
        total = total + dot_nn(score, keys)
        dkeys = dot_tn(score, q) * HD ** (-0.5)
        dvalues = dot_tn(p.astype(bf16), grad)
        mine[own, :] = jnp.where(first, dkeys, dvalues)
        theirs[own, :] = jnp.where(first, dvalues, dkeys).astype(bf16)
    total = total * HD ** (-0.5)
    dq = turned(total, table, -1.0).astype(bf16)
    for block in range(8):
        own = slice(SHARE * block, SHARE * (block + 1))
        to_rows = pl.ds(local_block(flags, block), SHARE)
        early[to_rows, 0:XLOC] = dz[own, :]
        early[to_rows, XLOC:512] = dq[own, :]


def intra_back_kernel(
    flags, dy, xc, shared, rates, rates_t, table, seg_rows, state, small,
    dx, dshared, drates, dskip, row_sums, dcum,
):
    inject, readout = inject_of(flags, shared), readout_of(flags, shared)
    both = dot_nt(readout, inject)
    allowed = allowed_pairs(table, seg_rows)
    low = lane_index((1, 128)) < HP
    carry = carry_of(rates, table)
    entering = state[...].astype(bf16)
    from_state = dot_nt(readout, entering)
    dboth = jnp.zeros((ROWS, ROWS), f32)
    row_sums[...] = jnp.zeros((128, ROWS), f32)
    dcum[...] = jnp.zeros((ROWS, 128), f32)
    carried = []
    for pair in range(PAIRS):
        own = lanes_of(pair)
        x = xc[:, own]
        xb = x.astype(bf16)
        grad = dy[:, own]
        dskip[:, own] = jnp.sum(grad * x, axis=0, keepdims=True)
        carried.append((grad * spread(carry, pair)).astype(bf16))
        through = grad * from_state[:, own]
        total = spread(small[2:3, 512:640], pair) * grad
        for head in (2 * pair, 2 * pair + 1):
            mine = low if head % 2 == 0 else jnp.logical_not(low)
            decay = head_decay(allowed, rates, rates_t, head)
            steps = rates_t[head : head + 1, :]
            head_grad = jnp.where(mine, grad, 0.0).astype(bf16)
            dmix = dot_nt(head_grad, xb)
            kept = dmix * decay
            dboth = dboth + kept * steps
            mixed = both * decay
            total = total + dot_tn((mixed * steps).astype(bf16), head_grad)
            passed = dmix * mixed
            row_sums[head : head + 1, :] = jnp.sum(passed, axis=0, keepdims=True)
            dcum[:, head : head + 1] = jnp.sum(passed * steps, axis=1, keepdims=True) + carry[
                :, head : head + 1
            ] * jnp.sum(jnp.where(mine, through, 0.0), axis=1, keepdims=True)
        dx[:, own] = total
    columns = row_sums[...].T
    drates[:, 0:128] = columns
    drates[:, 128:256] = dcum[...] - rates[:, 0:128] * columns
    dboth_b = dboth.astype(bf16)
    dshared[:, NSTATE:] = dot_nn(dboth_b, inject) + dot_nn(jnp.concatenate(carried, axis=1), entering)
    dshared[:, 0:NSTATE] = dot_tn(dboth_b, readout)


def packed_back_kernel(
    flags, msg1, msg2, msg3, shared, xc, rates, table, dshared, kv0, kv1, kv2, kv3, packed, state_grad,
):
    later = chained(msg1, msg2, msg3, 0)
    state_grad[...] = later
    _, weights = weights_in(rates, table)
    weighted = [(xc[:, lanes_of(pair)] * spread(weights, pair)).astype(bf16) for pair in range(PAIRS)]
    weighted = jnp.concatenate(weighted, axis=1)
    dinject = (dshared[:, 0:NSTATE] + dot_nn(weighted, later.astype(bf16))).astype(bf16)
    dreadout = dshared[:, NSTATE:].astype(bf16)
    packed[...] = jnp.zeros((8 * ROWS, 128), bf16)
    grads = kv0[...] + kv1[...].astype(f32) + kv2[...].astype(f32) + kv3[...].astype(f32)
    owner = 2 * flags[2] + flags[1] // 2
    packed[pl.ds(rank_block(flags, owner), ROWS), :] = grads.astype(bf16)
    packed[pl.ds(rank_block(flags, 4), ROWS), :] = dinject[:, 0:128]
    packed[pl.ds(rank_block(flags, 5), ROWS), :] = dinject[:, 128:256]
    packed[pl.ds(rank_block(flags, 6), ROWS), :] = dreadout[:, 0:128]
    packed[pl.ds(rank_block(flags, 7), ROWS), :] = dreadout[:, 128:256]


def state_back_kernel(
    flags, later, shared, xc, rates, rates_t, table, state, small, dtn, dx, drates, ext,
    dxpre, edge, gweight, ddt, heads, work, dconv, sums,
):
    inject = inject_of(flags, shared)
    low = lane_index((1, 128)) < HP
    params = small[:, 512:640]
    gap, weights = weights_in(rates, table)
    from_later = dot_nt(inject, later[...].astype(bf16))
    products = later[...] * state[...]
    decays = block_decays(flags, rates_t)
    sums[...] = jnp.zeros((ROWS, 128), f32)
    for pair in range(PAIRS):
        own = lanes_of(pair)
        dconv[:, own] = dx[:, own] + spread(weights, pair) * from_later[:, own]
        through = xc[:, own] * from_later[:, own]
        for head in (2 * pair, 2 * pair + 1):
            mine = low if head % 2 == 0 else jnp.logical_not(low)
            sums[:, head : head + 1] = jnp.sum(jnp.where(mine, through, 0.0), axis=1, keepdims=True)
    dweights = sums[...]
    moved = dweights * weights
    last = jnp.sum(moved, axis=0, keepdims=True)
    lanes = lane_index((1, 128))
    for head in range(HLOC):
        total = jnp.sum(
            jnp.sum(products[HP * head : HP * head + HP, :], axis=0, keepdims=True), axis=1, keepdims=True
        )
        last = last + jnp.where(lanes == head, total * decays[head : head + 1, :], 0.0)
    rows = lax.broadcasted_iota(i32, (ROWS, 128), 0)
    dcums = drates[:, 128:256] - moved + jnp.where(rows == ROWS - 1, last, 0.0)
    square = lax.broadcasted_iota(i32, (ROWS, ROWS), 0)
    upper = (square <= lane_index((ROWS, ROWS))).astype(f32)
    dlogs = jnp.dot(upper, dcums, precision=lax.Precision.HIGHEST, preferred_element_type=f32)
    rate = -jnp.exp(params[0:1, :])
    dsteps = drates[:, 0:128] + dweights * gap + dlogs * rate
    ddts = dsteps * sigmoid(dtn[...] + params[1:2, :])
    ddt[...] = ddts
    heads[...] = jnp.zeros((8, 128), f32)
    heads[0:1, :] = jnp.sum(dlogs * rate * rates[:, 0:128], axis=0, keepdims=True)
    heads[1:2, :] = jnp.sum(ddts, axis=0, keepdims=True)
    conv_back(dconv[...], ext, table, small[:, 0:XLOC], work, dxpre, edge, gweight)


def shared_back_kernel(flags, part0, part1, part2, part3, ext, table, small, out, edge, gweight, work):
    grad = part0[...] + part1[...].astype(f32) + part2[...].astype(f32) + part3[...].astype(f32)
    conv_back(grad, ext, table, small[:, XLOC:512], work, out, edge, gweight)
    rank = flags[0]
    of_conv = jnp.where(rank < 4, 0.0, 1.0)
    edge[...] = edge[...] * of_conv
    gweight[...] = gweight[...] * of_conv
    out[...] = jnp.where(rank < 2, turned(grad, table, -1.0), jnp.where(rank < 4, grad, out[...]))


def late_kernel(flags, dxpre, edge_x, dsh, edge_sh, ddt, out):
    for block in range(8):
        own = slice(SHARE * block, SHARE * (block + 1))
        to_rows = pl.ds(local_block(flags, block), SHARE)
        x, sh = dxpre[own, :], dsh[own, :]
        if block == 7:
            pad = jnp.zeros((SHARE - 8, 128), f32)
            sh = sh + jnp.concatenate([pad, edge_sh[...]], axis=0)
            x = x + jnp.concatenate([jnp.zeros((SHARE - 8, XLOC), f32), edge_x[...]], axis=0)
        out[to_rows, 0:XLOC] = x.astype(bf16)
        out[to_rows, 512:LATE] = sh.astype(bf16)
        out[to_rows, XLOC:512] = jnp.where(lane_index((1, 128)) < HLOC, ddt[own, :], 0.0).astype(bf16)


def half_sum_kernel(own, other, keep, send1, send2, send3):
    rows = own.shape[0] // 4
    keep[...] = own[0:rows, :] + other[0:rows, :].astype(f32)
    for index, send in ((1, send1), (2, send2), (3, send3)):
        part = slice(rows * index, rows * (index + 1))
        send[...] = (own[part, :].astype(f32) + other[part, :].astype(f32)).astype(bf16)


def parts_of_sum(own, other, along, sign):
    return parts_from(own, other_core(other), along, sign)


def parts_from(own, got, along, sign):
    rows, width = own.shape[0] // 4, own.shape[1]
    sent = shape_of((rows, width), bf16)
    keep, *sends = run_kernel(half_sum_kernel, [kept((rows, width)), sent, sent, sent], None, own, Columns(got))
    return (keep,) + tuple(along(send, sign * k) for k, send in zip((1, 2, 3), sends))


def split_kernel(*refs):
    lefts, weight, own, other = refs[:-3], refs[-3], refs[-2], refs[-1]
    left = lefts[0][...] if len(lefts) == 1 else jnp.concatenate([ref[...] for ref in lefts], axis=1)
    result = dot_nt(left, weight[...])
    own[...] = result[: ROWS // 2]
    other[...] = result[ROWS // 2 :].astype(bf16)


def summed_rows(lefts, weight):
    model, width = weight.shape
    own, other = pl.pallas_call(
        split_kernel,
        grid=(model // 512,),
        out_shape=(shape_of((ROWS // 2, model)), shape_of((ROWS // 2, model), bf16)),
        in_specs=[pl.BlockSpec(left.shape, lambda i: (0, 0)) for left in lefts]
        + [pl.BlockSpec((512, width), lambda i: (i, 0))],
        out_specs=(
            pl.BlockSpec((ROWS // 2, 512), lambda i: (0, i)),
            pl.BlockSpec((ROWS // 2, 512), lambda i: (0, i)),
        ),
        compiler_params=pltpu.CompilerParams(vmem_limit_bytes=VMEM_LIMIT),
        cost_estimate=pl.CostEstimate(
            flops=2 * ROWS * model * width, bytes_accessed=2 * model * width, transcendentals=0
        ),
    )(*lefts, weight)
    return parts_of_sum(own, other, along_y, 1)


def gate_up_kernel(p0, p1, p2, p3, p4, p5, p6, p7, weight, normed, gate, up, act):
    rows = joined((p0, p1, p2, p3, p4, p5, p6, p7))
    normed[...] = rows
    result = dot_nn(rows, weight[...])
    g, u = result[:, :512], result[:, 512:]
    gate[...] = g
    up[...] = u
    act[...] = (g * sigmoid(g) * u).astype(bf16)


def gate_up_back_kernel(*refs):
    parts, (weight, gate, up, dffn, out) = refs[:-5], refs[-5:]
    rows = joined(parts)
    dffn[...] = rows
    dact = dot_nn(rows, weight[...])
    g = gate[...]
    sig = sigmoid(g)
    out[:, :512] = (dact * up[...] * sig * (1.0 + g * (1.0 - sig))).astype(bf16)
    out[:, 512:] = (dact * g * sig).astype(bf16)


def natural_kernel(flags, p0, p1, p2, p3, p4, p5, p6, p7, out):
    local = joined((p0, p1, p2, p3, p4, p5, p6, p7)).astype(out.dtype)
    for block in range(8):
        out[pl.ds(pl.multiple_of(flags[24 + block] * SHARE, SHARE), SHARE), :] = local[
            SHARE * block : SHARE * (block + 1), :
        ]


def add_norm_kernel(hidden, part0, part1, part2, part3, gain, out_kept, normed, inverse):
    total = hidden[...] + part0[...] + (
        part1[...].astype(f32) + part2[...].astype(f32) + part3[...].astype(f32)
    )
    out_kept[...] = total
    scale = lax.rsqrt(jnp.mean(total * total, axis=1, keepdims=True) + norm_eps)
    inverse[...] = jnp.broadcast_to(scale, inverse.shape)
    normed[...] = (total * scale * gain[...]).astype(bf16)


def add_norm(hidden, parts, gain):
    shape = hidden.shape
    return run_kernel(
        add_norm_kernel,
        [shape_of(shape), shape_of(shape, bf16), shape_of((shape[0], 128))],
        None, hidden, *summands(parts), gain[None],
    )


def output_kernel(hidden, part0, part1, part2, part3, out):
    total = hidden[...] + part0[...] + (
        part1[...].astype(f32) + part2[...].astype(f32) + part3[...].astype(f32)
    )
    out[...] = total.astype(bf16)


def norm_back_kernel(grad, part0, part1, part2, part3, hidden, inverse, gain, out, rounded, ggain):
    received = part0[...] + (part1[...].astype(f32) + part2[...].astype(f32) + part3[...].astype(f32))
    scale = inverse[:, 0:1]
    unit = hidden[...] * scale
    scaled = received * gain[...]
    ggain[...] = jnp.sum(received * unit, axis=0, keepdims=True)
    total = grad[...] + scale * (scaled - unit * jnp.mean(scaled * unit, axis=1, keepdims=True))
    out[...] = total
    rounded[...] = total.astype(bf16)


def norm_back(parts, grad, hidden, inverse, gain):
    shape = hidden.shape
    return run_kernel(
        norm_back_kernel,
        [shape_of(shape), shape_of(shape, bf16), shape_of((1, shape[1]))],
        None, grad, *summands(parts), hidden, inverse, gain[None],
    )


def gradient_kernel(pairs, *refs):
    out, at = refs[-1], 0
    for index in range(pairs):
        left, right = refs[2 * index], refs[2 * index + 1]
        width = right.shape[1]
        out[:, at : at + width] = dot_tn(left[...], right[...]).astype(bf16)
        at += width
    if at < out.shape[1]:
        out[:, at:] = jnp.zeros((out.shape[0], out.shape[1] - at), bf16)


def weight_gradients(pairs, total, block, index, buffer=None):
    rows, model = pairs[0][0].shape
    width = sum(right.shape[1] for _, right in pairs)
    specs, args = [], []
    for left, right in pairs:
        block_right = right.block if isinstance(right, Columns) else 0
        specs += [
            pl.BlockSpec((rows, 512), lambda i: (0, i)),
            pl.BlockSpec(right.shape, lambda i, block=block_right: (0, block)),
        ]
        args += [left, right.array if isinstance(right, Columns) else right]
    aliases = {}
    kernel = partial(gradient_kernel, len(pairs))
    if buffer is not None:
        aliases = {len(args): 0}
        specs.append(pl.BlockSpec(memory_space=pltpu.HBM))
        args.append(buffer)

        def kernel(*refs):
            gradient_kernel(len(pairs), *refs[:-2], refs[-1])

    return pl.pallas_call(
        kernel,
        grid=(model // 512,),
        out_shape=pltpu.HBM((model, total), bf16),
        in_specs=specs,
        out_specs=pl.BlockSpec((512, block), lambda i: (i, index)),
        input_output_aliases=aliases,
        compiler_params=pltpu.CompilerParams(vmem_limit_bytes=VMEM_LIMIT),
        cost_estimate=pl.CostEstimate(
            flops=2 * rows * model * width, bytes_accessed=model * width * 2, transcendentals=0
        ),
    )(*args)


def owned_kernel(pairs, *refs):
    out, at = refs[-1], 0
    for pair in range(pairs):
        left, right = refs[2 * pair], refs[2 * pair + 1]
        result = dot_tn(left[...], right[...]).astype(bf16)
        width = right.shape[1]
        for index in range(2):
            out[index, :, at : at + width] = result[128 * index : 128 * (index + 1)]
        at += width


def insert_kernel(small, block, out):
    mine = lane_index((1, 1, 128)) < HLOC
    out[...] = jnp.where(mine, block[...], small[...][None])


def with_small(owned, small):
    spec = pl.BlockSpec((16, 128, 128), lambda i: (0, 0, XLOC // 128))
    return pl.pallas_call(
        insert_kernel,
        grid=(1,),
        out_shape=pltpu.HBM(owned.shape, bf16),
        in_specs=[pl.BlockSpec((128, 128), lambda i: (0, 0)), spec],
        out_specs=spec,
        input_output_aliases={1: 0},
        compiler_params=pltpu.CompilerParams(vmem_limit_bytes=VMEM_LIMIT),
        cost_estimate=pl.CostEstimate(flops=10**9, bytes_accessed=10**6, transcendentals=0),
    )(small, owned)


def owned_gradients(pairs):
    rows, model = pairs[0][0].shape
    width = sum(right.shape[1] for _, right in pairs)
    specs, args = [], []
    for left, right in pairs:
        block = right.block if isinstance(right, Columns) else 0
        specs += [
            pl.BlockSpec((rows, 256), lambda i: (0, i)),
            pl.BlockSpec(right.shape, lambda i, block=block: (0, block)),
        ]
        args += [left, right.array if isinstance(right, Columns) else right]
    return pl.pallas_call(
        partial(owned_kernel, len(pairs)),
        grid=(model // 256,),
        out_shape=pltpu.HBM((16, model // 16, width), bf16),
        in_specs=specs,
        out_specs=pl.BlockSpec((2, model // 16, width), lambda i: (i, 0, 0)),
        compiler_params=pltpu.CompilerParams(vmem_limit_bytes=VMEM_LIMIT),
        cost_estimate=pl.CostEstimate(
            flops=2 * rows * model * width, bytes_accessed=model * width * 2, transcendentals=0
        ),
    )(*args)


def small_kernel(gain1, gain2, conv_sh, conv_x, heads, skip, out):
    out[...] = jnp.zeros(out.shape, bf16)
    for row in range(16):
        own = slice(128 * row, 128 * row + 128)
        out[row : row + 1, :] = gain1[:, own].astype(bf16)
        out[16 + row : 17 + row, :] = gain2[:, own].astype(bf16)
    out[32:37, :] = conv_sh[0:5, :].astype(bf16)
    for tap in range(CONV + 1):
        for pair in range(PAIRS):
            row = 37 + PAIRS * tap + pair
            out[row : row + 1, :] = conv_x[tap : tap + 1, lanes_of(pair)].astype(bf16)
    out[52:54, :] = heads[0:2, :].astype(bf16)
    lanes = lane_index((1, 128))
    sums = jnp.zeros((1, 128), f32)
    for pair in range(PAIRS):
        part = skip[:, lanes_of(pair)]
        for half in range(2):
            mine = (lanes < HP) if half == 0 else (lanes >= HP)
            total = jnp.sum(jnp.where(mine, part, 0.0), axis=1, keepdims=True)
            sums = sums + jnp.where(lanes == 2 * pair + half, total, 0.0)
    out[54:55, :] = sums.astype(bf16)


def spread_kernel(small, out, work):
    work[...] = small[...].astype(f32)
    columns = work[...].T
    work[56:62, :] = columns[122:128, :]
    out[...] = pltpu.roll(work[...], HLOC, 1).astype(bf16)


def gathered_back(packed, work):
    rolled = pltpu.roll(packed, 128 - HLOC, 1)
    work[...] = jnp.zeros((128, 128), f32)
    work[122:128, :] = rolled[56:62, :]
    return jnp.where(lane_index((1, 128)) < 128 - HLOC, rolled, work[...].T)


def owner_sum(values):
    total = values[0].astype(f32)
    for index in range(1, 16):
        total = total + values[index].astype(f32)
    return total


def block_sum_kernel(values, over_tp, late, conv_x, heads, work):
    whole = owner_sum(values)
    late[...] = whole[:, 0:LATE]
    total = gathered_back(whole[:, XLOC:512], work)
    over_tp[0:128, :] = whole[:, 512:LATE].astype(bf16)
    over_tp[128:256, :] = whole[:, LATE : LATE + 128].astype(bf16)
    over_tp[256:352, :] = jnp.zeros((96, 128), bf16)
    for layer in range(2):
        first = 64 * layer
        over_tp[256 + 48 * layer : 293 + 48 * layer, :] = total[first : first + 37, :].astype(bf16)
        for tap in range(CONV + 1):
            for pair in range(PAIRS):
                row = first + 37 + PAIRS * tap + pair
                conv_x[5 * layer + tap : 5 * layer + tap + 1, lanes_of(pair)] = total[row : row + 1, :]
        heads[3 * layer : 3 * layer + 3, :] = total[first + 52 : first + 55, :]


def weight_outputs_kernel(lower, upper, late, attn, ssm, gate, up, down, query, zx, dt):
    for layer, ref in ((0, lower), (1, upper)):
        for index, out in enumerate((gate, up, down)):
            out[layer] = ref[:, 512 * index : 512 * (index + 1)].astype(f32)
        attn[layer] = ref[:, 1536:1664].astype(f32)
        ssm[layer] = ref[:, 1664:2048].astype(f32)
        zx[layer, :, 0, :] = ref[:, 2048:2432].astype(f32)
        query[layer] = ref[:, 2432:2560].astype(f32)
    zx[0, :, 1, :] = late[:, 0:XLOC]
    zx[1, :, 1, :] = lower[:, 2560:2944].astype(f32)
    dt[0] = late[:, XLOC : XLOC + HLOC]
    dt[1] = lower[:, 2944 : 2944 + HLOC].astype(f32)


def tp_outputs_kernel(flags, *refs):
    parts, (shared, gains1, gains2, conv_bc, every) = refs[:8], refs[8:]
    total = jnp.zeros((96, 128), f32)
    for index, part in enumerate(parts):
        every[index] = part[...].astype(f32)
        total = total + part[256:352, :].astype(f32)
    for layer in range(2):
        for rank in range(8):
            own = slice(128 * rank, 128 * rank + 128)
            shared[layer, :, own] = every[flags[16 + rank], 128 * layer : 128 * layer + 128, :]
        for row in range(16):
            own = slice(128 * row, 128 * row + 128)
            at = 48 * layer + row
            gains1[layer : layer + 1, own] = total[at : at + 1, :]
            gains2[layer : layer + 1, own] = total[at + 16 : at + 17, :]
        for rank in range(4):
            part = every[flags[20 + rank], 288 + 48 * layer : 296 + 48 * layer, :]
            conv_bc[5 * layer : 5 * layer + 5, 128 * rank : 128 * rank + 128] = part[0:5, :]


def body(
    inputs, cotangent, segment_ids, w_query, w_shared, w_zx, w_dt, w_attn_out, w_ssm_out, w_gate, w_up, w_down,
    gains, conv_x, conv_bc, head_params,
):
    layers = w_query.shape[0]
    rank, ctx = lax.axis_index("tp"), lax.axis_index("ctx")
    y, core = rank // 2, rank % 2
    model = inputs.shape[2]

    def local_of(block_y, block_core):
        return jnp.where(block_core == core, 0, 4) + (block_y - y) % 4

    seg_all = segment_ids[0]
    first_row = ctx * ROWS
    padded = jnp.concatenate([jnp.full((CONV - 1,), -1, i32), seg_all])
    seg_ext = lax.dynamic_slice_in_dim(padded, first_row, ROWS + CONV - 1)
    seg_own = seg_ext[CONV - 1 :]
    blocks = seg_all.reshape(SEQ_BLOCKS, ROWS)
    seg_rows = jnp.stack(
        [
            jnp.where(ctx >= back, lax.dynamic_index_in_dim(blocks, jnp.maximum(ctx - back, 0), 0, False), -1)
            for back in range(SEQ_BLOCKS)
        ]
        + [jnp.full((ROWS,), -1, i32)] * 4
    ).astype(f32)
    naturals = jnp.arange(8, dtype=i32)
    flags = jnp.concatenate(
        [
            jnp.stack([rank, y, core, ctx, seg_ext[CONV - 2], seg_own[-1], rank, rank]).astype(i32),
            local_of(naturals % 4, naturals // 4).astype(i32),
            local_of(naturals // 2, naturals % 2).astype(i32),
            (jnp.where(naturals < 4, core, 1 - core) * 4 + (y + naturals) % 4).astype(i32),
        ]
    )

    half_width = HD // 2
    frequency = rope_base ** (-jnp.arange(half_width, dtype=f32) / half_width)
    places = (first_row + jnp.arange(ROWS, dtype=i32)).astype(f32)
    angles = places[:, None] * frequency[None, :]
    cosine, sine = jnp.cos(angles), jnp.sin(angles)
    marks = [seg_ext[tap : tap + ROWS] == seg_own for tap in range(CONV - 1)]
    marks += [seg_own, seg_own == seg_ext[CONV - 2], seg_own == seg_own[-1]]
    marks = jnp.pad(jnp.stack([mark.astype(f32) for mark in marks], axis=1), ((0, 0), (0, 122)))
    table = jnp.concatenate([cosine, cosine, -sine, sine, marks], axis=1)

    own_conv = jnp.maximum(rank - 4, 0) * 128
    small = []
    for layer in range(layers):
        rows = [conv_x[layer], lax.dynamic_slice_in_dim(conv_bc[layer], own_conv, 128, 1)]
        rows.append(jnp.pad(head_params[layer], ((0, 2), (0, 128 - HLOC))))
        small.append(jnp.pad(jnp.concatenate(rows, axis=1), ((0, 3), (0, 0))))

    def packed(*members):
        width = sum(
            {4: 2 * XLOC}.get(member.ndim, 128 if member.shape[2] in (1024, HLOC) else member.shape[2])
            for member, _ in members
        )
        (columns,) = run_kernel(
            pack_kernel,
            [shape_of((w_query.shape[1], width), bf16)],
            rank.astype(i32).reshape(1),
            *(Layer(member, layer) for member, layer in members),
        )
        return lax.all_gather(columns, ("fsdp", "ctx"), axis=0, tiled=True)

    def proj_members(layer):
        return [(member, layer) for member in (w_zx, w_query, w_dt, w_shared)]

    weight_a = packed(*proj_members(0), (w_attn_out, 0), (w_ssm_out, 0))
    weight_b = packed(*proj_members(1), (w_gate, 0), (w_up, 0), (w_down, 0))
    weight_c = packed((w_gate, 1), (w_up, 1), (w_down, 1), (w_attn_out, 1), (w_ssm_out, 1))
    proj_place = [(weight_a, 0, PROJ), (weight_b, 0, PROJ)]
    out_place = [(weight_a, PROJ, 512), (weight_c, 1536, 512)]
    gate_up_place = [(weight_b, PROJ, 1024), (weight_c, 0, 1024)]
    down_place = [(weight_b, PROJ + 1024, 512), (weight_c, 1024, 512)]

    def together(*values):
        return lax.optimization_barrier(values)

    weight_a, table, seg_rows, small = together(weight_a, table, seg_rows, small)
    normed_shape = shape_of((ROWS, model), bf16)
    normed_kept = kept((ROWS, model), bf16)
    normed_b, inverse1, hidden, dffn_b, grad_hidden = run_kernel(
        first_kernel,
        [normed_kept, kept((SHARE, 128)), kept((SHARE, model)), normed_kept, kept((SHARE, model))],
        flags, inputs, cotangent, gains[0],
    )
    weight_a, normed_b = together(weight_a, normed_b)
    proj_place[0] = (weight_a, 0, PROJ)
    out_place[0] = (weight_a, PROJ, 512)
    dffn_parts = (dffn_b,)
    saved = []
    wide = shape_of((ROWS, 512))
    for layer in range(layers):
        if layer == 0:
            z, z_kept, xs, query, query_kept, dtn, dtn_kept = first_projections(flags, normed_b, weight_a, table)
        else:
            normed_b, z, z_kept, xs, query, query_kept, dtn, dtn_kept = run_kernel(
                proj_kernel,
                [
                    normed_kept, shape_of((ROWS, XLOC)), kept((ROWS, XLOC)), wide, shape_of((ROWS, HD), bf16),
                    kept((ROWS, HD), bf16), shape_of((ROWS, 128)), kept((ROWS, 128)),
                ],
                flags, *passed(normed_parts), proj_weight, table,
                scratch=[pltpu.VMEM((ROWS, PROJ), f32)], us=3.3,
            )
        halo = along_ctx(xs[ROWS - 8 :], 1)
        shared_own, shared_ext = run_kernel(
            shared_kernel,
            [shape_of((ROWS, 128), bf16), kept((264, 128))],
            flags, xs, Columns(halo), table, small[layer],
        )
        prepared = run_kernel(
            prep_kernel,
            [
                kept((264, XLOC)), shape_of((ROWS, XLOC)), kept((ROWS, XLOC)), shape_of((ROWS, 256)),
                kept((ROWS, 256)), shape_of((16, ROWS)), kept((16, ROWS)),
            ],
            None, xs, dtn, Columns(halo), table, small[layer], us=1.5,
        )
        shared_parts, prepared = from_all(shared_own, prepared)
        x_ext, xc, xc_kept, rates, rates_kept, rates_t, rates_t_kept = prepared
        message, shared, shared_kept = run_kernel(
            state_kernel,
            [shape_of((KV + MSG, NSTATE), bf16), shape_of((8 * ROWS, 128), bf16), kept((8 * ROWS, 128), bf16)],
            flags, *passed(shared_parts), xc, rates, rates_t, table, us=1.9,
        )
        earlier = tuple(along_ctx(message, back) for back in (1, 2, 3))
        (intra,) = run_kernel(
            intra_kernel, [shape_of((ROWS, XLOC))],
            flags, shared, xc, rates, rates_t, table, seg_rows, small[layer], us=1.3,
        )
        if layer > 0:
            earlier, intra = together(earlier, intra)
        else:
            earlier, intra, out_weight = together(earlier, intra, fetched(f"out_{layer}", *out_place[layer]))
        halves = [Columns(part, 0, NSTATE, rows=KV) for part in earlier]
        (swapped,) = run_kernel(halves_kernel, [shape_of((3 * KV, NSTATE), bf16)], None, *halves)
        state, ssm_y, gated, gated_kept = run_kernel(
            carry_kernel,
            [kept((XLOC, NSTATE)), kept((ROWS, XLOC)), shape_of((ROWS, XLOC), bf16), kept((ROWS, XLOC), bf16)],
            flags, *passed(earlier), shared, rates, table, intra, z, us=1.9,
        )
        swapped, gated = together(other_core(swapped), gated)
        attn, attn_kept, log_total, pairs = run_kernel(
            attention_kernel,
            [
                shape_of((ROWS, HD), bf16), kept((ROWS, HD), bf16), kept((ROWS, HD)),
                kept((SEQ_BLOCKS * ROWS, 2 * HD), bf16),
            ],
            flags, query, shared, *halves, Columns(swapped), table, seg_rows, us=2.0,
        )
        if layer > 0:
            out_weight = fetched(f"out_{layer}", *out_place[layer])
        parts = summed_rows([attn, gated], out_weight)
        if layer > 0:
            parts, gate_up_weight = together(parts, fetched(f"gate_up_{layer}", *gate_up_place[layer]))
        parts, (rows,) = together(parts, restored(f"hidden_{layer}", [hidden]))
        hidden1, normed2, inverse2 = add_norm(rows, parts, gains[layer, 1])
        rows = stashed(f"rows_{layer}", [hidden1, inverse2])
        if layer > 0:
            normed_parts, (down_weight, rows) = from_all(normed2, (fetched("down_1", *down_place[layer]), rows))
        else:
            normed_parts, rows = from_all(normed2, rows)
            gate_up_weight, down_weight = fetched_all("ffn_0", [gate_up_place[layer], down_place[layer]])
        hidden1, inverse2 = rows
        ffn = run_kernel(
            gate_up_kernel, [normed_shape, wide, wide, shape_of((ROWS, 512), bf16)],
            None, *passed(normed_parts), gate_up_weight, us=2.3,
        )
        if layer + 1 < layers:
            parts = summed_rows([ffn[3]], down_weight)
            parts, ffn, (rows,) = together(parts, stashed("ffn_kept", ffn), restored(f"hidden1_{layer}", [hidden1]))
        normed2_b, gate, up, act_b = ffn
        saved.append(
            (
                hidden, normed_b, inverse1, shared_ext, shared_kept, query_kept, x_ext, xc_kept, z_kept, dtn_kept,
                rates_kept, rates_t_kept, pairs, log_total, state, ssm_y, attn_kept, gated_kept, hidden1, inverse2, normed2_b,
                gate, up, act_b,
            )
        )
        if layer + 1 < layers:
            hidden, next_normed, inverse1 = add_norm(rows, parts, gains[layer + 1, 0])
            normed_parts, (proj_weight, rows) = from_all(
                next_normed,
                (fetched("proj_1", *proj_place[layer + 1]), stashed("rows_next", [hidden, inverse1])),
            )
            hidden, inverse1 = rows

    small_parts = [None] * layers
    inner = None
    for layer in reversed(range(layers)):
        (
            hidden, normed_b, inverse1, shared_ext, shared, query, x_ext, xc, z, dtn, rates, rates_t,
            pairs, log_total, state, ssm_y, attn, gated, hidden1, inverse2, normed2_b, gate, up, act_b,
        ) = saved[layer]
        last = layer == 0
        dffn_b, dgate_up = run_kernel(
            gate_up_back_kernel, [normed_shape, shape_of((ROWS, 1024), bf16)],
            None, *passed(dffn_parts), down_weight, *(map(stored, (gate, up)) if last else (gate, up)), us=2.7,
        )
        parts = summed_rows([dgate_up], gate_up_weight)
        outer = weight_gradients(
            [(normed2_b, dgate_up), (dffn_b, act_b)], 3072 if last else 2560, 1536, 0, inner
        )
        parts, outer = lax.optimization_barrier((parts, outer))
        parts, kept_rows = together(parts, restored(f"norm2_{layer}", [grad_hidden, hidden1, inverse2]))
        grad_mid, dmix, ggain2 = norm_back(parts, *kept_rows, gains[layer, 1])
        dmix_parts = from_all(dmix)
        beside = [grad_mid, ggain2] if last else [grad_mid, ggain2, act_b]
        dmix_parts, (fetch, rows) = from_all(
            dmix,
            (
                fetched_all(
                    f"mixer_{layer}",
                    [out_place[layer]]
                    + [
                        (array, 0, array.shape[1])
                        for array in (z, ssm_y, shared, rates, rates_t, xc, query, pairs, state)
                    ],
                ),
                stashed(f"grads_{layer}", beside),
            ),
        )
        grad_mid, ggain2 = rows[:2]
        if not last:
            last_act = rows[2]
        from_kept = [stored(array) for array in (shared, xc, rates, rates_t, state)]
        out_weight, z, ssm_y, shared, rates, rates_t, xc, query, pairs, state = fetch
        dmix_b, dattn, dy, dz, message = run_kernel(
            gate_back_kernel,
            [
                normed_kept, shape_of((ROWS, HD), bf16), shape_of((ROWS, XLOC)), shape_of((ROWS, XLOC), bf16),
                shape_of((MSG, NSTATE), bf16),
            ],
            flags, *passed(dmix_parts), out_weight, z, ssm_y, shared, rates, rates_t, table, us=2.6,
            scratch=[pltpu.VMEM((ROWS, XLOC), f32), pltpu.VMEM((ROWS, 512), f32)],
        )
        after = tuple(along_ctx(message, -ahead) for ahead in (1, 2, 3))
        early, mine, theirs = run_kernel(
            attention_back_kernel,
            [kept((ROWS, 512), bf16), shape_of((4 * ROWS, HD)), shape_of((4 * ROWS, HD), bf16)],
            flags, dattn, dz, query, pairs, stored(log_total), table, seg_rows, us=2.9,
        )
        got = other_core(theirs)
        dx, dshared, drates, dskip = run_kernel(
            intra_back_kernel,
            [kept((ROWS, XLOC)), kept((ROWS, 2 * NSTATE)), kept((ROWS, 256)), kept((1, XLOC))],
            flags, dy, xc, shared, rates, rates_t, table, seg_rows, state, small[layer], us=3.6,
            scratch=[pltpu.VMEM((128, ROWS), f32), pltpu.VMEM((ROWS, 128), f32)],
        )
        dkv = parts_from(mine, got, along_ctx, -1)
        width = outer.shape[1]
        outer = weight_gradients([(dmix_b, attn), (dmix_b, gated)], width, 512, 3, outer)
        outer = weight_gradients([(normed_b, early)], width, 512, 4, outer)
        if last:
            after, dkv, outer, dx, upper = together(after, dkv, outer, dx, upper)
            lower = lax.psum_scatter(outer, ("fsdp", "ctx"), scatter_dimension=0, tiled=True)
        else:
            after, dkv, outer, dx = together(after, dkv, outer, dx)
            upper = lax.psum_scatter(outer, ("fsdp", "ctx"), scatter_dimension=0, tiled=True)
        packed_grads, state_grad = run_kernel(
            packed_back_kernel, [shape_of((8 * ROWS, 128), bf16), kept((XLOC, NSTATE))],
            flags, *map(stored, after), *from_kept[:3], table, stored(dshared), *map(stored, dkv), us=2.5,
        )
        dshared_parts = parts_of_sum(packed_grads[: 4 * ROWS], packed_grads[4 * ROWS :], along_y, 1)
        dxpre, edge_x, gconv_x, ddt, gheads = run_kernel(
            state_back_kernel,
            [kept((ROWS, XLOC)), shape_of((8, XLOC)), kept((8, XLOC)), kept((ROWS, 128)), kept((8, 128))],
            flags, stored(state_grad), *from_kept[:4], table, from_kept[4], stored(small[layer]),
            stored(dtn), stored(dx), stored(drates), stored(x_ext),
            scratch=[pltpu.VMEM((272, XLOC), f32), pltpu.VMEM((ROWS, XLOC), f32), pltpu.VMEM((ROWS, 128), f32)],
            us=3.5,
        )
        dshared_parts, edge_x = together(dshared_parts, edge_x)
        edge_x = along_ctx(edge_x, -1)
        dsh, edge_sh, gconv_sh = run_kernel(
            shared_back_kernel,
            [shape_of((ROWS, 128)), shape_of((8, 128)), kept((8, 128))],
            flags, *summands(dshared_parts), stored(shared_ext), table, small[layer],
            scratch=[pltpu.VMEM((272, 128), f32)],
        )
        edge_sh, proj_weight = together(
            along_ctx(edge_sh, -1), fetched(f"proj_again_{layer}", *proj_place[layer])
        )
        (late,) = run_kernel(
            late_kernel, [shape_of((ROWS, LATE), bf16)], flags, stored(dxpre), Columns(edge_x), dsh,
            Columns(edge_sh), stored(ddt),
        )
        parts = summed_rows([early, late], proj_weight)
        if not last:
            inner = weight_gradients([(normed_b, Columns(late, 0, 512))], 3072, 512, 5)
            parts, inner = together(parts, inner)
            upper_pair = (normed_b, Columns(late, 4, 128))
        else:
            parts, owned = together(parts, owned_gradients([(normed_b, late), upper_pair]))
        parts, kept_rows = together(parts, restored(f"norm1_{layer}", [grad_mid, hidden, inverse1]))
        grad_hidden, rounded, ggain1 = norm_back(parts, *kept_rows, gains[layer, 0])
        if last:
            dffn_parts = from_all(rounded)
        else:
            dffn_parts, ((down_weight, gate_up_weight), (grad_hidden, ggain1)) = from_all(
                rounded,
                (
                    fetched_all("ffn_again", [down_place[layer - 1], gate_up_place[layer - 1]]),
                    stashed("grads_next", [grad_hidden, ggain1]),
                ),
            )
            last_hidden1 = hidden1
        (small_parts[layer],) = run_kernel(
            small_kernel, [shape_of((64, 128), bf16)],
            None, ggain1, *map(stored, (ggain2, gconv_sh, gconv_x, gheads, dskip)),
        )
    (small_all,) = run_kernel(
        spread_kernel, [shape_of((128, 128), bf16)], None, jnp.concatenate(small_parts, axis=0),
        scratch=[pltpu.VMEM((128, 128), f32)],
    )
    owned = lax.all_to_all(with_small(owned, small_all), ("fsdp", "ctx"), 0, 0, tiled=True)
    (input_grad,) = run_kernel(natural_kernel, [kept((ROWS, model))], flags, *passed(dffn_parts))
    last_act, down_weight, _ = together(last_act, fetched("down_last", *down_place[1]), small_parts[0])
    (layer_out,) = run_kernel(
        output_kernel, [shape_of((SHARE, model), bf16)], None,
        stored(last_hidden1), *summands(summed_rows([last_act], down_weight)),
    )
    (layer_out,) = run_kernel(natural_kernel, [normed_kept], flags, *passed(from_all(layer_out)))
    def pair_of(width):
        return shape_of((layers, model // 16, width))

    owned, layer_out, input_grad = together(owned, layer_out, input_grad)
    over_tp, late_sum, gconv_x, gheads = run_kernel(
        block_sum_kernel,
        [
            shape_of((352, 128), bf16), kept((model // 16, LATE)), shape_of((layers * (CONV + 1), XLOC)),
            shape_of((8, 128)),
        ],
        None, Columns(owned),
        scratch=[pltpu.VMEM((128, 128), f32)],
    )
    grad_shared, ggains1, ggains2, gconv_bc = run_kernel(
        tp_outputs_kernel,
        [
            pair_of(1024), shape_of((layers, model)), shape_of((layers, model)),
            shape_of((layers * (CONV + 1), 512)),
        ],
        flags, *passed(from_all(over_tp)),
        scratch=[pltpu.VMEM((8, 352, 128), f32)], us=2.0,
    )
    lower, grad_shared = together(lower, grad_shared)
    grad_attn, grad_ssm, grad_gate, grad_up, grad_down, grad_query, grad_zx, grad_dt = run_kernel(
        weight_outputs_kernel,
        [
            *(kept((layers, model // 16, width)) for width in (128, 384, 512, 512, 512, 128)),
            shape_of((layers, model // 16, 2, XLOC)), pair_of(HLOC),
        ],
        None, stored(lower), stored(upper), stored(late_sum), us=3.0,
    )
    gconv_x = gconv_x.reshape(layers, CONV + 1, XLOC)
    gconv_bc = gconv_bc.reshape(layers, CONV + 1, 512)
    gheads = gheads[: 3 * layers].reshape(layers, 3, 128)[:, :, :HLOC]
    return (
        layer_out[None],
        input_grad[None],
        grad_query,
        grad_shared,
        grad_zx,
        grad_dt,
        grad_attn,
        grad_ssm,
        grad_gate,
        grad_up,
        grad_down,
        ggains1,
        gconv_x,
        gconv_bc,
        gheads[:, :2],
        ggains2,
        gheads[:, 2],
    )


def solution(mesh):
    columns = P(None, ("fsdp", "ctx"), "tp")
    rows = P("fsdp", "ctx", None)
    return jax.shard_map(
        body,
        mesh=mesh,
        in_specs=(
            rows, rows, P("fsdp", None), columns, P(None, ("fsdp", "ctx"), None),
            P(None, ("fsdp", "ctx"), None, "tp"), columns, columns, columns, columns, columns, columns,
            P(), P(None, None, "tp"), P(), P(None, None, "tp"),
        ),
        out_specs=(
            rows, rows, columns, P(None, ("fsdp", "ctx"), None), P(None, ("fsdp", "ctx"), None, "tp"),
            columns, columns, columns, columns, columns, columns,
            P(), P(None, None, "tp"), P(), P(None, None, "tp"), P(), P(None, "tp"),
        ),
        check_vma=False,
    )
```

```python
import math
from functools import partial

import jax
import jax.numpy as jnp
from jax import lax
from jax.experimental import pallas as pl
from jax.experimental.pallas import tpu as pltpu
from jax.sharding import PartitionSpec as P

HD = 128
HP = 64
NSTATE = 256
CONV = 4
ROWS = 256
SHARE = 32
XLOC = 384
PROJ = 1152
LATE = 640
HLOC = 6
PAIRS = 3
SEQ_BLOCKS = 4
MSG = XLOC + 16
KV = 128
VMEM_LIMIT = 16 * 1024 * 1024

norm_eps = 1e-05
rope_base = 100000000000.0
bf16 = jnp.bfloat16
f32 = jnp.float32
i32 = jnp.int32


def along_y(value, steps):
    pairs = [(i, ((i // 2 + steps) % 4) * 2 + i % 2) for i in range(8)]
    return lax.ppermute(value, "tp", pairs)


def other_core(value):
    return lax.ppermute(value, "tp", [(i, i ^ 1) for i in range(8)])


def along_ctx(value, steps):
    first, last = max(0, -steps), min(4, 4 - steps)
    return lax.ppermute(value, "ctx", [(i, i + steps) for i in range(first, last)])


def ring(value, axis, steps):
    return lax.ppermute(value, axis, [(i, (i + steps) % 4) for i in range(4)])


def from_all(value, beside=None):
    half = [value] + [along_y(value, -k) for k in (1, 2, 3)]
    if beside is not None:
        half[1], beside = lax.optimization_barrier((half[1], beside))
    parts = tuple(half + [other_core(part) for part in half])
    return parts if beside is None else (parts, beside)


def dot_nn(a, b):
    return jnp.dot(a, b, preferred_element_type=f32)


def dot_nt(a, b):
    return lax.dot_general(a, b, (((1,), (1,)), ((), ())), preferred_element_type=f32)


def dot_tn(a, b):
    return lax.dot_general(a, b, (((0,), (0,)), ((), ())), preferred_element_type=f32)


def shape_of(shape, dtype=f32):
    return jax.ShapeDtypeStruct(shape, dtype)


class Columns:
    def __init__(self, array, block=0, width=None, rows=None, keep=False):
        self.array, self.block, self.keep = array, block, keep
        self.shape = (rows or array.shape[0],) + array.shape[1:-1] + (width or array.shape[-1],)

    def spec(self):
        place = (0,) * (len(self.shape) - 1) + (self.block,)
        return pl.BlockSpec(self.shape, lambda i: place, pipeline_mode=pl.Buffered(1))


class Layer:
    def __init__(self, array, layer):
        self.array, self.layer, self.keep = array, layer, True
        self.shape = (1,) + array.shape[1:]

    def spec(self):
        place = (self.layer,) + (0,) * (len(self.shape) - 1)
        return pl.BlockSpec(self.shape, lambda i: place, pipeline_mode=pl.Buffered(1))


def stored(array):
    return Columns(array, keep=True)


def summands(parts):
    return [stored(parts[0])] + passed(parts[1:])


def passed(arrays):
    return [Columns(array) for array in arrays]


def kept(shape, dtype=f32):
    return pltpu.HBM(shape, dtype)


def fetch_kernel(places, *refs):
    count = len(places)
    sources, outs, sems = refs[:count], refs[count : 2 * count], refs[-1]
    copies = []
    for (start, pieces), source, out in zip(places, sources, outs):
        rows, width = out.shape[0] // pieces, out.shape[1]
        for index in range(pieces):
            own = pl.ds(rows * index, rows)
            copies.append(
                pltpu.make_async_copy(
                    source.at[own, pl.ds(start, width)], out.at[own, :], sems.at[len(copies)]
                )
            )
    for copy in copies:
        copy.start()
    for copy in copies:
        copy.wait()


def fetched_all(name, sources):
    places = [(start, 4 if array.shape[0] == 2048 and width > 128 else 1) for array, start, width in sources]
    whole = pl.BlockSpec(memory_space=pltpu.VMEM)
    return pl.pallas_call(
        partial(fetch_kernel, places),
        name=name,
        out_shape=tuple(pltpu.VMEM((array.shape[0], width), array.dtype) for array, _, width in sources),
        in_specs=[pl.BlockSpec(memory_space=pltpu.HBM)] * len(sources),
        out_specs=tuple(whole for _ in sources),
        scratch_shapes=[pltpu.SemaphoreType.DMA((sum(pieces for _, pieces in places),))],
        compiler_params=pltpu.CompilerParams(vmem_limit_bytes=VMEM_LIMIT),
        cost_estimate=pl.CostEstimate(
            flops=0, bytes_accessed=sum(2 * array.shape[0] * width for array, _, width in sources), transcendentals=0
        ),
    )(*(pltpu.with_memory_space_constraint(array, pltpu.HBM) for array, _, _ in sources))


def fetched(name, array, start, width):
    return fetched_all(name, [(array, start, width)])[0]


def restored(name, arrays):
    return fetched_all(name, [(array, 0, array.shape[1]) for array in arrays])


def stash_kernel(*refs):
    count = len(refs) // 2
    sems = refs[-1]
    copies = [pltpu.make_async_copy(refs[k], refs[count + k], sems.at[k]) for k in range(count)]
    for copy in copies:
        copy.start()
    for copy in copies:
        copy.wait()


def stashed(name, arrays):
    return pl.pallas_call(
        stash_kernel,
        name=name,
        out_shape=tuple(pltpu.HBM(array.shape, array.dtype) for array in arrays),
        in_specs=[pl.BlockSpec(memory_space=pltpu.VMEM)] * len(arrays),
        out_specs=tuple(pl.BlockSpec(memory_space=pltpu.HBM) for _ in arrays),
        scratch_shapes=[pltpu.SemaphoreType.DMA((len(arrays),))],
        compiler_params=pltpu.CompilerParams(vmem_limit_bytes=VMEM_LIMIT),
        cost_estimate=pl.CostEstimate(flops=10**9, bytes_accessed=10**6, transcendentals=0),
    )(*arrays)


def run_kernel(kernel, outs, flags, *args, scratch=(), us=1.0):
    whole = pl.BlockSpec(memory_space=pltpu.VMEM)
    own = [isinstance(arg, (Columns, Layer)) for arg in args]
    specs, arrays, out_specs = [], [], []
    for arg, copied in zip(args, own):
        specs.append(arg.spec() if copied else whole)
        array = arg.array if copied else arg
        arrays.append(pltpu.with_memory_space_constraint(array, pltpu.HBM) if copied and arg.keep else array)
    for out in outs:
        in_vmem = isinstance(out, jax.ShapeDtypeStruct)
        out_specs.append(whole if in_vmem else pl.BlockSpec(out.shape, lambda i, n=len(out.shape): (0,) * n))
        own.append(not in_vmem)
    moved = sum(2 * math.prod(arg.shape) for arg in args) + sum(2 * math.prod(o.shape) for o in outs)
    if flags is not None:
        specs = [pl.BlockSpec(memory_space=pltpu.SMEM)] + specs
        arrays = [flags] + arrays
    return pl.pallas_call(
        kernel,
        grid=(1,) if any(own) else (),
        out_shape=tuple(outs),
        in_specs=specs,
        out_specs=tuple(out_specs),
        scratch_shapes=list(scratch),
        compiler_params=pltpu.CompilerParams(vmem_limit_bytes=VMEM_LIMIT),
        cost_estimate=pl.CostEstimate(flops=int(us * 1e9), bytes_accessed=moved, transcendentals=0),
    )(*arrays)


def local_block(flags, natural):
    return pl.multiple_of(flags[8 + natural] * SHARE, SHARE)


def rank_block(flags, rank):
    return pl.multiple_of(flags[16 + rank] * ROWS, ROWS)


def lane_index(shape):
    return lax.broadcasted_iota(i32, shape, len(shape) - 1)


def spread(columns, pair):
    low = lane_index((1, 128)) < HP
    return jnp.where(low, columns[:, 2 * pair : 2 * pair + 1], columns[:, 2 * pair + 1 : 2 * pair + 2])


def lanes_of(pair):
    return slice(128 * pair, 128 * pair + 128)


def turned(value, table, sign):
    return value * table[:, 0:128] + sign * (pltpu.roll(value, 64, 1) * table[:, 128:256])


def segments(table):
    return table[:, 259:260]


def sigmoid(v):
    return 1.0 / (1.0 + jnp.exp(-v))


def softplus(v):
    return jnp.maximum(v, 0.0) + jnp.log1p(jnp.exp(-jnp.abs(v)))


def conv_sum(ext, table, weight):
    total = weight[CONV : CONV + 1, :] + ext[8 : 8 + ROWS, :] * weight[3:4, :]
    for tap in range(CONV - 1):
        total = total + table[:, 256 + tap : 257 + tap] * ext[5 + tap : 5 + tap + ROWS, :] * weight[tap : tap + 1, :]
    return total


def conv_back(grad_out, ext, table, weight, work, grad_ref, edge_ref, gweight_ref):
    total = conv_sum(ext, table, weight)
    sig = sigmoid(total)
    grad = grad_out * sig * (1.0 + total * (1.0 - sig))
    width = grad.shape[1]
    gweight_ref[...] = jnp.zeros((8, width), f32)
    gweight_ref[CONV : CONV + 1, :] = jnp.sum(grad, axis=0, keepdims=True)
    gweight_ref[3:4, :] = jnp.sum(grad * ext[8 : 8 + ROWS, :], axis=0, keepdims=True)
    work[0:8, :] = jnp.zeros((8, width), f32)
    work[264:272, :] = jnp.zeros((8, width), f32)
    own = grad * weight[3:4, :]
    edge = jnp.zeros((8, width), f32)
    for tap in range(CONV - 1):
        part = grad * table[:, 256 + tap : 257 + tap]
        gweight_ref[tap : tap + 1, :] = jnp.sum(
            part * ext[5 + tap : 5 + tap + ROWS, :], axis=0, keepdims=True
        )
        work[8:264, :] = part * weight[tap : tap + 1, :]
        own = own + work[11 - tap : 11 - tap + ROWS, :]
        edge = edge + work[3 - tap : 11 - tap, :]
    grad_ref[...] = own
    edge_ref[...] = edge


def pack_kernel(place, *refs):
    out, at, index = refs[-1], 0, 0
    while index < len(refs) - 1:
        ref = refs[index]
        if len(ref.shape) == 4:
            out[:, at : at + XLOC] = ref[0, :, 0, :]
            out[:, at + XLOC : at + 512] = refs[index + 1][0]
            out[:, at + 512 : at + 896] = ref[0, :, 1, :]
            at, index = at + 896, index + 2
            continue
        width = min(ref.shape[2], 512)
        if width == HLOC:
            out[:, at : at + 128] = jnp.zeros((out.shape[0], 128), bf16)
            out[:, at : at + HLOC] = ref[0]
            width = 128
        elif ref.shape[2] == 1024:
            width = 128
            out[:, at : at + width] = ref[0, :, pl.ds(pl.multiple_of(place[0] * 128, 128), 128)]
        else:
            out[:, at : at + width] = ref[0]
        at, index = at + width, index + 1


def first_kernel(flags, rows, cotangent, gain, normed, inverse, hidden_kept, grads, grad):
    for block in range(8):
        own = slice(SHARE * block, SHARE * (block + 1))
        from_rows = pl.ds(pl.multiple_of(flags[24 + block] * SHARE, SHARE), SHARE)
        wide = rows[0, from_rows, :].astype(f32)
        scale = lax.rsqrt(jnp.mean(wide * wide, axis=1, keepdims=True) + norm_eps)
        normed[own, :] = (wide * scale * gain[0:1, :]).astype(bf16)
        grads[own, :] = cotangent[0, from_rows, :]
        if block == 0:
            hidden_kept[...] = wide
            inverse[...] = jnp.broadcast_to(scale, inverse.shape)
            grad[...] = cotangent[0, from_rows, :].astype(f32)


def joined(parts):
    return parts[0][...] if len(parts) == 1 else jnp.concatenate([part[...] for part in parts], axis=0)


def projections(flags, work, table, z, xs, query, dtn):
    for block in range(8):
        own = slice(SHARE * block, SHARE * (block + 1))
        from_rows = pl.ds(local_block(flags, block), SHARE)
        z[own, :] = work[from_rows, 0:XLOC]
        xs[own, 0:XLOC] = work[from_rows, 512:896]
        xs[own, XLOC:512] = work[from_rows, 1024:PROJ]
        query[own, :] = turned(work[from_rows, XLOC:512], table[own, :], 1.0).astype(bf16)
        dtn[own, :] = work[from_rows, 896:1024]


def proj_kernel(flags, p0, p1, p2, p3, p4, p5, p6, p7, weight, table, normed, *refs):
    rows = joined((p0, p1, p2, p3, p4, p5, p6, p7))
    normed[...] = rows
    work = refs[-1]
    work[...] = dot_nn(rows, weight[...])
    projections(flags, work, table, *refs[:-1])


def first_proj_kernel(flags, rows, weight, table, z, xs, query, dtn, work):
    step = pl.program_id(0)
    part = dot_nn(rows[...], weight[...])

    @pl.when(step == 0)
    def _():
        work[...] = part

    @pl.when(step > 0)
    def _():
        work[...] = work[...] + part

    @pl.when(step == 3)
    def _():
        projections(flags, work, table, z, xs, query, dtn)


def first_projections(flags, normed, weight, table):
    model = normed.shape[1]
    whole = pl.BlockSpec(memory_space=pltpu.VMEM)
    outs = [shape_of((ROWS, XLOC)), shape_of((ROWS, 512)), shape_of((ROWS, HD), bf16), shape_of((ROWS, 128))]
    return pl.pallas_call(
        first_proj_kernel,
        grid=(4,),
        out_shape=tuple(outs),
        in_specs=[
            pl.BlockSpec(memory_space=pltpu.SMEM),
            pl.BlockSpec((ROWS, model // 4), lambda i: (0, i)),
            pl.BlockSpec((model // 4, PROJ), lambda i: (i, 0)),
            whole,
        ],
        out_specs=tuple(
            whole if isinstance(out, jax.ShapeDtypeStruct) else pl.BlockSpec(out.shape, lambda i: (0, 0))
            for out in outs
        ),
        scratch_shapes=[pltpu.VMEM((ROWS, PROJ), f32)],
        compiler_params=pltpu.CompilerParams(vmem_limit_bytes=VMEM_LIMIT),
        cost_estimate=pl.CostEstimate(flops=4 * 10**9, bytes_accessed=2 * model * PROJ, transcendentals=0),
    )(flags, normed, pltpu.with_memory_space_constraint(weight, pltpu.HBM), table)


def shared_kernel(flags, xs, halo, table, small, out, ext):
    own = xs[:, XLOC:512]
    ext[0:8, :] = halo[:, XLOC:512]
    ext[8 : 8 + ROWS, :] = own
    total = conv_sum(ext, table, small[:, XLOC:512])
    rank = flags[0]
    out[...] = jnp.where(
        rank < 2, turned(own, table, 1.0), jnp.where(rank < 4, own, total * sigmoid(total))
    ).astype(bf16)


def prep_kernel(xs, dtn, halo, table, small, ext, xc, xc_kept, rates, rates_kept, rates_t, rates_t_kept):
    ext[0:8, :] = halo[:, 0:XLOC]
    ext[8 : 8 + ROWS, :] = xs[:, 0:XLOC]
    total = conv_sum(ext, table, small[:, 0:XLOC])
    for out in (xc, xc_kept):
        out[...] = total * sigmoid(total)
    params = small[:, 512:640]
    rate = softplus(dtn[...] + params[1:2, :])
    logs = -jnp.exp(params[0:1, :]) * rate
    rows = lax.broadcasted_iota(i32, (ROWS, ROWS), 0)
    lower = (rows >= lane_index((ROWS, ROWS))).astype(f32)
    running = jnp.dot(lower, logs, precision=lax.Precision.HIGHEST, preferred_element_type=f32)
    for out in (rates, rates_kept):
        out[:, 0:128] = rate
        out[:, 128:256] = running
    rate_t, running_t = rate.T[0:8, :], running.T[0:8, :]
    for out in (rates_t, rates_t_kept):
        out[0:8, :] = rate_t
        out[8:16, :] = running_t


def block_decays(flags, rates_t):
    kept = jnp.where(flags[4] == flags[5], 1.0, 0.0)
    return jnp.exp(rates_t[8:16, ROWS - 1 : ROWS]) * kept


def decay_rows(flags, rates_t):
    rows = jnp.broadcast_to(block_decays(flags, rates_t), (8, NSTATE))
    return jnp.concatenate([rows, jnp.zeros((8, NSTATE), f32)], axis=0).astype(bf16)


def weights_in(rates, table):
    last = rates[ROWS - 1 : ROWS, 128:256]
    gap = jnp.exp(last - rates[:, 128:256]) * table[:, 261:262]
    return gap, gap * rates[:, 0:128]


def rank_columns(flags, shared, first):
    return jnp.concatenate(
        [shared[pl.ds(rank_block(flags, rank), ROWS), :] for rank in (first, first + 1)], axis=1
    )


def inject_of(flags, shared):
    return rank_columns(flags, shared, 4)


def readout_of(flags, shared):
    return rank_columns(flags, shared, 6)


def carry_of(rates, table):
    return jnp.exp(rates[:, 128:256]) * table[:, 260:261]


def state_kernel(flags, s0, s1, s2, s3, s4, s5, s6, s7, xc, rates, rates_t, table, out, shared):
    for index, part in enumerate((s0, s1, s2, s3, s4, s5, s6, s7)):
        shared[ROWS * index : ROWS * (index + 1), :] = part[...]
    inject = inject_of(flags, shared)
    _, weight = weights_in(rates, table)
    for pair in range(PAIRS):
        weighted = (xc[:, lanes_of(pair)] * spread(weight, pair)).astype(bf16)
        out[KV + 128 * pair : KV + 128 * (pair + 1), :] = dot_tn(weighted, inject).astype(bf16)
    out[KV + XLOC : KV + MSG, :] = decay_rows(flags, rates_t)
    half = shared[pl.ds(rank_block(flags, 2 * flags[2] + flags[1] // 2), ROWS), :]
    out[0:KV, :] = jnp.concatenate([half[0:128], half[128:256]], axis=1)


def halves_kernel(msg1, msg2, msg3, out):
    for index, msg in enumerate((msg1, msg2, msg3)):
        out[KV * index : KV * (index + 1), :] = msg[...]


def allowed_pairs(table, seg_rows):
    rows = lax.broadcasted_iota(i32, (ROWS, ROWS), 0)
    return (rows >= lane_index((ROWS, ROWS))) & (segments(table) == seg_rows[0:1, :])


def head_decay(allowed, rates, rates_t, head):
    gap = rates[:, 128 + head : 129 + head] - rates_t[8 + head : 9 + head, :]
    return jnp.where(allowed, jnp.exp(jnp.where(allowed, gap, 0.0)), 0.0)


def intra_kernel(flags, shared, xc, rates, rates_t, table, seg_rows, small, out):
    inject, readout = inject_of(flags, shared), readout_of(flags, shared)
    both = dot_nt(readout, inject)
    allowed = allowed_pairs(table, seg_rows)
    low = lane_index((1, 128)) < HP
    for pair in range(PAIRS):
        x = xc[:, lanes_of(pair)]
        xb = x.astype(bf16)
        heads = []
        for head in (2 * pair, 2 * pair + 1):
            decay = head_decay(allowed, rates, rates_t, head)
            heads.append(dot_nn((both * decay * rates_t[head : head + 1, :]).astype(bf16), xb))
        out[:, lanes_of(pair)] = jnp.where(low, heads[0], heads[1]) + spread(small[2:3, 512:640], pair) * x


def keys_values(flags, shared, halves, swapped):
    head, first = flags[1] // 2, flags[2] == 0
    pairs = [
        (
            shared[pl.ds(rank_block(flags, head), ROWS), :],
            shared[pl.ds(rank_block(flags, 2 + head), ROWS), :],
        )
    ]
    for index, half in enumerate(halves):
        packed = half[...], swapped[KV * index : KV * (index + 1), :]
        mine, theirs = (jnp.concatenate([part[:, 0:128], part[:, 128:256]], axis=0) for part in packed)
        pairs.append((jnp.where(first, mine, theirs), jnp.where(first, theirs, mine)))
    return pairs


def masked_scores(query, pairs, table, seg_rows):
    parts = []
    for block, (keys, _) in enumerate(pairs):
        score = dot_nt(query, keys) * HD ** (-0.5)
        keep = segments(table) == seg_rows[block : block + 1, :]
        if block == 0:
            rows = lax.broadcasted_iota(i32, (ROWS, ROWS), 0)
            keep = keep & (rows >= lane_index((ROWS, ROWS)))
        parts.append(jnp.where(keep, score, -1e30))
    return parts


def attention_kernel(flags, query, shared, h1, h2, h3, swapped, table, seg_rows, out, log_total, kept):
    pairs = keys_values(flags, shared, (h1, h2, h3), swapped)
    for block, (keys, values) in enumerate(pairs):
        kept[ROWS * block : ROWS * (block + 1), 0:HD] = keys
        kept[ROWS * block : ROWS * (block + 1), HD : 2 * HD] = values
    parts = masked_scores(query[...], pairs, table, seg_rows)
    top = parts[0].max(axis=1, keepdims=True)
    for part in parts[1:]:
        top = jnp.maximum(top, part.max(axis=1, keepdims=True))
    parts = [jnp.exp(part - top) for part in parts]
    total = sum(part.sum(axis=1, keepdims=True) for part in parts)
    inverse = 1.0 / total
    result = jnp.zeros((ROWS, HD), f32)
    for part, (_, values) in zip(parts, pairs):
        result = result + dot_nn((part * inverse).astype(bf16), values)
    rounded = result.astype(bf16)
    for block in range(8):
        out[pl.ds(local_block(flags, block), SHARE), :] = rounded[SHARE * block : SHARE * (block + 1), :]
    log_total[...] = jnp.broadcast_to(top + jnp.log(total), (ROWS, HD))


def chained(first, second, third, base):
    rows1 = first[base + XLOC : base + MSG, :].astype(f32)
    rows2 = second[base + XLOC : base + MSG, :].astype(f32)
    parts = []
    for head in range(HLOC):
        own = slice(base + HP * head, base + HP * head + HP)
        older = second[own, :].astype(f32) + rows2[head : head + 1, :] * third[own, :].astype(f32)
        parts.append(first[own, :].astype(f32) + rows1[head : head + 1, :] * older)
    return jnp.concatenate(parts, axis=0)


def carry_kernel(flags, msg1, msg2, msg3, shared, rates, table, intra, z, state, ssm_y, cat):
    entering = chained(msg1, msg2, msg3, KV)
    state[...] = entering
    from_state = dot_nt(readout_of(flags, shared), entering.astype(bf16))
    carry = carry_of(rates, table)
    for pair in range(PAIRS):
        own = lanes_of(pair)
        y = intra[:, own] + spread(carry, pair) * from_state[:, own]
        ssm_y[:, own] = y
        gate = z[:, own]
        gated = (y * gate * sigmoid(gate)).astype(bf16)
        for block in range(8):
            cat[pl.ds(local_block(flags, block), SHARE), 128 * pair : 128 * (pair + 1)] = gated[
                SHARE * block : SHARE * (block + 1), :
            ]


def gate_back_kernel(
    flags, p0, p1, p2, p3, p4, p5, p6, p7, weight, z, ssm_y, shared, rates, rates_t, table,
    dmix, dattn, dy, dz, msg, work, local,
):
    rows = joined((p0, p1, p2, p3, p4, p5, p6, p7))
    dmix[...] = rows
    local[...] = dot_nn(rows, weight[...])
    for block in range(8):
        own = slice(SHARE * block, SHARE * (block + 1))
        from_rows = pl.ds(local_block(flags, block), SHARE)
        dattn[own, :] = local[from_rows, 0:128].astype(bf16)
        work[own, :] = local[from_rows, 128:512]
    readout = readout_of(flags, shared)
    carry = carry_of(rates, table)
    for pair in range(PAIRS):
        own = lanes_of(pair)
        gate, grad = z[:, own], work[:, own]
        sig = sigmoid(gate)
        y_grad = grad * gate * sig
        dy[:, own] = y_grad
        dz[:, own] = (grad * ssm_y[:, own] * sig * (1.0 + gate * (1.0 - sig))).astype(bf16)
        msg[own, :] = dot_tn((y_grad * spread(carry, pair)).astype(bf16), readout).astype(bf16)
    msg[XLOC:MSG, :] = decay_rows(flags, rates_t)


def attention_back_kernel(
    flags, dattn, dz, query, kept, log_total, table, seg_rows,
    early, mine, theirs,
):
    pairs = []
    for block in range(SEQ_BLOCKS):
        own = slice(ROWS * block, ROWS * (block + 1))
        pairs.append((kept[own, 0:HD], kept[own, HD : 2 * HD]))
    first = flags[2] == 0
    q = query[...]
    grad = dattn[...]
    parts = masked_scores(q, pairs, table, seg_rows)
    logs = log_total[:, 0:1]
    probs = [jnp.exp(part - logs) for part in parts]
    grads = [dot_nt(grad, values) for _, values in pairs]
    inner = sum((p * g).sum(axis=1, keepdims=True) for p, g in zip(probs, grads))
    total = jnp.zeros((ROWS, HD), f32)
    for block, (p, g, (keys, _)) in enumerate(zip(probs, grads, pairs)):
        own = slice(ROWS * block, ROWS * (block + 1))
        score = (p * (g - inner)).astype(bf16)
        total = total + dot_nn(score, keys)
        dkeys = dot_tn(score, q) * HD ** (-0.5)
        dvalues = dot_tn(p.astype(bf16), grad)
        mine[own, :] = jnp.where(first, dkeys, dvalues)
        theirs[own, :] = jnp.where(first, dvalues, dkeys).astype(bf16)
    total = total * HD ** (-0.5)
    dq = turned(total, table, -1.0).astype(bf16)
    for block in range(8):
        own = slice(SHARE * block, SHARE * (block + 1))
        to_rows = pl.ds(local_block(flags, block), SHARE)
        early[to_rows, 0:XLOC] = dz[own, :]
        early[to_rows, XLOC:512] = dq[own, :]


def intra_back_kernel(
    flags, dy, xc, shared, rates, rates_t, table, seg_rows, state, small,
    dx, dshared, drates, dskip, row_sums, dcum,
):
    inject, readout = inject_of(flags, shared), readout_of(flags, shared)
    both = dot_nt(readout, inject)
    allowed = allowed_pairs(table, seg_rows)
    low = lane_index((1, 128)) < HP
    carry = carry_of(rates, table)
    entering = state[...].astype(bf16)
    from_state = dot_nt(readout, entering)
    dboth = jnp.zeros((ROWS, ROWS), f32)
    row_sums[...] = jnp.zeros((128, ROWS), f32)
    dcum[...] = jnp.zeros((ROWS, 128), f32)
    carried = []
    for pair in range(PAIRS):
        own = lanes_of(pair)
        x = xc[:, own]
        xb = x.astype(bf16)
        grad = dy[:, own]
        dskip[:, own] = jnp.sum(grad * x, axis=0, keepdims=True)
        carried.append((grad * spread(carry, pair)).astype(bf16))
        through = grad * from_state[:, own]
        total = spread(small[2:3, 512:640], pair) * grad
        for head in (2 * pair, 2 * pair + 1):
            mine = low if head % 2 == 0 else jnp.logical_not(low)
            decay = head_decay(allowed, rates, rates_t, head)
            steps = rates_t[head : head + 1, :]
            head_grad = jnp.where(mine, grad, 0.0).astype(bf16)
            dmix = dot_nt(head_grad, xb)
            kept = dmix * decay
            dboth = dboth + kept * steps
            mixed = both * decay
            total = total + dot_tn((mixed * steps).astype(bf16), head_grad)
            passed = dmix * mixed
            row_sums[head : head + 1, :] = jnp.sum(passed, axis=0, keepdims=True)
            dcum[:, head : head + 1] = jnp.sum(passed * steps, axis=1, keepdims=True) + carry[
                :, head : head + 1
            ] * jnp.sum(jnp.where(mine, through, 0.0), axis=1, keepdims=True)
        dx[:, own] = total
    columns = row_sums[...].T
    drates[:, 0:128] = columns
    drates[:, 128:256] = dcum[...] - rates[:, 0:128] * columns
    dboth_b = dboth.astype(bf16)
    dshared[:, NSTATE:] = dot_nn(dboth_b, inject) + dot_nn(jnp.concatenate(carried, axis=1), entering)
    dshared[:, 0:NSTATE] = dot_tn(dboth_b, readout)


def packed_back_kernel(
    flags, msg1, msg2, msg3, shared, xc, rates, table, dshared, kv0, kv1, kv2, kv3, packed, state_grad,
):
    later = chained(msg1, msg2, msg3, 0)
    state_grad[...] = later
    _, weights = weights_in(rates, table)
    weighted = [(xc[:, lanes_of(pair)] * spread(weights, pair)).astype(bf16) for pair in range(PAIRS)]
    weighted = jnp.concatenate(weighted, axis=1)
    dinject = (dshared[:, 0:NSTATE] + dot_nn(weighted, later.astype(bf16))).astype(bf16)
    dreadout = dshared[:, NSTATE:].astype(bf16)
    packed[...] = jnp.zeros((8 * ROWS, 128), bf16)
    grads = kv0[...] + kv1[...].astype(f32) + kv2[...].astype(f32) + kv3[...].astype(f32)
    owner = 2 * flags[2] + flags[1] // 2
    packed[pl.ds(rank_block(flags, owner), ROWS), :] = grads.astype(bf16)
    packed[pl.ds(rank_block(flags, 4), ROWS), :] = dinject[:, 0:128]
    packed[pl.ds(rank_block(flags, 5), ROWS), :] = dinject[:, 128:256]
    packed[pl.ds(rank_block(flags, 6), ROWS), :] = dreadout[:, 0:128]
    packed[pl.ds(rank_block(flags, 7), ROWS), :] = dreadout[:, 128:256]


def state_back_kernel(
    flags, later, shared, xc, rates, rates_t, table, state, small, dtn, dx, drates, ext,
    dxpre, edge, gweight, ddt, heads, work, dconv, sums,
):
    inject = inject_of(flags, shared)
    low = lane_index((1, 128)) < HP
    params = small[:, 512:640]
    gap, weights = weights_in(rates, table)
    from_later = dot_nt(inject, later[...].astype(bf16))
    products = later[...] * state[...]
    decays = block_decays(flags, rates_t)
    sums[...] = jnp.zeros((ROWS, 128), f32)
    for pair in range(PAIRS):
        own = lanes_of(pair)
        dconv[:, own] = dx[:, own] + spread(weights, pair) * from_later[:, own]
        through = xc[:, own] * from_later[:, own]
        for head in (2 * pair, 2 * pair + 1):
            mine = low if head % 2 == 0 else jnp.logical_not(low)
            sums[:, head : head + 1] = jnp.sum(jnp.where(mine, through, 0.0), axis=1, keepdims=True)
    dweights = sums[...]
    moved = dweights * weights
    last = jnp.sum(moved, axis=0, keepdims=True)
    lanes = lane_index((1, 128))
    for head in range(HLOC):
        total = jnp.sum(
            jnp.sum(products[HP * head : HP * head + HP, :], axis=0, keepdims=True), axis=1, keepdims=True
        )
        last = last + jnp.where(lanes == head, total * decays[head : head + 1, :], 0.0)
    rows = lax.broadcasted_iota(i32, (ROWS, 128), 0)
    dcums = drates[:, 128:256] - moved + jnp.where(rows == ROWS - 1, last, 0.0)
    square = lax.broadcasted_iota(i32, (ROWS, ROWS), 0)
    upper = (square <= lane_index((ROWS, ROWS))).astype(f32)
    dlogs = jnp.dot(upper, dcums, precision=lax.Precision.HIGHEST, preferred_element_type=f32)
    rate = -jnp.exp(params[0:1, :])
    dsteps = drates[:, 0:128] + dweights * gap + dlogs * rate
    ddts = dsteps * sigmoid(dtn[...] + params[1:2, :])
    ddt[...] = ddts
    heads[...] = jnp.zeros((8, 128), f32)
    heads[0:1, :] = jnp.sum(dlogs * rate * rates[:, 0:128], axis=0, keepdims=True)
    heads[1:2, :] = jnp.sum(ddts, axis=0, keepdims=True)
    conv_back(dconv[...], ext, table, small[:, 0:XLOC], work, dxpre, edge, gweight)


def shared_back_kernel(flags, part0, part1, part2, part3, ext, table, small, out, edge, gweight, work):
    grad = part0[...] + part1[...].astype(f32) + part2[...].astype(f32) + part3[...].astype(f32)
    conv_back(grad, ext, table, small[:, XLOC:512], work, out, edge, gweight)
    rank = flags[0]
    of_conv = jnp.where(rank < 4, 0.0, 1.0)
    edge[...] = edge[...] * of_conv
    gweight[...] = gweight[...] * of_conv
    out[...] = jnp.where(rank < 2, turned(grad, table, -1.0), jnp.where(rank < 4, grad, out[...]))


def late_kernel(flags, dxpre, edge_x, dsh, edge_sh, ddt, out):
    for block in range(8):
        own = slice(SHARE * block, SHARE * (block + 1))
        to_rows = pl.ds(local_block(flags, block), SHARE)
        x, sh = dxpre[own, :], dsh[own, :]
        if block == 7:
            pad = jnp.zeros((SHARE - 8, 128), f32)
            sh = sh + jnp.concatenate([pad, edge_sh[...]], axis=0)
            x = x + jnp.concatenate([jnp.zeros((SHARE - 8, XLOC), f32), edge_x[...]], axis=0)
        out[to_rows, 0:XLOC] = x.astype(bf16)
        out[to_rows, 512:LATE] = sh.astype(bf16)
        out[to_rows, XLOC:512] = jnp.where(lane_index((1, 128)) < HLOC, ddt[own, :], 0.0).astype(bf16)


def half_sum_kernel(own, other, keep, send1, send2, send3):
    rows = own.shape[0] // 4
    keep[...] = own[0:rows, :] + other[0:rows, :].astype(f32)
    for index, send in ((1, send1), (2, send2), (3, send3)):
        part = slice(rows * index, rows * (index + 1))
        send[...] = (own[part, :].astype(f32) + other[part, :].astype(f32)).astype(bf16)


def parts_of_sum(own, other, along, sign):
    return parts_from(own, other_core(other), along, sign)


def parts_from(own, got, along, sign):
    rows, width = own.shape[0] // 4, own.shape[1]
    sent = shape_of((rows, width), bf16)
    keep, *sends = run_kernel(half_sum_kernel, [kept((rows, width)), sent, sent, sent], None, own, Columns(got))
    return (keep,) + tuple(along(send, sign * k) for k, send in zip((1, 2, 3), sends))


def split_kernel(*refs):
    lefts, weight, own, other = refs[:-3], refs[-3], refs[-2], refs[-1]
    left = lefts[0][...] if len(lefts) == 1 else jnp.concatenate([ref[...] for ref in lefts], axis=1)
    result = dot_nt(left, weight[...])
    own[...] = result[: ROWS // 2]
    other[...] = result[ROWS // 2 :].astype(bf16)


def summed_rows(lefts, weight):
    model, width = weight.shape
    own, other = pl.pallas_call(
        split_kernel,
        grid=(model // 512,),
        out_shape=(shape_of((ROWS // 2, model)), shape_of((ROWS // 2, model), bf16)),
        in_specs=[pl.BlockSpec(left.shape, lambda i: (0, 0)) for left in lefts]
        + [pl.BlockSpec((512, width), lambda i: (i, 0))],
        out_specs=(
            pl.BlockSpec((ROWS // 2, 512), lambda i: (0, i)),
            pl.BlockSpec((ROWS // 2, 512), lambda i: (0, i)),
        ),
        compiler_params=pltpu.CompilerParams(vmem_limit_bytes=VMEM_LIMIT),
        cost_estimate=pl.CostEstimate(
            flops=2 * ROWS * model * width, bytes_accessed=2 * model * width, transcendentals=0
        ),
    )(*lefts, weight)
    return parts_of_sum(own, other, along_y, 1)


def gate_up_kernel(p0, p1, p2, p3, p4, p5, p6, p7, weight, normed, gate, up, act):
    rows = joined((p0, p1, p2, p3, p4, p5, p6, p7))
    normed[...] = rows
    result = dot_nn(rows, weight[...])
    g, u = result[:, :512], result[:, 512:]
    gate[...] = g
    up[...] = u
    act[...] = (g * sigmoid(g) * u).astype(bf16)


def gate_up_back_kernel(*refs):
    parts, (weight, gate, up, dffn, out) = refs[:-5], refs[-5:]
    rows = joined(parts)
    dffn[...] = rows
    dact = dot_nn(rows, weight[...])
    g = gate[...]
    sig = sigmoid(g)
    out[:, :512] = (dact * up[...] * sig * (1.0 + g * (1.0 - sig))).astype(bf16)
    out[:, 512:] = (dact * g * sig).astype(bf16)


def natural_kernel(flags, p0, p1, p2, p3, p4, p5, p6, p7, out):
    local = joined((p0, p1, p2, p3, p4, p5, p6, p7)).astype(out.dtype)
    for block in range(8):
        out[pl.ds(pl.multiple_of(flags[24 + block] * SHARE, SHARE), SHARE), :] = local[
            SHARE * block : SHARE * (block + 1), :
        ]


def add_norm_kernel(hidden, part0, part1, part2, part3, gain, out_kept, normed, inverse):
    total = hidden[...] + part0[...] + (
        part1[...].astype(f32) + part2[...].astype(f32) + part3[...].astype(f32)
    )
    out_kept[...] = total
    scale = lax.rsqrt(jnp.mean(total * total, axis=1, keepdims=True) + norm_eps)
    inverse[...] = jnp.broadcast_to(scale, inverse.shape)
    normed[...] = (total * scale * gain[...]).astype(bf16)


def add_norm(hidden, parts, gain):
    shape = hidden.shape
    return run_kernel(
        add_norm_kernel,
        [shape_of(shape), shape_of(shape, bf16), shape_of((shape[0], 128))],
        None, hidden, *summands(parts), gain[None],
    )


def output_kernel(hidden, part0, part1, part2, part3, out):
    total = hidden[...] + part0[...] + (
        part1[...].astype(f32) + part2[...].astype(f32) + part3[...].astype(f32)
    )
    out[...] = total.astype(bf16)


def norm_back_kernel(grad, part0, part1, part2, part3, hidden, inverse, gain, out, rounded, ggain):
    received = part0[...] + (part1[...].astype(f32) + part2[...].astype(f32) + part3[...].astype(f32))
    scale = inverse[:, 0:1]
    unit = hidden[...] * scale
    scaled = received * gain[...]
    ggain[...] = jnp.sum(received * unit, axis=0, keepdims=True)
    total = grad[...] + scale * (scaled - unit * jnp.mean(scaled * unit, axis=1, keepdims=True))
    out[...] = total
    rounded[...] = total.astype(bf16)


def norm_back(parts, grad, hidden, inverse, gain):
    shape = hidden.shape
    return run_kernel(
        norm_back_kernel,
        [shape_of(shape), shape_of(shape, bf16), shape_of((1, shape[1]))],
        None, grad, *summands(parts), hidden, inverse, gain[None],
    )


def gradient_kernel(pairs, *refs):
    out, at = refs[-1], 0
    for index in range(pairs):
        left, right = refs[2 * index], refs[2 * index + 1]
        width = right.shape[1]
        out[:, at : at + width] = dot_tn(left[...], right[...]).astype(bf16)
        at += width
    if at < out.shape[1]:
        out[:, at:] = jnp.zeros((out.shape[0], out.shape[1] - at), bf16)


def weight_gradients(pairs, total, block, index, buffer=None):
    rows, model = pairs[0][0].shape
    width = sum(right.shape[1] for _, right in pairs)
    specs, args = [], []
    for left, right in pairs:
        block_right = right.block if isinstance(right, Columns) else 0
        specs += [
            pl.BlockSpec((rows, 512), lambda i: (0, i)),
            pl.BlockSpec(right.shape, lambda i, block=block_right: (0, block)),
        ]
        args += [left, right.array if isinstance(right, Columns) else right]
    aliases = {}
    kernel = partial(gradient_kernel, len(pairs))
    if buffer is not None:
        aliases = {len(args): 0}
        specs.append(pl.BlockSpec(memory_space=pltpu.HBM))
        args.append(buffer)

        def kernel(*refs):
            gradient_kernel(len(pairs), *refs[:-2], refs[-1])

    return pl.pallas_call(
        kernel,
        grid=(model // 512,),
        out_shape=pltpu.HBM((model, total), bf16),
        in_specs=specs,
        out_specs=pl.BlockSpec((512, block), lambda i: (i, index)),
        input_output_aliases=aliases,
        compiler_params=pltpu.CompilerParams(vmem_limit_bytes=VMEM_LIMIT),
        cost_estimate=pl.CostEstimate(
            flops=2 * rows * model * width, bytes_accessed=model * width * 2, transcendentals=0
        ),
    )(*args)


def owned_kernel(pairs, *refs):
    out, at = refs[-1], 0
    for pair in range(pairs):
        left, right = refs[2 * pair], refs[2 * pair + 1]
        result = dot_tn(left[...], right[...]).astype(bf16)
        width = right.shape[1]
        for index in range(2):
            out[index, :, at : at + width] = result[128 * index : 128 * (index + 1)]
        at += width


def insert_kernel(small, block, out):
    mine = lane_index((1, 1, 128)) < HLOC
    out[...] = jnp.where(mine, block[...], small[...][None])


def with_small(owned, small):
    spec = pl.BlockSpec((16, 128, 128), lambda i: (0, 0, XLOC // 128))
    return pl.pallas_call(
        insert_kernel,
        grid=(1,),
        out_shape=pltpu.HBM(owned.shape, bf16),
        in_specs=[pl.BlockSpec((128, 128), lambda i: (0, 0)), spec],
        out_specs=spec,
        input_output_aliases={1: 0},
        compiler_params=pltpu.CompilerParams(vmem_limit_bytes=VMEM_LIMIT),
        cost_estimate=pl.CostEstimate(flops=10**9, bytes_accessed=10**6, transcendentals=0),
    )(small, owned)


def owned_gradients(pairs):
    rows, model = pairs[0][0].shape
    width = sum(right.shape[1] for _, right in pairs)
    specs, args = [], []
    for left, right in pairs:
        block = right.block if isinstance(right, Columns) else 0
        specs += [
            pl.BlockSpec((rows, 256), lambda i: (0, i)),
            pl.BlockSpec(right.shape, lambda i, block=block: (0, block)),
        ]
        args += [left, right.array if isinstance(right, Columns) else right]
    return pl.pallas_call(
        partial(owned_kernel, len(pairs)),
        grid=(model // 256,),
        out_shape=pltpu.HBM((16, model // 16, width), bf16),
        in_specs=specs,
        out_specs=pl.BlockSpec((2, model // 16, width), lambda i: (i, 0, 0)),
        compiler_params=pltpu.CompilerParams(vmem_limit_bytes=VMEM_LIMIT),
        cost_estimate=pl.CostEstimate(
            flops=2 * rows * model * width, bytes_accessed=model * width * 2, transcendentals=0
        ),
    )(*args)


def small_kernel(gain1, gain2, conv_sh, conv_x, heads, skip, out):
    out[...] = jnp.zeros(out.shape, bf16)
    for row in range(16):
        own = slice(128 * row, 128 * row + 128)
        out[row : row + 1, :] = gain1[:, own].astype(bf16)
        out[16 + row : 17 + row, :] = gain2[:, own].astype(bf16)
    out[32:37, :] = conv_sh[0:5, :].astype(bf16)
    for tap in range(CONV + 1):
        for pair in range(PAIRS):
            row = 37 + PAIRS * tap + pair
            out[row : row + 1, :] = conv_x[tap : tap + 1, lanes_of(pair)].astype(bf16)
    out[52:54, :] = heads[0:2, :].astype(bf16)
    lanes = lane_index((1, 128))
    sums = jnp.zeros((1, 128), f32)
    for pair in range(PAIRS):
        part = skip[:, lanes_of(pair)]
        for half in range(2):
            mine = (lanes < HP) if half == 0 else (lanes >= HP)
            total = jnp.sum(jnp.where(mine, part, 0.0), axis=1, keepdims=True)
            sums = sums + jnp.where(lanes == 2 * pair + half, total, 0.0)
    out[54:55, :] = sums.astype(bf16)


def spread_kernel(small, out, work):
    work[...] = small[...].astype(f32)
    columns = work[...].T
    work[56:62, :] = columns[122:128, :]
    out[...] = pltpu.roll(work[...], HLOC, 1).astype(bf16)


def gathered_back(packed, work):
    rolled = pltpu.roll(packed, 128 - HLOC, 1)
    work[...] = jnp.zeros((128, 128), f32)
    work[122:128, :] = rolled[56:62, :]
    return jnp.where(lane_index((1, 128)) < 128 - HLOC, rolled, work[...].T)


def owner_sum(values):
    total = values[0].astype(f32)
    for index in range(1, 16):
        total = total + values[index].astype(f32)
    return total


def block_sum_kernel(values, over_tp, late, conv_x, heads, work):
    whole = owner_sum(values)
    late[...] = whole[:, 0:LATE]
    total = gathered_back(whole[:, XLOC:512], work)
    over_tp[0:128, :] = whole[:, 512:LATE].astype(bf16)
    over_tp[128:256, :] = whole[:, LATE : LATE + 128].astype(bf16)
    over_tp[256:352, :] = jnp.zeros((96, 128), bf16)
    for layer in range(2):
        first = 64 * layer
        over_tp[256 + 48 * layer : 293 + 48 * layer, :] = total[first : first + 37, :].astype(bf16)
        for tap in range(CONV + 1):
            for pair in range(PAIRS):
                row = first + 37 + PAIRS * tap + pair
                conv_x[5 * layer + tap : 5 * layer + tap + 1, lanes_of(pair)] = total[row : row + 1, :]
        heads[3 * layer : 3 * layer + 3, :] = total[first + 52 : first + 55, :]


def weight_outputs_kernel(lower, upper, late, attn, ssm, gate, up, down, query, zx, dt):
    for layer, ref in ((0, lower), (1, upper)):
        for index, out in enumerate((gate, up, down)):
            out[layer] = ref[:, 512 * index : 512 * (index + 1)].astype(f32)
        attn[layer] = ref[:, 1536:1664].astype(f32)
        ssm[layer] = ref[:, 1664:2048].astype(f32)
        zx[layer, :, 0, :] = ref[:, 2048:2432].astype(f32)
        query[layer] = ref[:, 2432:2560].astype(f32)
    zx[0, :, 1, :] = late[:, 0:XLOC]
    zx[1, :, 1, :] = lower[:, 2560:2944].astype(f32)
    dt[0] = late[:, XLOC : XLOC + HLOC]
    dt[1] = lower[:, 2944 : 2944 + HLOC].astype(f32)


def tp_outputs_kernel(flags, *refs):
    parts, (shared, gains1, gains2, conv_bc, every) = refs[:8], refs[8:]
    total = jnp.zeros((96, 128), f32)
    for index, part in enumerate(parts):
        every[index] = part[...].astype(f32)
        total = total + part[256:352, :].astype(f32)
    for layer in range(2):
        for rank in range(8):
            own = slice(128 * rank, 128 * rank + 128)
            shared[layer, :, own] = every[flags[16 + rank], 128 * layer : 128 * layer + 128, :]
        for row in range(16):
            own = slice(128 * row, 128 * row + 128)
            at = 48 * layer + row
            gains1[layer : layer + 1, own] = total[at : at + 1, :]
            gains2[layer : layer + 1, own] = total[at + 16 : at + 17, :]
        for rank in range(4):
            part = every[flags[20 + rank], 288 + 48 * layer : 296 + 48 * layer, :]
            conv_bc[5 * layer : 5 * layer + 5, 128 * rank : 128 * rank + 128] = part[0:5, :]


def body(
    inputs, cotangent, segment_ids, w_query, w_shared, w_zx, w_dt, w_attn_out, w_ssm_out, w_gate, w_up, w_down,
    gains, conv_x, conv_bc, head_params,
):
    layers = w_query.shape[0]
    rank, ctx = lax.axis_index("tp"), lax.axis_index("ctx")
    y, core = rank // 2, rank % 2
    model = inputs.shape[2]

    def local_of(block_y, block_core):
        return jnp.where(block_core == core, 0, 4) + (block_y - y) % 4

    seg_all = segment_ids[0]
    first_row = ctx * ROWS
    padded = jnp.concatenate([jnp.full((CONV - 1,), -1, i32), seg_all])
    seg_ext = lax.dynamic_slice_in_dim(padded, first_row, ROWS + CONV - 1)
    seg_own = seg_ext[CONV - 1 :]
    blocks = seg_all.reshape(SEQ_BLOCKS, ROWS)
    seg_rows = jnp.stack(
        [
            jnp.where(ctx >= back, lax.dynamic_index_in_dim(blocks, jnp.maximum(ctx - back, 0), 0, False), -1)
            for back in range(SEQ_BLOCKS)
        ]
        + [jnp.full((ROWS,), -1, i32)] * 4
    ).astype(f32)
    naturals = jnp.arange(8, dtype=i32)
    flags = jnp.concatenate(
        [
            jnp.stack([rank, y, core, ctx, seg_ext[CONV - 2], seg_own[-1], rank, rank]).astype(i32),
            local_of(naturals % 4, naturals // 4).astype(i32),
            local_of(naturals // 2, naturals % 2).astype(i32),
            (jnp.where(naturals < 4, core, 1 - core) * 4 + (y + naturals) % 4).astype(i32),
        ]
    )

    half_width = HD // 2
    frequency = rope_base ** (-jnp.arange(half_width, dtype=f32) / half_width)
    places = (first_row + jnp.arange(ROWS, dtype=i32)).astype(f32)
    angles = places[:, None] * frequency[None, :]
    cosine, sine = jnp.cos(angles), jnp.sin(angles)
    marks = [seg_ext[tap : tap + ROWS] == seg_own for tap in range(CONV - 1)]
    marks += [seg_own, seg_own == seg_ext[CONV - 2], seg_own == seg_own[-1]]
    marks = jnp.pad(jnp.stack([mark.astype(f32) for mark in marks], axis=1), ((0, 0), (0, 122)))
    table = jnp.concatenate([cosine, cosine, -sine, sine, marks], axis=1)

    own_conv = jnp.maximum(rank - 4, 0) * 128
    small = []
    for layer in range(layers):
        rows = [conv_x[layer], lax.dynamic_slice_in_dim(conv_bc[layer], own_conv, 128, 1)]
        rows.append(jnp.pad(head_params[layer], ((0, 2), (0, 128 - HLOC))))
        small.append(jnp.pad(jnp.concatenate(rows, axis=1), ((0, 3), (0, 0))))

    def packed(*members):
        width = sum(
            {4: 2 * XLOC}.get(member.ndim, 128 if member.shape[2] in (1024, HLOC) else member.shape[2])
            for member, _ in members
        )
        (columns,) = run_kernel(
            pack_kernel,
            [shape_of((w_query.shape[1], width), bf16)],
            rank.astype(i32).reshape(1),
            *(Layer(member, layer) for member, layer in members),
        )
        return lax.all_gather(columns, ("fsdp", "ctx"), axis=0, tiled=True)

    def proj_members(layer):
        return [(member, layer) for member in (w_zx, w_query, w_dt, w_shared)]

    weight_a = packed(*proj_members(0), (w_attn_out, 0), (w_ssm_out, 0))
    weight_b = packed(*proj_members(1), (w_gate, 0), (w_up, 0), (w_down, 0))
    weight_c = packed((w_gate, 1), (w_up, 1), (w_down, 1), (w_attn_out, 1), (w_ssm_out, 1))
    proj_place = [(weight_a, 0, PROJ), (weight_b, 0, PROJ)]
    out_place = [(weight_a, PROJ, 512), (weight_c, 1536, 512)]
    gate_up_place = [(weight_b, PROJ, 1024), (weight_c, 0, 1024)]
    down_place = [(weight_b, PROJ + 1024, 512), (weight_c, 1024, 512)]

    def together(*values):
        return lax.optimization_barrier(values)

    weight_a, table, seg_rows, small = together(weight_a, table, seg_rows, small)
    normed_shape = shape_of((ROWS, model), bf16)
    normed_kept = kept((ROWS, model), bf16)
    normed_b, inverse1, hidden, dffn_b, grad_hidden = run_kernel(
        first_kernel,
        [normed_kept, kept((SHARE, 128)), kept((SHARE, model)), normed_kept, kept((SHARE, model))],
        flags, inputs, cotangent, gains[0],
    )
    weight_a, normed_b = together(weight_a, normed_b)
    proj_place[0] = (weight_a, 0, PROJ)
    out_place[0] = (weight_a, PROJ, 512)
    dffn_parts = (dffn_b,)
    saved = []
    wide = shape_of((ROWS, 512))
    for layer in range(layers):
        if layer == 0:
            z, xs, query, dtn = first_projections(flags, normed_b, weight_a, table)
        else:
            normed_b, z, xs, query, dtn = run_kernel(
                proj_kernel,
                [normed_shape, shape_of((ROWS, XLOC)), wide, shape_of((ROWS, HD), bf16), shape_of((ROWS, 128))],
                flags, *passed(normed_parts), proj_weight, table,
                scratch=[pltpu.VMEM((ROWS, PROJ), f32)], us=3.3,
            )
        halo = along_ctx(xs[ROWS - 8 :], 1)
        shared_own, shared_ext = run_kernel(
            shared_kernel,
            [shape_of((ROWS, 128), bf16), kept((264, 128))],
            flags, xs, Columns(halo), table, small[layer],
        )
        prepared = run_kernel(
            prep_kernel,
            [
                kept((264, XLOC)), shape_of((ROWS, XLOC)), kept((ROWS, XLOC)), shape_of((ROWS, 256)),
                kept((ROWS, 256)), shape_of((16, ROWS)), kept((16, ROWS)),
            ],
            None, xs, dtn, Columns(halo), table, small[layer], us=1.5,
        )
        rows = stashed(f"proj_{layer}", [z, query, dtn] if layer == 0 else [z, query, dtn, normed_b])
        shared_parts, (prepared, rows) = from_all(shared_own, (prepared, rows))
        z_kept, query_kept, dtn_kept = rows[:3]
        if layer > 0:
            normed_b = rows[3]
        x_ext, xc, xc_kept, rates, rates_kept, rates_t, rates_t_kept = prepared
        message, shared = run_kernel(
            state_kernel, [shape_of((KV + MSG, NSTATE), bf16), shape_of((8 * ROWS, 128), bf16)],
            flags, *passed(shared_parts), xc, rates, rates_t, table, us=1.9,
        )
        earlier = tuple(along_ctx(message, back) for back in (1, 2, 3))
        (intra,) = run_kernel(
            intra_kernel, [shape_of((ROWS, XLOC))],
            flags, shared, xc, rates, rates_t, table, seg_rows, small[layer], us=1.3,
        )
        (shared_kept,) = stashed(f"shared_{layer}", [shared])
        if layer > 0:
            earlier, intra, shared_kept = together(earlier, intra, shared_kept)
        else:
            earlier, intra, shared_kept, out_weight = together(
                earlier, intra, shared_kept, fetched(f"out_{layer}", *out_place[layer])
            )
        halves = [Columns(part, 0, NSTATE, rows=KV) for part in earlier]
        (swapped,) = run_kernel(halves_kernel, [shape_of((3 * KV, NSTATE), bf16)], None, *halves)
        state, ssm_y, gated = run_kernel(
            carry_kernel,
            [shape_of((XLOC, NSTATE)), shape_of((ROWS, XLOC)), shape_of((ROWS, XLOC), bf16)],
            flags, *passed(earlier), shared, rates, table, intra, z, us=1.9,
        )
        swapped, gated = together(other_core(swapped), gated)
        attn, log_total, pairs = run_kernel(
            attention_kernel,
            [shape_of((ROWS, HD), bf16), shape_of((ROWS, HD)), shape_of((SEQ_BLOCKS * ROWS, 2 * HD), bf16)],
            flags, query, shared, *halves, Columns(swapped), table, seg_rows, us=2.0,
        )
        if layer > 0:
            out_weight = fetched(f"out_{layer}", *out_place[layer])
        parts = summed_rows([attn, gated], out_weight)
        rows = stashed(f"mixed_{layer}", [attn, gated, log_total, pairs, state, ssm_y])
        parts, rows = together(parts, rows)
        attn_kept, gated_kept, log_total, pairs, state, ssm_y = rows
        if layer > 0:
            parts, gate_up_weight = together(parts, fetched(f"gate_up_{layer}", *gate_up_place[layer]))
        parts, (rows,) = together(parts, restored(f"hidden_{layer}", [hidden]))
        hidden1, normed2, inverse2 = add_norm(rows, parts, gains[layer, 1])
        rows = stashed(f"rows_{layer}", [hidden1, inverse2])
        if layer > 0:
            normed_parts, (down_weight, rows) = from_all(normed2, (fetched("down_1", *down_place[layer]), rows))
        else:
            normed_parts, rows = from_all(normed2, rows)
            gate_up_weight, down_weight = fetched_all("ffn_0", [gate_up_place[layer], down_place[layer]])
        hidden1, inverse2 = rows
        ffn = run_kernel(
            gate_up_kernel, [normed_shape, wide, wide, shape_of((ROWS, 512), bf16)],
            None, *passed(normed_parts), gate_up_weight, us=2.3,
        )
        if layer + 1 < layers:
            parts = summed_rows([ffn[3]], down_weight)
            parts, ffn, (rows,) = together(parts, stashed("ffn_kept", ffn), restored(f"hidden1_{layer}", [hidden1]))
        normed2_b, gate, up, act_b = ffn
        saved.append(
            (
                hidden, normed_b, inverse1, shared_ext, shared_kept, query_kept, x_ext, xc_kept, z_kept, dtn_kept,
                rates_kept, rates_t_kept, pairs, log_total, state, ssm_y, attn_kept, gated_kept, hidden1, inverse2, normed2_b,
                gate, up, act_b,
            )
        )
        if layer + 1 < layers:
            hidden, next_normed, inverse1 = add_norm(rows, parts, gains[layer + 1, 0])
            normed_parts, (proj_weight, rows) = from_all(
                next_normed,
                (fetched("proj_1", *proj_place[layer + 1]), stashed("rows_next", [hidden, inverse1])),
            )
            hidden, inverse1 = rows

    small_parts = [None] * layers
    inner = None
    for layer in reversed(range(layers)):
        (
            hidden, normed_b, inverse1, shared_ext, shared, query, x_ext, xc, z, dtn, rates, rates_t,
            pairs, log_total, state, ssm_y, attn, gated, hidden1, inverse2, normed2_b, gate, up, act_b,
        ) = saved[layer]
        last = layer == 0
        dffn_b, dgate_up = run_kernel(
            gate_up_back_kernel, [normed_shape, shape_of((ROWS, 1024), bf16)],
            None, *passed(dffn_parts), down_weight, *(map(stored, (gate, up)) if last else (gate, up)), us=2.7,
        )
        parts = summed_rows([dgate_up], gate_up_weight)
        outer = weight_gradients(
            [(normed2_b, dgate_up), (dffn_b, act_b)], 3072 if last else 2560, 1536, 0, inner
        )
        parts, outer = lax.optimization_barrier((parts, outer))
        parts, kept_rows = together(parts, restored(f"norm2_{layer}", [grad_hidden, hidden1, inverse2]))
        grad_mid, dmix, ggain2 = norm_back(parts, *kept_rows, gains[layer, 1])
        dmix_parts = from_all(dmix)
        beside = [grad_mid, ggain2] if last else [grad_mid, ggain2, act_b]
        dmix_parts, (fetch, rows) = from_all(
            dmix,
            (
                fetched_all(
                    f"mixer_{layer}",
                    [out_place[layer]]
                    + [
                        (array, 0, array.shape[1])
                        for array in (z, ssm_y, shared, rates, rates_t, xc, query, pairs, state)
                    ],
                ),
                stashed(f"grads_{layer}", beside),
            ),
        )
        grad_mid, ggain2 = rows[:2]
        if not last:
            last_act = rows[2]
        from_kept = [stored(array) for array in (shared, xc, rates, rates_t, state)]
        out_weight, z, ssm_y, shared, rates, rates_t, xc, query, pairs, state = fetch
        dmix_b, dattn, dy, dz, message = run_kernel(
            gate_back_kernel,
            [
                normed_kept, shape_of((ROWS, HD), bf16), shape_of((ROWS, XLOC)), shape_of((ROWS, XLOC), bf16),
                shape_of((MSG, NSTATE), bf16),
            ],
            flags, *passed(dmix_parts), out_weight, z, ssm_y, shared, rates, rates_t, table, us=2.6,
            scratch=[pltpu.VMEM((ROWS, XLOC), f32), pltpu.VMEM((ROWS, 512), f32)],
        )
        after = tuple(along_ctx(message, -ahead) for ahead in (1, 2, 3))
        early, mine, theirs = run_kernel(
            attention_back_kernel,
            [kept((ROWS, 512), bf16), shape_of((4 * ROWS, HD)), shape_of((4 * ROWS, HD), bf16)],
            flags, dattn, dz, query, pairs, stored(log_total), table, seg_rows, us=2.9,
        )
        got = other_core(theirs)
        dx, dshared, drates, dskip = run_kernel(
            intra_back_kernel,
            [kept((ROWS, XLOC)), kept((ROWS, 2 * NSTATE)), kept((ROWS, 256)), kept((1, XLOC))],
            flags, dy, xc, shared, rates, rates_t, table, seg_rows, state, small[layer], us=3.6,
            scratch=[pltpu.VMEM((128, ROWS), f32), pltpu.VMEM((ROWS, 128), f32)],
        )
        dkv = parts_from(mine, got, along_ctx, -1)
        width = outer.shape[1]
        outer = weight_gradients([(dmix_b, attn), (dmix_b, gated)], width, 512, 3, outer)
        outer = weight_gradients([(normed_b, early)], width, 512, 4, outer)
        if last:
            after, dkv, _, dx, upper = together(after, dkv, outer, dx, upper)
            lower = lax.psum_scatter(outer, ("fsdp", "ctx"), scatter_dimension=0, tiled=True)
        else:
            after, dkv, outer, dx = together(after, dkv, outer, dx)
            upper = lax.psum_scatter(outer, ("fsdp", "ctx"), scatter_dimension=0, tiled=True)
        packed_grads, state_grad = run_kernel(
            packed_back_kernel, [shape_of((8 * ROWS, 128), bf16), kept((XLOC, NSTATE))],
            flags, *map(stored, after), *from_kept[:3], table, stored(dshared), *map(stored, dkv), us=2.5,
        )
        dshared_parts = parts_of_sum(packed_grads[: 4 * ROWS], packed_grads[4 * ROWS :], along_y, 1)
        dxpre, edge_x, gconv_x, ddt, gheads = run_kernel(
            state_back_kernel,
            [kept((ROWS, XLOC)), shape_of((8, XLOC)), kept((8, XLOC)), kept((ROWS, 128)), kept((8, 128))],
            flags, stored(state_grad), *from_kept[:4], table, from_kept[4], stored(small[layer]),
            stored(dtn), stored(dx), stored(drates), stored(x_ext),
            scratch=[pltpu.VMEM((272, XLOC), f32), pltpu.VMEM((ROWS, XLOC), f32), pltpu.VMEM((ROWS, 128), f32)],
            us=3.5,
        )
        dshared_parts, edge_x = together(dshared_parts, edge_x)
        edge_x = along_ctx(edge_x, -1)
        dsh, edge_sh, gconv_sh = run_kernel(
            shared_back_kernel,
            [shape_of((ROWS, 128)), shape_of((8, 128)), kept((8, 128))],
            flags, *summands(dshared_parts), stored(shared_ext), table, small[layer],
            scratch=[pltpu.VMEM((272, 128), f32)],
        )
        edge_sh, proj_weight = together(
            along_ctx(edge_sh, -1), fetched(f"proj_again_{layer}", *proj_place[layer])
        )
        (late,) = run_kernel(
            late_kernel, [shape_of((ROWS, LATE), bf16)], flags, stored(dxpre), Columns(edge_x), dsh,
            Columns(edge_sh), stored(ddt),
        )
        parts = summed_rows([early, late], proj_weight)
        if not last:
            inner = weight_gradients([(normed_b, Columns(late, 0, 512))], 3072, 512, 5)
            parts, inner = together(parts, inner)
            upper_pair = (normed_b, Columns(late, 4, 128))
        else:
            parts, owned = together(parts, owned_gradients([(normed_b, late), upper_pair]))
        parts, kept_rows = together(parts, restored(f"norm1_{layer}", [grad_mid, hidden, inverse1]))
        grad_hidden, rounded, ggain1 = norm_back(parts, *kept_rows, gains[layer, 0])
        if last:
            dffn_parts = from_all(rounded)
        else:
            dffn_parts, ((down_weight, gate_up_weight), (grad_hidden, ggain1)) = from_all(
                rounded,
                (
                    fetched_all("ffn_again", [down_place[layer - 1], gate_up_place[layer - 1]]),
                    stashed("grads_next", [grad_hidden, ggain1]),
                ),
            )
            last_hidden1 = hidden1
        (small_parts[layer],) = run_kernel(
            small_kernel, [shape_of((64, 128), bf16)],
            None, ggain1, *map(stored, (ggain2, gconv_sh, gconv_x, gheads, dskip)),
        )
    (small_all,) = run_kernel(
        spread_kernel, [shape_of((128, 128), bf16)], None, jnp.concatenate(small_parts, axis=0),
        scratch=[pltpu.VMEM((128, 128), f32)],
    )
    owned = lax.all_to_all(with_small(owned, small_all), ("fsdp", "ctx"), 0, 0, tiled=True)
    (input_grad,) = run_kernel(natural_kernel, [kept((ROWS, model))], flags, *passed(dffn_parts))
    last_act, down_weight, _ = together(last_act, fetched("down_last", *down_place[1]), small_parts[0])
    (layer_out,) = run_kernel(
        output_kernel, [shape_of((SHARE, model), bf16)], None,
        stored(last_hidden1), *summands(summed_rows([last_act], down_weight)),
    )
    (layer_out,) = run_kernel(natural_kernel, [normed_kept], flags, *passed(from_all(layer_out)))
    def pair_of(width):
        return shape_of((layers, model // 16, width))

    owned, layer_out, input_grad = together(owned, layer_out, input_grad)
    over_tp, late_sum, gconv_x, gheads = run_kernel(
        block_sum_kernel,
        [
            shape_of((352, 128), bf16), kept((model // 16, LATE)), shape_of((layers * (CONV + 1), XLOC)),
            shape_of((8, 128)),
        ],
        None, Columns(owned),
        scratch=[pltpu.VMEM((128, 128), f32)],
    )
    grad_shared, ggains1, ggains2, gconv_bc = run_kernel(
        tp_outputs_kernel,
        [
            pair_of(1024), shape_of((layers, model)), shape_of((layers, model)),
            shape_of((layers * (CONV + 1), 512)),
        ],
        flags, *passed(from_all(over_tp)),
        scratch=[pltpu.VMEM((8, 352, 128), f32)], us=2.0,
    )
    lower, grad_shared = together(lower, grad_shared)
    grad_attn, grad_ssm, grad_gate, grad_up, grad_down, grad_query, grad_zx, grad_dt = run_kernel(
        weight_outputs_kernel,
        [
            *(kept((layers, model // 16, width)) for width in (128, 384, 512, 512, 512, 128)),
            shape_of((layers, model // 16, 2, XLOC)), pair_of(HLOC),
        ],
        None, stored(lower), stored(upper), stored(late_sum), us=3.0,
    )
    gconv_x = gconv_x.reshape(layers, CONV + 1, XLOC)
    gconv_bc = gconv_bc.reshape(layers, CONV + 1, 512)
    gheads = gheads[: 3 * layers].reshape(layers, 3, 128)[:, :, :HLOC]
    return (
        layer_out[None],
        input_grad[None],
        grad_query,
        grad_shared,
        grad_zx,
        grad_dt,
        grad_attn,
        grad_ssm,
        grad_gate,
        grad_up,
        grad_down,
        ggains1,
        gconv_x,
        gconv_bc,
        gheads[:, :2],
        ggains2,
        gheads[:, 2],
    )


def solution(mesh):
    columns = P(None, ("fsdp", "ctx"), "tp")
    rows = P("fsdp", "ctx", None)
    return jax.shard_map(
        body,
        mesh=mesh,
        in_specs=(
            rows, rows, P("fsdp", None), columns, P(None, ("fsdp", "ctx"), None),
            P(None, ("fsdp", "ctx"), None, "tp"), columns, columns, columns, columns, columns, columns,
            P(), P(None, None, "tp"), P(), P(None, None, "tp"),
        ),
        out_specs=(
            rows, rows, columns, P(None, ("fsdp", "ctx"), None), P(None, ("fsdp", "ctx"), None, "tp"),
            columns, columns, columns, columns, columns, columns,
            P(), P(None, None, "tp"), P(), P(None, None, "tp"), P(), P(None, "tp"),
        ),
        check_vma=False,
    )
```

```python
import math
from functools import partial

import jax
import jax.numpy as jnp
from jax import lax
from jax.experimental import pallas as pl
from jax.experimental.pallas import tpu as pltpu
from jax.sharding import PartitionSpec as P

HD = 128
HP = 64
NSTATE = 256
CONV = 4
ROWS = 256
SHARE = 32
XLOC = 384
PROJ = 1152
LATE = 640
HLOC = 6
PAIRS = 3
SEQ_BLOCKS = 4
MSG = XLOC + 16
KV = 128
VMEM_LIMIT = 16 * 1024 * 1024

norm_eps = 1e-05
rope_base = 100000000000.0
bf16 = jnp.bfloat16
f32 = jnp.float32
i32 = jnp.int32


def along_y(value, steps):
    pairs = [(i, ((i // 2 + steps) % 4) * 2 + i % 2) for i in range(8)]
    return lax.ppermute(value, "tp", pairs)


def other_core(value):
    return lax.ppermute(value, "tp", [(i, i ^ 1) for i in range(8)])


def along_ctx(value, steps):
    first, last = max(0, -steps), min(4, 4 - steps)
    return lax.ppermute(value, "ctx", [(i, i + steps) for i in range(first, last)])


def ring(value, axis, steps):
    return lax.ppermute(value, axis, [(i, (i + steps) % 4) for i in range(4)])


def from_all(value, beside=None):
    half = [value] + [along_y(value, -k) for k in (1, 2, 3)]
    if beside is not None:
        half[1], beside = lax.optimization_barrier((half[1], beside))
    parts = tuple(half + [other_core(part) for part in half])
    return parts if beside is None else (parts, beside)


def dot_nn(a, b):
    return jnp.dot(a, b, preferred_element_type=f32)


def dot_nt(a, b):
    return lax.dot_general(a, b, (((1,), (1,)), ((), ())), preferred_element_type=f32)


def dot_tn(a, b):
    return lax.dot_general(a, b, (((0,), (0,)), ((), ())), preferred_element_type=f32)


def shape_of(shape, dtype=f32):
    return jax.ShapeDtypeStruct(shape, dtype)


class Columns:
    def __init__(self, array, block=0, width=None, rows=None, keep=False):
        self.array, self.block, self.keep = array, block, keep
        self.shape = (rows or array.shape[0],) + array.shape[1:-1] + (width or array.shape[-1],)

    def spec(self):
        place = (0,) * (len(self.shape) - 1) + (self.block,)
        return pl.BlockSpec(self.shape, lambda i: place, pipeline_mode=pl.Buffered(1))


class Layer:
    def __init__(self, array, layer):
        self.array, self.layer, self.keep = array, layer, True
        self.shape = (1,) + array.shape[1:]

    def spec(self):
        place = (self.layer,) + (0,) * (len(self.shape) - 1)
        return pl.BlockSpec(self.shape, lambda i: place, pipeline_mode=pl.Buffered(1))


def stored(array):
    return Columns(array, keep=True)


def summands(parts):
    return [stored(parts[0])] + passed(parts[1:])


def passed(arrays):
    return [Columns(array) for array in arrays]


def kept(shape, dtype=f32):
    return pltpu.HBM(shape, dtype)


def fetch_kernel(places, *refs):
    count = len(places)
    sources, outs, sems = refs[:count], refs[count : 2 * count], refs[-1]
    copies = []
    for (start, pieces), source, out in zip(places, sources, outs):
        rows, width = out.shape[0] // pieces, out.shape[1]
        for index in range(pieces):
            own = pl.ds(rows * index, rows)
            copies.append(
                pltpu.make_async_copy(
                    source.at[own, pl.ds(start, width)], out.at[own, :], sems.at[len(copies)]
                )
            )
    for copy in copies:
        copy.start()
    for copy in copies:
        copy.wait()


def fetched_all(name, sources):
    places = [(start, 4 if array.shape[0] == 2048 and width > 128 else 1) for array, start, width in sources]
    whole = pl.BlockSpec(memory_space=pltpu.VMEM)
    return pl.pallas_call(
        partial(fetch_kernel, places),
        name=name,
        out_shape=tuple(pltpu.VMEM((array.shape[0], width), array.dtype) for array, _, width in sources),
        in_specs=[pl.BlockSpec(memory_space=pltpu.HBM)] * len(sources),
        out_specs=tuple(whole for _ in sources),
        scratch_shapes=[pltpu.SemaphoreType.DMA((sum(pieces for _, pieces in places),))],
        compiler_params=pltpu.CompilerParams(vmem_limit_bytes=VMEM_LIMIT),
        cost_estimate=pl.CostEstimate(
            flops=0, bytes_accessed=sum(2 * array.shape[0] * width for array, _, width in sources), transcendentals=0
        ),
    )(*(pltpu.with_memory_space_constraint(array, pltpu.HBM) for array, _, _ in sources))


def fetched(name, array, start, width):
    return fetched_all(name, [(array, start, width)])[0]


def restored(name, arrays):
    return fetched_all(name, [(array, 0, array.shape[1]) for array in arrays])


def stash_kernel(*refs):
    count = len(refs) // 2
    sems = refs[-1]
    copies = [pltpu.make_async_copy(refs[k], refs[count + k], sems.at[k]) for k in range(count)]
    for copy in copies:
        copy.start()
    for copy in copies:
        copy.wait()


def stashed(name, arrays):
    return pl.pallas_call(
        stash_kernel,
        name=name,
        out_shape=tuple(pltpu.HBM(array.shape, array.dtype) for array in arrays),
        in_specs=[pl.BlockSpec(memory_space=pltpu.VMEM)] * len(arrays),
        out_specs=tuple(pl.BlockSpec(memory_space=pltpu.HBM) for _ in arrays),
        scratch_shapes=[pltpu.SemaphoreType.DMA((len(arrays),))],
        compiler_params=pltpu.CompilerParams(vmem_limit_bytes=VMEM_LIMIT),
        cost_estimate=pl.CostEstimate(flops=10**9, bytes_accessed=10**6, transcendentals=0),
    )(*arrays)


def run_kernel(kernel, outs, flags, *args, scratch=(), us=1.0):
    whole = pl.BlockSpec(memory_space=pltpu.VMEM)
    own = [isinstance(arg, (Columns, Layer)) for arg in args]
    specs, arrays, out_specs = [], [], []
    for arg, copied in zip(args, own):
        specs.append(arg.spec() if copied else whole)
        array = arg.array if copied else arg
        arrays.append(pltpu.with_memory_space_constraint(array, pltpu.HBM) if copied and arg.keep else array)
    for out in outs:
        in_vmem = isinstance(out, jax.ShapeDtypeStruct)
        out_specs.append(whole if in_vmem else pl.BlockSpec(out.shape, lambda i, n=len(out.shape): (0,) * n))
        own.append(not in_vmem)
    moved = sum(2 * math.prod(arg.shape) for arg in args) + sum(2 * math.prod(o.shape) for o in outs)
    if flags is not None:
        specs = [pl.BlockSpec(memory_space=pltpu.SMEM)] + specs
        arrays = [flags] + arrays
    return pl.pallas_call(
        kernel,
        grid=(1,) if any(own) else (),
        out_shape=tuple(outs),
        in_specs=specs,
        out_specs=tuple(out_specs),
        scratch_shapes=list(scratch),
        compiler_params=pltpu.CompilerParams(vmem_limit_bytes=VMEM_LIMIT),
        cost_estimate=pl.CostEstimate(flops=int(us * 1e9), bytes_accessed=moved, transcendentals=0),
    )(*arrays)


def local_block(flags, natural):
    return pl.multiple_of(flags[8 + natural] * SHARE, SHARE)


def rank_block(flags, rank):
    return pl.multiple_of(flags[16 + rank] * ROWS, ROWS)


def lane_index(shape):
    return lax.broadcasted_iota(i32, shape, len(shape) - 1)


def spread(columns, pair):
    low = lane_index((1, 128)) < HP
    return jnp.where(low, columns[:, 2 * pair : 2 * pair + 1], columns[:, 2 * pair + 1 : 2 * pair + 2])


def lanes_of(pair):
    return slice(128 * pair, 128 * pair + 128)


def turned(value, table, sign):
    return value * table[:, 0:128] + sign * (pltpu.roll(value, 64, 1) * table[:, 128:256])


def segments(table):
    return table[:, 259:260]


def sigmoid(v):
    return 1.0 / (1.0 + jnp.exp(-v))


def softplus(v):
    return jnp.maximum(v, 0.0) + jnp.log1p(jnp.exp(-jnp.abs(v)))


def conv_sum(ext, table, weight):
    total = weight[CONV : CONV + 1, :] + ext[8 : 8 + ROWS, :] * weight[3:4, :]
    for tap in range(CONV - 1):
        total = total + table[:, 256 + tap : 257 + tap] * ext[5 + tap : 5 + tap + ROWS, :] * weight[tap : tap + 1, :]
    return total


def conv_back(grad_out, ext, table, weight, work, grad_ref, edge_ref, gweight_ref):
    total = conv_sum(ext, table, weight)
    sig = sigmoid(total)
    grad = grad_out * sig * (1.0 + total * (1.0 - sig))
    width = grad.shape[1]
    gweight_ref[...] = jnp.zeros((8, width), f32)
    gweight_ref[CONV : CONV + 1, :] = jnp.sum(grad, axis=0, keepdims=True)
    gweight_ref[3:4, :] = jnp.sum(grad * ext[8 : 8 + ROWS, :], axis=0, keepdims=True)
    work[0:8, :] = jnp.zeros((8, width), f32)
    work[264:272, :] = jnp.zeros((8, width), f32)
    own = grad * weight[3:4, :]
    edge = jnp.zeros((8, width), f32)
    for tap in range(CONV - 1):
        part = grad * table[:, 256 + tap : 257 + tap]
        gweight_ref[tap : tap + 1, :] = jnp.sum(
            part * ext[5 + tap : 5 + tap + ROWS, :], axis=0, keepdims=True
        )
        work[8:264, :] = part * weight[tap : tap + 1, :]
        own = own + work[11 - tap : 11 - tap + ROWS, :]
        edge = edge + work[3 - tap : 11 - tap, :]
    grad_ref[...] = own
    edge_ref[...] = edge


def pack_kernel(place, *refs):
    out, at, index = refs[-1], 0, 0
    while index < len(refs) - 1:
        ref = refs[index]
        if len(ref.shape) == 4:
            out[:, at : at + XLOC] = ref[0, :, 0, :]
            out[:, at + XLOC : at + 512] = refs[index + 1][0]
            out[:, at + 512 : at + 896] = ref[0, :, 1, :]
            at, index = at + 896, index + 2
            continue
        width = min(ref.shape[2], 512)
        if width == HLOC:
            out[:, at : at + 128] = jnp.zeros((out.shape[0], 128), bf16)
            out[:, at : at + HLOC] = ref[0]
            width = 128
        elif ref.shape[2] == 1024:
            width = 128
            out[:, at : at + width] = ref[0, :, pl.ds(pl.multiple_of(place[0] * 128, 128), 128)]
        else:
            out[:, at : at + width] = ref[0]
        at, index = at + width, index + 1


def first_kernel(flags, rows, cotangent, gain, normed, inverse, hidden_kept, grads, grad):
    for block in range(8):
        own = slice(SHARE * block, SHARE * (block + 1))
        from_rows = pl.ds(pl.multiple_of(flags[24 + block] * SHARE, SHARE), SHARE)
        wide = rows[0, from_rows, :].astype(f32)
        scale = lax.rsqrt(jnp.mean(wide * wide, axis=1, keepdims=True) + norm_eps)
        normed[own, :] = (wide * scale * gain[0:1, :]).astype(bf16)
        grads[own, :] = cotangent[0, from_rows, :]
        if block == 0:
            hidden_kept[...] = wide
            inverse[...] = jnp.broadcast_to(scale, inverse.shape)
            grad[...] = cotangent[0, from_rows, :].astype(f32)


def joined(parts):
    return parts[0][...] if len(parts) == 1 else jnp.concatenate([part[...] for part in parts], axis=0)


def projections(flags, work, table, z, xs, query, dtn):
    for block in range(8):
        own = slice(SHARE * block, SHARE * (block + 1))
        from_rows = pl.ds(local_block(flags, block), SHARE)
        z[own, :] = work[from_rows, 0:XLOC]
        xs[own, 0:XLOC] = work[from_rows, 512:896]
        xs[own, XLOC:512] = work[from_rows, 1024:PROJ]
        query[own, :] = turned(work[from_rows, XLOC:512], table[own, :], 1.0).astype(bf16)
        dtn[own, :] = work[from_rows, 896:1024]


def proj_kernel(flags, p0, p1, p2, p3, p4, p5, p6, p7, weight, table, normed, *refs):
    rows = joined((p0, p1, p2, p3, p4, p5, p6, p7))
    normed[...] = rows
    work = refs[-1]
    work[...] = dot_nn(rows, weight[...])
    projections(flags, work, table, *refs[:-1])


def first_proj_kernel(flags, rows, weight, table, z, xs, query, dtn, work):
    step = pl.program_id(0)
    part = dot_nn(rows[...], weight[...])

    @pl.when(step == 0)
    def _():
        work[...] = part

    @pl.when(step > 0)
    def _():
        work[...] = work[...] + part

    @pl.when(step == 3)
    def _():
        projections(flags, work, table, z, xs, query, dtn)


def first_projections(flags, normed, weight, table):
    model = normed.shape[1]
    whole = pl.BlockSpec(memory_space=pltpu.VMEM)
    outs = [shape_of((ROWS, XLOC)), shape_of((ROWS, 512)), shape_of((ROWS, HD), bf16), shape_of((ROWS, 128))]
    return pl.pallas_call(
        first_proj_kernel,
        grid=(4,),
        out_shape=tuple(outs),
        in_specs=[
            pl.BlockSpec(memory_space=pltpu.SMEM),
            pl.BlockSpec((ROWS, model // 4), lambda i: (0, i)),
            pl.BlockSpec((model // 4, PROJ), lambda i: (i, 0)),
            whole,
        ],
        out_specs=tuple(
            whole if isinstance(out, jax.ShapeDtypeStruct) else pl.BlockSpec(out.shape, lambda i: (0, 0))
            for out in outs
        ),
        scratch_shapes=[pltpu.VMEM((ROWS, PROJ), f32)],
        compiler_params=pltpu.CompilerParams(vmem_limit_bytes=VMEM_LIMIT),
        cost_estimate=pl.CostEstimate(flops=4 * 10**9, bytes_accessed=2 * model * PROJ, transcendentals=0),
    )(flags, normed, pltpu.with_memory_space_constraint(weight, pltpu.HBM), table)


def shared_kernel(flags, xs, halo, table, small, out, ext):
    own = xs[:, XLOC:512]
    ext[0:8, :] = halo[:, XLOC:512]
    ext[8 : 8 + ROWS, :] = own
    total = conv_sum(ext, table, small[:, XLOC:512])
    rank = flags[0]
    out[...] = jnp.where(
        rank < 2, turned(own, table, 1.0), jnp.where(rank < 4, own, total * sigmoid(total))
    ).astype(bf16)


def prep_kernel(xs, dtn, halo, table, small, ext, xc, xc_kept, rates, rates_kept, rates_t, rates_t_kept):
    ext[0:8, :] = halo[:, 0:XLOC]
    ext[8 : 8 + ROWS, :] = xs[:, 0:XLOC]
    total = conv_sum(ext, table, small[:, 0:XLOC])
    for out in (xc, xc_kept):
        out[...] = total * sigmoid(total)
    params = small[:, 512:640]
    rate = softplus(dtn[...] + params[1:2, :])
    logs = -jnp.exp(params[0:1, :]) * rate
    rows = lax.broadcasted_iota(i32, (ROWS, ROWS), 0)
    lower = (rows >= lane_index((ROWS, ROWS))).astype(f32)
    running = jnp.dot(lower, logs, precision=lax.Precision.HIGHEST, preferred_element_type=f32)
    for out in (rates, rates_kept):
        out[:, 0:128] = rate
        out[:, 128:256] = running
    rate_t, running_t = rate.T[0:8, :], running.T[0:8, :]
    for out in (rates_t, rates_t_kept):
        out[0:8, :] = rate_t
        out[8:16, :] = running_t


def block_decays(flags, rates_t):
    kept = jnp.where(flags[4] == flags[5], 1.0, 0.0)
    return jnp.exp(rates_t[8:16, ROWS - 1 : ROWS]) * kept


def decay_rows(flags, rates_t):
    rows = jnp.broadcast_to(block_decays(flags, rates_t), (8, NSTATE))
    return jnp.concatenate([rows, jnp.zeros((8, NSTATE), f32)], axis=0).astype(bf16)


def weights_in(rates, table):
    last = rates[ROWS - 1 : ROWS, 128:256]
    gap = jnp.exp(last - rates[:, 128:256]) * table[:, 261:262]
    return gap, gap * rates[:, 0:128]


def rank_columns(flags, shared, first):
    return jnp.concatenate(
        [shared[pl.ds(rank_block(flags, rank), ROWS), :] for rank in (first, first + 1)], axis=1
    )


def inject_of(flags, shared):
    return rank_columns(flags, shared, 4)


def readout_of(flags, shared):
    return rank_columns(flags, shared, 6)


def carry_of(rates, table):
    return jnp.exp(rates[:, 128:256]) * table[:, 260:261]


def state_kernel(flags, s0, s1, s2, s3, s4, s5, s6, s7, xc, rates, rates_t, table, out, shared):
    for index, part in enumerate((s0, s1, s2, s3, s4, s5, s6, s7)):
        shared[ROWS * index : ROWS * (index + 1), :] = part[...]
    inject = inject_of(flags, shared)
    _, weight = weights_in(rates, table)
    for pair in range(PAIRS):
        weighted = (xc[:, lanes_of(pair)] * spread(weight, pair)).astype(bf16)
        out[KV + 128 * pair : KV + 128 * (pair + 1), :] = dot_tn(weighted, inject).astype(bf16)
    out[KV + XLOC : KV + MSG, :] = decay_rows(flags, rates_t)
    half = shared[pl.ds(rank_block(flags, 2 * flags[2] + flags[1] // 2), ROWS), :]
    out[0:KV, :] = jnp.concatenate([half[0:128], half[128:256]], axis=1)


def halves_kernel(msg1, msg2, msg3, out):
    for index, msg in enumerate((msg1, msg2, msg3)):
        out[KV * index : KV * (index + 1), :] = msg[...]


def allowed_pairs(table, seg_rows):
    rows = lax.broadcasted_iota(i32, (ROWS, ROWS), 0)
    return (rows >= lane_index((ROWS, ROWS))) & (segments(table) == seg_rows[0:1, :])


def head_decay(allowed, rates, rates_t, head):
    gap = rates[:, 128 + head : 129 + head] - rates_t[8 + head : 9 + head, :]
    return jnp.where(allowed, jnp.exp(jnp.where(allowed, gap, 0.0)), 0.0)


def intra_kernel(flags, shared, xc, rates, rates_t, table, seg_rows, small, out):
    inject, readout = inject_of(flags, shared), readout_of(flags, shared)
    both = dot_nt(readout, inject)
    allowed = allowed_pairs(table, seg_rows)
    low = lane_index((1, 128)) < HP
    for pair in range(PAIRS):
        x = xc[:, lanes_of(pair)]
        xb = x.astype(bf16)
        heads = []
        for head in (2 * pair, 2 * pair + 1):
            decay = head_decay(allowed, rates, rates_t, head)
            heads.append(dot_nn((both * decay * rates_t[head : head + 1, :]).astype(bf16), xb))
        out[:, lanes_of(pair)] = jnp.where(low, heads[0], heads[1]) + spread(small[2:3, 512:640], pair) * x


def keys_values(flags, shared, halves, swapped):
    head, first = flags[1] // 2, flags[2] == 0
    pairs = [
        (
            shared[pl.ds(rank_block(flags, head), ROWS), :],
            shared[pl.ds(rank_block(flags, 2 + head), ROWS), :],
        )
    ]
    for index, half in enumerate(halves):
        packed = half[...], swapped[KV * index : KV * (index + 1), :]
        mine, theirs = (jnp.concatenate([part[:, 0:128], part[:, 128:256]], axis=0) for part in packed)
        pairs.append((jnp.where(first, mine, theirs), jnp.where(first, theirs, mine)))
    return pairs


def masked_scores(query, pairs, table, seg_rows):
    parts = []
    for block, (keys, _) in enumerate(pairs):
        score = dot_nt(query, keys) * HD ** (-0.5)
        keep = segments(table) == seg_rows[block : block + 1, :]
        if block == 0:
            rows = lax.broadcasted_iota(i32, (ROWS, ROWS), 0)
            keep = keep & (rows >= lane_index((ROWS, ROWS)))
        parts.append(jnp.where(keep, score, -1e30))
    return parts


def attention_kernel(flags, query, shared, h1, h2, h3, swapped, table, seg_rows, out, log_total, kept):
    pairs = keys_values(flags, shared, (h1, h2, h3), swapped)
    for block, (keys, values) in enumerate(pairs):
        kept[ROWS * block : ROWS * (block + 1), 0:HD] = keys
        kept[ROWS * block : ROWS * (block + 1), HD : 2 * HD] = values
    parts = masked_scores(query[...], pairs, table, seg_rows)
    top = parts[0].max(axis=1, keepdims=True)
    for part in parts[1:]:
        top = jnp.maximum(top, part.max(axis=1, keepdims=True))
    parts = [jnp.exp(part - top) for part in parts]
    total = sum(part.sum(axis=1, keepdims=True) for part in parts)
    inverse = 1.0 / total
    result = jnp.zeros((ROWS, HD), f32)
    for part, (_, values) in zip(parts, pairs):
        result = result + dot_nn((part * inverse).astype(bf16), values)
    rounded = result.astype(bf16)
    for block in range(8):
        out[pl.ds(local_block(flags, block), SHARE), :] = rounded[SHARE * block : SHARE * (block + 1), :]
    log_total[...] = jnp.broadcast_to(top + jnp.log(total), (ROWS, HD))


def chained(first, second, third, base):
    rows1 = first[base + XLOC : base + MSG, :].astype(f32)
    rows2 = second[base + XLOC : base + MSG, :].astype(f32)
    parts = []
    for head in range(HLOC):
        own = slice(base + HP * head, base + HP * head + HP)
        older = second[own, :].astype(f32) + rows2[head : head + 1, :] * third[own, :].astype(f32)
        parts.append(first[own, :].astype(f32) + rows1[head : head + 1, :] * older)
    return jnp.concatenate(parts, axis=0)


def carry_kernel(flags, msg1, msg2, msg3, shared, rates, table, intra, z, state, ssm_y, cat):
    entering = chained(msg1, msg2, msg3, KV)
    state[...] = entering
    from_state = dot_nt(readout_of(flags, shared), entering.astype(bf16))
    carry = carry_of(rates, table)
    for pair in range(PAIRS):
        own = lanes_of(pair)
        y = intra[:, own] + spread(carry, pair) * from_state[:, own]
        ssm_y[:, own] = y
        gate = z[:, own]
        gated = (y * gate * sigmoid(gate)).astype(bf16)
        for block in range(8):
            cat[pl.ds(local_block(flags, block), SHARE), 128 * pair : 128 * (pair + 1)] = gated[
                SHARE * block : SHARE * (block + 1), :
            ]


def gate_back_kernel(
    flags, p0, p1, p2, p3, p4, p5, p6, p7, weight, z, ssm_y, shared, rates, rates_t, table,
    dmix, dattn, dy, dz, msg, work, local,
):
    rows = joined((p0, p1, p2, p3, p4, p5, p6, p7))
    dmix[...] = rows
    local[...] = dot_nn(rows, weight[...])
    for block in range(8):
        own = slice(SHARE * block, SHARE * (block + 1))
        from_rows = pl.ds(local_block(flags, block), SHARE)
        dattn[own, :] = local[from_rows, 0:128].astype(bf16)
        work[own, :] = local[from_rows, 128:512]
    readout = readout_of(flags, shared)
    carry = carry_of(rates, table)
    for pair in range(PAIRS):
        own = lanes_of(pair)
        gate, grad = z[:, own], work[:, own]
        sig = sigmoid(gate)
        y_grad = grad * gate * sig
        dy[:, own] = y_grad
        dz[:, own] = (grad * ssm_y[:, own] * sig * (1.0 + gate * (1.0 - sig))).astype(bf16)
        msg[own, :] = dot_tn((y_grad * spread(carry, pair)).astype(bf16), readout).astype(bf16)
    msg[XLOC:MSG, :] = decay_rows(flags, rates_t)


def attention_back_kernel(
    flags, dattn, dz, query, kept, log_total, table, seg_rows,
    early, mine, theirs,
):
    pairs = []
    for block in range(SEQ_BLOCKS):
        own = slice(ROWS * block, ROWS * (block + 1))
        pairs.append((kept[own, 0:HD], kept[own, HD : 2 * HD]))
    first = flags[2] == 0
    q = query[...]
    grad = dattn[...]
    parts = masked_scores(q, pairs, table, seg_rows)
    logs = log_total[:, 0:1]
    probs = [jnp.exp(part - logs) for part in parts]
    grads = [dot_nt(grad, values) for _, values in pairs]
    inner = sum((p * g).sum(axis=1, keepdims=True) for p, g in zip(probs, grads))
    total = jnp.zeros((ROWS, HD), f32)
    for block, (p, g, (keys, _)) in enumerate(zip(probs, grads, pairs)):
        own = slice(ROWS * block, ROWS * (block + 1))
        score = (p * (g - inner)).astype(bf16)
        total = total + dot_nn(score, keys)
        dkeys = dot_tn(score, q) * HD ** (-0.5)
        dvalues = dot_tn(p.astype(bf16), grad)
        mine[own, :] = jnp.where(first, dkeys, dvalues)
        theirs[own, :] = jnp.where(first, dvalues, dkeys).astype(bf16)
    total = total * HD ** (-0.5)
    dq = turned(total, table, -1.0).astype(bf16)
    for block in range(8):
        own = slice(SHARE * block, SHARE * (block + 1))
        to_rows = pl.ds(local_block(flags, block), SHARE)
        early[to_rows, 0:XLOC] = dz[own, :]
        early[to_rows, XLOC:512] = dq[own, :]


def intra_back_kernel(
    flags, dy, xc, shared, rates, rates_t, table, seg_rows, state, small,
    dx, dshared, drates, dskip, row_sums, dcum,
):
    inject, readout = inject_of(flags, shared), readout_of(flags, shared)
    both = dot_nt(readout, inject)
    allowed = allowed_pairs(table, seg_rows)
    low = lane_index((1, 128)) < HP
    carry = carry_of(rates, table)
    entering = state[...].astype(bf16)
    from_state = dot_nt(readout, entering)
    dboth = jnp.zeros((ROWS, ROWS), f32)
    row_sums[...] = jnp.zeros((128, ROWS), f32)
    dcum[...] = jnp.zeros((ROWS, 128), f32)
    carried = []
    for pair in range(PAIRS):
        own = lanes_of(pair)
        x = xc[:, own]
        xb = x.astype(bf16)
        grad = dy[:, own]
        dskip[:, own] = jnp.sum(grad * x, axis=0, keepdims=True)
        carried.append((grad * spread(carry, pair)).astype(bf16))
        through = grad * from_state[:, own]
        total = spread(small[2:3, 512:640], pair) * grad
        for head in (2 * pair, 2 * pair + 1):
            mine = low if head % 2 == 0 else jnp.logical_not(low)
            decay = head_decay(allowed, rates, rates_t, head)
            steps = rates_t[head : head + 1, :]
            head_grad = jnp.where(mine, grad, 0.0).astype(bf16)
            dmix = dot_nt(head_grad, xb)
            kept = dmix * decay
            dboth = dboth + kept * steps
            mixed = both * decay
            total = total + dot_tn((mixed * steps).astype(bf16), head_grad)
            passed = dmix * mixed
            row_sums[head : head + 1, :] = jnp.sum(passed, axis=0, keepdims=True)
            dcum[:, head : head + 1] = jnp.sum(passed * steps, axis=1, keepdims=True) + carry[
                :, head : head + 1
            ] * jnp.sum(jnp.where(mine, through, 0.0), axis=1, keepdims=True)
        dx[:, own] = total
    columns = row_sums[...].T
    drates[:, 0:128] = columns
    drates[:, 128:256] = dcum[...] - rates[:, 0:128] * columns
    dboth_b = dboth.astype(bf16)
    dshared[:, NSTATE:] = dot_nn(dboth_b, inject) + dot_nn(jnp.concatenate(carried, axis=1), entering)
    dshared[:, 0:NSTATE] = dot_tn(dboth_b, readout)


def packed_back_kernel(
    flags, msg1, msg2, msg3, shared, xc, rates, table, dshared, kv0, kv1, kv2, kv3, packed, state_grad,
):
    later = chained(msg1, msg2, msg3, 0)
    state_grad[...] = later
    _, weights = weights_in(rates, table)
    weighted = [(xc[:, lanes_of(pair)] * spread(weights, pair)).astype(bf16) for pair in range(PAIRS)]
    weighted = jnp.concatenate(weighted, axis=1)
    dinject = (dshared[:, 0:NSTATE] + dot_nn(weighted, later.astype(bf16))).astype(bf16)
    dreadout = dshared[:, NSTATE:].astype(bf16)
    packed[...] = jnp.zeros((8 * ROWS, 128), bf16)
    grads = kv0[...] + kv1[...].astype(f32) + kv2[...].astype(f32) + kv3[...].astype(f32)
    owner = 2 * flags[2] + flags[1] // 2
    packed[pl.ds(rank_block(flags, owner), ROWS), :] = grads.astype(bf16)
    packed[pl.ds(rank_block(flags, 4), ROWS), :] = dinject[:, 0:128]
    packed[pl.ds(rank_block(flags, 5), ROWS), :] = dinject[:, 128:256]
    packed[pl.ds(rank_block(flags, 6), ROWS), :] = dreadout[:, 0:128]
    packed[pl.ds(rank_block(flags, 7), ROWS), :] = dreadout[:, 128:256]


def state_back_kernel(
    flags, later, shared, xc, rates, rates_t, table, state, small, dtn, dx, drates, ext,
    dxpre, edge, gweight, ddt, heads, work, dconv, sums,
):
    inject = inject_of(flags, shared)
    low = lane_index((1, 128)) < HP
    params = small[:, 512:640]
    gap, weights = weights_in(rates, table)
    from_later = dot_nt(inject, later[...].astype(bf16))
    products = later[...] * state[...]
    decays = block_decays(flags, rates_t)
    sums[...] = jnp.zeros((ROWS, 128), f32)
    for pair in range(PAIRS):
        own = lanes_of(pair)
        dconv[:, own] = dx[:, own] + spread(weights, pair) * from_later[:, own]
        through = xc[:, own] * from_later[:, own]
        for head in (2 * pair, 2 * pair + 1):
            mine = low if head % 2 == 0 else jnp.logical_not(low)
            sums[:, head : head + 1] = jnp.sum(jnp.where(mine, through, 0.0), axis=1, keepdims=True)
    dweights = sums[...]
    moved = dweights * weights
    last = jnp.sum(moved, axis=0, keepdims=True)
    lanes = lane_index((1, 128))
    for head in range(HLOC):
        total = jnp.sum(
            jnp.sum(products[HP * head : HP * head + HP, :], axis=0, keepdims=True), axis=1, keepdims=True
        )
        last = last + jnp.where(lanes == head, total * decays[head : head + 1, :], 0.0)
    rows = lax.broadcasted_iota(i32, (ROWS, 128), 0)
    dcums = drates[:, 128:256] - moved + jnp.where(rows == ROWS - 1, last, 0.0)
    square = lax.broadcasted_iota(i32, (ROWS, ROWS), 0)
    upper = (square <= lane_index((ROWS, ROWS))).astype(f32)
    dlogs = jnp.dot(upper, dcums, precision=lax.Precision.HIGHEST, preferred_element_type=f32)
    rate = -jnp.exp(params[0:1, :])
    dsteps = drates[:, 0:128] + dweights * gap + dlogs * rate
    ddts = dsteps * sigmoid(dtn[...] + params[1:2, :])
    ddt[...] = ddts
    heads[...] = jnp.zeros((8, 128), f32)
    heads[0:1, :] = jnp.sum(dlogs * rate * rates[:, 0:128], axis=0, keepdims=True)
    heads[1:2, :] = jnp.sum(ddts, axis=0, keepdims=True)
    conv_back(dconv[...], ext, table, small[:, 0:XLOC], work, dxpre, edge, gweight)


def shared_back_kernel(flags, part0, part1, part2, part3, ext, table, small, out, edge, gweight, work):
    grad = part0[...] + part1[...].astype(f32) + part2[...].astype(f32) + part3[...].astype(f32)
    conv_back(grad, ext, table, small[:, XLOC:512], work, out, edge, gweight)
    rank = flags[0]
    of_conv = jnp.where(rank < 4, 0.0, 1.0)
    edge[...] = edge[...] * of_conv
    gweight[...] = gweight[...] * of_conv
    out[...] = jnp.where(rank < 2, turned(grad, table, -1.0), jnp.where(rank < 4, grad, out[...]))


def late_kernel(flags, dxpre, edge_x, dsh, edge_sh, ddt, out):
    for block in range(8):
        own = slice(SHARE * block, SHARE * (block + 1))
        to_rows = pl.ds(local_block(flags, block), SHARE)
        x, sh = dxpre[own, :], dsh[own, :]
        if block == 7:
            pad = jnp.zeros((SHARE - 8, 128), f32)
            sh = sh + jnp.concatenate([pad, edge_sh[...]], axis=0)
            x = x + jnp.concatenate([jnp.zeros((SHARE - 8, XLOC), f32), edge_x[...]], axis=0)
        out[to_rows, 0:XLOC] = x.astype(bf16)
        out[to_rows, 512:LATE] = sh.astype(bf16)
        out[to_rows, XLOC:512] = jnp.where(lane_index((1, 128)) < HLOC, ddt[own, :], 0.0).astype(bf16)


def half_sum_kernel(own, other, keep, send1, send2, send3):
    rows = own.shape[0] // 4
    keep[...] = own[0:rows, :] + other[0:rows, :].astype(f32)
    for index, send in ((1, send1), (2, send2), (3, send3)):
        part = slice(rows * index, rows * (index + 1))
        send[...] = (own[part, :].astype(f32) + other[part, :].astype(f32)).astype(bf16)


def parts_of_sum(own, other, along, sign):
    return parts_from(own, other_core(other), along, sign)


def parts_from(own, got, along, sign):
    rows, width = own.shape[0] // 4, own.shape[1]
    sent = shape_of((rows, width), bf16)
    keep, *sends = run_kernel(half_sum_kernel, [kept((rows, width)), sent, sent, sent], None, own, Columns(got))
    return (keep,) + tuple(along(send, sign * k) for k, send in zip((1, 2, 3), sends))


def split_kernel(*refs):
    lefts, weight, own, other = refs[:-3], refs[-3], refs[-2], refs[-1]
    left = lefts[0][...] if len(lefts) == 1 else jnp.concatenate([ref[...] for ref in lefts], axis=1)
    result = dot_nt(left, weight[...])
    own[...] = result[: ROWS // 2]
    other[...] = result[ROWS // 2 :].astype(bf16)


def summed_rows(lefts, weight):
    model, width = weight.shape
    own, other = pl.pallas_call(
        split_kernel,
        grid=(model // 512,),
        out_shape=(shape_of((ROWS // 2, model)), shape_of((ROWS // 2, model), bf16)),
        in_specs=[pl.BlockSpec(left.shape, lambda i: (0, 0)) for left in lefts]
        + [pl.BlockSpec((512, width), lambda i: (i, 0))],
        out_specs=(
            pl.BlockSpec((ROWS // 2, 512), lambda i: (0, i)),
            pl.BlockSpec((ROWS // 2, 512), lambda i: (0, i)),
        ),
        compiler_params=pltpu.CompilerParams(vmem_limit_bytes=VMEM_LIMIT),
        cost_estimate=pl.CostEstimate(
            flops=2 * ROWS * model * width, bytes_accessed=2 * model * width, transcendentals=0
        ),
    )(*lefts, weight)
    return parts_of_sum(own, other, along_y, 1)


def gate_up_kernel(p0, p1, p2, p3, p4, p5, p6, p7, weight, normed, gate, up, act):
    rows = joined((p0, p1, p2, p3, p4, p5, p6, p7))
    normed[...] = rows
    result = dot_nn(rows, weight[...])
    g, u = result[:, :512], result[:, 512:]
    gate[...] = g
    up[...] = u
    act[...] = (g * sigmoid(g) * u).astype(bf16)


def gate_up_back_kernel(*refs):
    parts, (weight, gate, up, dffn, out) = refs[:-5], refs[-5:]
    rows = joined(parts)
    dffn[...] = rows
    dact = dot_nn(rows, weight[...])
    g = gate[...]
    sig = sigmoid(g)
    out[:, :512] = (dact * up[...] * sig * (1.0 + g * (1.0 - sig))).astype(bf16)
    out[:, 512:] = (dact * g * sig).astype(bf16)


def natural_kernel(flags, p0, p1, p2, p3, p4, p5, p6, p7, out):
    local = joined((p0, p1, p2, p3, p4, p5, p6, p7)).astype(out.dtype)
    for block in range(8):
        out[pl.ds(pl.multiple_of(flags[24 + block] * SHARE, SHARE), SHARE), :] = local[
            SHARE * block : SHARE * (block + 1), :
        ]


def add_norm_kernel(hidden, part0, part1, part2, part3, gain, out_kept, normed, inverse):
    total = hidden[...] + part0[...] + (
        part1[...].astype(f32) + part2[...].astype(f32) + part3[...].astype(f32)
    )
    out_kept[...] = total
    scale = lax.rsqrt(jnp.mean(total * total, axis=1, keepdims=True) + norm_eps)
    inverse[...] = jnp.broadcast_to(scale, inverse.shape)
    normed[...] = (total * scale * gain[...]).astype(bf16)


def add_norm(hidden, parts, gain):
    shape = hidden.shape
    return run_kernel(
        add_norm_kernel,
        [shape_of(shape), shape_of(shape, bf16), shape_of((shape[0], 128))],
        None, hidden, *summands(parts), gain[None],
    )


def output_kernel(hidden, part0, part1, part2, part3, out):
    total = hidden[...] + part0[...] + (
        part1[...].astype(f32) + part2[...].astype(f32) + part3[...].astype(f32)
    )
    out[...] = total.astype(bf16)


def norm_back_kernel(grad, part0, part1, part2, part3, hidden, inverse, gain, out, rounded, ggain):
    received = part0[...] + (part1[...].astype(f32) + part2[...].astype(f32) + part3[...].astype(f32))
    scale = inverse[:, 0:1]
    unit = hidden[...] * scale
    scaled = received * gain[...]
    ggain[...] = jnp.sum(received * unit, axis=0, keepdims=True)
    total = grad[...] + scale * (scaled - unit * jnp.mean(scaled * unit, axis=1, keepdims=True))
    out[...] = total
    rounded[...] = total.astype(bf16)


def norm_back(parts, grad, hidden, inverse, gain):
    shape = hidden.shape
    return run_kernel(
        norm_back_kernel,
        [shape_of(shape), shape_of(shape, bf16), shape_of((1, shape[1]))],
        None, grad, *summands(parts), hidden, inverse, gain[None],
    )


def gradient_kernel(pairs, *refs):
    out, at = refs[-1], 0
    for index in range(pairs):
        left, right = refs[2 * index], refs[2 * index + 1]
        width = right.shape[1]
        out[:, at : at + width] = dot_tn(left[...], right[...]).astype(bf16)
        at += width
    if at < out.shape[1]:
        out[:, at:] = jnp.zeros((out.shape[0], out.shape[1] - at), bf16)


def weight_gradients(pairs, total, block, index, buffer=None):
    rows, model = pairs[0][0].shape
    width = sum(right.shape[1] for _, right in pairs)
    specs, args = [], []
    for left, right in pairs:
        block_right = right.block if isinstance(right, Columns) else 0
        specs += [
            pl.BlockSpec((rows, 512), lambda i: (0, i)),
            pl.BlockSpec(right.shape, lambda i, block=block_right: (0, block)),
        ]
        args += [left, right.array if isinstance(right, Columns) else right]
    aliases = {}
    kernel = partial(gradient_kernel, len(pairs))
    if buffer is not None:
        aliases = {len(args): 0}
        specs.append(pl.BlockSpec(memory_space=pltpu.HBM))
        args.append(buffer)

        def kernel(*refs):
            gradient_kernel(len(pairs), *refs[:-2], refs[-1])

    return pl.pallas_call(
        kernel,
        grid=(model // 512,),
        out_shape=pltpu.HBM((model, total), bf16),
        in_specs=specs,
        out_specs=pl.BlockSpec((512, block), lambda i: (i, index)),
        input_output_aliases=aliases,
        compiler_params=pltpu.CompilerParams(vmem_limit_bytes=VMEM_LIMIT),
        cost_estimate=pl.CostEstimate(
            flops=2 * rows * model * width, bytes_accessed=model * width * 2, transcendentals=0
        ),
    )(*args)


def owned_kernel(pairs, *refs):
    out, at = refs[-1], 0
    for pair in range(pairs):
        left, right = refs[2 * pair], refs[2 * pair + 1]
        result = dot_tn(left[...], right[...]).astype(bf16)
        width = right.shape[1]
        for index in range(2):
            out[index, :, at : at + width] = result[128 * index : 128 * (index + 1)]
        at += width


def insert_kernel(small, block, out):
    mine = lane_index((1, 1, 128)) < HLOC
    out[...] = jnp.where(mine, block[...], small[...][None])


def with_small(owned, small):
    spec = pl.BlockSpec((16, 128, 128), lambda i: (0, 0, XLOC // 128))
    return pl.pallas_call(
        insert_kernel,
        grid=(1,),
        out_shape=pltpu.HBM(owned.shape, bf16),
        in_specs=[pl.BlockSpec((128, 128), lambda i: (0, 0)), spec],
        out_specs=spec,
        input_output_aliases={1: 0},
        compiler_params=pltpu.CompilerParams(vmem_limit_bytes=VMEM_LIMIT),
        cost_estimate=pl.CostEstimate(flops=10**9, bytes_accessed=10**6, transcendentals=0),
    )(small, owned)


def owned_gradients(pairs):
    rows, model = pairs[0][0].shape
    width = sum(right.shape[1] for _, right in pairs)
    specs, args = [], []
    for left, right in pairs:
        block = right.block if isinstance(right, Columns) else 0
        specs += [
            pl.BlockSpec((rows, 256), lambda i: (0, i)),
            pl.BlockSpec(right.shape, lambda i, block=block: (0, block)),
        ]
        args += [left, right.array if isinstance(right, Columns) else right]
    return pl.pallas_call(
        partial(owned_kernel, len(pairs)),
        grid=(model // 256,),
        out_shape=pltpu.HBM((16, model // 16, width), bf16),
        in_specs=specs,
        out_specs=pl.BlockSpec((2, model // 16, width), lambda i: (i, 0, 0)),
        compiler_params=pltpu.CompilerParams(vmem_limit_bytes=VMEM_LIMIT),
        cost_estimate=pl.CostEstimate(
            flops=2 * rows * model * width, bytes_accessed=model * width * 2, transcendentals=0
        ),
    )(*args)


def small_kernel(gain1, gain2, conv_sh, conv_x, heads, skip, out):
    out[...] = jnp.zeros(out.shape, bf16)
    for row in range(16):
        own = slice(128 * row, 128 * row + 128)
        out[row : row + 1, :] = gain1[:, own].astype(bf16)
        out[16 + row : 17 + row, :] = gain2[:, own].astype(bf16)
    out[32:37, :] = conv_sh[0:5, :].astype(bf16)
    for tap in range(CONV + 1):
        for pair in range(PAIRS):
            row = 37 + PAIRS * tap + pair
            out[row : row + 1, :] = conv_x[tap : tap + 1, lanes_of(pair)].astype(bf16)
    out[52:54, :] = heads[0:2, :].astype(bf16)
    lanes = lane_index((1, 128))
    sums = jnp.zeros((1, 128), f32)
    for pair in range(PAIRS):
        part = skip[:, lanes_of(pair)]
        for half in range(2):
            mine = (lanes < HP) if half == 0 else (lanes >= HP)
            total = jnp.sum(jnp.where(mine, part, 0.0), axis=1, keepdims=True)
            sums = sums + jnp.where(lanes == 2 * pair + half, total, 0.0)
    out[54:55, :] = sums.astype(bf16)


def spread_kernel(small, out, work):
    work[...] = small[...].astype(f32)
    columns = work[...].T
    work[56:62, :] = columns[122:128, :]
    out[...] = pltpu.roll(work[...], HLOC, 1).astype(bf16)


def gathered_back(packed, work):
    rolled = pltpu.roll(packed, 128 - HLOC, 1)
    work[...] = jnp.zeros((128, 128), f32)
    work[122:128, :] = rolled[56:62, :]
    return jnp.where(lane_index((1, 128)) < 128 - HLOC, rolled, work[...].T)


def owner_sum(values):
    total = values[0].astype(f32)
    for index in range(1, 16):
        total = total + values[index].astype(f32)
    return total


def block_sum_kernel(values, over_tp, late, conv_x, heads, work):
    whole = owner_sum(values)
    late[...] = whole[:, 0:LATE]
    total = gathered_back(whole[:, XLOC:512], work)
    over_tp[0:128, :] = whole[:, 512:LATE].astype(bf16)
    over_tp[128:256, :] = whole[:, LATE : LATE + 128].astype(bf16)
    over_tp[256:352, :] = jnp.zeros((96, 128), bf16)
    for layer in range(2):
        first = 64 * layer
        over_tp[256 + 48 * layer : 293 + 48 * layer, :] = total[first : first + 37, :].astype(bf16)
        for tap in range(CONV + 1):
            for pair in range(PAIRS):
                row = first + 37 + PAIRS * tap + pair
                conv_x[5 * layer + tap : 5 * layer + tap + 1, lanes_of(pair)] = total[row : row + 1, :]
        heads[3 * layer : 3 * layer + 3, :] = total[first + 52 : first + 55, :]


def weight_outputs_kernel(lower, upper, late, attn, ssm, gate, up, down, query, zx, dt):
    for layer, ref in ((0, lower), (1, upper)):
        for index, out in enumerate((gate, up, down)):
            out[layer] = ref[:, 512 * index : 512 * (index + 1)].astype(f32)
        attn[layer] = ref[:, 1536:1664].astype(f32)
        ssm[layer] = ref[:, 1664:2048].astype(f32)
        zx[layer, :, 0, :] = ref[:, 2048:2432].astype(f32)
        query[layer] = ref[:, 2432:2560].astype(f32)
    zx[0, :, 1, :] = late[:, 0:XLOC]
    zx[1, :, 1, :] = lower[:, 2560:2944].astype(f32)
    dt[0] = late[:, XLOC : XLOC + HLOC]
    dt[1] = lower[:, 2944 : 2944 + HLOC].astype(f32)


def tp_outputs_kernel(flags, *refs):
    parts, (shared, gains1, gains2, conv_bc, every) = refs[:8], refs[8:]
    total = jnp.zeros((96, 128), f32)
    for index, part in enumerate(parts):
        every[index] = part[...].astype(f32)
        total = total + part[256:352, :].astype(f32)
    for layer in range(2):
        for rank in range(8):
            own = slice(128 * rank, 128 * rank + 128)
            shared[layer, :, own] = every[flags[16 + rank], 128 * layer : 128 * layer + 128, :]
        for row in range(16):
            own = slice(128 * row, 128 * row + 128)
            at = 48 * layer + row
            gains1[layer : layer + 1, own] = total[at : at + 1, :]
            gains2[layer : layer + 1, own] = total[at + 16 : at + 17, :]
        for rank in range(4):
            part = every[flags[20 + rank], 288 + 48 * layer : 296 + 48 * layer, :]
            conv_bc[5 * layer : 5 * layer + 5, 128 * rank : 128 * rank + 128] = part[0:5, :]


def body(
    inputs, cotangent, segment_ids, w_query, w_shared, w_zx, w_dt, w_attn_out, w_ssm_out, w_gate, w_up, w_down,
    gains, conv_x, conv_bc, head_params,
):
    layers = w_query.shape[0]
    rank, ctx = lax.axis_index("tp"), lax.axis_index("ctx")
    y, core = rank // 2, rank % 2
    model = inputs.shape[2]

    def local_of(block_y, block_core):
        return jnp.where(block_core == core, 0, 4) + (block_y - y) % 4

    seg_all = segment_ids[0]
    first_row = ctx * ROWS
    padded = jnp.concatenate([jnp.full((CONV - 1,), -1, i32), seg_all])
    seg_ext = lax.dynamic_slice_in_dim(padded, first_row, ROWS + CONV - 1)
    seg_own = seg_ext[CONV - 1 :]
    blocks = seg_all.reshape(SEQ_BLOCKS, ROWS)
    seg_rows = jnp.stack(
        [
            jnp.where(ctx >= back, lax.dynamic_index_in_dim(blocks, jnp.maximum(ctx - back, 0), 0, False), -1)
            for back in range(SEQ_BLOCKS)
        ]
        + [jnp.full((ROWS,), -1, i32)] * 4
    ).astype(f32)
    naturals = jnp.arange(8, dtype=i32)
    flags = jnp.concatenate(
        [
            jnp.stack([rank, y, core, ctx, seg_ext[CONV - 2], seg_own[-1], rank, rank]).astype(i32),
            local_of(naturals % 4, naturals // 4).astype(i32),
            local_of(naturals // 2, naturals % 2).astype(i32),
            (jnp.where(naturals < 4, core, 1 - core) * 4 + (y + naturals) % 4).astype(i32),
        ]
    )

    half_width = HD // 2
    frequency = rope_base ** (-jnp.arange(half_width, dtype=f32) / half_width)
    places = (first_row + jnp.arange(ROWS, dtype=i32)).astype(f32)
    angles = places[:, None] * frequency[None, :]
    cosine, sine = jnp.cos(angles), jnp.sin(angles)
    marks = [seg_ext[tap : tap + ROWS] == seg_own for tap in range(CONV - 1)]
    marks += [seg_own, seg_own == seg_ext[CONV - 2], seg_own == seg_own[-1]]
    marks = jnp.pad(jnp.stack([mark.astype(f32) for mark in marks], axis=1), ((0, 0), (0, 122)))
    table = jnp.concatenate([cosine, cosine, -sine, sine, marks], axis=1)

    own_conv = jnp.maximum(rank - 4, 0) * 128
    small = []
    for layer in range(layers):
        rows = [conv_x[layer], lax.dynamic_slice_in_dim(conv_bc[layer], own_conv, 128, 1)]
        rows.append(jnp.pad(head_params[layer], ((0, 2), (0, 128 - HLOC))))
        small.append(jnp.pad(jnp.concatenate(rows, axis=1), ((0, 3), (0, 0))))

    def packed(*members):
        width = sum(
            {4: 2 * XLOC}.get(member.ndim, 128 if member.shape[2] in (1024, HLOC) else member.shape[2])
            for member, _ in members
        )
        (columns,) = run_kernel(
            pack_kernel,
            [shape_of((w_query.shape[1], width), bf16)],
            rank.astype(i32).reshape(1),
            *(Layer(member, layer) for member, layer in members),
        )
        return lax.all_gather(columns, ("fsdp", "ctx"), axis=0, tiled=True)

    def proj_members(layer):
        return [(member, layer) for member in (w_zx, w_query, w_dt, w_shared)]

    weight_a = packed(*proj_members(0), (w_attn_out, 0), (w_ssm_out, 0))
    weight_b = packed(*proj_members(1), (w_gate, 0), (w_up, 0), (w_down, 0))
    weight_c = packed((w_gate, 1), (w_up, 1), (w_down, 1), (w_attn_out, 1), (w_ssm_out, 1))
    proj_place = [(weight_a, 0, PROJ), (weight_b, 0, PROJ)]
    out_place = [(weight_a, PROJ, 512), (weight_c, 1536, 512)]
    gate_up_place = [(weight_b, PROJ, 1024), (weight_c, 0, 1024)]
    down_place = [(weight_b, PROJ + 1024, 512), (weight_c, 1024, 512)]

    def together(*values):
        return lax.optimization_barrier(values)

    weight_a, table, seg_rows, small = together(weight_a, table, seg_rows, small)
    normed_shape = shape_of((ROWS, model), bf16)
    normed_kept = kept((ROWS, model), bf16)
    normed_b, inverse1, hidden, dffn_b, grad_hidden = run_kernel(
        first_kernel,
        [normed_kept, kept((SHARE, 128)), kept((SHARE, model)), normed_kept, kept((SHARE, model))],
        flags, inputs, cotangent, gains[0],
    )
    weight_a, normed_b = together(weight_a, normed_b)
    proj_place[0] = (weight_a, 0, PROJ)
    out_place[0] = (weight_a, PROJ, 512)
    dffn_parts = (dffn_b,)
    saved = []
    wide = shape_of((ROWS, 512))
    for layer in range(layers):
        if layer == 0:
            z, xs, query, dtn = first_projections(flags, normed_b, weight_a, table)
        else:
            normed_b, z, xs, query, dtn = run_kernel(
                proj_kernel,
                [normed_shape, shape_of((ROWS, XLOC)), wide, shape_of((ROWS, HD), bf16), shape_of((ROWS, 128))],
                flags, *passed(normed_parts), proj_weight, table,
                scratch=[pltpu.VMEM((ROWS, PROJ), f32)], us=3.3,
            )
        halo = along_ctx(xs[ROWS - 8 :], 1)
        shared_own, shared_ext = run_kernel(
            shared_kernel,
            [shape_of((ROWS, 128), bf16), kept((264, 128))],
            flags, xs, Columns(halo), table, small[layer],
        )
        prepared = run_kernel(
            prep_kernel,
            [
                kept((264, XLOC)), shape_of((ROWS, XLOC)), kept((ROWS, XLOC)), shape_of((ROWS, 256)),
                kept((ROWS, 256)), shape_of((16, ROWS)), kept((16, ROWS)),
            ],
            None, xs, dtn, Columns(halo), table, small[layer], us=1.5,
        )
        rows = stashed(f"proj_{layer}", [z, query, dtn] if layer == 0 else [z, query, dtn, normed_b])
        shared_parts, (prepared, rows) = from_all(shared_own, (prepared, rows))
        z_kept, query_kept, dtn_kept = rows[:3]
        if layer > 0:
            normed_b = rows[3]
        x_ext, xc, xc_kept, rates, rates_kept, rates_t, rates_t_kept = prepared
        message, shared = run_kernel(
            state_kernel, [shape_of((KV + MSG, NSTATE), bf16), shape_of((8 * ROWS, 128), bf16)],
            flags, *passed(shared_parts), xc, rates, rates_t, table, us=1.9,
        )
        earlier = tuple(along_ctx(message, back) for back in (1, 2, 3))
        (intra,) = run_kernel(
            intra_kernel, [shape_of((ROWS, XLOC))],
            flags, shared, xc, rates, rates_t, table, seg_rows, small[layer], us=1.3,
        )
        (shared_kept,) = stashed(f"shared_{layer}", [shared])
        if layer > 0:
            earlier, intra, shared_kept = together(earlier, intra, shared_kept)
        else:
            earlier, intra, shared_kept, out_weight = together(
                earlier, intra, shared_kept, fetched(f"out_{layer}", *out_place[layer])
            )
        halves = [Columns(part, 0, NSTATE, rows=KV) for part in earlier]
        (swapped,) = run_kernel(halves_kernel, [shape_of((3 * KV, NSTATE), bf16)], None, *halves)
        state, ssm_y, gated = run_kernel(
            carry_kernel,
            [shape_of((XLOC, NSTATE)), shape_of((ROWS, XLOC)), shape_of((ROWS, XLOC), bf16)],
            flags, *passed(earlier), shared, rates, table, intra, z, us=1.9,
        )
        swapped, gated = together(other_core(swapped), gated)
        attn, log_total, pairs = run_kernel(
            attention_kernel,
            [shape_of((ROWS, HD), bf16), shape_of((ROWS, HD)), shape_of((SEQ_BLOCKS * ROWS, 2 * HD), bf16)],
            flags, query, shared, *halves, Columns(swapped), table, seg_rows, us=2.0,
        )
        if layer > 0:
            out_weight = fetched(f"out_{layer}", *out_place[layer])
        parts = summed_rows([attn, gated], out_weight)
        rows = stashed(f"mixed_{layer}", [attn, gated, log_total, pairs, state, ssm_y])
        parts, rows = together(parts, rows)
        attn_kept, gated_kept, log_total, pairs, state, ssm_y = rows
        if layer > 0:
            parts, gate_up_weight = together(parts, fetched(f"gate_up_{layer}", *gate_up_place[layer]))
        parts, (rows,) = together(parts, restored(f"hidden_{layer}", [hidden]))
        hidden1, normed2, inverse2 = add_norm(rows, parts, gains[layer, 1])
        rows = stashed(f"rows_{layer}", [hidden1, inverse2])
        if layer > 0:
            normed_parts, (down_weight, rows) = from_all(normed2, (fetched("down_1", *down_place[layer]), rows))
        else:
            normed_parts, rows = from_all(normed2, rows)
            gate_up_weight, down_weight = fetched_all("ffn_0", [gate_up_place[layer], down_place[layer]])
        hidden1, inverse2 = rows
        ffn = run_kernel(
            gate_up_kernel, [normed_shape, wide, wide, shape_of((ROWS, 512), bf16)],
            None, *passed(normed_parts), gate_up_weight, us=2.3,
        )
        if layer + 1 < layers:
            parts = summed_rows([ffn[3]], down_weight)
            parts, ffn, (rows,) = together(parts, stashed("ffn_kept", ffn), restored(f"hidden1_{layer}", [hidden1]))
        normed2_b, gate, up, act_b = ffn
        saved.append(
            (
                hidden, normed_b, inverse1, shared_ext, shared_kept, query_kept, x_ext, xc_kept, z_kept, dtn_kept,
                rates_kept, rates_t_kept, pairs, log_total, state, ssm_y, attn_kept, gated_kept, hidden1, inverse2, normed2_b,
                gate, up, act_b,
            )
        )
        if layer + 1 < layers:
            hidden, next_normed, inverse1 = add_norm(rows, parts, gains[layer + 1, 0])
            normed_parts, (proj_weight, rows) = from_all(
                next_normed,
                (fetched("proj_1", *proj_place[layer + 1]), stashed("rows_next", [hidden, inverse1])),
            )
            hidden, inverse1 = rows

    small_parts = [None] * layers
    inner = None
    for layer in reversed(range(layers)):
        (
            hidden, normed_b, inverse1, shared_ext, shared, query, x_ext, xc, z, dtn, rates, rates_t,
            pairs, log_total, state, ssm_y, attn, gated, hidden1, inverse2, normed2_b, gate, up, act_b,
        ) = saved[layer]
        last = layer == 0
        dffn_b, dgate_up = run_kernel(
            gate_up_back_kernel, [normed_shape, shape_of((ROWS, 1024), bf16)],
            None, *passed(dffn_parts), down_weight, *(map(stored, (gate, up)) if last else (gate, up)), us=2.7,
        )
        parts = summed_rows([dgate_up], gate_up_weight)
        outer = weight_gradients(
            [(normed2_b, dgate_up), (dffn_b, act_b)], 3072 if last else 2560, 1536, 0, inner
        )
        parts, outer = lax.optimization_barrier((parts, outer))
        parts, kept_rows = together(parts, restored(f"norm2_{layer}", [grad_hidden, hidden1, inverse2]))
        grad_mid, dmix, ggain2 = norm_back(parts, *kept_rows, gains[layer, 1])
        dmix_parts = from_all(dmix)
        beside = [grad_mid, ggain2] if last else [grad_mid, ggain2, act_b]
        dmix_parts, (fetch, rows) = from_all(
            dmix,
            (
                fetched_all(
                    f"mixer_{layer}",
                    [out_place[layer]]
                    + [
                        (array, 0, array.shape[1])
                        for array in (z, ssm_y, shared, rates, rates_t, xc, query, pairs, state)
                    ],
                ),
                stashed(f"grads_{layer}", beside),
            ),
        )
        grad_mid, ggain2 = rows[:2]
        if not last:
            last_act = rows[2]
        from_kept = [stored(array) for array in (shared, xc, rates, rates_t, state)]
        out_weight, z, ssm_y, shared, rates, rates_t, xc, query, pairs, state = fetch
        dmix_b, dattn, dy, dz, message = run_kernel(
            gate_back_kernel,
            [
                normed_kept, shape_of((ROWS, HD), bf16), shape_of((ROWS, XLOC)), shape_of((ROWS, XLOC), bf16),
                shape_of((MSG, NSTATE), bf16),
            ],
            flags, *passed(dmix_parts), out_weight, z, ssm_y, shared, rates, rates_t, table, us=2.6,
            scratch=[pltpu.VMEM((ROWS, XLOC), f32), pltpu.VMEM((ROWS, 512), f32)],
        )
        after = tuple(along_ctx(message, -ahead) for ahead in (1, 2, 3))
        early, mine, theirs = run_kernel(
            attention_back_kernel,
            [kept((ROWS, 512), bf16), shape_of((4 * ROWS, HD)), shape_of((4 * ROWS, HD), bf16)],
            flags, dattn, dz, query, pairs, stored(log_total), table, seg_rows, us=2.9,
        )
        got = other_core(theirs)
        dx, dshared, drates, dskip = run_kernel(
            intra_back_kernel,
            [kept((ROWS, XLOC)), kept((ROWS, 2 * NSTATE)), kept((ROWS, 256)), kept((1, XLOC))],
            flags, dy, xc, shared, rates, rates_t, table, seg_rows, state, small[layer], us=3.6,
            scratch=[pltpu.VMEM((128, ROWS), f32), pltpu.VMEM((ROWS, 128), f32)],
        )
        dkv = parts_from(mine, got, along_ctx, -1)
        width = outer.shape[1]
        outer = weight_gradients([(dmix_b, attn), (dmix_b, gated)], width, 512, 3, outer)
        outer = weight_gradients([(normed_b, early)], width, 512, 4, outer)
        if last:
            after, dkv, outer, dx, upper = together(after, dkv, outer, dx, upper)
            lower = lax.psum_scatter(outer, ("fsdp", "ctx"), scatter_dimension=0, tiled=True)
        else:
            after, dkv, outer, dx = together(after, dkv, outer, dx)
            upper = lax.psum_scatter(outer, ("fsdp", "ctx"), scatter_dimension=0, tiled=True)
        packed_grads, state_grad = run_kernel(
            packed_back_kernel, [shape_of((8 * ROWS, 128), bf16), kept((XLOC, NSTATE))],
            flags, *map(stored, after), *from_kept[:3], table, stored(dshared), *map(stored, dkv), us=2.5,
        )
        dshared_parts = parts_of_sum(packed_grads[: 4 * ROWS], packed_grads[4 * ROWS :], along_y, 1)
        dxpre, edge_x, gconv_x, ddt, gheads = run_kernel(
            state_back_kernel,
            [kept((ROWS, XLOC)), shape_of((8, XLOC)), kept((8, XLOC)), kept((ROWS, 128)), kept((8, 128))],
            flags, stored(state_grad), *from_kept[:4], table, from_kept[4], stored(small[layer]),
            stored(dtn), stored(dx), stored(drates), stored(x_ext),
            scratch=[pltpu.VMEM((272, XLOC), f32), pltpu.VMEM((ROWS, XLOC), f32), pltpu.VMEM((ROWS, 128), f32)],
            us=3.5,
        )
        dshared_parts, edge_x = together(dshared_parts, edge_x)
        edge_x = along_ctx(edge_x, -1)
        dsh, edge_sh, gconv_sh = run_kernel(
            shared_back_kernel,
            [shape_of((ROWS, 128)), shape_of((8, 128)), kept((8, 128))],
            flags, *summands(dshared_parts), stored(shared_ext), table, small[layer],
            scratch=[pltpu.VMEM((272, 128), f32)],
        )
        edge_sh, proj_weight = together(
            along_ctx(edge_sh, -1), fetched(f"proj_again_{layer}", *proj_place[layer])
        )
        (late,) = run_kernel(
            late_kernel, [shape_of((ROWS, LATE), bf16)], flags, stored(dxpre), Columns(edge_x), dsh,
            Columns(edge_sh), stored(ddt),
        )
        parts = summed_rows([early, late], proj_weight)
        if not last:
            inner = weight_gradients([(normed_b, Columns(late, 0, 512))], 3072, 512, 5)
            parts, inner = together(parts, inner)
            upper_pair = (normed_b, Columns(late, 4, 128))
        else:
            parts, owned = together(parts, owned_gradients([(normed_b, late), upper_pair]))
        parts, kept_rows = together(parts, restored(f"norm1_{layer}", [grad_mid, hidden, inverse1]))
        grad_hidden, rounded, ggain1 = norm_back(parts, *kept_rows, gains[layer, 0])
        if last:
            dffn_parts = from_all(rounded)
        else:
            dffn_parts, ((down_weight, gate_up_weight), (grad_hidden, ggain1)) = from_all(
                rounded,
                (
                    fetched_all("ffn_again", [down_place[layer - 1], gate_up_place[layer - 1]]),
                    stashed("grads_next", [grad_hidden, ggain1]),
                ),
            )
            last_hidden1 = hidden1
        (small_parts[layer],) = run_kernel(
            small_kernel, [shape_of((64, 128), bf16)],
            None, ggain1, *map(stored, (ggain2, gconv_sh, gconv_x, gheads, dskip)),
        )
    (small_all,) = run_kernel(
        spread_kernel, [shape_of((128, 128), bf16)], None, jnp.concatenate(small_parts, axis=0),
        scratch=[pltpu.VMEM((128, 128), f32)],
    )
    owned = lax.all_to_all(with_small(owned, small_all), ("fsdp", "ctx"), 0, 0, tiled=True)
    (input_grad,) = run_kernel(natural_kernel, [kept((ROWS, model))], flags, *passed(dffn_parts))
    last_act, down_weight, _ = together(last_act, fetched("down_last", *down_place[1]), small_parts[0])
    (layer_out,) = run_kernel(
        output_kernel, [shape_of((SHARE, model), bf16)], None,
        stored(last_hidden1), *summands(summed_rows([last_act], down_weight)),
    )
    (layer_out,) = run_kernel(natural_kernel, [normed_kept], flags, *passed(from_all(layer_out)))
    def pair_of(width):
        return shape_of((layers, model // 16, width))

    owned, layer_out, input_grad = together(owned, layer_out, input_grad)
    over_tp, late_sum, gconv_x, gheads = run_kernel(
        block_sum_kernel,
        [
            shape_of((352, 128), bf16), kept((model // 16, LATE)), shape_of((layers * (CONV + 1), XLOC)),
            shape_of((8, 128)),
        ],
        None, Columns(owned),
        scratch=[pltpu.VMEM((128, 128), f32)],
    )
    grad_shared, ggains1, ggains2, gconv_bc = run_kernel(
        tp_outputs_kernel,
        [
            pair_of(1024), shape_of((layers, model)), shape_of((layers, model)),
            shape_of((layers * (CONV + 1), 512)),
        ],
        flags, *passed(from_all(over_tp)),
        scratch=[pltpu.VMEM((8, 352, 128), f32)], us=2.0,
    )
    lower, grad_shared = together(lower, grad_shared)
    grad_attn, grad_ssm, grad_gate, grad_up, grad_down, grad_query, grad_zx, grad_dt = run_kernel(
        weight_outputs_kernel,
        [
            *(kept((layers, model // 16, width)) for width in (128, 384, 512, 512, 512, 128)),
            shape_of((layers, model // 16, 2, XLOC)), pair_of(HLOC),
        ],
        None, stored(lower), stored(upper), stored(late_sum), us=3.0,
    )
    gconv_x = gconv_x.reshape(layers, CONV + 1, XLOC)
    gconv_bc = gconv_bc.reshape(layers, CONV + 1, 512)
    gheads = gheads[: 3 * layers].reshape(layers, 3, 128)[:, :, :HLOC]
    return (
        layer_out[None],
        input_grad[None],
        grad_query,
        grad_shared,
        grad_zx,
        grad_dt,
        grad_attn,
        grad_ssm,
        grad_gate,
        grad_up,
        grad_down,
        ggains1,
        gconv_x,
        gconv_bc,
        gheads[:, :2],
        ggains2,
        gheads[:, 2],
    )


def solution(mesh):
    columns = P(None, ("fsdp", "ctx"), "tp")
    rows = P("fsdp", "ctx", None)
    return jax.shard_map(
        body,
        mesh=mesh,
        in_specs=(
            rows, rows, P("fsdp", None), columns, P(None, ("fsdp", "ctx"), None),
            P(None, ("fsdp", "ctx"), None, "tp"), columns, columns, columns, columns, columns, columns,
            P(), P(None, None, "tp"), P(), P(None, None, "tp"),
        ),
        out_specs=(
            rows, rows, columns, P(None, ("fsdp", "ctx"), None), P(None, ("fsdp", "ctx"), None, "tp"),
            columns, columns, columns, columns, columns, columns,
            P(), P(None, None, "tp"), P(), P(None, None, "tp"), P(), P(None, "tp"),
        ),
        check_vma=False,
    )
```
